32 devices in a mesh: dp: 2 (over x), seq: 8 (over z, y), tensor: 2 (over core).
Axes of the slice: x: 2, y: 2, z: 4, core: 2. Of those that a mesh axis runs over, the one named last changes fastest.
Arguments:
- tokens: bfloat16 [2, 4096, 1536], P('dp', ('seq', 'tensor')), may hold values from -6 to 6
- cotangent: bfloat16 [2, 4096, 1536], P('dp', ('seq', 'tensor')), may hold values from -6 to 6
- positions: int32 [2, 4096], P('dp', 'seq'), may hold values from 0 to 4095, as said below
- adapter_choice: int32 [2], replicated, may hold values from 0 to 7
- attn_gain: bfloat16 [1536], replicated, may hold values from 0.25 to 1.75
- query_weight: bfloat16 [1536, 1536], P(None, 'tensor'), may hold values from -0.21875 to 0.21875
- query_bias: bfloat16 [1536], P('tensor'), may hold values from -4 to 4
- key_value_weight: bfloat16 [2, 1536, 256], P(None, None, 'tensor'), may hold values from -0.21875 to 0.21875
- key_value_bias: bfloat16 [2, 256], P(None, 'tensor'), may hold values from -4 to 4
- output_weight: bfloat16 [1536, 1536], P('tensor'), may hold values from -0.875 to 0.875
- ffn_gain: bfloat16 [1536], replicated, may hold values from 0.25 to 1.75
- gate_upper_weight: bfloat16 [2, 1536, 8960], P(None, None, 'tensor'), may hold values from -0.15625 to 0.15625
- down_weight: bfloat16 [8960, 1536], P('tensor'), may hold values from -0.0625 to 0.0625
- adapt_in: bfloat16 [8, 16, 18176], P(None, None, ('dp', 'seq', 'tensor')), may hold values from -0.15625 to 0.15625
- adapt_out: bfloat16 [8, 16, 23040], P(None, None, ('dp', 'seq', 'tensor')), may hold values from -0.75 to 0.75
Outputs:
- output: bfloat16 [2, 4096, 1536], P('dp', ('seq', 'tensor'))
- token_grad: float32 [2, 4096, 1536], P('dp', ('seq', 'tensor'))
- adapt_in_grad: float32 [8, 16, 18176], P(None, None, ('dp', 'seq', 'tensor'))
- adapt_out_grad: float32 [8, 16, 23040], P(None, None, ('dp', 'seq', 'tensor'))
The draws below stay inside these ranges and needn't reach their ends.
Inputs may be any that keep to these rules, and one draw needn't show every extreme that they name: Each row holds every position of 0 to 4095 once. Cut the positions into 16 runs of 256 consecutive ones; the j-th stored group of 512 tokens holds run k and then run 2 * 8 - 1 - k, each ascending, for a k that differs from group to group.
All inputs are finite; a program needn't handle non-finite values.
Results may differ from the reference program's by a relative error of at most 0.02.
Values may be sent and summed in bfloat16 or wider, within the bound.
No kernel may reach another device: no remote copies, remote signals or barrier semaphores. Data moves between devices by JAX's collectives and lax.ppermute only.
A program may use at most 448 MiB of HBM per device.

```python
import jax
import jax.numpy as jnp
from jax import lax

MODEL_WIDTH = 1536
HEADS = 12
KV_HEADS = 2
HEAD_DIM = 128
HIDDEN_UNITS = 8960
RANK = 16
ADAPTERS = 8
TOK_SEQ = 512
SEQS = 2
LEN = 4096
KV_WIDTH = 256
ADAPT_IN = 18176
ADAPT_OUT = 23040


def draw_positions(key, part):
    key = jax.random.fold_in(key, 7)
    block_count = LEN // TOK_SEQ
    half_rows = TOK_SEQ // 2
    seq_rows = []
    for seq_index in range(SEQS):
        order_draw = jax.random.permutation(jax.random.fold_in(key, seq_index), block_count)
        block_pairs = jnp.stack([order_draw, 2 * block_count - 1 - order_draw], axis=1).reshape(-1)
        position = block_pairs[:, None] * half_rows + jnp.arange(half_rows)[None, :]
        seq_rows.append(position.reshape(-1))
    return jnp.stack(seq_rows).astype(jnp.int32)


def steps_of(rng, extent, cuts, least, high):
    factor_of, own = 1.0, jax.random.fold_in(rng, 6)
    for axis_at, blocks in cuts:
        heights = jnp.exp(jax.random.uniform(jax.random.fold_in(own, axis_at), (blocks,), jnp.float32, least / len(cuts), high / len(cuts)))
        factor_of = factor_of * jnp.repeat(heights, extent[axis_at] // blocks).reshape([-1 if axis == axis_at else 1 for axis in range(len(extent))])
    return factor_of


def gaussian(stream_key, extent, deviation, limit, shards=(), kind=jnp.bfloat16):
    drawn = deviation * jax.random.normal(stream_key, extent, jnp.float32)
    if shards:
        drawn = drawn * steps_of(stream_key, extent, shards, -0.22, 0.18)
    return jnp.clip(drawn, -limit, limit).astype(kind)


def setup_inputs(seed: int = 0) -> dict:
    streams_of = jax.random.split(jax.random.key(seed), 16)
    return {
        "tokens": gaussian(streams_of[0], (SEQS, LEN, MODEL_WIDTH), 1.0, 6.0, ((0, 2), (1, 16))),
        "cotangent": gaussian(streams_of[1], (SEQS, LEN, MODEL_WIDTH), 1.0, 6.0, ((0, 2), (1, 16))),
        "positions": draw_positions(jax.random.fold_in(streams_of[15], 71), 0),
        "adapter_choice": jax.random.randint(streams_of[3], (SEQS,), 0, ADAPTERS).astype(jnp.int32),
        "attn_gain": jnp.clip(1.0 + 0.15 * jax.random.normal(streams_of[4], (MODEL_WIDTH,), jnp.float32), 0.25, 1.75).astype(jnp.bfloat16),
        "query_weight": gaussian(streams_of[5], (MODEL_WIDTH, MODEL_WIDTH), (MODEL_WIDTH // 2) ** -0.5, 0.21875, ((1, 2),)),
        "query_bias": gaussian(streams_of[6], (MODEL_WIDTH,), 0.3, 4.0, ((0, 2),)),
        "key_value_weight": gaussian(streams_of[7], (2, MODEL_WIDTH, KV_WIDTH), (MODEL_WIDTH // 2) ** -0.5, 0.21875, ((2, 2),)),
        "key_value_bias": gaussian(streams_of[8], (2, KV_WIDTH), 0.3, 4.0, ((1, 2),)),
        "output_weight": gaussian(streams_of[9], (MODEL_WIDTH, MODEL_WIDTH), (MODEL_WIDTH // 32) ** -0.5, 0.875, ((0, 2),)),
        "ffn_gain": jnp.clip(1.0 + 0.15 * jax.random.normal(streams_of[10], (MODEL_WIDTH,), jnp.float32), 0.25, 1.75).astype(jnp.bfloat16),
        "gate_upper_weight": gaussian(streams_of[11], (2, MODEL_WIDTH, HIDDEN_UNITS), MODEL_WIDTH ** -0.5, 0.15625, ((2, 2),)),
        "down_weight": gaussian(streams_of[12], (HIDDEN_UNITS, MODEL_WIDTH), HIDDEN_UNITS ** -0.5, 0.0625, ((0, 2),)),
        "adapt_in": gaussian(streams_of[13], (ADAPTERS, RANK, ADAPT_IN), MODEL_WIDTH ** -0.5, 0.15625, ((2, 32),)),
        "adapt_out": gaussian(streams_of[14], (ADAPTERS, RANK, ADAPT_OUT), 0.05, 0.75, ((2, 32),)),
    }


eps = 1e-06
adapter_scale = 2.0
rope_base = 1000000.0
mask_fill = -1e+30
highest = lax.Precision.HIGHEST

@jax.custom_vjp
def low(v):
    return lax.optimization_barrier(v.astype(jnp.bfloat16)).astype(jnp.float32)

@jax.custom_vjp
def lowrank_backtrack(v):
    return v

def low_keep(v):
    return (low(v), None)

def low_pass(kept, grad):
    return (grad,)

def back_keep(v):
    return (v, None)

def back_low(kept, grad):
    return (low(grad),)
low.defvjp(low_keep, low_pass)
lowrank_backtrack.defvjp(back_keep, back_low)

def matrix_multiply(left_side, right_side):
    return jnp.dot(left_side, right_side, precision=highest)

def norm_rows(value_rows, gain):
    return value_rows * lax.rsqrt(lax.optimization_barrier(jnp.mean(value_rows * value_rows, axis=-1, keepdims=True)) + eps) * gain

def rope_tables(token_pos):
    frequency = jnp.power(rope_base, -(jnp.arange(HEAD_DIM // 2, dtype=jnp.float32) * 2.0) / HEAD_DIM)
    angles = token_pos.astype(jnp.float32)[:, None] * frequency[None, :]
    return (jnp.cos(angles), jnp.sin(angles))

def rotate(value_rows, cosine_table, sine_table):
    half_dim = value_rows.shape[-1] // 2
    front_half = value_rows[..., :half_dim]
    back_half = value_rows[..., half_dim:]
    return jnp.concatenate([front_half * cosine_table - back_half * sine_table, back_half * cosine_table + front_half * sine_table], axis=-1)

def attend(queries, keys_rot, values_low, token_pos):
    group_size = HEADS // KV_HEADS
    block_rows = 512 if LEN % 512 == 0 else LEN
    query_blocks = queries.reshape(LEN // block_rows, block_rows, KV_HEADS, group_size, HEAD_DIM)
    pos_blocks = token_pos.reshape(LEN // block_rows, block_rows)

    def one_block(pair_in):
        query_part, query_pos = pair_in
        scores = lowrank_backtrack(jnp.einsum('qkgd,skd->kgqs', query_part, keys_rot, precision=highest) * HEAD_DIM ** (-0.5))
        allowed = token_pos[None, :] <= query_pos[:, None]
        scores = jnp.where(allowed[None, None], scores, mask_fill)
        weights = jax.nn.softmax(scores, axis=-1)
        return jnp.einsum('kgqs,skd->qkgd', low(weights), values_low, precision=highest)
    blended_rows = lax.map(jax.checkpoint(one_block), (query_blocks, pos_blocks))
    return blended_rows.reshape(LEN, HEADS * HEAD_DIM)

def layer(inputs, down_sel, up_sel, token_pos, params):
    attn_gain, query_weight, query_bias, key_value_weight, key_value_bias, output_weight, ffn_gain, gate_upper_weight, down_weight = params
    key_value_width = KV_HEADS * HEAD_DIM
    upper_baseline = 2 * MODEL_WIDTH + 2 * key_value_width

    def lowrank_adapter(value_rows, lower_begin, lower_length, upper_begin, upper_length):
        lower_portion = down_sel[:, lower_begin:lower_begin + lower_length]
        upper_portion = up_sel[:, upper_begin:upper_begin + upper_length]
        return adapter_scale * matrix_multiply(matrix_multiply(value_rows, lower_portion.T), upper_portion)
    normalized_rows = low(norm_rows(inputs, attn_gain))
    query_projected = lowrank_backtrack(matrix_multiply(normalized_rows, query_weight) + query_bias + lowrank_adapter(normalized_rows, 0, MODEL_WIDTH, 0, MODEL_WIDTH))
    key_projected = lowrank_backtrack(matrix_multiply(normalized_rows, key_value_weight[0]) + key_value_bias[0] + lowrank_adapter(normalized_rows, MODEL_WIDTH, MODEL_WIDTH, MODEL_WIDTH, key_value_width))
    value_projected = lowrank_backtrack(matrix_multiply(normalized_rows, key_value_weight[1]) + key_value_bias[1] + lowrank_adapter(normalized_rows, 2 * MODEL_WIDTH, MODEL_WIDTH, MODEL_WIDTH + key_value_width, key_value_width))
    cosine_table, sine_table = rope_tables(token_pos)
    query_rot = low(rotate(query_projected.reshape(LEN, HEADS, HEAD_DIM), cosine_table[:, None], sine_table[:, None]))
    key_rot = low(rotate(key_projected.reshape(LEN, KV_HEADS, HEAD_DIM), cosine_table[:, None], sine_table[:, None]))
    value_low = low(value_projected).reshape(LEN, KV_HEADS, HEAD_DIM)
    blended_rows = low(lowrank_backtrack(attend(query_rot, key_rot, value_low, token_pos)))
    branch_result = lowrank_backtrack(matrix_multiply(blended_rows, output_weight) + lowrank_adapter(blended_rows, 3 * MODEL_WIDTH, MODEL_WIDTH, MODEL_WIDTH + 2 * key_value_width, MODEL_WIDTH))
    hidden_rows = inputs + branch_result
    normalized_feedforward = low(norm_rows(hidden_rows, ffn_gain))
    gate_projected = lowrank_backtrack(matrix_multiply(normalized_feedforward, gate_upper_weight[0]) + lowrank_adapter(normalized_feedforward, 4 * MODEL_WIDTH, MODEL_WIDTH, upper_baseline, HIDDEN_UNITS))
    upward_rows = lowrank_backtrack(matrix_multiply(normalized_feedforward, gate_upper_weight[1]) + lowrank_adapter(normalized_feedforward, 5 * MODEL_WIDTH, MODEL_WIDTH, upper_baseline + HIDDEN_UNITS, HIDDEN_UNITS))
    activated_rows = low(jax.nn.silu(gate_projected) * upward_rows)
    return hidden_rows + lowrank_backtrack(matrix_multiply(activated_rows, down_weight) + lowrank_adapter(activated_rows, 6 * MODEL_WIDTH, HIDDEN_UNITS, upper_baseline + 2 * HIDDEN_UNITS, MODEL_WIDTH))

def reference(tokens, cotangent, positions, adapter_choice, attn_gain, query_weight, query_bias, key_value_weight, key_value_bias, output_weight, ffn_gain, gate_upper_weight, down_weight, adapt_in, adapt_out):
    params = tuple((entry_value.astype(jnp.float32) for entry_value in (attn_gain, query_weight, query_bias, key_value_weight, key_value_bias, output_weight, ffn_gain, gate_upper_weight, down_weight)))
    grad_in = jnp.zeros((ADAPTERS, RANK, ADAPT_IN), jnp.float32)
    grad_out = jnp.zeros((ADAPTERS, RANK, ADAPT_OUT), jnp.float32)
    outputs = []
    token_grads = []
    for seq_index in range(SEQS):
        chosen = adapter_choice[seq_index]
        down_sel = adapt_in[chosen].astype(jnp.float32)
        up_sel = adapt_out[chosen].astype(jnp.float32)
        seq_pos = positions[seq_index]

        def forward(inputs, lower_portion, upper_portion):
            return layer(inputs, lower_portion, upper_portion, seq_pos, params)
        result, pullback = jax.vjp(forward, tokens[seq_index].astype(jnp.float32), down_sel, up_sel)
        grad_tokens, grad_down, grad_up = pullback(cotangent[seq_index].astype(jnp.float32))
        picked = (jnp.arange(ADAPTERS) == chosen).astype(jnp.float32)
        grad_in = grad_in + picked[:, None, None] * grad_down[None]
        grad_out = grad_out + picked[:, None, None] * grad_up[None]
        outputs.append(result.astype(jnp.bfloat16))
        token_grads.append(grad_tokens)
    factor_total = (SEQS * LEN) ** (-0.5)
    return (jnp.stack(outputs), jnp.stack(token_grads), grad_in * factor_total, grad_out * factor_total)
```

```python
import functools
import math

import jax
import jax.numpy as jnp
from jax import lax
from jax.experimental import pallas as pl
from jax.experimental.pallas import tpu as pltpu
from jax.sharding import PartitionSpec as P

HEAD_DIM = 128
RANK = 16
eps = 1e-06
adapter_scale = 2.0
rope_base = 1000000.0
mask_fill = -1e30
bf = jnp.bfloat16
f32 = jnp.float32
VM = pl.BlockSpec(memory_space=pltpu.VMEM)
SM = pl.BlockSpec(memory_space=pltpu.SMEM)


def nn(a, b):
    return jnp.dot(a, b, preferred_element_type=f32)


def nt(a, b):
    return lax.dot_general(a, b, (((1,), (1,)), ((), ())), preferred_element_type=f32)


def shape(*dims, dtype=f32):
    return jax.ShapeDtypeStruct(dims, dtype)


def call(kernel, name, out, ins, scratch=(), flops=0, smem=1, out_specs=None):
    moved = sum(math.prod(v.shape) * v.dtype.itemsize for v in list(ins) + list(out))
    return pl.pallas_call(
        kernel,
        out_shape=tuple(out),
        in_specs=[SM] * smem + [VM] * (len(ins) - smem),
        out_specs=out_specs or (VM,) * len(out),
        scratch_shapes=list(scratch),
        cost_estimate=pl.CostEstimate(flops=flops, bytes_accessed=moved, transcendentals=0),
        compiler_params=pltpu.CompilerParams(vmem_limit_bytes=56 << 20),
        name=name,
    )(*ins)


def rounded_up(value, unit):
    return -(-value // unit) * unit


def select_kernel(lanes_in, meta_ref, in_ref, out_ref, own_ref, other_ref):
    wide_in, wide_out = in_ref.shape[2], out_ref.shape[2]
    run = jnp.full((RANK, lanes_in), meta_ref[2], jnp.int32).astype(f32).astype(bf)
    for target, slot in ((own_ref, 0), (other_ref, 1)):
        chosen = meta_ref[slot]
        target[...] = jnp.zeros_like(target)
        target[:, :lanes_in] = run
        target[:, :wide_in] = in_ref[chosen]
        target[:, lanes_in : lanes_in + wide_out] = out_ref[chosen]


def unpack_kernel(
    groups, wide_in, wide_out, lanes_in, widths, meta_ref, own_ref, pair_ref,
    flags_ref, adqkv, auq, auk, auv, ado, auo, adgu, augu, adf, auf, slots, ad, au,
):
    dp, seq, shard = meta_ref[0], meta_ref[1], meta_ref[2]
    width, head_width, hidden = widths
    rings = groups // 2
    lanes = own_ref.shape[-1]
    ring, side = seq // 2, seq % 2
    own_run = jnp.max(own_ref[0, 0, :, wide_in:lanes_in].astype(f32))
    for place in range(groups):
        source_ring = lax.rem(ring - place // 2 + rings, rings)
        source_side = side if place % 2 == 0 else 1 - side
        source = source_ring * 2 + source_side
        run = jnp.max(own_ref[place, 0, :, wide_in:lanes_in].astype(f32))
        flags_ref[place] = (run < own_run).astype(jnp.int32)
        for core, ref in ((shard, own_ref), (1 - shard, pair_ref)):
            for part, row in ((0, dp), (1, 1 - dp)):
                slots[row * 2 * groups + source * 2 + core] = ref[place, part]
    ad[...] = jnp.zeros_like(ad)
    au[...] = jnp.zeros_like(au)
    for target, begin, wide in ((ad, 0, wide_in), (au, lanes_in, wide_out)):
        held = rounded_up(wide, 128)
        span = held + 128
        inside = lax.broadcasted_iota(jnp.int32, (RANK, held), 1) < wide
        for index in range(4 * groups):
            part = jnp.where(inside, slots[index, :, begin : begin + held].astype(f32), 0.0)
            part = jnp.concatenate([part, jnp.zeros((RANK, 128), f32)], axis=1)
            offset = index * wide
            base = offset // 128 * 128
            if offset != base:
                part = pltpu.roll(part, offset - base, 1)
            target[:, base : base + span] += part

    def column(begin, size):
        return pl.ds(pl.multiple_of(begin, 128), size)

    for index in range(3):
        adqkv[index * RANK : (index + 1) * RANK, :] = ad[:, index * width : (index + 1) * width].astype(bf)
    ado[...] = ad[:, column(3 * width + shard * head_width, head_width)].astype(bf)
    for index in range(2):
        adgu[index * RANK : (index + 1) * RANK, :] = ad[:, (4 + index) * width : (5 + index) * width].astype(bf)
    adf[...] = ad[:, column(6 * width + shard * hidden, hidden)].astype(bf)
    auq[...] = au[:, column(shard * head_width, head_width)].astype(bf)
    auk[...] = au[:, column(width + shard * HEAD_DIM, HEAD_DIM)].astype(bf)
    auv[...] = au[:, column(width + (2 + shard) * HEAD_DIM, HEAD_DIM)].astype(bf)
    base = width + 4 * HEAD_DIM
    auo[...] = au[:, base : base + width].astype(bf)
    base = base + width
    for index in range(2):
        augu[index * RANK : (index + 1) * RANK, :] = au[
            :, column(base + (2 * index + shard) * hidden, hidden)
        ].astype(bf)
    auf[...] = au[:, base + 4 * hidden : base + 4 * hidden + width].astype(bf)


def pack_kernel(
    groups, wide_in, wide_out, lanes_in, widths, meta_ref,
    dadqkv, dauq, dauk, dauv, dado, dauo, dadgu, daugu, dadf, dauf,
    keep_ref, send_ref, ad, au,
):
    dp, seq, shard = meta_ref[0], meta_ref[1], meta_ref[2]
    width, head_width, hidden = widths
    rings = groups // 2
    ring, side = seq // 2, seq % 2

    def column(begin, size):
        return pl.ds(pl.multiple_of(begin, 128), size)

    ad[...] = jnp.zeros_like(ad)
    au[...] = jnp.zeros_like(au)
    for index in range(3):
        ad[:, index * width : (index + 1) * width] = dadqkv[index * RANK : (index + 1) * RANK, :]
    ad[:, column(3 * width + shard * head_width, head_width)] = dado[...]
    for index in range(2):
        ad[:, (4 + index) * width : (5 + index) * width] = dadgu[index * RANK : (index + 1) * RANK, :]
    ad[:, column(6 * width + shard * hidden, hidden)] = dadf[...]
    au[:, column(shard * head_width, head_width)] = dauq[...]
    au[:, column(width + shard * HEAD_DIM, HEAD_DIM)] = dauk[...]
    au[:, column(width + (2 + shard) * HEAD_DIM, HEAD_DIM)] = dauv[...]
    base = width + 4 * HEAD_DIM
    au[:, base : base + width] = dauo[...]
    base = base + width
    for index in range(2):
        au[:, column(base + (2 * index + shard) * hidden, hidden)] = daugu[index * RANK : (index + 1) * RANK, :]
    au[:, base + 4 * hidden : base + 4 * hidden + width] = dauf[...]
    lanes = keep_ref.shape[-1]
    for index in range(4 * groups):
        to_dp, to_seq, to_core = index // (2 * groups), index // 2 % groups, index % 2
        parts = []
        for source, wide in ((ad, wide_in), (au, wide_out)):
            held = rounded_up(wide, 128)
            offset = index * wide
            base = offset // 128 * 128
            part = source[:, base : base + held + 128]
            if offset != base:
                part = pltpu.roll(part, held + 128 - (offset - base), 1)
            parts.append(part[:, :held])
            if source is ad and lanes_in > held:
                parts.append(jnp.zeros((RANK, lanes_in - held), f32))
        packed = jnp.concatenate(parts, axis=1).astype(bf)
        place = lax.rem(ring - to_seq // 2 + rings, rings)
        row = lax.rem(side + to_seq % 2, 2)
        part = lax.rem(dp + to_dp, 2)

        @pl.when(shard == to_core)
        def kept():
            keep_ref[row, place, part] = packed

        @pl.when(shard != to_core)
        def sent():
            send_ref[row, place, part] = packed


def place_kernel(lanes_in, factor, meta_ref, own_ref, other_ref, in_ref, out_ref):
    wide_in, wide_out = in_ref.shape[2], out_ref.shape[2]
    in_ref[...] = jnp.zeros_like(in_ref)
    out_ref[...] = jnp.zeros_like(out_ref)
    for source, slot in ((own_ref, 0), (other_ref, 1)):
        chosen = meta_ref[slot]
        part = source[...].astype(f32) * factor
        in_ref[chosen] = in_ref[chosen] + part[:, :wide_in]
        out_ref[chosen] = out_ref[chosen] + part[:, lanes_in : lanes_in + wide_out]


def factor_of(rows):
    return lax.rsqrt(jnp.mean(rows * rows, axis=-1, keepdims=True) + eps)


def norm_back(rows, gain, grad):
    factor = factor_of(rows)
    scaled = rows * factor
    grad_scaled = grad * gain
    return factor * (grad_scaled - scaled * jnp.mean(grad_scaled * scaled, axis=-1, keepdims=True))


def norm_kernel(rows_ref, gain_ref, normed_ref):
    rows = rows_ref[...].astype(f32)
    normed_ref[...] = (rows * factor_of(rows) * gain_ref[...].astype(f32)).astype(bf)


def residual_kernel(rows_ref, own_ref, other_ref, gain_ref, hidden_ref, normed_ref):
    rows = rows_ref[...].astype(f32) + (own_ref[...] + other_ref[...].astype(f32))
    hidden_ref[...] = rows
    normed_ref[...] = (rows * factor_of(rows) * gain_ref[...].astype(f32)).astype(bf)


def hidden_back_kernel(hidden_ref, grad_ref, own_ref, other_ref, gain_ref, out_ref, low_ref):
    grad = own_ref[...] + other_ref[...].astype(f32)
    total = grad_ref[...].astype(f32) + norm_back(hidden_ref[...], gain_ref[...].astype(f32), grad)
    out_ref[...] = total
    low_ref[...] = total.astype(bf)


def token_back_kernel(rows_ref, grad_ref, own_ref, other_ref, gain_ref, out_ref):
    grad = own_ref[...] + other_ref[...].astype(f32)
    out_ref[...] = grad_ref[...] + norm_back(rows_ref[...].astype(f32), gain_ref[...].astype(f32), grad)


def turned(rows, cosine, sine):
    return rows * cosine + pltpu.roll(rows, HEAD_DIM // 2, 1) * sine


def key_value_kernel(
    meta_ref, own_ref, other_ref, wkv_ref, bias_ref, adqkv_ref, auk_ref, auv_ref, cos_ref, sin_ref,
    kv_ref, rows_ref, low_ref, low_t_ref,
):
    shard = meta_ref[2]
    half = own_ref.shape[0]
    rows_ref[pl.ds(pl.multiple_of(shard * half, half), half), :] = own_ref[...]
    rows_ref[pl.ds(pl.multiple_of((1 - shard) * half, half), half), :] = other_ref[...]
    rows = rows_ref[...]
    low = nt(rows, adqkv_ref[...])
    low_ref[...] = (2.0 * low).astype(bf)
    low_t_ref[...] = low.T.astype(bf)
    lowered = (2.0 * low).astype(bf)
    key = nn(rows, wkv_ref[0]) + bias_ref[0:1, :].astype(f32) + nn(lowered[:, RANK : 2 * RANK], auk_ref[...])
    value = nn(rows, wkv_ref[1]) + bias_ref[1:2, :].astype(f32) + nn(lowered[:, 2 * RANK :], auv_ref[...])
    kv_ref[:, :HEAD_DIM] = turned(key, cos_ref[...], sin_ref[...]).astype(bf)
    kv_ref[:, HEAD_DIM:] = value.astype(bf)


def query_kernel(rows_ref, wq_ref, bias_ref, low_ref, auq_ref, cos_ref, sin_ref, q_ref):
    heads, span = q_ref.shape[1], q_ref.shape[2]
    query = nn(rows_ref[...], wq_ref[...]) + bias_ref[...].astype(f32) + nn(low_ref[:, :RANK], auq_ref[...])
    for h in range(heads):
        head = turned(query[:, h * HEAD_DIM : (h + 1) * HEAD_DIM], cos_ref[...], sin_ref[...]).astype(bf)
        q_ref[0, h] = head[:span]
        q_ref[1, h] = head[span:]


def mix_out_kernel(meta_ref, mixed_ref, wo_ref, ado_ref, auo_ref, own_ref, send_ref, low_t_ref, total):
    shard = meta_ref[2]
    half = own_ref.shape[0]
    mixed = mixed_ref[...]
    low = nt(mixed, ado_ref[...])
    low_t_ref[...] = low.T.astype(bf)
    total[...] = nn(mixed, wo_ref[...]) + nn((2.0 * low).astype(bf), auo_ref[...])
    own_ref[...] = total[pl.ds(pl.multiple_of(shard * half, half), half), :]
    send_ref[...] = total[pl.ds(pl.multiple_of((1 - shard) * half, half), half), :].astype(bf)


def mix_back_kernel(
    meta_ref, own_ref, other_ref, wo_ref, ado_ref, auo_ref, mixed_ref, low_t_ref,
    do_ref, delta_ref, dado_ref, dauo_ref, rows_ref,
):
    shard = meta_ref[2]
    half = own_ref.shape[0]
    heads, span = do_ref.shape[1], do_ref.shape[2]
    rows_ref[pl.ds(pl.multiple_of(shard * half, half), half), :] = own_ref[...]
    rows_ref[pl.ds(pl.multiple_of((1 - shard) * half, half), half), :] = other_ref[...]
    rows = rows_ref[...]
    back = nt(rows, auo_ref[...])
    grad = (nt(rows, wo_ref[...]) + nn((2.0 * back).astype(bf), ado_ref[...])).astype(bf)
    dado_ref[...] = nn(back.T.astype(bf), mixed_ref[...])
    dauo_ref[...] = nn(low_t_ref[...], rows)
    for h in range(heads):
        cols = slice(h * HEAD_DIM, (h + 1) * HEAD_DIM)
        product = (grad[:, cols].astype(f32) * mixed_ref[:, cols].astype(f32)).T
        row = jnp.sum(product, axis=0, keepdims=True)
        for part in range(2):
            do_ref[part, h] = grad[part * span : (part + 1) * span, cols]
            delta_ref[part, h : h + 1, :] = row[:, part * span : (part + 1) * span]


def back_kernel(
    scale, meta_ref, dq_ref, dkv_ref, wq_ref, wkv_ref, adqkv_ref, auq_ref, auk_ref, auv_ref, low_t_ref, rows_ref,
    cos_ref, sin_ref,
    own_ref, send_ref, dadqkv_ref, dauq_ref, dauk_ref, dauv_ref, eq, total, back_ref,
):
    shard = meta_ref[2]
    half = own_ref.shape[0]
    heads, span = dq_ref.shape[1], dq_ref.shape[3]
    for part in range(2):
        rows = slice(part * span, (part + 1) * span)
        for h in range(heads):
            grad = dq_ref[part, h].T * scale
            eq[rows, h * HEAD_DIM : (h + 1) * HEAD_DIM] = turned(grad, cos_ref[rows, :], -sin_ref[rows, :]).astype(bf)
    ek = turned(dkv_ref[:, :HEAD_DIM].astype(f32), cos_ref[...], -sin_ref[...]).astype(bf)
    ev = dkv_ref[:, HEAD_DIM:].astype(bf)
    query = eq[...]
    back_ref[:, :RANK] = nt(query, auq_ref[...])
    back_ref[:, RANK : 2 * RANK] = nt(ek, auk_ref[...])
    back_ref[:, 2 * RANK :] = nt(ev, auv_ref[...])
    back = back_ref[...]
    total[...] = (
        nt(query, wq_ref[...])
        + nt(ek, wkv_ref[0])
        + nt(ev, wkv_ref[1])
        + nn((2.0 * back).astype(bf), adqkv_ref[...])
    )
    own_ref[...] = total[pl.ds(pl.multiple_of(shard * half, half), half), :]
    send_ref[...] = total[pl.ds(pl.multiple_of((1 - shard) * half, half), half), :].astype(bf)
    dadqkv_ref[...] = nn(back.T.astype(bf), rows_ref[...])
    dauq_ref[...] = nn(low_t_ref[:RANK, :], query)
    dauk_ref[...] = nn(low_t_ref[RANK : 2 * RANK, :], ek)
    dauv_ref[...] = nn(low_t_ref[2 * RANK :, :], ev)


def future_mask(span):
    return lax.broadcasted_iota(jnp.int32, (span, span), 0) <= lax.broadcasted_iota(jnp.int32, (span, span), 1)

def fold(s, values_t, m, l, o, coef, mask):
    if mask is not None:
        s = jnp.where(mask, s, mask_fill)
    m_next = jnp.maximum(m, jnp.max(s, axis=0, keepdims=True))
    p = jnp.exp2((s - m_next) * coef)
    alpha = jnp.exp2((m - m_next) * coef)
    l_next = l * alpha + jnp.sum(p, axis=0, keepdims=True)
    o_next = o * alpha + nn(values_t, p.astype(bf))
    return m_next, l_next, o_next

def pipelined(items, first, second):
    ahead = first(items[0])
    for i, item in enumerate(items):
        now = ahead
        if i + 1 < len(items):
            ahead = first(items[i + 1])
        second(item, now)

def attn_fwd_own_kernel(coef, q_ref, kv_ref, m_ref, l_ref, o_ref, vt):
    heads, span = q_ref.shape[1], q_ref.shape[2]
    vt[...] = kv_ref[:, HEAD_DIM:].astype(f32).T.astype(bf)
    mask = future_mask(span)
    both_mask = lax.broadcasted_iota(jnp.int32, (2 * span, span), 0) <= lax.broadcasted_iota(jnp.int32, (2 * span, span), 1) + span
    def first(item):
        half, h = item
        return nt(kv_ref[: (half + 1) * span, :HEAD_DIM], q_ref[half, h])
    def second(item, s):
        half, h = item
        m = jnp.full((1, span), mask_fill, f32)
        l = jnp.zeros((1, span), f32)
        o = jnp.zeros((HEAD_DIM, span), f32)
        m, l, o = fold(s, vt[:, : (half + 1) * span], m, l, o, coef, both_mask if half else mask)
        m_ref[half, h : h + 1, :] = m
        l_ref[half, h : h + 1, :] = l
        o_ref[half, h] = o
    pipelined([(half, h) for h in range(heads) for half in range(2)], first, second)

def attn_fwd_pieces_kernel(coef, n, last, flag_ref, q_ref, *refs):
    kv_refs = refs[:n]
    m_in, l_in, o_in = refs[n : n + 3]
    if last:
        mixed_ref, lse_ref, m_ref, l_ref, o_ref, vt = refs[n + 3 :]
    else:
        m_ref, l_ref, o_ref, vt = refs[n + 3 :]
    heads, span = q_ref.shape[1], q_ref.shape[2]
    src = [(m_in, l_in, o_in)] + [(m_ref, l_ref, o_ref)] * n
    m_ref[...] = m_in[...]
    l_ref[...] = l_in[...]
    o_ref[...] = o_in[...]
    def update(half, h, s, values_t):
        m, l, o = fold(s, values_t, m_ref[half, h : h + 1, :], l_ref[half, h : h + 1, :], o_ref[half, h], coef, None)
        m_ref[half, h : h + 1, :] = m
        l_ref[half, h : h + 1, :] = l
        o_ref[half, h] = o
    for i in range(n):
        kv_ref = kv_refs[i]
        vt[...] = kv_ref[:, HEAD_DIM:].astype(f32).T.astype(bf)
        @pl.when(flag_ref[i] == 1)
        def before():
            pipelined([(half, h) for h in range(heads) for half in range(2)],
                lambda it: nt(kv_ref[:span, :HEAD_DIM], q_ref[it[0], it[1]]),
                lambda it, s: update(it[0], it[1], s, vt[:, :span]))
        @pl.when(flag_ref[i] != 1)
        def after():
            pipelined([(1, h) for h in range(heads)],
                lambda it: nt(kv_ref[:, :HEAD_DIM], q_ref[1, it[1]]),
                lambda it, s: update(1, it[1], s, vt[...]))
    if last:
        for half in range(2):
            for h in range(heads):
                o = o_ref[half, h] / l_ref[half, h : h + 1, :]
                mixed_ref[half * span : (half + 1) * span, h * HEAD_DIM : (h + 1) * HEAD_DIM] = o.T.astype(bf)
        lse_ref[...] = m_ref[...] * coef + jnp.log2(l_ref[...])


def attn_fwd_own(q, kv, coef):
    _, heads, span, _ = q.shape
    st = (jax.ShapeDtypeStruct((2, heads, span), f32),) * 2 + (jax.ShapeDtypeStruct((2, heads, HEAD_DIM, span), f32),)
    return pl.pallas_call(functools.partial(attn_fwd_own_kernel, coef), out_shape=st, in_specs=[VM, VM], out_specs=(VM,) * 3,
        scratch_shapes=[pltpu.VMEM((HEAD_DIM, 2 * span), bf)],
        cost_estimate=pl.CostEstimate(flops=2*2*3*heads*span*span*HEAD_DIM*2, bytes_accessed=4_000_000, transcendentals=0),
        compiler_params=pltpu.CompilerParams(vmem_limit_bytes=48 << 20), name="attn_fwd_own")(q, kv)

def attn_fwd_pieces(flags, q, pieces, state, coef, last):
    _, heads, span, _ = q.shape
    n = len(pieces)
    st = (jax.ShapeDtypeStruct((2, heads, span), f32),) * 2 + (jax.ShapeDtypeStruct((2, heads, HEAD_DIM, span), f32),)
    if last:
        st = (jax.ShapeDtypeStruct((2 * span, heads * HEAD_DIM), bf), jax.ShapeDtypeStruct((2, heads, span), f32)) + st
    r = pl.pallas_call(functools.partial(attn_fwd_pieces_kernel, coef, n, last), out_shape=st, in_specs=[SM] + [VM] * (n + 4), out_specs=(VM,) * len(st),
        scratch_shapes=[pltpu.VMEM((HEAD_DIM, 2 * span), bf)],
        cost_estimate=pl.CostEstimate(flops=2*2*2*n*heads*span*span*HEAD_DIM*2, bytes_accessed=4_000_000, transcendentals=0),
        compiler_params=pltpu.CompilerParams(vmem_limit_bytes=48 << 20), name="attn_fwd_pieces")(flags, q, *pieces, *state)
    return r

def bwd_block(s, dp, lse_ref, delta_ref, half, h, coef, mask):
    p = jnp.exp2(s * coef - lse_ref[half, h : h + 1, :])
    if mask is not None:
        p = jnp.where(mask, p, 0.0)
    ds = p * (dp - delta_ref[half, h : h + 1, :])
    return p.astype(bf), ds.astype(bf)

def attn_bwd_kernel(coef, scale, n, own, has_state, flag_ref, q_ref, do_ref, lse_ref, delta_ref, *refs):
    kv_refs = refs[:n]
    k = n
    if has_state:
        dq_in = refs[k]; k += 1
    dkv_refs = refs[k : k + n]
    dq_ref, kt, pbuf, sbuf = refs[k + n :]
    heads, span = q_ref.shape[1], q_ref.shape[2]
    if has_state:
        dq_ref[...] = dq_in[...]
    else:
        dq_ref[...] = jnp.zeros_like(dq_ref)
    def do_item(kv_ref, items, keyrows, mask_of):
        nk = keyrows.stop - keyrows.start
        def first(it):
            i, half, h = it
            return nt(kv_ref[keyrows, :HEAD_DIM], q_ref[half, h]), nt(kv_ref[keyrows, HEAD_DIM:], do_ref[half, h])
        def second(it, sd):
            i, half, h = it
            p, ds = bwd_block(sd[0], sd[1], lse_ref, delta_ref, half, h, coef, mask_of(half))
            cols = slice((i * heads + h) * span, (i * heads + h + 1) * span)
            pbuf[:nk, cols] = p
            sbuf[:nk, cols] = ds
            dq_ref[half, h] += nn(kt[:, keyrows], ds)
        pipelined([(i, half, h) for i, half in enumerate(items) for h in range(heads)], first, second)
        width = len(items) * heads * span
        lo = items[0]
        q_all = q_ref[lo : lo + len(items)].reshape(width, HEAD_DIM)
        do_all = do_ref[lo : lo + len(items)].reshape(width, HEAD_DIM)
        return nn(sbuf[:nk, :width], q_all) * scale, nn(pbuf[:nk, :width], do_all)
    for i in range(n):
        kv_ref, out = kv_refs[i], dkv_refs[i]
        kt[...] = kv_ref[:, :HEAD_DIM].astype(f32).T.astype(bf)
        lo, hi, both = slice(0, span), slice(span, 2 * span), slice(0, 2 * span)
        if own and i == 0:
            mask = future_mask(span)
            dk, dv = do_item(kv_ref, [0, 1], lo, lambda half: mask if half == 0 else None)
            out[lo, :HEAD_DIM] = dk.astype(bf)
            out[lo, HEAD_DIM:] = dv.astype(bf)
            dk, dv = do_item(kv_ref, [1], hi, lambda half: mask)
            out[hi, :HEAD_DIM] = dk.astype(bf)
            out[hi, HEAD_DIM:] = dv.astype(bf)
        else:
            @pl.when(flag_ref[i] == 1)
            def before():
                dk, dv = do_item(kv_ref, [0, 1], lo, lambda half: None)
                out[lo, :HEAD_DIM] = dk.astype(bf)
                out[lo, HEAD_DIM:] = dv.astype(bf)
                out[hi, :] = jnp.zeros((span, 2 * HEAD_DIM), bf)
            @pl.when(flag_ref[i] != 1)
            def after():
                dk, dv = do_item(kv_ref, [1], both, lambda half: None)
                out[:, :HEAD_DIM] = dk.astype(bf)
                out[:, HEAD_DIM:] = dv.astype(bf)

def attn_bwd(flags, q, do, lse, delta, pieces, dq_state, coef, scale, own):
    _, heads, span, _ = q.shape
    n = len(pieces)
    outs = tuple(jax.ShapeDtypeStruct((2 * span, 2 * HEAD_DIM), bf) for _ in range(n)) + (jax.ShapeDtypeStruct((2, heads, HEAD_DIM, span), f32),)
    ins = [flags, q, do, lse, delta, *pieces] + ([dq_state] if dq_state is not None else [])
    return pl.pallas_call(functools.partial(attn_bwd_kernel, coef, scale, n, own, dq_state is not None), out_shape=outs,
        in_specs=[SM] + [VM] * (len(ins) - 1), out_specs=(VM,) * len(outs),
        scratch_shapes=[pltpu.VMEM((HEAD_DIM, 2 * span), bf), pltpu.VMEM((2 * span, 2 * heads * span), bf), pltpu.VMEM((2 * span, 2 * heads * span), bf)],
        cost_estimate=pl.CostEstimate(flops=2*5*2*n*heads*span*span*HEAD_DIM*2, bytes_accessed=4_000_000, transcendentals=0),
        compiler_params=pltpu.CompilerParams(vmem_limit_bytes=48 << 20), name="attn_bwd_pieces")(*ins)


def ffn_kernel(tile, tiles, hidden, x_own, x_other, g_own, g_other, adgu_ref, auf_ref, wgu_ref, wd_ref, adf_ref, augu_ref,
               out_own, out_send, gx_own, gx_send, dadgu_ref, dauf_ref, daugu_ref, dadf_ref,
               x_ref, g_ref, out_acc, gx_acc, xlow, xlow_t, fback, fback_t, flow, back):
    step = pl.program_id(0)
    half_rows = x_ref.shape[0] // 2

    @pl.when(step == 0)
    def prepare():
        for target, own, other in ((x_ref, x_own, x_other), (g_ref, g_own, g_other)):
            target[:half_rows, :] = own[...]
            target[half_rows:, :] = other[...]
        low = nt(x_ref[...], adgu_ref[...])
        xlow[...] = (low * 2.0).astype(bf)
        xlow_t[...] = low.T.astype(bf)
        fb = nt(g_ref[...], auf_ref[...])
        fback[...] = (fb * 2.0).astype(bf)
        fback_t[...] = fb.T.astype(bf)
        out_acc[...] = jnp.zeros_like(out_acc)
        gx_acc[...] = jnp.zeros_like(gx_acc)
        flow[...] = jnp.zeros_like(flow)
        back[...] = jnp.zeros_like(back)

    def work(width):
        x, g = x_ref[...], g_ref[...]
        wg, wu, wd = wgu_ref[0, :, :width], wgu_ref[1, :, :width], wd_ref[:width, :]
        aug, auu, adf = augu_ref[:RANK, :width], augu_ref[RANK:, :width], adf_ref[:, :width]
        gate = nn(x, wg) + nn(xlow[:, :RANK], aug)
        up = nn(x, wu) + nn(xlow[:, RANK:], auu)
        gact = nt(g, wd) + nn(fback[...], adf)
        sig = 1.0 / (1.0 + jnp.exp(-gate))
        silu = gate * sig
        act = (silu * up).astype(bf)
        ggate = (gact * up * (sig + silu * (1.0 - sig))).astype(bf)
        gup = (gact * silu).astype(bf)
        out_acc[...] += nn(act, wd)
        flow[...] += nt(act, adf)
        gx_acc[...] += nt(ggate, wg) + nt(gup, wu)
        back[:, :RANK] += nt(ggate, aug)
        back[:, RANK:] += nt(gup, auu)
        daugu_ref[:RANK, :width] = nn(xlow_t[:RANK, :], ggate)
        daugu_ref[RANK:, :width] = nn(xlow_t[RANK:, :], gup)
        dadf_ref[:, :width] = nn(fback_t[...], act)

    tail = hidden - (tiles - 1) * tile
    if tail == tile:
        work(tile)
    else:
        @pl.when(step < tiles - 1)
        def whole():
            work(tile)

        @pl.when(step == tiles - 1)
        def part():
            work(tail)

    @pl.when(step == tiles - 1)
    def finish():
        out_acc[...] += nn((flow[...] * 2.0).astype(bf), auf_ref[...])
        gx_acc[...] += nn((back[...] * 2.0).astype(bf), adgu_ref[...])
        dadgu_ref[...] = nn(back[...].T.astype(bf), x_ref[...])
        dauf_ref[...] = nn(flow[...].T.astype(bf), g_ref[...])
        out_own[...] = out_acc[:half_rows, :]
        out_send[...] = out_acc[half_rows:, :].astype(bf)
        gx_own[...] = gx_acc[:half_rows, :]
        gx_send[...] = gx_acc[half_rows:, :].astype(bf)

def ffn(x_own, x_other, g_own, g_other, adgu, auf, wgu, wd, adf, augu, tile=512):
    rows, width = 2 * x_own.shape[0], x_own.shape[1]
    hidden = wd.shape[0]
    tiles = -(-hidden // tile)
    S = jax.ShapeDtypeStruct
    const = lambda s: pl.BlockSpec(s, lambda i: (0,) * len(s), pipeline_mode=pl.Buffered(1))
    half = rows // 2
    outs = (S((half, width), f32), S((half, width), bf), S((half, width), f32), S((half, width), bf),
            S((2 * RANK, width), f32), S((RANK, width), f32), S((2 * RANK, hidden), f32), S((RANK, hidden), f32))
    col = lambda r: pl.BlockSpec((r, tile), lambda i: (0, i))
    return pl.pallas_call(
        functools.partial(ffn_kernel, tile, tiles, hidden), grid=(tiles,), out_shape=outs,
        in_specs=[const((half, width))] * 4 + [const((2 * RANK, width)), const((RANK, width)),
                  pl.BlockSpec((2, width, tile), lambda i: (0, 0, i)), pl.BlockSpec((tile, width), lambda i: (i, 0)), col(RANK), col(2 * RANK)],
        out_specs=(const((half, width)),) * 4 + (const((2 * RANK, width)), const((RANK, width)), col(2 * RANK), col(RANK)),
        scratch_shapes=[pltpu.VMEM((rows, width), bf), pltpu.VMEM((rows, width), bf), pltpu.VMEM((rows, width), f32), pltpu.VMEM((rows, width), f32), pltpu.VMEM((rows, 2 * RANK), bf), pltpu.VMEM((2 * RANK, rows), bf),
                        pltpu.VMEM((rows, RANK), bf), pltpu.VMEM((RANK, rows), bf), pltpu.VMEM((rows, RANK), f32), pltpu.VMEM((rows, 2 * RANK), f32)],
        cost_estimate=pl.CostEstimate(flops=2 * 6 * rows * width * hidden, bytes_accessed=3 * width * hidden * 2, transcendentals=rows * hidden),
        compiler_params=pltpu.CompilerParams(vmem_limit_bytes=56 << 20), name="ffn")(x_own, x_other, g_own, g_other, adgu, auf, wgu, wd, adf, augu)


def per_device(
    tokens, cotangent, positions, adapter_choice, attn_gain, query_weight, query_bias, key_value_weight,
    key_value_bias, output_weight, ffn_gain, gate_upper_weight, down_weight, adapt_in, adapt_out,
):
    shard, dp, seq = lax.axis_index("tensor"), lax.axis_index("dp"), lax.axis_index("seq")
    groups = lax.axis_size("seq")
    rings = groups // 2
    width, head_width = query_weight.shape
    heads = head_width // HEAD_DIM
    hidden = down_weight.shape[0]
    token_pos = positions[0]
    tok_count = token_pos.shape[0]
    span = tok_count // 2
    scale = HEAD_DIM ** (-0.5)
    coef = scale * math.log2(math.e)
    wide_in, wide_out = adapt_in.shape[2], adapt_out.shape[2]
    lanes_in = rounded_up(wide_in + 1, 128)
    lanes = lanes_in + rounded_up(wide_out, 128)
    widths = (width, head_width, hidden)
    meta = jnp.stack([dp, seq, shard]).astype(jnp.int32)

    def to_pair(value):
        return lax.ppermute(value, "tensor", [(0, 1), (1, 0)])

    def to_other_sequence(value):
        return lax.ppermute(value, "dp", [(0, 1), (1, 0)])

    def to_side(value):
        return lax.ppermute(value, "seq", [(i, i ^ 1) for i in range(groups)])

    def along_ring(value):
        return lax.ppermute(value, "seq", [(i, (i + 2) % groups) for i in range(groups)])

    def gathered(piece):
        pieces = []
        for place in range(rings):
            pieces += [piece, to_side(piece)]
            if place + 1 < rings:
                piece = along_ring(piece)
        return pieces

    choice_here = lax.dynamic_index_in_dim(adapter_choice, dp, 0, keepdims=False)
    choice_there = lax.dynamic_index_in_dim(adapter_choice, 1 - dp, 0, keepdims=False)
    run = token_pos[0] // span
    chosen = jnp.stack([choice_here, choice_there, run]).astype(jnp.int32)
    slice_own, slice_other = call(
        functools.partial(select_kernel, lanes_in), "select",
        [shape(RANK, lanes, dtype=bf)] * 2, [chosen, adapt_in, adapt_out],
    )
    pair_slices = jnp.stack([slice_own, to_other_sequence(slice_other)])
    own_slices = jnp.stack(gathered(pair_slices))
    pair_slices = to_pair(own_slices)
    ad_lanes = rounded_up(4 * groups * wide_in, 128) + 256
    au_lanes = rounded_up(4 * groups * wide_out, 128) + 256
    flags, adqkv, auq, auk, auv, ado, auo, adgu, augu, adf, auf = call(
        functools.partial(unpack_kernel, groups, wide_in, wide_out, lanes_in, widths), "unpack",
        [shape(groups, dtype=jnp.int32)]
        + [
            shape(*dims, dtype=bf)
            for dims in (
                (3 * RANK, width), (RANK, head_width), (RANK, HEAD_DIM), (RANK, HEAD_DIM), (RANK, head_width),
                (RANK, width), (2 * RANK, width), (2 * RANK, hidden), (RANK, hidden), (RANK, width),
            )
        ],
        [meta, own_slices, pair_slices],
        [pltpu.VMEM((4 * groups, RANK, lanes), bf), pltpu.VMEM((RANK, ad_lanes), f32), pltpu.VMEM((RANK, au_lanes), f32)],
        out_specs=(SM,) + (VM,) * 10,
    )

    frequency = jnp.power(rope_base, -(jnp.arange(HEAD_DIM // 2, dtype=f32) * 2.0) / HEAD_DIM)
    angles = token_pos.astype(f32)[:, None] * frequency[None, :]
    cosine, sine = jnp.cos(angles), jnp.sin(angles)
    cosine = jnp.concatenate([cosine, cosine], axis=1)
    sine = jnp.concatenate([-sine, sine], axis=1)

    inputs, grad_out = tokens[0], cotangent[0]
    half = inputs.shape[0]
    grad_other = to_pair(grad_out)
    attn_gain, ffn_gain = attn_gain[None], ffn_gain[None]
    (normed,) = call(norm_kernel, "norm", [shape(half, width, dtype=bf)], [inputs, attn_gain], smem=0)
    normed_other = to_pair(normed)
    kv, normed_rows, low, low_t = call(
        key_value_kernel, "key_value",
        [
            shape(tok_count, 2 * HEAD_DIM, dtype=bf), shape(tok_count, width, dtype=bf),
            shape(tok_count, 3 * RANK, dtype=bf), shape(3 * RANK, tok_count, dtype=bf),
        ],
        [meta, normed, normed_other, key_value_weight, key_value_bias, adqkv, auk, auv, cosine, sine],
        flops=2 * tok_count * width * 2 * HEAD_DIM * 2,
    )
    pieces = gathered(kv)
    (queries,) = call(
        query_kernel, "query", [shape(2, heads, span, HEAD_DIM, dtype=bf)],
        [normed_rows, query_weight, query_bias[None], low, auq, cosine, sine], smem=0,
        flops=2 * tok_count * width * head_width,
    )
    state = attn_fwd_own(queries, kv, coef)
    for begin, end in forward_parts(groups):
        result = attn_fwd_pieces(flags[begin:end], queries, pieces[begin:end], state, coef, end == groups)
        state = result[-3:]
    mixed, lse = result[0], result[1]
    branch_own, branch_send, mix_low_t = call(
        mix_out_kernel, "mix_out",
        [shape(half, width), shape(half, width, dtype=bf), shape(RANK, tok_count, dtype=bf)],
        [meta, mixed, output_weight, ado, auo],
        [pltpu.VMEM((tok_count, width), f32)], flops=2 * tok_count * width * head_width,
    )
    hidden_rows, normed_ffn = call(
        residual_kernel, "residual", [shape(half, width), shape(half, width, dtype=bf)],
        [inputs, branch_own, to_pair(branch_send), ffn_gain], smem=0,
    )
    out_own, out_send, gx_own, gx_send, dadgu, dauf, daugu, dadf = ffn(
        normed_ffn, to_pair(normed_ffn), grad_out, grad_other, adgu, auf, gate_upper_weight, down_weight, adf, augu
    )
    grad_hidden, grad_low = call(
        hidden_back_kernel, "hidden_back", [shape(half, width), shape(half, width, dtype=bf)],
        [hidden_rows, grad_out, gx_own, to_pair(gx_send), ffn_gain], smem=0,
    )
    output = (hidden_rows + (out_own + to_pair(out_send).astype(f32))).astype(bf)
    grad_mixed, delta, dado, dauo = call(
        mix_back_kernel, "mix_back",
        [shape(2, heads, span, HEAD_DIM, dtype=bf), shape(2, heads, span), shape(RANK, head_width), shape(RANK, width)],
        [meta, grad_low, to_pair(grad_low), output_weight, ado, auo, mixed, mix_low_t],
        [pltpu.VMEM((tok_count, width), bf)], flops=2 * tok_count * width * head_width,
    )

    state_dq, moving = None, None
    for place in list(range(1, rings)) + [0]:
        *terms, state_dq = attn_bwd(
            flags[2 * place : 2 * place + 2], queries, grad_mixed, lse, delta, pieces[2 * place : 2 * place + 2],
            state_dq, coef, scale, place == 0,
        )
        mine = terms[0].astype(f32) + to_side(terms[1]).astype(f32)
        if moving is not None:
            mine = mine + moving.astype(f32)
        if place != 0:
            moving = along_ring(mine.astype(bf))
    key_value_grad = mine
    gn_own, gn_send, dadqkv, dauq, dauk, dauv = call(
        functools.partial(back_kernel, scale), "back",
        [
            shape(half, width), shape(half, width, dtype=bf), shape(3 * RANK, width), shape(RANK, head_width),
            shape(RANK, HEAD_DIM), shape(RANK, HEAD_DIM),
        ],
        [
            meta, state_dq, key_value_grad, query_weight, key_value_weight, adqkv, auq, auk, auv, low_t, normed_rows,
            cosine, sine,
        ],
        [pltpu.VMEM((tok_count, head_width), bf), pltpu.VMEM((tok_count, width), f32), pltpu.VMEM((tok_count, 3 * RANK), f32)],
        flops=2 * tok_count * width * (head_width + 2 * HEAD_DIM),
    )
    (grad_tokens,) = call(
        token_back_kernel, "token_back", [shape(half, width)],
        [inputs, grad_hidden, gn_own, to_pair(gn_send), attn_gain], smem=0,
    )

    keep, send = call(
        functools.partial(pack_kernel, groups, wide_in, wide_out, lanes_in, widths), "pack",
        [shape(2, rings, 2, RANK, lanes, dtype=bf)] * 2,
        [meta, dadqkv, dauq, dauk, dauv, dado, dauo, dadgu, daugu, dadf, dauf],
        [pltpu.VMEM((RANK, ad_lanes), f32), pltpu.VMEM((RANK, au_lanes), f32)],
    )
    total = keep.astype(f32) + to_pair(send).astype(f32)
    total = total[0] + to_side(total[1].astype(bf)).astype(f32)
    moving = total[1 % rings]
    for place in range(2, rings + 1):
        moving = along_ring(moving.astype(bf)).astype(f32) + total[place % rings]
    factor = adapter_scale * (adapter_choice.shape[0] * tok_count * groups) ** (-0.5)
    adapt_in_grad, adapt_out_grad = call(
        functools.partial(place_kernel, lanes_in, factor), "place",
        [shape(*adapt_in.shape), shape(*adapt_out.shape)],
        [chosen, moving[0], to_other_sequence(moving[1].astype(bf)).astype(f32)],
    )
    return (output[None], grad_tokens[None], adapt_in_grad, adapt_out_grad)


def forward_parts(groups):
    if groups <= 4:
        return [(1, groups)]
    return [(1, groups // 2), (groups // 2, groups)]


def solution(mesh):
    return jax.shard_map(
        per_device,
        mesh=mesh,
        in_specs=(
            P("dp", ("seq", "tensor"), None),
            P("dp", ("seq", "tensor"), None),
            P("dp", "seq"),
            P(),
            P(),
            P(None, "tensor"),
            P("tensor"),
            P(None, None, "tensor"),
            P(None, "tensor"),
            P("tensor", None),
            P(),
            P(None, None, "tensor"),
            P("tensor", None),
            P(None, None, ("dp", "seq", "tensor")),
            P(None, None, ("dp", "seq", "tensor")),
        ),
        out_specs=(
            P("dp", ("seq", "tensor"), None),
            P("dp", ("seq", "tensor"), None),
            P(None, None, ("dp", "seq", "tensor")),
            P(None, None, ("dp", "seq", "tensor")),
        ),
        check_vma=False,
    )
```

```python
import functools
import math

import jax
import jax.numpy as jnp
from jax import lax
from jax.experimental import pallas as pl
from jax.experimental.pallas import tpu as pltpu
from jax.sharding import PartitionSpec as P

HEAD_DIM = 128
RANK = 16
eps = 1e-06
adapter_scale = 2.0
rope_base = 1000000.0
mask_fill = -1e30
bf = jnp.bfloat16
f32 = jnp.float32
VM = pl.BlockSpec(memory_space=pltpu.VMEM)
SM = pl.BlockSpec(memory_space=pltpu.SMEM)


def nn(a, b):
    return jnp.dot(a, b, preferred_element_type=f32)


def nt(a, b):
    return lax.dot_general(a, b, (((1,), (1,)), ((), ())), preferred_element_type=f32)


def shape(*dims, dtype=f32):
    return jax.ShapeDtypeStruct(dims, dtype)


def call(kernel, name, out, ins, scratch=(), flops=0, smem=0, out_specs=None, limit=16, left=0):
    moved = sum(math.prod(v.shape) * v.dtype.itemsize for v in list(ins) + list(out))
    ins = list(ins[: len(ins) - left]) + [in_hbm(value) for value in ins[len(ins) - left :]]
    return pl.pallas_call(
        kernel,
        out_shape=tuple(out),
        in_specs=[SM] * smem + [VM] * (len(ins) - smem - left) + [HB] * left,
        out_specs=out_specs or (VM,) * len(out),
        scratch_shapes=list(scratch),
        cost_estimate=pl.CostEstimate(flops=flops, bytes_accessed=moved, transcendentals=0),
        compiler_params=pltpu.CompilerParams(vmem_limit_bytes=limit << 20),
        name=name,
    )(*ins)


HB = pl.BlockSpec(memory_space=pltpu.HBM)


def in_hbm(value):
    return pltpu.with_memory_space_constraint(value, pltpu.HBM)


def rounded_up(value, unit):
    return -(-value // unit) * unit


def select_kernel(lanes_in, span, choice_ref, pos_ref, in_ref, out_ref, own_ref, other_ref, held_in, held_out, sems):
    wide_in, wide_out = in_ref.shape[2], out_ref.shape[2]
    dp = lax.axis_index("dp")
    copies = []
    for slot, sequence in ((0, dp), (1, 1 - dp)):
        chosen = choice_ref[sequence]
        copies.append(pltpu.make_async_copy(in_ref.at[chosen], held_in.at[slot], sems.at[2 * slot]))
        copies.append(pltpu.make_async_copy(out_ref.at[chosen], held_out.at[slot], sems.at[2 * slot + 1]))
    for copy in copies:
        copy.start()
    run = jnp.full((RANK, lanes_in), pos_ref[0, 0] // span, jnp.int32).astype(f32).astype(bf)
    for target in (own_ref, other_ref):
        target[...] = jnp.zeros_like(target)
        target[:, :lanes_in] = run
    for copy in copies:
        copy.wait()
    for slot, target in ((0, own_ref), (1, other_ref)):
        target[:, :wide_in] = held_in[slot]
        target[:, lanes_in : lanes_in + wide_out] = held_out[slot]


def column(begin, size):
    return pl.ds(pl.multiple_of(begin, 128), size)


def source_of(place, side, rings, seq):
    ring = lax.rem(seq // 2 - place + rings, rings)
    own_side = lax.rem(seq, 2)
    return ring * 2 + (own_side if side == 0 else 1 - own_side)


def spread(slots, target, begin, wide, first, low, high):
    held = rounded_up(wide, 128)
    inside = lax.broadcasted_iota(jnp.int32, (RANK, held), 1) < wide
    target[...] = jnp.zeros_like(target)
    for index in range(low // wide, -(-high // wide)):
        part = jnp.where(inside, slots[index, :, begin : begin + held].astype(f32), 0.0)
        part = jnp.concatenate([part, jnp.zeros((RANK, 128), f32)], axis=1)
        offset = index * wide - first
        base = offset // 128 * 128
        if offset != base:
            part = pltpu.roll(part, offset - base, 1)
        target[:, base : base + held + 128] += part


def collect(slots, refs, rings, part):
    seq, shard = lax.axis_index("seq"), lax.axis_index("tensor")
    for number, ref in enumerate(refs):
        side, core = number % 2, shard if number < 2 else 1 - shard
        for place in range(rings):
            slots[part * 4 * rings + source_of(place, side, rings, seq) * 2 + core] = ref[place]


def unpack_first_kernel(
    rings, wide_in, wide_out, lanes_in, widths, own, own_side, pair, pair_side,
    flags_ref, adqkv, auq, auk, auv, ado, auo, slots, ad, au,
):
    shard = lax.axis_index("tensor")
    width, head_width, hidden = widths
    own_run = jnp.max(own[0, :, wide_in:lanes_in].astype(f32))
    for place in range(rings):
        for side, ref in ((0, own), (1, own_side)):
            run = jnp.max(ref[place, :, wide_in:lanes_in].astype(f32))
            flags_ref[2 * place + side] = (run < own_run).astype(jnp.int32)
    collect(slots, (own, own_side, pair, pair_side), rings, 0)
    spread(slots, ad, 0, wide_in, 0, 0, 4 * width)
    spread(slots, au, lanes_in, wide_out, 0, 0, 2 * width + 4 * HEAD_DIM)
    for index in range(3):
        adqkv[index * RANK : (index + 1) * RANK, :] = ad[:, index * width : (index + 1) * width].astype(bf)
    ado[...] = ad[:, column(3 * width + shard * head_width, head_width)].astype(bf)
    auq[...] = au[:, column(shard * head_width, head_width)].astype(bf)
    auk[...] = au[:, column(width + shard * HEAD_DIM, HEAD_DIM)].astype(bf)
    auv[...] = au[:, column(width + (2 + shard) * HEAD_DIM, HEAD_DIM)].astype(bf)
    base = width + 4 * HEAD_DIM
    auo[...] = au[:, base : base + width].astype(bf)


def bases(wide_in, wide_out, widths):
    width = widths[0]
    begin_in, begin_out = 4 * width, 2 * width + 4 * HEAD_DIM
    return begin_in, begin_out, begin_in // wide_in * wide_in // 128 * 128, begin_out // wide_out * wide_out // 128 * 128


def unpack_second_kernel(
    rings, wide_in, wide_out, lanes_in, widths, *refs
):
    firsts, seconds = refs[:4], refs[4:8]
    adgu, augu, adf, auf, slots, ad, au = refs[8:]
    shard = lax.axis_index("tensor")
    width, head_width, hidden = widths
    collect(slots, firsts, rings, 0)
    collect(slots, seconds, rings, 1)
    begin_in, begin_out, first_in, first_out = bases(wide_in, wide_out, widths)
    total_in, total_out = 8 * rings * wide_in, 8 * rings * wide_out
    spread(slots, ad, 0, wide_in, first_in, begin_in, total_in)
    spread(slots, au, lanes_in, wide_out, first_out, begin_out, total_out)
    base = begin_in - first_in
    for index in range(2):
        adgu[index * RANK : (index + 1) * RANK, :] = ad[:, base + index * width : base + (index + 1) * width].astype(bf)
    adf[...] = ad[:, column(base + 2 * width + shard * hidden, hidden)].astype(bf)
    base = begin_out - first_out
    for index in range(2):
        augu[index * RANK : (index + 1) * RANK, :] = au[
            :, column(base + (2 * index + shard) * hidden, hidden)
        ].astype(bf)
    auf[...] = au[:, base + 4 * hidden : base + 4 * hidden + width].astype(bf)


def put_slices(rings, wide_in, wide_out, lanes_in, ad, au, limits, parts, write):
    dp, seq = lax.axis_index("dp"), lax.axis_index("seq")
    for index in range(4 * rings * parts):
        to_dp, to_seq, to_core = index // (4 * rings), index // 2 % (2 * rings), index % 2
        pieces = []
        for source, wide, (low, high, first) in ((ad, wide_in, limits[0]), (au, wide_out, limits[1])):
            held = rounded_up(wide, 128)
            if index * wide >= high or (index + 1) * wide <= low:
                part = jnp.zeros((RANK, held), f32)
            else:
                offset = index * wide - first
                base = offset // 128 * 128
                part = source[:, base : base + held + 128]
                if offset != base:
                    part = pltpu.roll(part, held + 128 - (offset - base), 1)
                part = part[:, :held]
            pieces.append(part)
            if source is ad and lanes_in > held:
                pieces.append(jnp.zeros((RANK, lanes_in - held), f32))
        packed = jnp.concatenate(pieces, axis=1).astype(bf)
        place = lax.rem(seq // 2 - to_seq // 2 + rings, rings)
        write(to_seq, to_core, place, lax.rem(dp + to_dp, 2), packed)


def pack_kernel(
    rings, wide_in, wide_out, lanes_in, widths,
    dadq, dadkv, dado, dadgu, dadf, dauq, dauk, dauv, dauo, daugu, dauf, keep_ref, send_ref, ad, au,
):
    shard, side = lax.axis_index("tensor"), lax.rem(lax.axis_index("seq"), 2)
    width, head_width, hidden = widths
    ad[...] = jnp.zeros_like(ad)
    au[...] = jnp.zeros_like(au)
    ad[:, :width] = dadq[...]
    for index in range(2):
        ad[:, (1 + index) * width : (2 + index) * width] = dadkv[index * RANK : (index + 1) * RANK, :]
        ad[:, (4 + index) * width : (5 + index) * width] = dadgu[index * RANK : (index + 1) * RANK, :]
    ad[:, column(3 * width + shard * head_width, head_width)] = dado[...]
    ad[:, column(6 * width + shard * hidden, hidden)] = dadf[...]
    au[:, column(shard * head_width, head_width)] = dauq[...]
    au[:, column(width + shard * HEAD_DIM, HEAD_DIM)] = dauk[...]
    au[:, column(width + (2 + shard) * HEAD_DIM, HEAD_DIM)] = dauv[...]
    base = width + 4 * HEAD_DIM
    au[:, base : base + width] = dauo[...]
    base = base + width
    for index in range(2):
        au[:, column(base + (2 * index + shard) * hidden, hidden)] = daugu[index * RANK : (index + 1) * RANK, :]
    au[:, base + 4 * hidden : base + 4 * hidden + width] = dauf[...]

    def write(to_seq, to_core, place, part, packed):
        row = lax.rem(side + to_seq % 2, 2)

        @pl.when(shard == to_core)
        def kept():
            keep_ref[row, place, part] = packed

        @pl.when(shard != to_core)
        def sent():
            send_ref[row, place, part] = packed

    limits = ((0, 8 * rings * wide_in, 0), (0, 8 * rings * wide_out, 0))
    put_slices(rings, wide_in, wide_out, lanes_in, ad, au, limits, 2, write)


def place_kernel(lanes_in, factor, choice_ref, own_ref, other_ref, in_ref, out_ref):
    wide_in, wide_out = in_ref.shape[2], out_ref.shape[2]
    dp = lax.axis_index("dp")
    in_ref[...] = jnp.zeros_like(in_ref)
    out_ref[...] = jnp.zeros_like(out_ref)
    for ref, sequence in ((own_ref, dp), (other_ref, 1 - dp)):
        chosen = choice_ref[sequence]
        part = ref[...].astype(f32) * factor
        in_ref[chosen] = in_ref[chosen] + part[:, :wide_in]
        out_ref[chosen] = out_ref[chosen] + part[:, lanes_in : lanes_in + wide_out]


def factor_of(rows):
    return lax.rsqrt(jnp.mean(rows * rows, axis=-1, keepdims=True) + eps)


def norm_back(rows, gain, grad):
    factor = factor_of(rows)
    scaled = rows * factor
    grad_scaled = grad * gain
    return factor * (grad_scaled - scaled * jnp.mean(grad_scaled * scaled, axis=-1, keepdims=True))


def norm_kernel(rows_ref, gain_ref, normed_ref):
    rows = rows_ref[...].astype(f32)
    normed_ref[...] = (rows * factor_of(rows) * gain_ref[...].astype(f32)).astype(bf)


def residual_kernel(rows_ref, own_ref, other_ref, gain_ref, hidden_ref, normed_ref):
    rows = rows_ref[...].astype(f32) + (own_ref[...] + other_ref[...].astype(f32))
    hidden_ref[...] = rows
    normed_ref[...] = (rows * factor_of(rows) * gain_ref[...].astype(f32)).astype(bf)


def hidden_back_kernel(hidden_ref, grad_ref, own_ref, other_ref, gain_ref, out_ref, low_ref):
    grad = own_ref[...] + other_ref[...].astype(f32)
    total = grad_ref[...].astype(f32) + norm_back(hidden_ref[...], gain_ref[...].astype(f32), grad)
    out_ref[...] = total
    low_ref[...] = total.astype(bf)


def token_back_kernel(rows_ref, grad_ref, own_ref, other_ref, gain_ref, out_ref):
    grad = own_ref[...] + other_ref[...].astype(f32)
    out_ref[...] = grad_ref[...] + norm_back(rows_ref[...].astype(f32), gain_ref[...].astype(f32), grad)


def turned(rows, cosine, sine):
    return rows * cosine + pltpu.roll(rows, HEAD_DIM // 2, 1) * sine


def dense_kernel(own_ref, other_ref, wq_ref, wkv_ref, rows_ref, query_ref, kv_ref):
    shard = lax.axis_index("tensor")
    half = own_ref.shape[0]
    rows_ref[pl.ds(pl.multiple_of(shard * half, half), half), :] = own_ref[...]
    rows_ref[pl.ds(pl.multiple_of((1 - shard) * half, half), half), :] = other_ref[...]
    rows = rows_ref[...]
    query_ref[...] = nn(rows, wq_ref[...])
    kv_ref[:, :HEAD_DIM] = nn(rows, wkv_ref[0])
    kv_ref[:, HEAD_DIM:] = nn(rows, wkv_ref[1])


def key_value_kernel(
    rows_ref, dense_ref, bias_ref, adqkv_ref, auk_ref, auv_ref, cos_ref, sin_ref, kv_ref, low_ref, low_t_ref
):
    low = nt(rows_ref[...], adqkv_ref[...])
    low_ref[...] = (2.0 * low).astype(bf)
    low_t_ref[...] = low.T.astype(bf)
    key = dense_ref[:, :HEAD_DIM] + bias_ref[0:1, :].astype(f32) + nn(low_ref[:, RANK : 2 * RANK], auk_ref[...])
    value = dense_ref[:, HEAD_DIM:] + bias_ref[1:2, :].astype(f32) + nn(low_ref[:, 2 * RANK :], auv_ref[...])
    kv_ref[:, :HEAD_DIM] = turned(key, cos_ref[...], sin_ref[...]).astype(bf)
    kv_ref[:, HEAD_DIM:] = value.astype(bf)


def query_kernel(dense_ref, bias_ref, low_ref, auq_ref, cos_ref, sin_ref, q_ref):
    heads, span = q_ref.shape[1], q_ref.shape[2]
    query = dense_ref[...] + bias_ref[...].astype(f32) + nn(low_ref[:, :RANK], auq_ref[...])
    for h in range(heads):
        head = turned(query[:, h * HEAD_DIM : (h + 1) * HEAD_DIM], cos_ref[...], sin_ref[...]).astype(bf)
        q_ref[0, h] = head[:span]
        q_ref[1, h] = head[span:]


def mix_out_kernel(mixed_ref, wo_ref, ado_ref, auo_ref, own_ref, send_ref, low_t_ref, total):
    shard = lax.axis_index("tensor")
    half = own_ref.shape[0]
    mixed = mixed_ref[...]
    low = nt(mixed, ado_ref[...])
    low_t_ref[...] = low.T.astype(bf)
    total[...] = nn(mixed, wo_ref[...]) + nn((2.0 * low).astype(bf), auo_ref[...])
    own_ref[...] = total[pl.ds(pl.multiple_of(shard * half, half), half), :]
    send_ref[...] = total[pl.ds(pl.multiple_of((1 - shard) * half, half), half), :].astype(bf)


def mix_back_kernel(
    own_ref, other_ref, wo_ref, ado_ref, auo_ref, mixed_ref, low_t_ref,
    do_ref, delta_ref, dado_ref, dauo_ref, rows_ref,
):
    shard = lax.axis_index("tensor")
    half = own_ref.shape[0]
    heads, span = do_ref.shape[1], do_ref.shape[2]
    rows_ref[pl.ds(pl.multiple_of(shard * half, half), half), :] = own_ref[...]
    rows_ref[pl.ds(pl.multiple_of((1 - shard) * half, half), half), :] = other_ref[...]
    rows = rows_ref[...]
    back = nt(rows, auo_ref[...])
    grad = (nt(rows, wo_ref[...]) + nn((2.0 * back).astype(bf), ado_ref[...])).astype(bf)
    dado_ref[...] = nn(back.T.astype(bf), mixed_ref[...])
    dauo_ref[...] = nn(low_t_ref[...], rows)
    for h in range(heads):
        cols = slice(h * HEAD_DIM, (h + 1) * HEAD_DIM)
        product = (grad[:, cols].astype(f32) * mixed_ref[:, cols].astype(f32)).T
        row = jnp.sum(product, axis=0, keepdims=True)
        for part in range(2):
            do_ref[part, h] = grad[part * span : (part + 1) * span, cols]
            delta_ref[part, h : h + 1, :] = row[:, part * span : (part + 1) * span]


def back_query_kernel(
    scale, dq_ref, wq_ref, adq_ref, auq_ref, low_t_ref, rows_ref, cos_ref, sin_ref, total_ref, dadq_ref, dauq_ref, eq
):
    heads, span = dq_ref.shape[1], dq_ref.shape[3]
    for part in range(2):
        rows = slice(part * span, (part + 1) * span)
        for h in range(heads):
            grad = dq_ref[part, h].T * scale
            eq[rows, h * HEAD_DIM : (h + 1) * HEAD_DIM] = turned(grad, cos_ref[rows, :], -sin_ref[rows, :]).astype(bf)
    query = eq[...]
    back = nt(query, auq_ref[...])
    total_ref[...] = nt(query, wq_ref[...]) + nn((2.0 * back).astype(bf), adq_ref[:RANK, :])
    dadq_ref[...] = nn(back.T.astype(bf), rows_ref[...])
    dauq_ref[...] = nn(low_t_ref[:RANK, :], query)


def back_key_value_kernel(
    dkv_ref, query_ref, wkv_ref, adqkv_ref, auk_ref, auv_ref, low_t_ref, rows_ref, cos_ref, sin_ref, *refs
):
    others = refs[: len(refs) - 7]
    own_ref, send_ref, dadkv_ref, dauk_ref, dauv_ref, total, back_ref = refs[len(refs) - 7 :]
    shard = lax.axis_index("tensor")
    half = own_ref.shape[0]
    grad = dkv_ref[...].astype(f32)
    for ref in others:
        grad = grad + ref[...].astype(f32)
    ek = turned(grad[:, :HEAD_DIM], cos_ref[...], -sin_ref[...]).astype(bf)
    ev = grad[:, HEAD_DIM:].astype(bf)
    back_ref[:, :RANK] = nt(ek, auk_ref[...])
    back_ref[:, RANK:] = nt(ev, auv_ref[...])
    back = back_ref[...]
    total[...] = (
        query_ref[...] + nt(ek, wkv_ref[0]) + nt(ev, wkv_ref[1]) + nn((2.0 * back).astype(bf), adqkv_ref[RANK:, :])
    )
    own_ref[...] = total[pl.ds(pl.multiple_of(shard * half, half), half), :]
    send_ref[...] = total[pl.ds(pl.multiple_of((1 - shard) * half, half), half), :].astype(bf)
    dadkv_ref[...] = nn(back.T.astype(bf), rows_ref[...])
    dauk_ref[...] = nn(low_t_ref[RANK : 2 * RANK, :], ek)
    dauv_ref[...] = nn(low_t_ref[2 * RANK :, :], ev)


def future_mask(span):
    return lax.broadcasted_iota(jnp.int32, (span, span), 0) <= lax.broadcasted_iota(jnp.int32, (span, span), 1)

def fold(s, values_t, m, l, o, coef, mask):
    if mask is not None:
        s = jnp.where(mask, s, mask_fill)
    m_next = jnp.maximum(m, jnp.max(s, axis=0, keepdims=True))
    p = jnp.exp2((s - m_next) * coef)
    alpha = jnp.exp2((m - m_next) * coef)
    l_next = l * alpha + jnp.sum(p, axis=0, keepdims=True)
    o_next = o * alpha + nn(values_t, p.astype(bf))
    return m_next, l_next, o_next

def pipelined(items, first, second):
    ahead = first(items[0])
    for i, item in enumerate(items):
        now = ahead
        if i + 1 < len(items):
            ahead = first(items[i + 1])
        second(item, now)

def attn_fwd_own_kernel(coef, q_ref, kv_ref, m_ref, l_ref, o_ref, vt):
    heads, span = q_ref.shape[1], q_ref.shape[2]
    vt[...] = kv_ref[:, HEAD_DIM:].astype(f32).T.astype(bf)
    mask = future_mask(span)
    both_mask = lax.broadcasted_iota(jnp.int32, (2 * span, span), 0) <= lax.broadcasted_iota(jnp.int32, (2 * span, span), 1) + span
    def first(item):
        half, h = item
        return nt(kv_ref[: (half + 1) * span, :HEAD_DIM], q_ref[half, h])
    def second(item, s):
        half, h = item
        m = jnp.full((1, span), mask_fill, f32)
        l = jnp.zeros((1, span), f32)
        o = jnp.zeros((HEAD_DIM, span), f32)
        m, l, o = fold(s, vt[:, : (half + 1) * span], m, l, o, coef, both_mask if half else mask)
        m_ref[half, h : h + 1, :] = m
        l_ref[half, h : h + 1, :] = l
        o_ref[half, h] = o
    pipelined([(half, h) for h in range(heads) for half in range(2)], first, second)

def attn_fwd_pieces_kernel(coef, n, last, flag_ref, q_ref, *refs):
    kv_refs = refs[:n]
    m_in, l_in, o_in = refs[n : n + 3]
    if last:
        mixed_ref, lse_ref, m_ref, l_ref, o_ref, vt = refs[n + 3 :]
    else:
        m_ref, l_ref, o_ref, vt = refs[n + 3 :]
    heads, span = q_ref.shape[1], q_ref.shape[2]
    src = [(m_in, l_in, o_in)] + [(m_ref, l_ref, o_ref)] * n
    m_ref[...] = m_in[...]
    l_ref[...] = l_in[...]
    o_ref[...] = o_in[...]
    def update(half, h, s, values_t):
        m, l, o = fold(s, values_t, m_ref[half, h : h + 1, :], l_ref[half, h : h + 1, :], o_ref[half, h], coef, None)
        m_ref[half, h : h + 1, :] = m
        l_ref[half, h : h + 1, :] = l
        o_ref[half, h] = o
    for i in range(n):
        kv_ref = kv_refs[i]
        vt[...] = kv_ref[:, HEAD_DIM:].astype(f32).T.astype(bf)
        @pl.when(flag_ref[i] == 1)
        def before():
            pipelined([(half, h) for h in range(heads) for half in range(2)],
                lambda it: nt(kv_ref[:span, :HEAD_DIM], q_ref[it[0], it[1]]),
                lambda it, s: update(it[0], it[1], s, vt[:, :span]))
        @pl.when(flag_ref[i] != 1)
        def after():
            pipelined([(1, h) for h in range(heads)],
                lambda it: nt(kv_ref[:, :HEAD_DIM], q_ref[1, it[1]]),
                lambda it, s: update(1, it[1], s, vt[...]))
    if last:
        for half in range(2):
            for h in range(heads):
                o = o_ref[half, h] / l_ref[half, h : h + 1, :]
                mixed_ref[half * span : (half + 1) * span, h * HEAD_DIM : (h + 1) * HEAD_DIM] = o.T.astype(bf)
        lse_ref[...] = m_ref[...] * coef + jnp.log2(l_ref[...])


def attn_fwd_own(q, kv, coef):
    _, heads, span, _ = q.shape
    st = (jax.ShapeDtypeStruct((2, heads, span), f32),) * 2 + (jax.ShapeDtypeStruct((2, heads, HEAD_DIM, span), f32),)
    return pl.pallas_call(functools.partial(attn_fwd_own_kernel, coef), out_shape=st, in_specs=[VM, VM], out_specs=(VM,) * 3,
        scratch_shapes=[pltpu.VMEM((HEAD_DIM, 2 * span), bf)],
        cost_estimate=pl.CostEstimate(flops=2*2*3*heads*span*span*HEAD_DIM*2, bytes_accessed=4_000_000, transcendentals=0),
        compiler_params=pltpu.CompilerParams(vmem_limit_bytes=20 << 20), name="attn_fwd_own")(q, kv)

def attn_fwd_pieces(flags, q, pieces, state, coef, last):
    _, heads, span, _ = q.shape
    n = len(pieces)
    st = (jax.ShapeDtypeStruct((2, heads, span), f32),) * 2 + (jax.ShapeDtypeStruct((2, heads, HEAD_DIM, span), f32),)
    if last:
        st = (jax.ShapeDtypeStruct((2 * span, heads * HEAD_DIM), bf), jax.ShapeDtypeStruct((2, heads, span), f32)) + st
    r = pl.pallas_call(functools.partial(attn_fwd_pieces_kernel, coef, n, last), out_shape=st, in_specs=[SM] + [VM] * (n + 4), out_specs=(VM,) * len(st),
        scratch_shapes=[pltpu.VMEM((HEAD_DIM, 2 * span), bf)],
        cost_estimate=pl.CostEstimate(flops=2*2*2*n*heads*span*span*HEAD_DIM*2, bytes_accessed=4_000_000, transcendentals=0),
        compiler_params=pltpu.CompilerParams(vmem_limit_bytes=20 << 20), name="attn_fwd_pieces")(flags, q, *pieces, *state)
    return r

def bwd_block(s, dp, lse_ref, delta_ref, half, h, coef, mask):
    p = jnp.exp2(s * coef - lse_ref[half, h : h + 1, :])
    if mask is not None:
        p = jnp.where(mask, p, 0.0)
    ds = p * (dp - delta_ref[half, h : h + 1, :])
    return p.astype(bf), ds.astype(bf)

def attn_bwd_kernel(coef, scale, n, own, has_state, flag_ref, q_ref, do_ref, lse_ref, delta_ref, *refs):
    kv_refs = refs[:n]
    k = n
    if has_state:
        dq_in = refs[k]; k += 1
    dkv_refs = refs[k : k + n]
    dq_ref, kt, pbuf, sbuf = refs[k + n :]
    heads, span = q_ref.shape[1], q_ref.shape[2]
    if has_state:
        dq_ref[...] = dq_in[...]
    else:
        dq_ref[...] = jnp.zeros_like(dq_ref)
    def do_item(kv_ref, items, keyrows, mask_of):
        nk = keyrows.stop - keyrows.start
        def first(it):
            i, half, h = it
            return nt(kv_ref[keyrows, :HEAD_DIM], q_ref[half, h]), nt(kv_ref[keyrows, HEAD_DIM:], do_ref[half, h])
        def second(it, sd):
            i, half, h = it
            p, ds = bwd_block(sd[0], sd[1], lse_ref, delta_ref, half, h, coef, mask_of(half))
            cols = slice((i * heads + h) * span, (i * heads + h + 1) * span)
            pbuf[:nk, cols] = p
            sbuf[:nk, cols] = ds
            dq_ref[half, h] += nn(kt[:, keyrows], ds)
        pipelined([(i, half, h) for i, half in enumerate(items) for h in range(heads)], first, second)
        width = len(items) * heads * span
        lo = items[0]
        q_all = q_ref[lo : lo + len(items)].reshape(width, HEAD_DIM)
        do_all = do_ref[lo : lo + len(items)].reshape(width, HEAD_DIM)
        return nn(sbuf[:nk, :width], q_all) * scale, nn(pbuf[:nk, :width], do_all)
    for i in range(n):
        kv_ref, out = kv_refs[i], dkv_refs[i]
        kt[...] = kv_ref[:, :HEAD_DIM].astype(f32).T.astype(bf)
        lo, hi, both = slice(0, span), slice(span, 2 * span), slice(0, 2 * span)
        if own and i == 0:
            mask = future_mask(span)
            dk, dv = do_item(kv_ref, [0, 1], lo, lambda half: mask if half == 0 else None)
            out[lo, :HEAD_DIM] = dk.astype(bf)
            out[lo, HEAD_DIM:] = dv.astype(bf)
            dk, dv = do_item(kv_ref, [1], hi, lambda half: mask)
            out[hi, :HEAD_DIM] = dk.astype(bf)
            out[hi, HEAD_DIM:] = dv.astype(bf)
        else:
            @pl.when(flag_ref[i] == 1)
            def before():
                dk, dv = do_item(kv_ref, [0, 1], lo, lambda half: None)
                out[lo, :HEAD_DIM] = dk.astype(bf)
                out[lo, HEAD_DIM:] = dv.astype(bf)
                out[hi, :] = jnp.zeros((span, 2 * HEAD_DIM), bf)
            @pl.when(flag_ref[i] != 1)
            def after():
                dk, dv = do_item(kv_ref, [1], both, lambda half: None)
                out[:, :HEAD_DIM] = dk.astype(bf)
                out[:, HEAD_DIM:] = dv.astype(bf)

def attn_bwd(flags, q, do, lse, delta, pieces, dq_state, coef, scale, own):
    _, heads, span, _ = q.shape
    n = len(pieces)
    outs = tuple(jax.ShapeDtypeStruct((2 * span, 2 * HEAD_DIM), bf) for _ in range(n)) + (jax.ShapeDtypeStruct((2, heads, HEAD_DIM, span), f32),)
    ins = [flags, q, do, lse, delta, *pieces] + ([dq_state] if dq_state is not None else [])
    return pl.pallas_call(functools.partial(attn_bwd_kernel, coef, scale, n, own, dq_state is not None), out_shape=outs,
        in_specs=[SM] + [VM] * (len(ins) - 1), out_specs=(VM,) * len(outs),
        scratch_shapes=[pltpu.VMEM((HEAD_DIM, 2 * span), bf), pltpu.VMEM((2 * span, 2 * heads * span), bf), pltpu.VMEM((2 * span, 2 * heads * span), bf)],
        cost_estimate=pl.CostEstimate(flops=2*5*2*n*heads*span*span*HEAD_DIM*2, bytes_accessed=4_000_000, transcendentals=0),
        compiler_params=pltpu.CompilerParams(vmem_limit_bytes=30 << 20), name="attn_bwd_pieces")(*ins)


CHUNK = 1024


def chunks_of(hidden):
    return [(low, min(low + CHUNK, hidden)) for low in range(0, hidden, CHUNK)]


def act_back_kernel(own_ref, other_ref, wd_hbm, out_hbm, rows_ref, wd, out, in_sems, out_sems):
    half = own_ref.shape[0]
    bounds = chunks_of(wd.shape[0])
    copies = [
        pltpu.make_async_copy(wd_hbm.at[low:high], wd.at[low:high], in_sems.at[i]) for i, (low, high) in enumerate(bounds)
    ]
    for copy in copies:
        copy.start()
    rows_ref[:half, :] = own_ref[...]
    rows_ref[half:, :] = other_ref[...]
    results = []
    for i, (low, high) in enumerate(bounds):
        copies[i].wait()
        out[:, low:high] = nt(rows_ref[...], wd[low:high, :])
        result = pltpu.make_async_copy(out.at[:, low:high], out_hbm.at[:, low:high], out_sems.at[i])
        result.start()
        results.append(result)
    for result in results:
        result.wait()


def act_back(own, other, wd):
    half, width = own.shape
    hidden = wd.shape[0]
    count = len(chunks_of(hidden))
    return pl.pallas_call(
        act_back_kernel,
        out_shape=pltpu.HBM((2 * half, hidden), f32),
        in_specs=[VM, VM, HB],
        out_specs=HB,
        scratch_shapes=[
            pltpu.VMEM((2 * half, width), bf), pltpu.VMEM((hidden, width), bf), pltpu.VMEM((2 * half, hidden), f32),
            pltpu.SemaphoreType.DMA((count,)), pltpu.SemaphoreType.DMA((count,)),
        ],
        cost_estimate=pl.CostEstimate(flops=4 * half * width * hidden, bytes_accessed=2 * width * hidden, transcendentals=0),
        compiler_params=pltpu.CompilerParams(vmem_limit_bytes=36 << 20),
        name="act_back",
    )(own, other, in_hbm(wd))


def whole(*dims):
    return pl.BlockSpec(dims, lambda i: (0,) * len(dims), pipeline_mode=pl.Buffered(1))


def ffn_kernel(
    tile, tiles, hidden, x_own, x_other, g_own, g_other, gact_ref, adgu_ref, auf_ref, wgu_ref, adf_ref, augu_ref,
    gx_own, gx_send, act_ref, flow_ref, dadgu_ref, dauf_ref, daugu_ref, dadf_ref,
    x_ref, g_ref, gx_acc, xlow, xlow_t, fback, fback_t, flow, back,
):
    step = pl.program_id(0)
    half = x_own.shape[0]

    @pl.when(step == 0)
    def prepare():
        for target, own, other in ((x_ref, x_own, x_other), (g_ref, g_own, g_other)):
            target[:half, :] = own[...]
            target[half:, :] = other[...]
        low = nt(x_ref[...], adgu_ref[...])
        xlow[...] = (low * 2.0).astype(bf)
        xlow_t[...] = low.T.astype(bf)
        fb = nt(g_ref[...], auf_ref[...])
        fback[...] = (fb * 2.0).astype(bf)
        fback_t[...] = fb.T.astype(bf)
        gx_acc[...] = jnp.zeros_like(gx_acc)
        flow[...] = jnp.zeros_like(flow)
        back[...] = jnp.zeros_like(back)

    def work(width):
        x = x_ref[...]
        wg, wu = wgu_ref[0, :, :width], wgu_ref[1, :, :width]
        aug, auu, adf = augu_ref[:RANK, :width], augu_ref[RANK:, :width], adf_ref[:, :width]
        gate = nn(x, wg) + nn(xlow[:, :RANK], aug)
        up = nn(x, wu) + nn(xlow[:, RANK:], auu)
        gact = gact_ref[:, :width] + nn(fback[...], adf)
        sig = 1.0 / (1.0 + jnp.exp(-gate))
        silu = gate * sig
        act = (silu * up).astype(bf)
        ggate = (gact * up * (sig + silu * (1.0 - sig))).astype(bf)
        gup = (gact * silu).astype(bf)
        act_ref[:, :width] = act
        flow[...] += nt(act, adf)
        gx_acc[...] += nt(ggate, wg) + nt(gup, wu)
        back[:, :RANK] += nt(ggate, aug)
        back[:, RANK:] += nt(gup, auu)
        daugu_ref[:RANK, :width] = nn(xlow_t[:RANK, :], ggate)
        daugu_ref[RANK:, :width] = nn(xlow_t[RANK:, :], gup)
        dadf_ref[:, :width] = nn(fback_t[...], act)

    tail = hidden - (tiles - 1) * tile
    if tail == tile:
        work(tile)
    else:
        @pl.when(step < tiles - 1)
        def body():
            work(tile)

        @pl.when(step == tiles - 1)
        def part():
            work(tail)

    @pl.when(step == tiles - 1)
    def finish():
        gx_acc[...] += nn((back[...] * 2.0).astype(bf), adgu_ref[...])
        gx_own[...] = gx_acc[:half, :]
        gx_send[...] = gx_acc[half:, :].astype(bf)
        flow_ref[...] = (flow[...] * 2.0).astype(bf)
        dadgu_ref[...] = nn(back[...].T.astype(bf), x_ref[...])
        dauf_ref[...] = nn(flow[...].T.astype(bf), g_ref[...])


def ffn(x_own, x_other, g_own, g_other, gact, adgu, auf, wgu, adf, augu, tile=512):
    rows, width = 2 * x_own.shape[0], x_own.shape[1]
    hidden = wgu.shape[2]
    tiles = -(-hidden // tile)
    half = rows // 2
    cols = lambda r: pl.BlockSpec((r, tile), lambda i: (0, i))
    outs = (
        shape(half, width), shape(half, width, dtype=bf), pltpu.HBM((rows, hidden), bf), shape(rows, RANK, dtype=bf),
        shape(2 * RANK, width), shape(RANK, width), shape(2 * RANK, hidden), shape(RANK, hidden),
    )
    return pl.pallas_call(
        functools.partial(ffn_kernel, tile, tiles, hidden),
        grid=(tiles,),
        out_shape=outs,
        in_specs=[whole(half, width)] * 4 + [cols(rows), whole(2 * RANK, width), whole(RANK, width),
                  pl.BlockSpec((2, width, tile), lambda i: (0, 0, i)), cols(RANK), cols(2 * RANK)],
        out_specs=(whole(half, width), whole(half, width), cols(rows), whole(rows, RANK), whole(2 * RANK, width),
                   whole(RANK, width), cols(2 * RANK), cols(RANK)),
        scratch_shapes=[
            pltpu.VMEM((rows, width), bf), pltpu.VMEM((rows, width), bf), pltpu.VMEM((rows, width), f32),
            pltpu.VMEM((rows, 2 * RANK), bf), pltpu.VMEM((2 * RANK, rows), bf), pltpu.VMEM((rows, RANK), bf),
            pltpu.VMEM((RANK, rows), bf), pltpu.VMEM((rows, RANK), f32), pltpu.VMEM((rows, 2 * RANK), f32),
        ],
        cost_estimate=pl.CostEstimate(flops=8 * rows * width * hidden, bytes_accessed=6 * width * hidden, transcendentals=rows * hidden),
        compiler_params=pltpu.CompilerParams(vmem_limit_bytes=36 << 20),
        name="ffn",
    )(in_hbm(x_own), in_hbm(x_other), in_hbm(g_own), in_hbm(g_other), in_hbm(gact), adgu, auf, in_hbm(wgu), adf, augu)


def down_kernel(bounds, start_refs, act_hbm, wd_hbm, total, act, wd, act_sems, wd_sems):
    low = bounds[0][0]
    copies = []
    for i, (begin, end) in enumerate(bounds):
        rows = slice(begin - low, end - low)
        copies.append((
            pltpu.make_async_copy(act_hbm.at[:, begin:end], act.at[:, rows], act_sems.at[i]),
            pltpu.make_async_copy(wd_hbm.at[begin:end], wd.at[rows], wd_sems.at[i]),
        ))
        for copy in copies[-1]:
            copy.start()
    total[...] = nn(start_refs[0][...], start_refs[1][...]) if len(start_refs) == 2 else start_refs[0][...]
    for i, (begin, end) in enumerate(bounds):
        rows = slice(begin - low, end - low)
        for copy in copies[i]:
            copy.wait()
        total[...] += nn(act[:, rows], wd[rows, :])


def down_first_kernel(bounds, flow_ref, auf_ref, act_hbm, wd_hbm, total, *scratch):
    down_kernel(bounds, (flow_ref, auf_ref), act_hbm, wd_hbm, total, *scratch)


def down_last_kernel(bounds, start_ref, act_hbm, wd_hbm, own_ref, send_ref, total, *scratch):
    down_kernel(bounds, (start_ref,), act_hbm, wd_hbm, total, *scratch)
    half = own_ref.shape[0]
    own_ref[...] = total[:half, :]
    send_ref[...] = total[half:, :].astype(bf)


def down(act, wd, start, bounds, last):
    rows, width = act.shape[0], wd.shape[1]
    half, columns, count = rows // 2, bounds[-1][1] - bounds[0][0], len(bounds)
    outs = (shape(half, width), shape(half, width, dtype=bf)) if last else (shape(rows, width),)
    scratch = [
        pltpu.VMEM((rows, columns), bf), pltpu.VMEM((columns, width), bf), pltpu.SemaphoreType.DMA((count,)),
        pltpu.SemaphoreType.DMA((count,)),
    ]
    return pl.pallas_call(
        functools.partial(down_last_kernel if last else down_first_kernel, bounds),
        out_shape=outs,
        in_specs=[VM] * len(start) + [HB, HB],
        out_specs=(VM,) * len(outs),
        scratch_shapes=([pltpu.VMEM((rows, width), f32)] if last else []) + scratch,
        cost_estimate=pl.CostEstimate(flops=2 * rows * width * columns, bytes_accessed=2 * width * columns, transcendentals=0),
        compiler_params=pltpu.CompilerParams(vmem_limit_bytes=28 << 20),
        name="down",
    )(*start, in_hbm(act), in_hbm(wd))


def per_device(
    tokens, cotangent, positions, adapter_choice, attn_gain, query_weight, query_bias, key_value_weight,
    key_value_bias, output_weight, ffn_gain, gate_upper_weight, down_weight, adapt_in, adapt_out,
):
    dp = lax.axis_index("dp")
    groups = lax.axis_size("seq")
    rings = groups // 2
    width, head_width = query_weight.shape
    heads = head_width // HEAD_DIM
    hidden = down_weight.shape[0]
    token_pos = positions[0]
    tok_count = token_pos.shape[0]
    span = tok_count // 2
    scale = HEAD_DIM ** (-0.5)
    coef = scale * math.log2(math.e)
    wide_in, wide_out = adapt_in.shape[2], adapt_out.shape[2]
    lanes_in = rounded_up(wide_in + 1, 128)
    lanes = lanes_in + rounded_up(wide_out, 128)
    widths = (width, head_width, hidden)
    sizes = (rings, wide_in, wide_out, lanes_in, widths)

    def to_pair(value):
        return lax.ppermute(value, "tensor", [(0, 1), (1, 0)])

    def to_other_sequence(value, pairs=((0, 1), (1, 0))):
        return lax.ppermute(value, "dp", list(pairs))

    def to_side(value):
        return lax.ppermute(value, "seq", [(i, i ^ 1) for i in range(groups)])

    def along_ring(value, steps):
        return lax.ppermute(value, "seq", [(i, (i + 2 * steps) % groups) for i in range(groups)])

    def after(value, *others):
        return lax.optimization_barrier((value, *others))[0]

    inputs, grad_out = tokens[0], cotangent[0]
    half = inputs.shape[0]
    attn_gain, ffn_gain = attn_gain[None], ffn_gain[None]

    def over_ring(piece):
        return [piece] + [along_ring(piece, step) for step in range(1, rings)]

    slice_own, slice_other = call(
        functools.partial(select_kernel, lanes_in, span), "select",
        [shape(RANK, lanes, dtype=bf)] * 2, [adapter_choice, positions, adapt_in, adapt_out],
        [pltpu.VMEM((2, RANK, wide_in), bf), pltpu.VMEM((2, RANK, wide_out), bf), pltpu.SemaphoreType.DMA((4,))],
        smem=2, left=2,
    )
    slice_other = to_other_sequence(slice_other)
    lane = lax.broadcasted_iota(jnp.int32, (RANK, lanes), 1)
    run_lane = (lane >= wide_in) & (lane < lanes_in)
    grad_other = to_pair(grad_out)
    slice_other = after(slice_other, grad_other)
    first_slice = jnp.where((dp == 0) | run_lane, slice_own, slice_other)
    second_slice = jnp.where(dp == 0, slice_other, slice_own)

    (normed,) = call(norm_kernel, "norm", [shape(half, width, dtype=bf)], [inputs, attn_gain])
    normed_other = to_pair(normed)
    arrived = over_ring(jnp.stack([first_slice, second_slice]))
    act_grad = act_back(grad_out, grad_other, down_weight)
    arrived[1] = after(arrived[1], act_grad)
    own_slices = jnp.stack([piece[0] for piece in arrived])
    own_second = jnp.stack([piece[1] for piece in arrived])
    side_slices = to_side(own_slices)
    pair_slices = to_pair(own_slices)
    normed_rows, query_dense, kv_dense = call(
        dense_kernel, "dense", [shape(tok_count, width, dtype=bf), shape(tok_count, head_width), shape(tok_count, 2 * HEAD_DIM)],
        [normed, normed_other, query_weight, key_value_weight],
        flops=2 * tok_count * width * (head_width + 2 * HEAD_DIM),
    )
    frequency = jnp.power(rope_base, -(jnp.arange(HEAD_DIM // 2, dtype=f32) * 2.0) / HEAD_DIM)
    angles = token_pos.astype(f32)[:, None] * frequency[None, :]
    cosine, sine = jnp.cos(angles), jnp.sin(angles)
    cosine = jnp.concatenate([cosine, cosine], axis=1)
    sine = jnp.concatenate([-sine, sine], axis=1)

    side_slices = after(side_slices, kv_dense)
    first_slices = [own_slices, side_slices, pair_slices, to_pair(side_slices)]
    side_second = to_side(after(own_second, side_slices))
    pair_second = to_pair(after(own_second, side_slices))
    slices_in = -(-4 * width // wide_in)
    slices_out = -(-(2 * width + 4 * HEAD_DIM) // wide_out)
    flags, adqkv, auq, auk, auv, ado, auo = call(
        functools.partial(unpack_first_kernel, *sizes), "unpack_first",
        [shape(groups, dtype=jnp.int32)]
        + [
            shape(*dims, dtype=bf)
            for dims in (
                (3 * RANK, width), (RANK, head_width), (RANK, HEAD_DIM), (RANK, HEAD_DIM), (RANK, head_width), (RANK, width),
            )
        ],
        list(first_slices),
        [
            pltpu.VMEM((2 * groups, RANK, lanes), bf),
            pltpu.VMEM((RANK, rounded_up(slices_in * wide_in, 128) + 256), f32),
            pltpu.VMEM((RANK, rounded_up(slices_out * wide_out, 128) + 256), f32),
        ],
        out_specs=(SM,) + (VM,) * 6,
    )
    kv, low, low_t = call(
        key_value_kernel, "key_value",
        [shape(tok_count, 2 * HEAD_DIM, dtype=bf), shape(tok_count, 3 * RANK, dtype=bf), shape(3 * RANK, tok_count, dtype=bf)],
        [normed_rows, kv_dense, key_value_bias, adqkv, auk, auv, cosine, sine],
        flops=2 * tok_count * width * 2 * RANK,
    )

    (queries,) = call(
        query_kernel, "query", [shape(2, heads, span, HEAD_DIM, dtype=bf)],
        [query_dense, query_bias[None], low, auq, cosine, sine], flops=2 * tok_count * width * RANK,
    )
    state = attn_fwd_own(queries, kv, coef)
    ring_piece, side_piece = kv, to_side(kv)
    pieces = [kv, side_piece]
    for begin in range(1, groups, 2):
        end = min(begin + 2, groups)
        if end - begin == 2:
            ring_piece = after(along_ring(ring_piece, 1), state[0])
            side_piece = to_side(after(ring_piece, side_piece))
            pieces += [ring_piece, side_piece]
        if begin == 1:
            state = (after(state[0], side_second, pair_second), *state[1:])
            far_second = to_pair(after(side_second, state[0]))
        if end == groups:
            state = (after(state[0], far_second), *state[1:])
        result = attn_fwd_pieces(flags[begin:end], queries, pieces[begin:end], state, coef, end == groups)
        state = result[-3:]
    mixed, lse = result[0], result[1]
    second_slices = [own_second, side_second, pair_second, far_second]

    branch_own, branch_send, mix_low_t = call(
        mix_out_kernel, "mix_out",
        [shape(half, width), shape(half, width, dtype=bf), shape(RANK, tok_count, dtype=bf)],
        [mixed, output_weight, ado, auo],
        [pltpu.VMEM((tok_count, width), f32)], flops=2 * tok_count * width * head_width,
    )
    hidden_rows, normed_ffn = call(
        residual_kernel, "residual", [pltpu.HBM((half, width), f32), pltpu.HBM((half, width), bf)],
        [inputs, branch_own, to_pair(branch_send), ffn_gain],
    )
    begin_in, begin_out, first_in, first_out = bases(wide_in, wide_out, widths)
    adgu, augu, adf, auf = call(
        functools.partial(unpack_second_kernel, *sizes), "unpack_second",
        [shape(*dims, dtype=bf) for dims in ((2 * RANK, width), (2 * RANK, hidden), (RANK, hidden), (RANK, width))],
        list(first_slices) + list(second_slices),
        [
            pltpu.VMEM((4 * groups, RANK, lanes), bf),
            pltpu.VMEM((RANK, rounded_up(4 * groups * wide_in, 128) + 256 - first_in), f32),
            pltpu.VMEM((RANK, rounded_up(4 * groups * wide_out, 128) + 256 - first_out), f32),
        ],
    )
    gx_own, gx_send, act, flow, dadgu, dauf, daugu, dadf = ffn(
        normed_ffn, to_pair(normed_ffn), grad_out, grad_other, act_grad, adgu, auf, gate_upper_weight, adf, augu
    )
    ad_lanes = rounded_up(4 * groups * wide_in, 128) + 256
    au_lanes = rounded_up(4 * groups * wide_out, 128) + 256

    def added(*values):
        total = values[0].astype(f32)
        for value in values[1:]:
            total = total + value.astype(f32)
        return total.astype(bf)

    grad_hidden, grad_low = call(
        hidden_back_kernel, "hidden_back", [shape(half, width), shape(half, width, dtype=bf)],
        [hidden_rows, grad_out, gx_own, to_pair(gx_send), ffn_gain],
    )
    grad_mixed, delta, dado, dauo = call(
        mix_back_kernel, "mix_back",
        [shape(2, heads, span, HEAD_DIM, dtype=bf), shape(2, heads, span), shape(RANK, head_width), shape(RANK, width)],
        [grad_low, to_pair(grad_low), output_weight, ado, auo, mixed, mix_low_t],
        [pltpu.VMEM((tok_count, width), bf)], flops=2 * tok_count * width * head_width,
    )
    state_dq, arrived, held = None, [], None
    for turn, place in enumerate(list(range(1, rings)) + [0]):
        if turn >= 2:
            mine = added(*held)
            held = terms[0], to_side(after(terms[1], mine))
            state_dq = after(state_dq, mine, *arrived[-1:])
            arrived.append(along_ring(mine, -(turn - 1)))
        elif turn == 1:
            held = terms[0], to_side(terms[1])
        *terms, state_dq = attn_bwd(
            flags[2 * place : 2 * place + 2], queries, grad_mixed, lse, delta, pieces[2 * place : 2 * place + 2],
            state_dq, coef, scale, place == 0,
        )
    mine = added(*held)
    state_dq = after(state_dq, mine, *arrived[-1:])
    arrived.append(along_ring(mine, -(rings - 1)))
    side_term = to_side(after(terms[1], mine))
    gn_query, dadq, dauq = call(
        functools.partial(back_query_kernel, scale), "back_query",
        [shape(tok_count, width), shape(RANK, width), shape(RANK, head_width)],
        [state_dq, query_weight, adqkv, auq, low_t, normed_rows, cosine, sine],
        [pltpu.VMEM((tok_count, head_width), bf)], flops=2 * tok_count * width * head_width,
    )
    side_term = after(side_term, gn_query)
    gn_own, gn_send, dadkv, dauk, dauv = call(
        back_key_value_kernel, "back_key_value",
        [
            shape(half, width), shape(half, width, dtype=bf), shape(2 * RANK, width), shape(RANK, HEAD_DIM),
            shape(RANK, HEAD_DIM),
        ],
        [
            terms[0], gn_query, key_value_weight, adqkv, auk, auv, low_t, normed_rows, cosine, sine, side_term,
            *arrived,
        ],
        [pltpu.VMEM((tok_count, width), f32), pltpu.VMEM((tok_count, 2 * RANK), f32)],
        flops=2 * tok_count * width * 2 * HEAD_DIM, limit=20,
    )
    keep, send = call(
        functools.partial(pack_kernel, *sizes), "pack", [shape(2, rings, 2, RANK, lanes, dtype=bf)] * 2,
        [dadq, dadkv, dado, dadgu, dadf, dauq, dauk, dauv, dauo, daugu, dauf],
        [pltpu.VMEM((RANK, ad_lanes), f32), pltpu.VMEM((RANK, au_lanes), f32)],
    )
    from_pair = to_pair(send)
    near, far = added(keep[0], from_pair[0]), added(keep[1], from_pair[1])
    from_side = to_side(far)
    bounds = chunks_of(hidden)
    (out_total,) = down(after(act, far), down_weight, (flow, auf), bounds[: len(bounds) // 2], False)
    from_side = after(from_side, out_total)
    sums = [added(near[place], from_side[place]) for place in range(rings)]
    from_ring = [along_ring(sums[place], -place) for place in range(1, rings)]
    out_own, out_send = down(after(act, sums[0]), down_weight, (out_total,), bounds[len(bounds) // 2 :], True)
    (grad_tokens,) = call(
        token_back_kernel, "token_back", [shape(half, width)],
        [inputs, grad_hidden, gn_own, after(to_pair(gn_send), out_own), attn_gain],
    )
    output = (hidden_rows + (out_own + to_pair(out_send).astype(f32))).astype(bf)
    from_ring[0] = after(from_ring[0], out_own)
    total = added(sums[0], *from_ring)
    other_total = after(to_other_sequence(total[1]), output, grad_tokens)
    factor = adapter_scale * (adapter_choice.shape[0] * tok_count * groups) ** (-0.5)
    adapt_in_grad, adapt_out_grad = call(
        functools.partial(place_kernel, lanes_in, factor), "place",
        [shape(*adapt_in.shape), shape(*adapt_out.shape)],
        [adapter_choice, total[0], other_total], smem=1,
    )
    return (output[None], grad_tokens[None], adapt_in_grad, adapt_out_grad)


def solution(mesh):
    return jax.shard_map(
        per_device,
        mesh=mesh,
        in_specs=(
            P("dp", ("seq", "tensor"), None),
            P("dp", ("seq", "tensor"), None),
            P("dp", "seq"),
            P(),
            P(),
            P(None, "tensor"),
            P("tensor"),
            P(None, None, "tensor"),
            P(None, "tensor"),
            P("tensor", None),
            P(),
            P(None, None, "tensor"),
            P("tensor", None),
            P(None, None, ("dp", "seq", "tensor")),
            P(None, None, ("dp", "seq", "tensor")),
        ),
        out_specs=(
            P("dp", ("seq", "tensor"), None),
            P("dp", ("seq", "tensor"), None),
            P(None, None, ("dp", "seq", "tensor")),
            P(None, None, ("dp", "seq", "tensor")),
        ),
        check_vma=False,
    )
```

```python
import functools
import math

import jax
import jax.numpy as jnp
from jax import lax
from jax.experimental import pallas as pl
from jax.experimental.pallas import tpu as pltpu
from jax.sharding import PartitionSpec as P

HEAD_DIM = 128
RANK = 16
eps = 1e-06
adapter_scale = 2.0
rope_base = 1000000.0
mask_fill = -1e30
bf = jnp.bfloat16
f32 = jnp.float32
VM = pl.BlockSpec(memory_space=pltpu.VMEM)
SM = pl.BlockSpec(memory_space=pltpu.SMEM)


def nn(a, b):
    return jnp.dot(a, b, preferred_element_type=f32)


def nt(a, b):
    return lax.dot_general(a, b, (((1,), (1,)), ((), ())), preferred_element_type=f32)


def shape(*dims, dtype=f32):
    return jax.ShapeDtypeStruct(dims, dtype)


def call(kernel, name, out, ins, scratch=(), flops=0, smem=0, out_specs=None, limit=16, left=0):
    moved = sum(math.prod(v.shape) * v.dtype.itemsize for v in list(ins) + list(out))
    ins = list(ins[: len(ins) - left]) + [in_hbm(value) for value in ins[len(ins) - left :]]
    return pl.pallas_call(
        kernel,
        out_shape=tuple(out),
        in_specs=[SM] * smem + [VM] * (len(ins) - smem - left) + [HB] * left,
        out_specs=out_specs or (VM,) * len(out),
        scratch_shapes=list(scratch),
        cost_estimate=pl.CostEstimate(flops=flops, bytes_accessed=moved, transcendentals=0),
        compiler_params=pltpu.CompilerParams(vmem_limit_bytes=limit << 20),
        name=name,
    )(*ins)


HB = pl.BlockSpec(memory_space=pltpu.HBM)


def in_hbm(value):
    return pltpu.with_memory_space_constraint(value, pltpu.HBM)


def rounded_up(value, unit):
    return -(-value // unit) * unit


def select_kernel(lanes_in, span, choice_ref, pos_ref, in_ref, out_ref, own_ref, other_ref, held_in, held_out, sems):
    wide_in, wide_out = in_ref.shape[2], out_ref.shape[2]
    dp = lax.axis_index("dp")
    copies = []
    for slot, sequence in ((0, dp), (1, 1 - dp)):
        chosen = choice_ref[sequence]
        copies.append(pltpu.make_async_copy(in_ref.at[chosen], held_in.at[slot], sems.at[2 * slot]))
        copies.append(pltpu.make_async_copy(out_ref.at[chosen], held_out.at[slot], sems.at[2 * slot + 1]))
    for copy in copies:
        copy.start()
    run = jnp.full((RANK, lanes_in), pos_ref[0, 0] // span, jnp.int32).astype(f32).astype(bf)
    for target in (own_ref, other_ref):
        target[...] = jnp.zeros_like(target)
        target[:, :lanes_in] = run
    for copy in copies:
        copy.wait()
    for slot, target in ((0, own_ref), (1, other_ref)):
        target[:, :wide_in] = held_in[slot]
        target[:, lanes_in : lanes_in + wide_out] = held_out[slot]


def column(begin, size):
    return pl.ds(pl.multiple_of(begin, 128), size)


def source_of(place, side, rings, seq):
    ring = lax.rem(seq // 2 - place + rings, rings)
    own_side = lax.rem(seq, 2)
    return ring * 2 + (own_side if side == 0 else 1 - own_side)


def spread(slots, target, begin, wide, first, low, high):
    held = rounded_up(wide, 128)
    inside = lax.broadcasted_iota(jnp.int32, (RANK, held), 1) < wide
    target[...] = jnp.zeros_like(target)
    for index in range(low // wide, -(-high // wide)):
        part = jnp.where(inside, slots[index, :, begin : begin + held].astype(f32), 0.0)
        part = jnp.concatenate([part, jnp.zeros((RANK, 128), f32)], axis=1)
        offset = index * wide - first
        base = offset // 128 * 128
        if offset != base:
            part = pltpu.roll(part, offset - base, 1)
        target[:, base : base + held + 128] += part


def collect(slots, refs, rings, part):
    seq, shard = lax.axis_index("seq"), lax.axis_index("tensor")
    for number, ref in enumerate(refs):
        side, core = number % 2, shard if number < 2 else 1 - shard
        for place in range(rings):
            slots[part * 4 * rings + source_of(place, side, rings, seq) * 2 + core] = ref[place]


def unpack_first_kernel(
    rings, wide_in, wide_out, lanes_in, widths, own, own_side, pair, pair_side,
    flags_ref, adqkv, auq, auk, auv, ado, auo, slots, ad, au, runs,
):
    shard, seq = lax.axis_index("tensor"), lax.axis_index("seq")
    width, head_width, hidden = widths
    for place in range(rings):
        for side, ref in ((0, own), (1, own_side)):
            run = jnp.max(ref[place, :, wide_in:lanes_in].astype(f32))
            runs[source_of(place, side, rings, seq)] = run.astype(jnp.int32)
    groups = 2 * rings
    place = jnp.where(lax.rem(seq, 2) == 0, seq // 2, groups - 1 - seq // 2)
    for index in range(groups):
        step = (index + 1) // 2
        other = lax.rem(place + (groups - step if index % 2 == 1 else step), groups)
        source = jnp.where(other < rings, 2 * other, 2 * (groups - 1 - other) + 1)
        flags_ref[index] = (runs[source] < runs[seq]).astype(jnp.int32)
    collect(slots, (own, own_side, pair, pair_side), rings, 0)
    spread(slots, ad, 0, wide_in, 0, 0, 4 * width)
    spread(slots, au, lanes_in, wide_out, 0, 0, 2 * width + 4 * HEAD_DIM)
    for index in range(3):
        adqkv[index * RANK : (index + 1) * RANK, :] = ad[:, index * width : (index + 1) * width].astype(bf)
    ado[...] = ad[:, column(3 * width + shard * head_width, head_width)].astype(bf)
    auq[...] = au[:, column(shard * head_width, head_width)].astype(bf)
    auk[...] = au[:, column(width + shard * HEAD_DIM, HEAD_DIM)].astype(bf)
    auv[...] = au[:, column(width + (2 + shard) * HEAD_DIM, HEAD_DIM)].astype(bf)
    base = width + 4 * HEAD_DIM
    auo[...] = au[:, base : base + width].astype(bf)


def bases(wide_in, wide_out, widths):
    width = widths[0]
    begin_in, begin_out = 4 * width, 2 * width + 4 * HEAD_DIM
    return begin_in, begin_out, begin_in // wide_in * wide_in // 128 * 128, begin_out // wide_out * wide_out // 128 * 128


def unpack_second_kernel(
    rings, wide_in, wide_out, lanes_in, widths, *refs
):
    firsts, seconds = refs[:4], refs[4:8]
    adgu, augu, adf, auf, slots, ad, au = refs[8:]
    shard = lax.axis_index("tensor")
    width, head_width, hidden = widths
    collect(slots, firsts, rings, 0)
    collect(slots, seconds, rings, 1)
    begin_in, begin_out, first_in, first_out = bases(wide_in, wide_out, widths)
    total_in, total_out = 8 * rings * wide_in, 8 * rings * wide_out
    spread(slots, ad, 0, wide_in, first_in, begin_in, total_in)
    spread(slots, au, lanes_in, wide_out, first_out, begin_out, total_out)
    base = begin_in - first_in
    for index in range(2):
        adgu[index * RANK : (index + 1) * RANK, :] = ad[:, base + index * width : base + (index + 1) * width].astype(bf)
    adf[...] = ad[:, column(base + 2 * width + shard * hidden, hidden)].astype(bf)
    base = begin_out - first_out
    for index in range(2):
        augu[index * RANK : (index + 1) * RANK, :] = au[
            :, column(base + (2 * index + shard) * hidden, hidden)
        ].astype(bf)
    auf[...] = au[:, base + 4 * hidden : base + 4 * hidden + width].astype(bf)


def put_slices(rings, wide_in, wide_out, lanes_in, ad, au, limits, parts, write):
    dp, seq = lax.axis_index("dp"), lax.axis_index("seq")
    for index in range(4 * rings * parts):
        to_dp, to_seq, to_core = index // (4 * rings), index // 2 % (2 * rings), index % 2
        pieces = []
        for source, wide, (low, high, first) in ((ad, wide_in, limits[0]), (au, wide_out, limits[1])):
            held = rounded_up(wide, 128)
            if index * wide >= high or (index + 1) * wide <= low:
                part = jnp.zeros((RANK, held), f32)
            else:
                offset = index * wide - first
                base = offset // 128 * 128
                part = source[:, base : base + held + 128]
                if offset != base:
                    part = pltpu.roll(part, held + 128 - (offset - base), 1)
                part = part[:, :held]
            pieces.append(part)
            if source is ad and lanes_in > held:
                pieces.append(jnp.zeros((RANK, lanes_in - held), f32))
        packed = jnp.concatenate(pieces, axis=1).astype(bf)
        place = lax.rem(seq // 2 - to_seq // 2 + rings, rings)
        write(to_seq, to_core, place, lax.rem(dp + to_dp, 2), packed)


def pack_kernel(
    rings, wide_in, wide_out, lanes_in, widths,
    dadq, dadkv, dado, dadgu, dadf, dauq, dauk, dauv, dauo, daugu, dauf, out_ref, ad, au,
):
    shard, side = lax.axis_index("tensor"), lax.rem(lax.axis_index("seq"), 2)
    width, head_width, hidden = widths
    ad[...] = jnp.zeros_like(ad)
    au[...] = jnp.zeros_like(au)
    ad[:, :width] = dadq[...]
    for index in range(2):
        ad[:, (1 + index) * width : (2 + index) * width] = dadkv[index * RANK : (index + 1) * RANK, :]
        ad[:, (4 + index) * width : (5 + index) * width] = dadgu[index * RANK : (index + 1) * RANK, :]
    ad[:, column(3 * width + shard * head_width, head_width)] = dado[...]
    ad[:, column(6 * width + shard * hidden, hidden)] = dadf[...]
    au[:, column(shard * head_width, head_width)] = dauq[...]
    au[:, column(width + shard * HEAD_DIM, HEAD_DIM)] = dauk[...]
    au[:, column(width + (2 + shard) * HEAD_DIM, HEAD_DIM)] = dauv[...]
    base = width + 4 * HEAD_DIM
    au[:, base : base + width] = dauo[...]
    base = base + width
    for index in range(2):
        au[:, column(base + (2 * index + shard) * hidden, hidden)] = daugu[index * RANK : (index + 1) * RANK, :]
    au[:, base + 4 * hidden : base + 4 * hidden + width] = dauf[...]

    def write(to_seq, to_core, place, part, packed):
        out_ref[lax.rem(shard + to_core, 2), lax.rem(side + to_seq % 2, 2), place, part] = packed

    limits = ((0, 8 * rings * wide_in, 0), (0, 8 * rings * wide_out, 0))
    put_slices(rings, wide_in, wide_out, lanes_in, ad, au, limits, 2, write)


def place_kernel(lanes_in, factor, choice_ref, own_ref, other_ref, in_ref, out_ref):
    wide_in, wide_out = in_ref.shape[2], out_ref.shape[2]
    dp = lax.axis_index("dp")
    in_ref[...] = jnp.zeros_like(in_ref)
    out_ref[...] = jnp.zeros_like(out_ref)
    for ref, sequence in ((own_ref, dp), (other_ref, 1 - dp)):
        chosen = choice_ref[sequence]
        part = ref[...].astype(f32) * factor
        in_ref[chosen] = in_ref[chosen] + part[:, :wide_in]
        out_ref[chosen] = out_ref[chosen] + part[:, lanes_in : lanes_in + wide_out]


def factor_of(rows):
    return lax.rsqrt(jnp.mean(rows * rows, axis=-1, keepdims=True) + eps)


def norm_back(rows, gain, grad):
    factor = factor_of(rows)
    scaled = rows * factor
    grad_scaled = grad * gain
    return factor * (grad_scaled - scaled * jnp.mean(grad_scaled * scaled, axis=-1, keepdims=True))


def norm_kernel(rows_ref, gain_ref, normed_ref):
    rows = rows_ref[...].astype(f32)
    normed_ref[...] = (rows * factor_of(rows) * gain_ref[...].astype(f32)).astype(bf)


def residual_kernel(rows_ref, own_ref, other_ref, gain_ref, hidden_ref, normed_ref):
    rows = rows_ref[...].astype(f32) + (own_ref[...] + other_ref[...].astype(f32))
    hidden_ref[...] = rows
    normed_ref[...] = (rows * factor_of(rows) * gain_ref[...].astype(f32)).astype(bf)


def hidden_back_kernel(hidden_ref, grad_ref, own_ref, other_ref, gain_ref, out_ref, low_ref):
    grad = own_ref[...] + other_ref[...].astype(f32)
    total = grad_ref[...].astype(f32) + norm_back(hidden_ref[...], gain_ref[...].astype(f32), grad)
    out_ref[...] = total
    low_ref[...] = total.astype(bf)


def token_back_kernel(rows_ref, grad_ref, own_ref, other_ref, gain_ref, out_ref):
    grad = own_ref[...] + other_ref[...].astype(f32)
    out_ref[...] = grad_ref[...] + norm_back(rows_ref[...].astype(f32), gain_ref[...].astype(f32), grad)


def turned(rows, cosine, sine):
    return rows * cosine + pltpu.roll(rows, HEAD_DIM // 2, 1) * sine


def dense_kernel(own_ref, other_ref, wq_ref, wkv_ref, rows_ref, query_ref, kv_ref):
    shard = lax.axis_index("tensor")
    half = own_ref.shape[0]
    rows_ref[pl.ds(pl.multiple_of(shard * half, half), half), :] = own_ref[...]
    rows_ref[pl.ds(pl.multiple_of((1 - shard) * half, half), half), :] = other_ref[...]
    rows = rows_ref[...]
    query_ref[...] = nn(rows, wq_ref[...])
    kv_ref[:, :HEAD_DIM] = nn(rows, wkv_ref[0])
    kv_ref[:, HEAD_DIM:] = nn(rows, wkv_ref[1])


def key_value_kernel(
    rows_ref, dense_ref, bias_ref, adqkv_ref, auk_ref, auv_ref, cos_ref, sin_ref, kv_ref, low_ref, low_t_ref
):
    low = nt(rows_ref[...], adqkv_ref[...])
    low_ref[...] = (2.0 * low).astype(bf)
    low_t_ref[...] = low.T.astype(bf)
    key = dense_ref[:, :HEAD_DIM] + bias_ref[0:1, :].astype(f32) + nn(low_ref[:, RANK : 2 * RANK], auk_ref[...])
    value = dense_ref[:, HEAD_DIM:] + bias_ref[1:2, :].astype(f32) + nn(low_ref[:, 2 * RANK :], auv_ref[...])
    kv_ref[:, :HEAD_DIM] = turned(key, cos_ref[...], sin_ref[...]).astype(bf)
    kv_ref[:, HEAD_DIM:] = value.astype(bf)


def query_kernel(dense_ref, bias_ref, low_ref, auq_ref, cos_ref, sin_ref, q_ref):
    heads, span = q_ref.shape[1], q_ref.shape[2]
    query = dense_ref[...] + bias_ref[...].astype(f32) + nn(low_ref[:, :RANK], auq_ref[...])
    for h in range(heads):
        head = turned(query[:, h * HEAD_DIM : (h + 1) * HEAD_DIM], cos_ref[...], sin_ref[...]).astype(bf)
        q_ref[0, h] = head[:span]
        q_ref[1, h] = head[span:]


def mix_out_kernel(mixed_ref, wo_ref, ado_ref, auo_ref, own_ref, send_ref, low_t_ref, total):
    shard = lax.axis_index("tensor")
    half = own_ref.shape[0]
    mixed = mixed_ref[...]
    low = nt(mixed, ado_ref[...])
    low_t_ref[...] = low.T.astype(bf)
    total[...] = nn(mixed, wo_ref[...]) + nn((2.0 * low).astype(bf), auo_ref[...])
    own_ref[...] = total[pl.ds(pl.multiple_of(shard * half, half), half), :]
    send_ref[...] = total[pl.ds(pl.multiple_of((1 - shard) * half, half), half), :].astype(bf)


def mix_back_kernel(
    own_ref, other_ref, wo_ref, ado_ref, auo_ref, mixed_ref, low_t_ref,
    do_ref, delta_ref, dado_ref, dauo_ref, rows_ref,
):
    shard = lax.axis_index("tensor")
    half = own_ref.shape[0]
    heads, span = do_ref.shape[1], do_ref.shape[2]
    rows_ref[pl.ds(pl.multiple_of(shard * half, half), half), :] = own_ref[...]
    rows_ref[pl.ds(pl.multiple_of((1 - shard) * half, half), half), :] = other_ref[...]
    rows = rows_ref[...]
    back = nt(rows, auo_ref[...])
    grad = (nt(rows, wo_ref[...]) + nn((2.0 * back).astype(bf), ado_ref[...])).astype(bf)
    dado_ref[...] = nn(back.T.astype(bf), mixed_ref[...])
    dauo_ref[...] = nn(low_t_ref[...], rows)
    for h in range(heads):
        cols = slice(h * HEAD_DIM, (h + 1) * HEAD_DIM)
        product = (grad[:, cols].astype(f32) * mixed_ref[:, cols].astype(f32)).T
        row = jnp.sum(product, axis=0, keepdims=True)
        for part in range(2):
            do_ref[part, h] = grad[part * span : (part + 1) * span, cols]
            delta_ref[part, h : h + 1, :] = row[:, part * span : (part + 1) * span]


def back_query_kernel(
    scale, dq_ref, wq_ref, adq_ref, auq_ref, low_t_ref, rows_ref, cos_ref, sin_ref, total_ref, dadq_ref, dauq_ref, eq
):
    heads, span = dq_ref.shape[1], dq_ref.shape[3]
    for part in range(2):
        rows = slice(part * span, (part + 1) * span)
        for h in range(heads):
            grad = dq_ref[part, h].T * scale
            eq[rows, h * HEAD_DIM : (h + 1) * HEAD_DIM] = turned(grad, cos_ref[rows, :], -sin_ref[rows, :]).astype(bf)
    query = eq[...]
    back = nt(query, auq_ref[...])
    total_ref[...] = nt(query, wq_ref[...]) + nn((2.0 * back).astype(bf), adq_ref[:RANK, :])
    dadq_ref[...] = nn(back.T.astype(bf), rows_ref[...])
    dauq_ref[...] = nn(low_t_ref[:RANK, :], query)


def back_key_value_kernel(
    dkv_ref, query_ref, wkv_ref, adqkv_ref, auk_ref, auv_ref, low_t_ref, rows_ref, cos_ref, sin_ref, *refs
):
    others = refs[: len(refs) - 7]
    own_ref, send_ref, dadkv_ref, dauk_ref, dauv_ref, total, back_ref = refs[len(refs) - 7 :]
    shard = lax.axis_index("tensor")
    half = own_ref.shape[0]
    grad = dkv_ref[...].astype(f32)
    for ref in others:
        grad = grad + ref[...].astype(f32)
    ek = turned(grad[:, :HEAD_DIM], cos_ref[...], -sin_ref[...]).astype(bf)
    ev = grad[:, HEAD_DIM:].astype(bf)
    back_ref[:, :RANK] = nt(ek, auk_ref[...])
    back_ref[:, RANK:] = nt(ev, auv_ref[...])
    back = back_ref[...]
    total[...] = (
        query_ref[...] + nt(ek, wkv_ref[0]) + nt(ev, wkv_ref[1]) + nn((2.0 * back).astype(bf), adqkv_ref[RANK:, :])
    )
    own_ref[...] = total[pl.ds(pl.multiple_of(shard * half, half), half), :]
    send_ref[...] = total[pl.ds(pl.multiple_of((1 - shard) * half, half), half), :].astype(bf)
    dadkv_ref[...] = nn(back.T.astype(bf), rows_ref[...])
    dauk_ref[...] = nn(low_t_ref[RANK : 2 * RANK, :], ek)
    dauv_ref[...] = nn(low_t_ref[2 * RANK :, :], ev)


def future_mask(span):
    return lax.broadcasted_iota(jnp.int32, (span, span), 0) <= lax.broadcasted_iota(jnp.int32, (span, span), 1)

def fold(s, values_t, m, l, o, coef, mask):
    if mask is not None:
        s = jnp.where(mask, s, mask_fill)
    m_next = jnp.maximum(m, jnp.max(s, axis=0, keepdims=True))
    p = jnp.exp2((s - m_next) * coef)
    alpha = jnp.exp2((m - m_next) * coef)
    l_next = l * alpha + jnp.sum(p, axis=0, keepdims=True)
    o_next = o * alpha + nn(values_t, p.astype(bf))
    return m_next, l_next, o_next

def pipelined(items, first, second):
    ahead = first(items[0])
    for i, item in enumerate(items):
        now = ahead
        if i + 1 < len(items):
            ahead = first(items[i + 1])
        second(item, now)

def attn_fwd_own_kernel(coef, q_ref, kv_ref, m_ref, l_ref, o_ref, vt):
    heads, span = q_ref.shape[1], q_ref.shape[2]
    vt[...] = kv_ref[:, HEAD_DIM:].astype(f32).T.astype(bf)
    mask = future_mask(span)
    both_mask = lax.broadcasted_iota(jnp.int32, (2 * span, span), 0) <= lax.broadcasted_iota(jnp.int32, (2 * span, span), 1) + span
    def first(item):
        half, h = item
        return nt(kv_ref[: (half + 1) * span, :HEAD_DIM], q_ref[half, h])
    def second(item, s):
        half, h = item
        m = jnp.full((1, span), mask_fill, f32)
        l = jnp.zeros((1, span), f32)
        o = jnp.zeros((HEAD_DIM, span), f32)
        m, l, o = fold(s, vt[:, : (half + 1) * span], m, l, o, coef, both_mask if half else mask)
        m_ref[half, h : h + 1, :] = m
        l_ref[half, h : h + 1, :] = l
        o_ref[half, h] = o
    pipelined([(half, h) for h in range(heads) for half in range(2)], first, second)

def attn_fwd_pieces_kernel(coef, indices, last, flag_ref, q_ref, *refs):
    n = len(indices)
    kv_refs = refs[:n]
    m_in, l_in, o_in = refs[n : n + 3]
    if last:
        mixed_ref, lse_ref, m_ref, l_ref, o_ref, vt = refs[n + 3 :]
    else:
        m_ref, l_ref, o_ref, vt = refs[n + 3 :]
    heads, span = q_ref.shape[1], q_ref.shape[2]
    src = [(m_in, l_in, o_in)] + [(m_ref, l_ref, o_ref)] * n
    m_ref[...] = m_in[...]
    l_ref[...] = l_in[...]
    o_ref[...] = o_in[...]
    def update(half, h, s, values_t):
        m, l, o = fold(s, values_t, m_ref[half, h : h + 1, :], l_ref[half, h : h + 1, :], o_ref[half, h], coef, None)
        m_ref[half, h : h + 1, :] = m
        l_ref[half, h : h + 1, :] = l
        o_ref[half, h] = o
    for i in range(n):
        kv_ref = kv_refs[i]
        vt[...] = kv_ref[:, HEAD_DIM:].astype(f32).T.astype(bf)
        @pl.when(flag_ref[indices[i]] == 1)
        def before():
            pipelined([(half, h) for h in range(heads) for half in range(2)],
                lambda it: nt(kv_ref[:span, :HEAD_DIM], q_ref[it[0], it[1]]),
                lambda it, s: update(it[0], it[1], s, vt[:, :span]))
        @pl.when(flag_ref[indices[i]] != 1)
        def after():
            pipelined([(1, h) for h in range(heads)],
                lambda it: nt(kv_ref[:, :HEAD_DIM], q_ref[1, it[1]]),
                lambda it, s: update(1, it[1], s, vt[...]))
    if last:
        for half in range(2):
            for h in range(heads):
                o = o_ref[half, h] / l_ref[half, h : h + 1, :]
                mixed_ref[half * span : (half + 1) * span, h * HEAD_DIM : (h + 1) * HEAD_DIM] = o.T.astype(bf)
        lse_ref[...] = m_ref[...] * coef + jnp.log2(l_ref[...])


def attn_fwd_own(q, kv, coef):
    _, heads, span, _ = q.shape
    st = (jax.ShapeDtypeStruct((2, heads, span), f32),) * 2 + (jax.ShapeDtypeStruct((2, heads, HEAD_DIM, span), f32),)
    return pl.pallas_call(functools.partial(attn_fwd_own_kernel, coef), out_shape=st, in_specs=[VM, VM], out_specs=(VM,) * 3,
        scratch_shapes=[pltpu.VMEM((HEAD_DIM, 2 * span), bf)],
        cost_estimate=pl.CostEstimate(flops=2*2*3*heads*span*span*HEAD_DIM*2, bytes_accessed=4_000_000, transcendentals=0),
        compiler_params=pltpu.CompilerParams(vmem_limit_bytes=20 << 20), name="attn_fwd_own")(q, kv)

def attn_fwd_pieces(flags, indices, q, pieces, state, coef, last):
    _, heads, span, _ = q.shape
    n = len(pieces)
    st = (jax.ShapeDtypeStruct((2, heads, span), f32),) * 2 + (jax.ShapeDtypeStruct((2, heads, HEAD_DIM, span), f32),)
    if last:
        st = (jax.ShapeDtypeStruct((2 * span, heads * HEAD_DIM), bf), jax.ShapeDtypeStruct((2, heads, span), f32)) + st
    r = pl.pallas_call(functools.partial(attn_fwd_pieces_kernel, coef, indices, last), out_shape=st, in_specs=[SM] + [VM] * (n + 4), out_specs=(VM,) * len(st),
        scratch_shapes=[pltpu.VMEM((HEAD_DIM, 2 * span), bf)],
        cost_estimate=pl.CostEstimate(flops=2*2*2*n*heads*span*span*HEAD_DIM*2, bytes_accessed=4_000_000, transcendentals=0),
        compiler_params=pltpu.CompilerParams(vmem_limit_bytes=20 << 20), name="attn_fwd_pieces")(flags, q, *pieces, *state)
    return r

def bwd_block(s, dp, lse_ref, delta_ref, half, h, coef, mask):
    p = jnp.exp2(s * coef - lse_ref[half, h : h + 1, :])
    if mask is not None:
        p = jnp.where(mask, p, 0.0)
    ds = p * (dp - delta_ref[half, h : h + 1, :])
    return p.astype(bf), ds.astype(bf)

def attn_bwd_kernel(coef, scale, indices, own, has_state, flag_ref, q_ref, do_ref, lse_ref, delta_ref, *refs):
    n = len(indices)
    kv_refs = refs[:n]
    k = n
    if has_state:
        dq_in = refs[k]; k += 1
    dkv_refs = refs[k : k + n]
    dq_ref, kt, pbuf, sbuf = refs[k + n :]
    heads, span = q_ref.shape[1], q_ref.shape[2]
    if has_state:
        dq_ref[...] = dq_in[...]
    else:
        dq_ref[...] = jnp.zeros_like(dq_ref)
    def do_item(kv_ref, items, keyrows, mask_of):
        nk = keyrows.stop - keyrows.start
        def first(it):
            i, half, h = it
            return nt(kv_ref[keyrows, :HEAD_DIM], q_ref[half, h]), nt(kv_ref[keyrows, HEAD_DIM:], do_ref[half, h])
        def second(it, sd):
            i, half, h = it
            p, ds = bwd_block(sd[0], sd[1], lse_ref, delta_ref, half, h, coef, mask_of(half))
            cols = slice((i * heads + h) * span, (i * heads + h + 1) * span)
            pbuf[:nk, cols] = p
            sbuf[:nk, cols] = ds
            dq_ref[half, h] += nn(kt[:, keyrows], ds)
        pipelined([(i, half, h) for i, half in enumerate(items) for h in range(heads)], first, second)
        width = len(items) * heads * span
        lo = items[0]
        q_all = q_ref[lo : lo + len(items)].reshape(width, HEAD_DIM)
        do_all = do_ref[lo : lo + len(items)].reshape(width, HEAD_DIM)
        return nn(sbuf[:nk, :width], q_all) * scale, nn(pbuf[:nk, :width], do_all)
    for i in range(n):
        kv_ref, out = kv_refs[i], dkv_refs[i]
        kt[...] = kv_ref[:, :HEAD_DIM].astype(f32).T.astype(bf)
        lo, hi, both = slice(0, span), slice(span, 2 * span), slice(0, 2 * span)
        if own and i == 0:
            mask = future_mask(span)
            dk, dv = do_item(kv_ref, [0, 1], lo, lambda half: mask if half == 0 else None)
            out[lo, :HEAD_DIM] = dk.astype(bf)
            out[lo, HEAD_DIM:] = dv.astype(bf)
            dk, dv = do_item(kv_ref, [1], hi, lambda half: mask)
            out[hi, :HEAD_DIM] = dk.astype(bf)
            out[hi, HEAD_DIM:] = dv.astype(bf)
        else:
            @pl.when(flag_ref[indices[i]] == 1)
            def before():
                dk, dv = do_item(kv_ref, [0, 1], lo, lambda half: None)
                out[lo, :HEAD_DIM] = dk.astype(bf)
                out[lo, HEAD_DIM:] = dv.astype(bf)
                out[hi, :] = jnp.zeros((span, 2 * HEAD_DIM), bf)
            @pl.when(flag_ref[indices[i]] != 1)
            def after():
                dk, dv = do_item(kv_ref, [1], both, lambda half: None)
                out[:, :HEAD_DIM] = dk.astype(bf)
                out[:, HEAD_DIM:] = dv.astype(bf)

def attn_bwd(flags, indices, q, do, lse, delta, pieces, dq_state, coef, scale, own):
    _, heads, span, _ = q.shape
    n = len(pieces)
    outs = tuple(jax.ShapeDtypeStruct((2 * span, 2 * HEAD_DIM), bf) for _ in range(n)) + (jax.ShapeDtypeStruct((2, heads, HEAD_DIM, span), f32),)
    ins = [flags, q, do, lse, delta, *pieces] + ([dq_state] if dq_state is not None else [])
    return pl.pallas_call(functools.partial(attn_bwd_kernel, coef, scale, indices, own, dq_state is not None), out_shape=outs,
        in_specs=[SM] + [VM] * (len(ins) - 1), out_specs=(VM,) * len(outs),
        scratch_shapes=[pltpu.VMEM((HEAD_DIM, 2 * span), bf), pltpu.VMEM((2 * span, 2 * heads * span), bf), pltpu.VMEM((2 * span, 2 * heads * span), bf)],
        cost_estimate=pl.CostEstimate(flops=2*5*2*n*heads*span*span*HEAD_DIM*2, bytes_accessed=4_000_000, transcendentals=0),
        compiler_params=pltpu.CompilerParams(vmem_limit_bytes=30 << 20), name="attn_bwd_pieces")(*ins)


TILE = 512


def steps_of(columns, begin=0):
    edges = [begin, begin + TILE // 2, begin + TILE]
    while columns - edges[-1] > 2 * TILE:
        edges.append(edges[-1] + 2 * TILE)
    if columns - edges[-1] > TILE:
        edges.append(edges[-1] + TILE)
    edges.append(columns)
    return list(zip(edges, edges[1:]))


def act_back_kernel(bounds, own_ref, other_ref, wd_hbm, out_hbm, rows_ref, wd, out, in_sems, out_sems):
    half, first = own_ref.shape[0], bounds[0][0]
    parts = [slice(low - first, high - first) for low, high in bounds]
    copies = [
        pltpu.make_async_copy(wd_hbm.at[low:high], wd.at[part], in_sems.at[i])
        for i, ((low, high), part) in enumerate(zip(bounds, parts))
    ]
    for copy in copies:
        copy.start()
    rows_ref[:half, :] = own_ref[...]
    rows_ref[half:, :] = other_ref[...]
    results = []
    for i, part in enumerate(parts):
        copies[i].wait()
        out[:, part] = nt(rows_ref[...], wd[part, :])
        result = pltpu.make_async_copy(out.at[:, part], out_hbm.at[:, part], out_sems.at[i])
        result.start()
        results.append(result)
    for result in results:
        result.wait()


def act_back(own, other, wd, bounds):
    half, width = own.shape
    columns, count = bounds[-1][1] - bounds[0][0], len(bounds)
    return pl.pallas_call(
        functools.partial(act_back_kernel, bounds),
        out_shape=pltpu.HBM((2 * half, columns), f32),
        in_specs=[VM, VM, HB],
        out_specs=HB,
        scratch_shapes=[
            pltpu.VMEM((2 * half, width), bf), pltpu.VMEM((columns, width), bf), pltpu.VMEM((2 * half, columns), f32),
            pltpu.SemaphoreType.DMA((count,)), pltpu.SemaphoreType.DMA((count,)),
        ],
        cost_estimate=pl.CostEstimate(flops=4 * half * width * columns, bytes_accessed=2 * width * columns, transcendentals=0),
        compiler_params=pltpu.CompilerParams(vmem_limit_bytes=36 << 20),
        name="act_back",
    )(own, other, in_hbm(wd))


def whole(*dims):
    return pl.BlockSpec(dims, lambda i: (0,) * len(dims), pipeline_mode=pl.Buffered(1))


def ffn_kernel(
    tile, tiles, hidden, x_own, x_other, g_own, g_other, gact_ref, adgu_ref, auf_ref, wgu_ref, adf_ref, augu_ref,
    gx_own, gx_send, act_ref, flow_ref, dadgu_ref, dauf_ref, daugu_ref, dadf_ref,
    x_ref, g_ref, gx_acc, xlow, xlow_t, fback, fback_t, flow, back,
):
    step = pl.program_id(0)
    half = x_own.shape[0]

    @pl.when(step == 0)
    def prepare():
        for target, own, other in ((x_ref, x_own, x_other), (g_ref, g_own, g_other)):
            target[:half, :] = own[...]
            target[half:, :] = other[...]
        low = nt(x_ref[...], adgu_ref[...])
        xlow[...] = (low * 2.0).astype(bf)
        xlow_t[...] = low.T.astype(bf)
        fb = nt(g_ref[...], auf_ref[...])
        fback[...] = (fb * 2.0).astype(bf)
        fback_t[...] = fb.T.astype(bf)
        gx_acc[...] = jnp.zeros_like(gx_acc)
        flow[...] = jnp.zeros_like(flow)
        back[...] = jnp.zeros_like(back)

    def work(width):
        x = x_ref[...]
        wg, wu = wgu_ref[0, :, :width], wgu_ref[1, :, :width]
        aug, auu, adf = augu_ref[:RANK, :width], augu_ref[RANK:, :width], adf_ref[:, :width]
        gate = nn(x, wg) + nn(xlow[:, :RANK], aug)
        up = nn(x, wu) + nn(xlow[:, RANK:], auu)
        gact = gact_ref[:, :width] + nn(fback[...], adf)
        sig = 1.0 / (1.0 + jnp.exp(-gate))
        silu = gate * sig
        act = (silu * up).astype(bf)
        ggate = (gact * up * (sig + silu * (1.0 - sig))).astype(bf)
        gup = (gact * silu).astype(bf)
        act_ref[:, :width] = act
        flow[...] += nt(act, adf)
        gx_acc[...] += nt(ggate, wg) + nt(gup, wu)
        back[:, :RANK] += nt(ggate, aug)
        back[:, RANK:] += nt(gup, auu)
        daugu_ref[:RANK, :width] = nn(xlow_t[:RANK, :], ggate)
        daugu_ref[RANK:, :width] = nn(xlow_t[RANK:, :], gup)
        dadf_ref[:, :width] = nn(fback_t[...], act)

    tail = hidden - (tiles - 1) * tile
    if tail == tile:
        work(tile)
    else:
        @pl.when(step < tiles - 1)
        def body():
            work(tile)

        @pl.when(step == tiles - 1)
        def part():
            work(tail)

    @pl.when(step == tiles - 1)
    def finish():
        gx_acc[...] += nn((back[...] * 2.0).astype(bf), adgu_ref[...])
        gx_own[...] = gx_acc[:half, :]
        gx_send[...] = gx_acc[half:, :].astype(bf)
        flow_ref[...] = (flow[...] * 2.0).astype(bf)
        dadgu_ref[...] = nn(back[...].T.astype(bf), x_ref[...])
        dauf_ref[...] = nn(flow[...].T.astype(bf), g_ref[...])


def ffn(x_own, x_other, g_own, g_other, gact, adgu, auf, wgu, adf, augu, tile=TILE):
    rows, width = 2 * x_own.shape[0], x_own.shape[1]
    hidden = wgu.shape[2]
    tiles = -(-hidden // tile)
    half = rows // 2
    cols = lambda r: pl.BlockSpec((r, tile), lambda i: (0, i))
    outs = (
        shape(half, width), shape(half, width, dtype=bf), pltpu.HBM((rows, hidden), bf), shape(rows, RANK, dtype=bf),
        shape(2 * RANK, width), shape(RANK, width), shape(2 * RANK, hidden), shape(RANK, hidden),
    )
    return pl.pallas_call(
        functools.partial(ffn_kernel, tile, tiles, hidden),
        grid=(tiles,),
        out_shape=outs,
        in_specs=[whole(half, width)] * 4 + [cols(rows), whole(2 * RANK, width), whole(RANK, width),
                  pl.BlockSpec((2, width, tile), lambda i: (0, 0, i)), cols(RANK), cols(2 * RANK)],
        out_specs=(whole(half, width), whole(half, width), cols(rows), whole(rows, RANK), whole(2 * RANK, width),
                   whole(RANK, width), cols(2 * RANK), cols(RANK)),
        scratch_shapes=[
            pltpu.VMEM((rows, width), bf), pltpu.VMEM((rows, width), bf), pltpu.VMEM((rows, width), f32),
            pltpu.VMEM((rows, 2 * RANK), bf), pltpu.VMEM((2 * RANK, rows), bf), pltpu.VMEM((rows, RANK), bf),
            pltpu.VMEM((RANK, rows), bf), pltpu.VMEM((rows, RANK), f32), pltpu.VMEM((rows, 2 * RANK), f32),
        ],
        cost_estimate=pl.CostEstimate(flops=8 * rows * width * hidden, bytes_accessed=6 * width * hidden, transcendentals=rows * hidden),
        compiler_params=pltpu.CompilerParams(vmem_limit_bytes=36 << 20),
        name="ffn",
    )(x_own, x_other, in_hbm(g_own), in_hbm(g_other), in_hbm(gact), adgu, auf, in_hbm(wgu), adf, augu)


def down_kernel(bounds, start_refs, act_hbm, wd_hbm, total, act, wd, act_sems, wd_sems):
    low = bounds[0][0]
    copies = []
    for i, (begin, end) in enumerate(bounds):
        rows = slice(begin - low, end - low)
        copies.append((
            pltpu.make_async_copy(act_hbm.at[:, begin:end], act.at[:, rows], act_sems.at[i]),
            pltpu.make_async_copy(wd_hbm.at[begin:end], wd.at[rows], wd_sems.at[i]),
        ))
        for copy in copies[-1]:
            copy.start()
    total[...] = nn(start_refs[0][...], start_refs[1][...]) if len(start_refs) == 2 else start_refs[0][...]
    for i, (begin, end) in enumerate(bounds):
        rows = slice(begin - low, end - low)
        for copy in copies[i]:
            copy.wait()
        total[...] += nn(act[:, rows], wd[rows, :])


def down_first_kernel(bounds, flow_ref, auf_ref, act_hbm, wd_hbm, total, *scratch):
    down_kernel(bounds, (flow_ref, auf_ref), act_hbm, wd_hbm, total, *scratch)


def down_last_kernel(bounds, start_ref, act_hbm, wd_hbm, own_ref, send_ref, total, *scratch):
    down_kernel(bounds, (start_ref,), act_hbm, wd_hbm, total, *scratch)
    half = own_ref.shape[0]
    own_ref[...] = total[:half, :]
    send_ref[...] = total[half:, :].astype(bf)


def down(act, wd, start, bounds, last):
    rows, width = act.shape[0], wd.shape[1]
    half, columns, count = rows // 2, bounds[-1][1] - bounds[0][0], len(bounds)
    outs = (shape(half, width), shape(half, width, dtype=bf)) if last else (shape(rows, width),)
    scratch = [
        pltpu.VMEM((rows, columns), bf), pltpu.VMEM((columns, width), bf), pltpu.SemaphoreType.DMA((count,)),
        pltpu.SemaphoreType.DMA((count,)),
    ]
    return pl.pallas_call(
        functools.partial(down_last_kernel if last else down_first_kernel, bounds),
        out_shape=outs,
        in_specs=[VM] * len(start) + [HB, HB],
        out_specs=(VM,) * len(outs),
        scratch_shapes=([pltpu.VMEM((rows, width), f32)] if last else []) + scratch,
        cost_estimate=pl.CostEstimate(flops=2 * rows * width * columns, bytes_accessed=2 * width * columns, transcendentals=0),
        compiler_params=pltpu.CompilerParams(vmem_limit_bytes=28 << 20),
        name="down",
    )(*start, in_hbm(act), in_hbm(wd))


def per_device(
    tokens, cotangent, positions, adapter_choice, attn_gain, query_weight, query_bias, key_value_weight,
    key_value_bias, output_weight, ffn_gain, gate_upper_weight, down_weight, adapt_in, adapt_out,
):
    dp = lax.axis_index("dp")
    groups = lax.axis_size("seq")
    rings = groups // 2
    width, head_width = query_weight.shape
    heads = head_width // HEAD_DIM
    hidden = down_weight.shape[0]
    token_pos = positions[0]
    tok_count = token_pos.shape[0]
    span = tok_count // 2
    scale = HEAD_DIM ** (-0.5)
    coef = scale * math.log2(math.e)
    wide_in, wide_out = adapt_in.shape[2], adapt_out.shape[2]
    lanes_in = rounded_up(wide_in + 1, 128)
    lanes = lanes_in + rounded_up(wide_out, 128)
    widths = (width, head_width, hidden)
    sizes = (rings, wide_in, wide_out, lanes_in, widths)

    def to_pair(value):
        return lax.ppermute(value, "tensor", [(0, 1), (1, 0)])

    def to_other_sequence(value, pairs=((0, 1), (1, 0))):
        return lax.ppermute(value, "dp", list(pairs))

    def to_side(value):
        return lax.ppermute(value, "seq", [(i, i ^ 1) for i in range(groups)])

    def along_ring(value, steps):
        return lax.ppermute(value, "seq", [(i, (i + 2 * steps) % groups) for i in range(groups)])

    cycle = list(range(0, groups, 2)) + list(range(groups - 1, 0, -2))
    hops = [(cycle[i], cycle[(i + 1) % groups]) for i in range(groups)]

    def to_next(value):
        return lax.ppermute(value, "seq", hops)

    def to_last(value):
        return lax.ppermute(value, "seq", [(end, begin) for begin, end in hops])

    def after(value, *others):
        return lax.optimization_barrier((value, *others))[0]

    inputs, grad_out = tokens[0], cotangent[0]
    half = inputs.shape[0]
    attn_gain, ffn_gain = attn_gain[None], ffn_gain[None]

    def over_ring(piece):
        return [piece] + [along_ring(piece, step) for step in range(1, rings)]

    slice_own, slice_other = call(
        functools.partial(select_kernel, lanes_in, span), "select",
        [shape(RANK, lanes, dtype=bf)] * 2, [adapter_choice, positions, adapt_in, adapt_out],
        [pltpu.VMEM((2, RANK, wide_in), bf), pltpu.VMEM((2, RANK, wide_out), bf), pltpu.SemaphoreType.DMA((4,))],
        smem=2, left=2,
    )
    slice_other = to_other_sequence(slice_other)
    lane = lax.broadcasted_iota(jnp.int32, (RANK, lanes), 1)
    run_lane = (lane >= wide_in) & (lane < lanes_in)
    grad_other = to_pair(grad_out)
    slice_other = after(slice_other, grad_other)
    first_slice = jnp.where((dp == 0) | run_lane, slice_own, slice_other)
    second_slice = jnp.where(dp == 0, slice_other, slice_own)

    (normed,) = call(norm_kernel, "norm", [shape(half, width, dtype=bf)], [inputs, attn_gain])
    normed_other = to_pair(normed)
    arrived = over_ring(jnp.stack([first_slice, second_slice]))
    act_grad = act_back(grad_out, grad_other, down_weight, steps_of(hidden))
    arrived[1] = after(arrived[1], act_grad)
    own_slices = jnp.stack([piece[0] for piece in arrived])
    own_second = jnp.stack([piece[1] for piece in arrived])
    side_slices = to_side(own_slices)
    pair_slices = to_pair(own_slices)
    normed_rows, query_dense, kv_dense = call(
        dense_kernel, "dense", [shape(tok_count, width, dtype=bf), shape(tok_count, head_width), shape(tok_count, 2 * HEAD_DIM)],
        [normed, after(normed_other, own_slices), query_weight, key_value_weight],
        flops=2 * tok_count * width * (head_width + 2 * HEAD_DIM),
    )
    frequency = jnp.power(rope_base, -(jnp.arange(HEAD_DIM // 2, dtype=f32) * 2.0) / HEAD_DIM)
    angles = token_pos.astype(f32)[:, None] * frequency[None, :]
    cosine, sine = jnp.cos(angles), jnp.sin(angles)
    cosine = jnp.concatenate([cosine, cosine], axis=1)
    sine = jnp.concatenate([-sine, sine], axis=1)

    side_slices = after(side_slices, kv_dense)
    first_slices = [own_slices, side_slices, pair_slices, to_pair(side_slices)]
    side_second = to_side(after(own_second, side_slices))
    pair_second = to_pair(after(own_second, side_slices))
    slices_in = -(-4 * width // wide_in)
    slices_out = -(-(2 * width + 4 * HEAD_DIM) // wide_out)
    flags, adqkv, auq, auk, auv, ado, auo = call(
        functools.partial(unpack_first_kernel, *sizes), "unpack_first",
        [shape(groups, dtype=jnp.int32)]
        + [
            shape(*dims, dtype=bf)
            for dims in (
                (3 * RANK, width), (RANK, head_width), (RANK, HEAD_DIM), (RANK, HEAD_DIM), (RANK, head_width), (RANK, width),
            )
        ],
        list(first_slices),
        [
            pltpu.VMEM((2 * groups, RANK, lanes), bf),
            pltpu.VMEM((RANK, rounded_up(slices_in * wide_in, 128) + 256), f32),
            pltpu.VMEM((RANK, rounded_up(slices_out * wide_out, 128) + 256), f32),
            pltpu.SMEM((groups,), jnp.int32),
        ],
        out_specs=(SM,) + (VM,) * 6,
    )
    kv, low, low_t = call(
        key_value_kernel, "key_value",
        [shape(tok_count, 2 * HEAD_DIM, dtype=bf), shape(tok_count, 3 * RANK, dtype=bf), shape(3 * RANK, tok_count, dtype=bf)],
        [normed_rows, kv_dense, key_value_bias, adqkv, auk, auv, cosine, sine],
        flops=2 * tok_count * width * 2 * RANK,
    )

    (queries,) = call(
        query_kernel, "query", [shape(2, heads, span, HEAD_DIM, dtype=bf)],
        [query_dense, query_bias[None], low, auq, cosine, sine], flops=2 * tok_count * width * RANK,
    )
    state = attn_fwd_own(queries, kv, coef)
    pieces, from_last, from_next = [kv], kv, kv
    for step in range(1, rings + 1):
        from_last, from_next = to_next(from_last), to_last(from_next)
        if step < rings:
            from_last, from_next, _ = lax.optimization_barrier((from_last, from_next, state[0]))
        if step == 1:
            state = (after(state[0], side_second, pair_second), *state[1:])
            far_second = to_pair(after(side_second, state[0]))
        if step == rings:
            state = (after(state[0], far_second), *state[1:])
        pieces += [from_last, from_next][: 2 if step < rings else 1]
        indices = tuple(range(2 * step - 1, len(pieces)))
        result = attn_fwd_pieces(flags, indices, queries, pieces[2 * step - 1 :], state, coef, step == rings)
        state = result[-3:]
    mixed, lse = result[0], result[1]
    second_slices = [own_second, side_second, pair_second, far_second]

    branch_own, branch_send, mix_low_t = call(
        mix_out_kernel, "mix_out",
        [shape(half, width), shape(half, width, dtype=bf), shape(RANK, tok_count, dtype=bf)],
        [mixed, output_weight, ado, auo],
        [pltpu.VMEM((tok_count, width), f32)], flops=2 * tok_count * width * head_width,
    )
    hidden_rows, normed_ffn = call(
        residual_kernel, "residual", [pltpu.HBM((half, width), f32), shape(half, width, dtype=bf)],
        [inputs, branch_own, to_pair(branch_send), ffn_gain],
    )
    begin_in, begin_out, first_in, first_out = bases(wide_in, wide_out, widths)
    adgu, augu, adf, auf = call(
        functools.partial(unpack_second_kernel, *sizes), "unpack_second",
        [shape(*dims, dtype=bf) for dims in ((2 * RANK, width), (2 * RANK, hidden), (RANK, hidden), (RANK, width))],
        list(first_slices) + list(second_slices),
        [
            pltpu.VMEM((4 * groups, RANK, lanes), bf),
            pltpu.VMEM((RANK, rounded_up(4 * groups * wide_in, 128) + 256 - first_in), f32),
            pltpu.VMEM((RANK, rounded_up(4 * groups * wide_out, 128) + 256 - first_out), f32),
        ],
    )
    gx_own, gx_send, act, flow, dadgu, dauf, daugu, dadf = ffn(
        normed_ffn, to_pair(normed_ffn), grad_out, grad_other, act_grad, adgu, auf, gate_upper_weight, adf, augu
    )
    ad_lanes = rounded_up(4 * groups * wide_in, 128) + 256
    au_lanes = rounded_up(4 * groups * wide_out, 128) + 256

    def added(*values):
        total = values[0].astype(f32)
        for value in values[1:]:
            total = total + value.astype(f32)
        return total.astype(bf)

    grad_hidden, grad_low = call(
        hidden_back_kernel, "hidden_back", [shape(half, width), shape(half, width, dtype=bf)],
        [hidden_rows, grad_out, gx_own, to_pair(gx_send), ffn_gain],
    )
    grad_mixed, delta, dado, dauo = call(
        mix_back_kernel, "mix_back",
        [shape(2, heads, span, HEAD_DIM, dtype=bf), shape(2, heads, span), shape(RANK, head_width), shape(RANK, width)],
        [grad_low, to_pair(grad_low), output_weight, ado, auo, mixed, mix_low_t],
        [pltpu.VMEM((tok_count, width), bf)], flops=2 * tok_count * width * head_width,
    )
    def backward(indices, state_dq):
        return attn_bwd(
            flags, indices, queries, grad_mixed, lse, delta, [pieces[index] for index in indices], state_dq, coef, scale,
            indices == (0,),
        )

    state_dq, from_last, from_next = None, None, None
    for step in range(rings, 0, -1):
        ahead = 2 * step if step < rings else 2 * rings - 1
        onward, *backward_term, state_dq = backward((ahead, 2 * step - 3) if step > 1 else (ahead,), state_dq)
        onward = onward if from_last is None else added(onward, from_last)
        pinned = [onward]
        if step > 1:
            returned = backward_term[0] if from_next is None else added(backward_term[0], from_next)
            from_next = to_last(returned)
            pinned.append(returned)
        from_last = to_next(onward)
        state_dq = after(state_dq, *pinned)
    own_term, state_dq = backward((0,), state_dq)
    gn_query, dadq, dauq = call(
        functools.partial(back_query_kernel, scale), "back_query",
        [shape(tok_count, width), shape(RANK, width), shape(RANK, head_width)],
        [state_dq, query_weight, adqkv, auq, low_t, normed_rows, cosine, sine],
        [pltpu.VMEM((tok_count, head_width), bf)], flops=2 * tok_count * width * head_width,
    )
    from_last = after(from_last, gn_query)
    gn_own, gn_send, dadkv, dauk, dauv = call(
        back_key_value_kernel, "back_key_value",
        [
            shape(half, width), shape(half, width, dtype=bf), shape(2 * RANK, width), shape(RANK, HEAD_DIM),
            shape(RANK, HEAD_DIM),
        ],
        [
            own_term, gn_query, key_value_weight, adqkv, auk, auv, low_t, normed_rows, cosine, sine, from_last, from_next,
        ],
        [pltpu.VMEM((tok_count, width), f32), pltpu.VMEM((tok_count, 2 * RANK), f32)],
        flops=2 * tok_count * width * 2 * HEAD_DIM, limit=20,
    )
    (packed,) = call(
        functools.partial(pack_kernel, *sizes), "pack", [shape(2, 2, rings, 2, RANK, lanes, dtype=bf)],
        [dadq, dadkv, dado, dadgu, dadf, dauq, dauk, dauv, dauo, daugu, dauf],
        [pltpu.VMEM((RANK, ad_lanes), f32), pltpu.VMEM((RANK, au_lanes), f32)],
    )
    from_pair = to_pair(packed[1])
    near, far = added(packed[0, 0], from_pair[0]), added(packed[0, 1], from_pair[1])
    from_side = to_side(far)
    middle = 4 * TILE
    (out_total,) = down(after(act, far), down_weight, (flow, auf), steps_of(middle), False)
    from_side = after(from_side, out_total)
    sums = [added(near[place], from_side[place]) for place in range(rings)]
    from_ring = [along_ring(sums[place], -place) for place in range(1, rings)]
    out_own, out_send = down(after(act, sums[0]), down_weight, (out_total,), steps_of(hidden, middle), True)
    (grad_tokens,) = call(
        token_back_kernel, "token_back", [shape(half, width)],
        [inputs, grad_hidden, gn_own, after(to_pair(gn_send), out_own), attn_gain],
    )
    output = (hidden_rows + (out_own + to_pair(out_send).astype(f32))).astype(bf)
    from_ring[0] = after(from_ring[0], out_own)
    total = added(sums[0], *from_ring)
    other_total = after(to_other_sequence(total[1]), output, grad_tokens)
    factor = adapter_scale * (adapter_choice.shape[0] * tok_count * groups) ** (-0.5)
    adapt_in_grad, adapt_out_grad = call(
        functools.partial(place_kernel, lanes_in, factor), "place",
        [shape(*adapt_in.shape), shape(*adapt_out.shape)],
        [adapter_choice, total[0], other_total], smem=1,
    )
    return (output[None], grad_tokens[None], adapt_in_grad, adapt_out_grad)


def solution(mesh):
    return jax.shard_map(
        per_device,
        mesh=mesh,
        in_specs=(
            P("dp", ("seq", "tensor"), None),
            P("dp", ("seq", "tensor"), None),
            P("dp", "seq"),
            P(),
            P(),
            P(None, "tensor"),
            P("tensor"),
            P(None, None, "tensor"),
            P(None, "tensor"),
            P("tensor", None),
            P(),
            P(None, None, "tensor"),
            P("tensor", None),
            P(None, None, ("dp", "seq", "tensor")),
            P(None, None, ("dp", "seq", "tensor")),
        ),
        out_specs=(
            P("dp", ("seq", "tensor"), None),
            P("dp", ("seq", "tensor"), None),
            P(None, None, ("dp", "seq", "tensor")),
            P(None, None, ("dp", "seq", "tensor")),
        ),
        check_vma=False,
    )
```

```python
import functools
import math

import jax
import jax.numpy as jnp
from jax import lax
from jax.experimental import pallas as pl
from jax.experimental.pallas import tpu as pltpu
from jax.sharding import PartitionSpec as P

HEAD_DIM = 128
RANK = 16
eps = 1e-06
adapter_scale = 2.0
rope_base = 1000000.0
mask_fill = -1e30
bf = jnp.bfloat16
f32 = jnp.float32
VM = pl.BlockSpec(memory_space=pltpu.VMEM)
SM = pl.BlockSpec(memory_space=pltpu.SMEM)


def nn(a, b):
    return jnp.dot(a, b, preferred_element_type=f32)


def nt(a, b):
    return lax.dot_general(a, b, (((1,), (1,)), ((), ())), preferred_element_type=f32)


def shape(*dims, dtype=f32):
    return jax.ShapeDtypeStruct(dims, dtype)


def call(kernel, name, out, ins, scratch=(), flops=0, smem=0, out_specs=None, limit=16, left=0, aliases=None):
    moved = sum(math.prod(v.shape) * v.dtype.itemsize for v in list(ins) + list(out))
    ins = list(ins[: len(ins) - left]) + [in_hbm(value) for value in ins[len(ins) - left :]]
    return pl.pallas_call(
        kernel,
        out_shape=tuple(out),
        in_specs=[SM] * smem + [VM] * (len(ins) - smem - left) + [HB] * left,
        out_specs=out_specs or (VM,) * len(out),
        scratch_shapes=list(scratch),
        input_output_aliases=aliases or {},
        cost_estimate=pl.CostEstimate(flops=flops, bytes_accessed=moved, transcendentals=0),
        compiler_params=pltpu.CompilerParams(vmem_limit_bytes=limit << 20),
        name=name,
    )(*ins)


HB = pl.BlockSpec(memory_space=pltpu.HBM)


def in_hbm(value):
    return pltpu.with_memory_space_constraint(value, pltpu.HBM)


def rounded_up(value, unit):
    return -(-value // unit) * unit


def select_kernel(lanes_in, span, choice_ref, pos_ref, in_ref, out_ref, own_ref, other_ref, held_in, held_out, sems):
    wide_in, wide_out = in_ref.shape[2], out_ref.shape[2]
    dp = lax.axis_index("dp")
    copies = []
    for slot, sequence in ((0, dp), (1, 1 - dp)):
        chosen = choice_ref[sequence]
        copies.append(pltpu.make_async_copy(in_ref.at[chosen], held_in.at[slot], sems.at[2 * slot]))
        copies.append(pltpu.make_async_copy(out_ref.at[chosen], held_out.at[slot], sems.at[2 * slot + 1]))
    for copy in copies:
        copy.start()
    run = jnp.full((RANK, lanes_in), pos_ref[0, 0] // span, jnp.int32).astype(f32).astype(bf)
    for target in (own_ref, other_ref):
        target[...] = jnp.zeros_like(target)
        target[:, :lanes_in] = run
    for copy in copies:
        copy.wait()
    for slot, target in ((0, own_ref), (1, other_ref)):
        target[:, :wide_in] = held_in[slot]
        target[:, lanes_in : lanes_in + wide_out] = held_out[slot]


def column(begin, size):
    return pl.ds(pl.multiple_of(begin, 128), size)


def source_of(place, side, rings, seq):
    ring = lax.rem(seq // 2 - place + rings, rings)
    own_side = lax.rem(seq, 2)
    return ring * 2 + (own_side if side == 0 else 1 - own_side)


def spread(slots, target, begin, wide, first, low, high):
    held = rounded_up(wide, 128)
    inside = lax.broadcasted_iota(jnp.int32, (RANK, held), 1) < wide
    target[...] = jnp.zeros_like(target)
    for index in range(low // wide, -(-high // wide)):
        part = jnp.where(inside, slots[index, :, begin : begin + held].astype(f32), 0.0)
        part = jnp.concatenate([part, jnp.zeros((RANK, 128), f32)], axis=1)
        offset = index * wide - first
        base = offset // 128 * 128
        if offset != base:
            part = pltpu.roll(part, offset - base, 1)
        target[:, base : base + held + 128] += part


def collect(slots, refs, rings, part):
    seq, shard = lax.axis_index("seq"), lax.axis_index("tensor")
    for number, ref in enumerate(refs):
        side, core = number % 2, shard if number < 2 else 1 - shard
        for place in range(rings):
            slots[part * 4 * rings + source_of(place, side, rings, seq) * 2 + core] = ref[place]


def unpack_first_kernel(
    rings, wide_in, wide_out, lanes_in, widths, own, own_side, pair, pair_side,
    flags_ref, adqkv, auq, auk, auv, ado, auo, slots, ad, au, runs,
):
    shard, seq = lax.axis_index("tensor"), lax.axis_index("seq")
    width, head_width, hidden = widths
    for place in range(rings):
        for side, ref in ((0, own), (1, own_side)):
            run = jnp.max(ref[place, :, wide_in:lanes_in].astype(f32))
            runs[source_of(place, side, rings, seq)] = run.astype(jnp.int32)
    groups = 2 * rings
    place = jnp.where(lax.rem(seq, 2) == 0, seq // 2, groups - 1 - seq // 2)
    for index in range(groups):
        step = (index + 1) // 2
        other = lax.rem(place + (groups - step if index % 2 == 1 else step), groups)
        source = jnp.where(other < rings, 2 * other, 2 * (groups - 1 - other) + 1)
        flags_ref[index] = (runs[source] < runs[seq]).astype(jnp.int32)
    collect(slots, (own, own_side, pair, pair_side), rings, 0)
    spread(slots, ad, 0, wide_in, 0, 0, 4 * width)
    spread(slots, au, lanes_in, wide_out, 0, 0, 2 * width + 4 * HEAD_DIM)
    for index in range(3):
        adqkv[index * RANK : (index + 1) * RANK, :] = ad[:, index * width : (index + 1) * width].astype(bf)
    ado[...] = ad[:, column(3 * width + shard * head_width, head_width)].astype(bf)
    auq[...] = au[:, column(shard * head_width, head_width)].astype(bf)
    auk[...] = au[:, column(width + shard * HEAD_DIM, HEAD_DIM)].astype(bf)
    auv[...] = au[:, column(width + (2 + shard) * HEAD_DIM, HEAD_DIM)].astype(bf)
    base = width + 4 * HEAD_DIM
    auo[...] = au[:, base : base + width].astype(bf)


def bases(wide_in, wide_out, widths):
    width = widths[0]
    begin_in, begin_out = 4 * width, 2 * width + 4 * HEAD_DIM
    return begin_in, begin_out, begin_in // wide_in * wide_in // 128 * 128, begin_out // wide_out * wide_out // 128 * 128


def unpack_second_kernel(
    rings, wide_in, wide_out, lanes_in, widths, *refs
):
    firsts, seconds = refs[:4], refs[4:8]
    adgu, augu, adf, auf, slots, ad, au = refs[8:]
    shard = lax.axis_index("tensor")
    width, head_width, hidden = widths
    collect(slots, firsts, rings, 0)
    collect(slots, seconds, rings, 1)
    begin_in, begin_out, first_in, first_out = bases(wide_in, wide_out, widths)
    total_in, total_out = 8 * rings * wide_in, 8 * rings * wide_out
    spread(slots, ad, 0, wide_in, first_in, begin_in, total_in)
    spread(slots, au, lanes_in, wide_out, first_out, begin_out, total_out)
    base = begin_in - first_in
    for index in range(2):
        adgu[index * RANK : (index + 1) * RANK, :] = ad[:, base + index * width : base + (index + 1) * width].astype(bf)
    adf[...] = ad[:, column(base + 2 * width + shard * hidden, hidden)].astype(bf)
    base = begin_out - first_out
    for index in range(2):
        augu[index * RANK : (index + 1) * RANK, :] = au[
            :, column(base + (2 * index + shard) * hidden, hidden)
        ].astype(bf)
    auf[...] = au[:, base + 4 * hidden : base + 4 * hidden + width].astype(bf)


def put_slices(rings, wide_in, wide_out, lanes_in, ad, au, limits, parts, write):
    dp, seq = lax.axis_index("dp"), lax.axis_index("seq")
    for index in range(4 * rings * parts):
        to_dp, to_seq, to_core = index // (4 * rings), index // 2 % (2 * rings), index % 2
        pieces = []
        for source, wide, (low, high, first) in ((ad, wide_in, limits[0]), (au, wide_out, limits[1])):
            held = rounded_up(wide, 128)
            if index * wide >= high or (index + 1) * wide <= low:
                part = jnp.zeros((RANK, held), f32)
            else:
                offset = index * wide - first
                base = offset // 128 * 128
                part = source[:, base : base + held + 128]
                if offset != base:
                    part = pltpu.roll(part, held + 128 - (offset - base), 1)
                part = part[:, :held]
            pieces.append(part)
            if source is ad and lanes_in > held:
                pieces.append(jnp.zeros((RANK, lanes_in - held), f32))
        packed = jnp.concatenate(pieces, axis=1).astype(bf)
        place = lax.rem(seq // 2 - to_seq // 2 + rings, rings)
        write(to_seq, to_core, place, lax.rem(dp + to_dp, 2), packed)


def pack_kernel(
    rings, wide_in, wide_out, lanes_in, widths,
    dadq, dadkv, dado, dadgu, dadf, dauq, dauk, dauv, dauo, daugu, dauf, out_ref, ad, au,
):
    shard, side = lax.axis_index("tensor"), lax.rem(lax.axis_index("seq"), 2)
    width, head_width, hidden = widths
    ad[...] = jnp.zeros_like(ad)
    au[...] = jnp.zeros_like(au)
    ad[:, :width] = dadq[...]
    for index in range(2):
        ad[:, (1 + index) * width : (2 + index) * width] = dadkv[index * RANK : (index + 1) * RANK, :]
        ad[:, (4 + index) * width : (5 + index) * width] = dadgu[index * RANK : (index + 1) * RANK, :]
    ad[:, column(3 * width + shard * head_width, head_width)] = dado[...]
    ad[:, column(6 * width + shard * hidden, hidden)] = dadf[...]
    au[:, column(shard * head_width, head_width)] = dauq[...]
    au[:, column(width + shard * HEAD_DIM, HEAD_DIM)] = dauk[...]
    au[:, column(width + (2 + shard) * HEAD_DIM, HEAD_DIM)] = dauv[...]
    base = width + 4 * HEAD_DIM
    au[:, base : base + width] = dauo[...]
    base = base + width
    for index in range(2):
        au[:, column(base + (2 * index + shard) * hidden, hidden)] = daugu[index * RANK : (index + 1) * RANK, :]
    au[:, base + 4 * hidden : base + 4 * hidden + width] = dauf[...]

    def write(to_seq, to_core, place, part, packed):
        out_ref[lax.rem(shard + to_core, 2), lax.rem(side + to_seq % 2, 2), place, part] = packed

    limits = ((0, 8 * rings * wide_in, 0), (0, 8 * rings * wide_out, 0))
    put_slices(rings, wide_in, wide_out, lanes_in, ad, au, limits, 2, write)


def place_kernel(lanes_in, factor, choice_ref, own_ref, other_ref, in_ref, out_ref):
    wide_in, wide_out = in_ref.shape[2], out_ref.shape[2]
    dp = lax.axis_index("dp")
    in_ref[...] = jnp.zeros_like(in_ref)
    out_ref[...] = jnp.zeros_like(out_ref)
    for ref, sequence in ((own_ref, dp), (other_ref, 1 - dp)):
        chosen = choice_ref[sequence]
        part = ref[...].astype(f32) * factor
        in_ref[chosen] = in_ref[chosen] + part[:, :wide_in]
        out_ref[chosen] = out_ref[chosen] + part[:, lanes_in : lanes_in + wide_out]


def factor_of(rows):
    return lax.rsqrt(jnp.mean(rows * rows, axis=-1, keepdims=True) + eps)


def norm_back(rows, gain, grad):
    factor = factor_of(rows)
    scaled = rows * factor
    grad_scaled = grad * gain
    return factor * (grad_scaled - scaled * jnp.mean(grad_scaled * scaled, axis=-1, keepdims=True))


def norm_kernel(rows_ref, gain_ref, normed_ref):
    rows = rows_ref[...].astype(f32)
    normed_ref[...] = (rows * factor_of(rows) * gain_ref[...].astype(f32)).astype(bf)


def residual_kernel(rows_ref, own_ref, other_ref, gain_ref, hidden_ref, normed_ref):
    rows = rows_ref[...].astype(f32) + (own_ref[...] + other_ref[...].astype(f32))
    hidden_ref[...] = rows
    normed_ref[...] = (rows * factor_of(rows) * gain_ref[...].astype(f32)).astype(bf)


def hidden_back_kernel(hidden_ref, grad_ref, own_ref, other_ref, gain_ref, out_ref, low_ref):
    grad = own_ref[...] + other_ref[...].astype(f32)
    total = grad_ref[...].astype(f32) + norm_back(hidden_ref[...], gain_ref[...].astype(f32), grad)
    out_ref[...] = total
    low_ref[...] = total.astype(bf)


def token_back_kernel(rows_ref, grad_ref, own_ref, other_ref, gain_ref, out_ref):
    grad = own_ref[...] + other_ref[...].astype(f32)
    out_ref[...] = grad_ref[...] + norm_back(rows_ref[...].astype(f32), gain_ref[...].astype(f32), grad)


def turned(rows, cosine, sine):
    return rows * cosine + pltpu.roll(rows, HEAD_DIM // 2, 1) * sine


def dense_kernel(own_ref, other_ref, wq_ref, wkv_ref, rows_ref, query_ref, kv_ref):
    shard = lax.axis_index("tensor")
    half = own_ref.shape[0]
    rows_ref[pl.ds(pl.multiple_of(shard * half, half), half), :] = own_ref[...]
    rows_ref[pl.ds(pl.multiple_of((1 - shard) * half, half), half), :] = other_ref[...]
    rows = rows_ref[...]
    query_ref[...] = nn(rows, wq_ref[...])
    kv_ref[:, :HEAD_DIM] = nn(rows, wkv_ref[0])
    kv_ref[:, HEAD_DIM:] = nn(rows, wkv_ref[1])


def key_value_kernel(
    rows_ref, dense_ref, bias_ref, adqkv_ref, auk_ref, auv_ref, cos_ref, sin_ref, kv_ref, low_ref, low_t_ref
):
    low = nt(rows_ref[...], adqkv_ref[...])
    low_ref[...] = (2.0 * low).astype(bf)
    low_t_ref[...] = low.T.astype(bf)
    key = dense_ref[:, :HEAD_DIM] + bias_ref[0:1, :].astype(f32) + nn(low_ref[:, RANK : 2 * RANK], auk_ref[...])
    value = dense_ref[:, HEAD_DIM:] + bias_ref[1:2, :].astype(f32) + nn(low_ref[:, 2 * RANK :], auv_ref[...])
    kv_ref[:, :HEAD_DIM] = turned(key, cos_ref[...], sin_ref[...]).astype(bf)
    kv_ref[:, HEAD_DIM:] = value.astype(bf)


def query_kernel(dense_ref, bias_ref, low_ref, auq_ref, cos_ref, sin_ref, q_ref):
    heads, span = q_ref.shape[1], q_ref.shape[2]
    query = dense_ref[...] + bias_ref[...].astype(f32) + nn(low_ref[:, :RANK], auq_ref[...])
    for h in range(heads):
        head = turned(query[:, h * HEAD_DIM : (h + 1) * HEAD_DIM], cos_ref[...], sin_ref[...]).astype(bf)
        q_ref[0, h] = head[:span]
        q_ref[1, h] = head[span:]


def rows_of(own, half):
    shard = lax.axis_index("tensor")
    return pl.ds(pl.multiple_of((shard if own else 1 - shard) * half, half), half)


def mix_send_kernel(mixed_ref, wo_ref, ado_ref, auo_ref, send_ref, low_ref, low_t_ref):
    low = nt(mixed_ref[...], ado_ref[...])
    low_ref[...] = (2.0 * low).astype(bf)
    low_t_ref[...] = low.T.astype(bf)
    rows = rows_of(False, send_ref.shape[0])
    send_ref[...] = (nn(mixed_ref[rows, :], wo_ref[...]) + nn(low_ref[rows, :], auo_ref[...])).astype(bf)


def mix_own_kernel(mixed_ref, wo_ref, low_ref, auo_ref, own_ref):
    rows = rows_of(True, own_ref.shape[0])
    own_ref[...] = nn(mixed_ref[rows, :], wo_ref[...]) + nn(low_ref[rows, :], auo_ref[...])


def mix_back_kernel(own, rows_ref, wo_ref, ado_ref, auo_ref, mixed_ref, low_t_ref, *refs):
    do_ref, delta_ref, dado_ref, dauo_ref = refs[-4:]
    half = rows_ref.shape[0]
    heads = do_ref.shape[1]
    part = lax.axis_index("tensor") if own else 1 - lax.axis_index("tensor")
    places = rows_of(own, half)
    rows, mixed = rows_ref[...], mixed_ref[places, :]
    back = nt(rows, auo_ref[...])
    grad = (nt(rows, wo_ref[...]) + nn((2.0 * back).astype(bf), ado_ref[...])).astype(bf)
    dado = nn(back.T.astype(bf), mixed)
    dauo = nn(low_t_ref[:, places], rows)
    dado_ref[...] = dado if own else refs[2][...] + dado
    dauo_ref[...] = dauo if own else refs[3][...] + dauo
    for h in range(heads):
        cols = slice(h * HEAD_DIM, (h + 1) * HEAD_DIM)
        product = (grad[:, cols].astype(f32) * mixed[:, cols].astype(f32)).T
        do_ref[part, h] = grad[:, cols]
        delta_ref[part, h : h + 1, :] = jnp.sum(product, axis=0, keepdims=True)


def back_query_kernel(
    scale, dq_ref, wq_ref, adq_ref, auq_ref, low_t_ref, rows_ref, cos_ref, sin_ref, total_ref, dadq_ref, dauq_ref, eq
):
    heads, span = dq_ref.shape[1], dq_ref.shape[3]
    for part in range(2):
        rows = slice(part * span, (part + 1) * span)
        for h in range(heads):
            grad = dq_ref[part, h].T * scale
            eq[rows, h * HEAD_DIM : (h + 1) * HEAD_DIM] = turned(grad, cos_ref[rows, :], -sin_ref[rows, :]).astype(bf)
    query = eq[...]
    back = nt(query, auq_ref[...])
    total_ref[...] = nt(query, wq_ref[...]) + nn((2.0 * back).astype(bf), adq_ref[:RANK, :])
    dadq_ref[...] = nn(back.T.astype(bf), rows_ref[...])
    dauq_ref[...] = nn(low_t_ref[:RANK, :], query)


def back_key_value_kernel(
    dkv_ref, query_ref, wkv_ref, adqkv_ref, auk_ref, auv_ref, low_t_ref, rows_ref, cos_ref, sin_ref, *refs
):
    others = refs[: len(refs) - 7]
    own_ref, send_ref, dadkv_ref, dauk_ref, dauv_ref, total, back_ref = refs[len(refs) - 7 :]
    shard = lax.axis_index("tensor")
    half = own_ref.shape[0]
    grad = dkv_ref[...].astype(f32)
    for ref in others:
        grad = grad + ref[...].astype(f32)
    ek = turned(grad[:, :HEAD_DIM], cos_ref[...], -sin_ref[...]).astype(bf)
    ev = grad[:, HEAD_DIM:].astype(bf)
    back_ref[:, :RANK] = nt(ek, auk_ref[...])
    back_ref[:, RANK:] = nt(ev, auv_ref[...])
    back = back_ref[...]
    total[...] = (
        query_ref[...] + nt(ek, wkv_ref[0]) + nt(ev, wkv_ref[1]) + nn((2.0 * back).astype(bf), adqkv_ref[RANK:, :])
    )
    own_ref[...] = total[pl.ds(pl.multiple_of(shard * half, half), half), :]
    send_ref[...] = total[pl.ds(pl.multiple_of((1 - shard) * half, half), half), :].astype(bf)
    dadkv_ref[...] = nn(back.T.astype(bf), rows_ref[...])
    dauk_ref[...] = nn(low_t_ref[RANK : 2 * RANK, :], ek)
    dauv_ref[...] = nn(low_t_ref[2 * RANK :, :], ev)


def future_mask(span):
    return lax.broadcasted_iota(jnp.int32, (span, span), 0) <= lax.broadcasted_iota(jnp.int32, (span, span), 1)

def fold(s, values_t, m, l, o, coef, mask):
    if mask is not None:
        s = jnp.where(mask, s, mask_fill)
    m_next = jnp.maximum(m, jnp.max(s, axis=0, keepdims=True))
    p = jnp.exp2((s - m_next) * coef)
    alpha = jnp.exp2((m - m_next) * coef)
    l_next = l * alpha + jnp.sum(p, axis=0, keepdims=True)
    o_next = o * alpha + nn(values_t, p.astype(bf))
    return m_next, l_next, o_next

def pipelined(items, first, second):
    ahead = first(items[0])
    for i, item in enumerate(items):
        now = ahead
        if i + 1 < len(items):
            ahead = first(items[i + 1])
        second(item, now)

def attn_fwd_own_kernel(coef, q_ref, kv_ref, m_ref, l_ref, o_ref, vt):
    heads, span = q_ref.shape[1], q_ref.shape[2]
    vt[...] = kv_ref[:, HEAD_DIM:].astype(f32).T.astype(bf)
    mask = future_mask(span)
    both_mask = lax.broadcasted_iota(jnp.int32, (2 * span, span), 0) <= lax.broadcasted_iota(jnp.int32, (2 * span, span), 1) + span
    def first(item):
        half, h = item
        return nt(kv_ref[: (half + 1) * span, :HEAD_DIM], q_ref[half, h])
    def second(item, s):
        half, h = item
        m = jnp.full((1, span), mask_fill, f32)
        l = jnp.zeros((1, span), f32)
        o = jnp.zeros((HEAD_DIM, span), f32)
        m, l, o = fold(s, vt[:, : (half + 1) * span], m, l, o, coef, both_mask if half else mask)
        m_ref[half, h : h + 1, :] = m
        l_ref[half, h : h + 1, :] = l
        o_ref[half, h] = o
    pipelined([(half, h) for h in range(heads) for half in range(2)], first, second)

def attn_fwd_pieces_kernel(coef, indices, last, flag_ref, q_ref, *refs):
    n = len(indices)
    kv_refs = refs[:n]
    m_in, l_in, o_in = refs[n : n + 3]
    if last:
        mixed_ref, lse_ref, m_ref, l_ref, o_ref, vt = refs[n + 3 :]
    else:
        m_ref, l_ref, o_ref, vt = refs[n + 3 :]
    heads, span = q_ref.shape[1], q_ref.shape[2]
    src = [(m_in, l_in, o_in)] + [(m_ref, l_ref, o_ref)] * n
    m_ref[...] = m_in[...]
    l_ref[...] = l_in[...]
    o_ref[...] = o_in[...]
    def update(half, h, s, values_t):
        m, l, o = fold(s, values_t, m_ref[half, h : h + 1, :], l_ref[half, h : h + 1, :], o_ref[half, h], coef, None)
        m_ref[half, h : h + 1, :] = m
        l_ref[half, h : h + 1, :] = l
        o_ref[half, h] = o
    for i in range(n):
        kv_ref = kv_refs[i]
        vt[...] = kv_ref[:, HEAD_DIM:].astype(f32).T.astype(bf)
        @pl.when(flag_ref[indices[i]] == 1)
        def before():
            pipelined([(half, h) for h in range(heads) for half in range(2)],
                lambda it: nt(kv_ref[:span, :HEAD_DIM], q_ref[it[0], it[1]]),
                lambda it, s: update(it[0], it[1], s, vt[:, :span]))
        @pl.when(flag_ref[indices[i]] != 1)
        def after():
            pipelined([(1, h) for h in range(heads)],
                lambda it: nt(kv_ref[:, :HEAD_DIM], q_ref[1, it[1]]),
                lambda it, s: update(1, it[1], s, vt[...]))
    if last:
        for half in range(2):
            for h in range(heads):
                o = o_ref[half, h] / l_ref[half, h : h + 1, :]
                mixed_ref[half * span : (half + 1) * span, h * HEAD_DIM : (h + 1) * HEAD_DIM] = o.T.astype(bf)
        lse_ref[...] = m_ref[...] * coef + jnp.log2(l_ref[...])


def attn_fwd_own(q, kv, coef):
    _, heads, span, _ = q.shape
    st = (jax.ShapeDtypeStruct((2, heads, span), f32),) * 2 + (jax.ShapeDtypeStruct((2, heads, HEAD_DIM, span), f32),)
    return pl.pallas_call(functools.partial(attn_fwd_own_kernel, coef), out_shape=st, in_specs=[VM, VM], out_specs=(VM,) * 3,
        scratch_shapes=[pltpu.VMEM((HEAD_DIM, 2 * span), bf)],
        cost_estimate=pl.CostEstimate(flops=2*2*3*heads*span*span*HEAD_DIM*2, bytes_accessed=4_000_000, transcendentals=0),
        compiler_params=pltpu.CompilerParams(vmem_limit_bytes=20 << 20), name="attn_fwd_own")(q, kv)

def attn_fwd_pieces(flags, indices, q, pieces, state, coef, last):
    _, heads, span, _ = q.shape
    n = len(pieces)
    st = (jax.ShapeDtypeStruct((2, heads, span), f32),) * 2 + (jax.ShapeDtypeStruct((2, heads, HEAD_DIM, span), f32),)
    if last:
        st = (jax.ShapeDtypeStruct((2 * span, heads * HEAD_DIM), bf), jax.ShapeDtypeStruct((2, heads, span), f32)) + st
    r = pl.pallas_call(functools.partial(attn_fwd_pieces_kernel, coef, indices, last), out_shape=st, in_specs=[SM] + [VM] * (n + 4), out_specs=(VM,) * len(st),
        scratch_shapes=[pltpu.VMEM((HEAD_DIM, 2 * span), bf)],
        cost_estimate=pl.CostEstimate(flops=2*2*2*n*heads*span*span*HEAD_DIM*2, bytes_accessed=4_000_000, transcendentals=0),
        compiler_params=pltpu.CompilerParams(vmem_limit_bytes=20 << 20), name="attn_fwd_pieces")(flags, q, *pieces, *state)
    return r

def bwd_block(s, dp, lse_ref, delta_ref, half, h, coef, mask):
    p = jnp.exp2(s * coef - lse_ref[half, h : h + 1, :])
    if mask is not None:
        p = jnp.where(mask, p, 0.0)
    ds = p * (dp - delta_ref[half, h : h + 1, :])
    return p.astype(bf), ds.astype(bf)

def attn_bwd_kernel(coef, scale, indices, own, has_state, flag_ref, q_ref, do_ref, lse_ref, delta_ref, *refs):
    n = len(indices)
    kv_refs = refs[:n]
    k = n
    if has_state:
        dq_in = refs[k]; k += 1
    dkv_refs = refs[k : k + n]
    dq_ref, kt, pbuf, sbuf = refs[k + n :]
    heads, span = q_ref.shape[1], q_ref.shape[2]
    if has_state:
        dq_ref[...] = dq_in[...]
    else:
        dq_ref[...] = jnp.zeros_like(dq_ref)
    def do_item(kv_ref, items, keyrows, mask_of):
        nk = keyrows.stop - keyrows.start
        def first(it):
            i, half, h = it
            return nt(kv_ref[keyrows, :HEAD_DIM], q_ref[half, h]), nt(kv_ref[keyrows, HEAD_DIM:], do_ref[half, h])
        def second(it, sd):
            i, half, h = it
            p, ds = bwd_block(sd[0], sd[1], lse_ref, delta_ref, half, h, coef, mask_of(half))
            cols = slice((i * heads + h) * span, (i * heads + h + 1) * span)
            pbuf[:nk, cols] = p
            sbuf[:nk, cols] = ds
            dq_ref[half, h] += nn(kt[:, keyrows], ds)
        pipelined([(i, half, h) for i, half in enumerate(items) for h in range(heads)], first, second)
        width = len(items) * heads * span
        lo = items[0]
        q_all = q_ref[lo : lo + len(items)].reshape(width, HEAD_DIM)
        do_all = do_ref[lo : lo + len(items)].reshape(width, HEAD_DIM)
        return nn(sbuf[:nk, :width], q_all) * scale, nn(pbuf[:nk, :width], do_all)
    for i in range(n):
        kv_ref, out = kv_refs[i], dkv_refs[i]
        kt[...] = kv_ref[:, :HEAD_DIM].astype(f32).T.astype(bf)
        lo, hi, both = slice(0, span), slice(span, 2 * span), slice(0, 2 * span)
        if own and i == 0:
            mask = future_mask(span)
            dk, dv = do_item(kv_ref, [0, 1], lo, lambda half: mask if half == 0 else None)
            out[lo, :HEAD_DIM] = dk.astype(bf)
            out[lo, HEAD_DIM:] = dv.astype(bf)
            dk, dv = do_item(kv_ref, [1], hi, lambda half: mask)
            out[hi, :HEAD_DIM] = dk.astype(bf)
            out[hi, HEAD_DIM:] = dv.astype(bf)
        else:
            @pl.when(flag_ref[indices[i]] == 1)
            def before():
                dk, dv = do_item(kv_ref, [0, 1], lo, lambda half: None)
                out[lo, :HEAD_DIM] = dk.astype(bf)
                out[lo, HEAD_DIM:] = dv.astype(bf)
                out[hi, :] = jnp.zeros((span, 2 * HEAD_DIM), bf)
            @pl.when(flag_ref[indices[i]] != 1)
            def after():
                dk, dv = do_item(kv_ref, [1], both, lambda half: None)
                out[:, :HEAD_DIM] = dk.astype(bf)
                out[:, HEAD_DIM:] = dv.astype(bf)

def attn_bwd(flags, indices, q, do, lse, delta, pieces, dq_state, coef, scale, own):
    _, heads, span, _ = q.shape
    n = len(pieces)
    outs = tuple(jax.ShapeDtypeStruct((2 * span, 2 * HEAD_DIM), bf) for _ in range(n)) + (jax.ShapeDtypeStruct((2, heads, HEAD_DIM, span), f32),)
    ins = [flags, q, do, lse, delta, *pieces] + ([dq_state] if dq_state is not None else [])
    return pl.pallas_call(functools.partial(attn_bwd_kernel, coef, scale, indices, own, dq_state is not None), out_shape=outs,
        in_specs=[SM] + [VM] * (len(ins) - 1), out_specs=(VM,) * len(outs),
        scratch_shapes=[pltpu.VMEM((HEAD_DIM, 2 * span), bf), pltpu.VMEM((2 * span, 2 * heads * span), bf), pltpu.VMEM((2 * span, 2 * heads * span), bf)],
        cost_estimate=pl.CostEstimate(flops=2*5*2*n*heads*span*span*HEAD_DIM*2, bytes_accessed=4_000_000, transcendentals=0),
        compiler_params=pltpu.CompilerParams(vmem_limit_bytes=30 << 20), name="attn_bwd_pieces")(*ins)


TILE = 512


def steps_of(columns, begin=0):
    edges = [begin, begin + TILE // 2, begin + TILE]
    while columns - edges[-1] > 2 * TILE:
        edges.append(edges[-1] + 2 * TILE)
    if columns - edges[-1] > TILE:
        edges.append(edges[-1] + TILE)
    edges.append(columns)
    return list(zip(edges, edges[1:]))


def act_back_kernel(bounds, own_ref, other_ref, wd_hbm, out_hbm, rows_ref, wd, out, in_sems, out_sems):
    half, first = own_ref.shape[0], bounds[0][0]
    parts = [slice(low - first, high - first) for low, high in bounds]
    copies = [
        pltpu.make_async_copy(wd_hbm.at[low:high], wd.at[part], in_sems.at[i])
        for i, ((low, high), part) in enumerate(zip(bounds, parts))
    ]
    for copy in copies:
        copy.start()
    rows_ref[:half, :] = own_ref[...]
    rows_ref[half:, :] = other_ref[...]
    results = []
    for i, part in enumerate(parts):
        copies[i].wait()
        out[:, part] = nt(rows_ref[...], wd[part, :])
        result = pltpu.make_async_copy(out.at[:, part], out_hbm.at[:, part], out_sems.at[i])
        result.start()
        results.append(result)
    for result in results:
        result.wait()


def act_back(own, other, wd, bounds):
    half, width = own.shape
    columns, count = bounds[-1][1] - bounds[0][0], len(bounds)
    return pl.pallas_call(
        functools.partial(act_back_kernel, bounds),
        out_shape=pltpu.HBM((2 * half, columns), f32),
        in_specs=[VM, VM, HB],
        out_specs=HB,
        scratch_shapes=[
            pltpu.VMEM((2 * half, width), bf), pltpu.VMEM((columns, width), bf), pltpu.VMEM((2 * half, columns), f32),
            pltpu.SemaphoreType.DMA((count,)), pltpu.SemaphoreType.DMA((count,)),
        ],
        cost_estimate=pl.CostEstimate(flops=4 * half * width * columns, bytes_accessed=2 * width * columns, transcendentals=0),
        compiler_params=pltpu.CompilerParams(vmem_limit_bytes=36 << 20),
        name="act_back",
    )(own, other, in_hbm(wd))


def whole(*dims):
    return pl.BlockSpec(dims, lambda i: (0,) * len(dims), pipeline_mode=pl.Buffered(1))


def ffn_kernel(
    tile, tiles, hidden, x_own, x_other, g_own, g_other, gact_ref, adgu_ref, auf_ref, wgu_ref, adf_ref, augu_ref,
    gx_own, gx_send, act_ref, flow_ref, dadgu_ref, dauf_ref, daugu_ref, dadf_ref,
    x_ref, g_ref, gx_acc, xlow, xlow_t, fback, fback_t, flow, back,
):
    step = pl.program_id(0)
    half = x_own.shape[0]

    @pl.when(step == 0)
    def prepare():
        for target, own, other in ((x_ref, x_own, x_other), (g_ref, g_own, g_other)):
            target[:half, :] = own[...]
            target[half:, :] = other[...]
        low = nt(x_ref[...], adgu_ref[...])
        xlow[...] = (low * 2.0).astype(bf)
        xlow_t[...] = low.T.astype(bf)
        fb = nt(g_ref[...], auf_ref[...])
        fback[...] = (fb * 2.0).astype(bf)
        fback_t[...] = fb.T.astype(bf)
        gx_acc[...] = jnp.zeros_like(gx_acc)
        flow[...] = jnp.zeros_like(flow)
        back[...] = jnp.zeros_like(back)

    def work(width):
        x = x_ref[...]
        wg, wu = wgu_ref[0, :, :width], wgu_ref[1, :, :width]
        aug, auu, adf = augu_ref[:RANK, :width], augu_ref[RANK:, :width], adf_ref[:, :width]
        gate = nn(x, wg) + nn(xlow[:, :RANK], aug)
        up = nn(x, wu) + nn(xlow[:, RANK:], auu)
        gact = gact_ref[:, :width] + nn(fback[...], adf)
        sig = 1.0 / (1.0 + jnp.exp(-gate))
        silu = gate * sig
        act = (silu * up).astype(bf)
        ggate = (gact * up * (sig + silu * (1.0 - sig))).astype(bf)
        gup = (gact * silu).astype(bf)
        act_ref[:, :width] = act
        flow[...] += nt(act, adf)
        gx_acc[...] += nt(ggate, wg) + nt(gup, wu)
        back[:, :RANK] += nt(ggate, aug)
        back[:, RANK:] += nt(gup, auu)
        daugu_ref[:RANK, :width] = nn(xlow_t[:RANK, :], ggate)
        daugu_ref[RANK:, :width] = nn(xlow_t[RANK:, :], gup)
        dadf_ref[:, :width] = nn(fback_t[...], act)

    tail = hidden - (tiles - 1) * tile
    if tail == tile:
        work(tile)
    else:
        @pl.when(step < tiles - 1)
        def body():
            work(tile)

        @pl.when(step == tiles - 1)
        def part():
            work(tail)

    @pl.when(step == tiles - 1)
    def finish():
        gx_acc[...] += nn((back[...] * 2.0).astype(bf), adgu_ref[...])
        gx_own[...] = gx_acc[:half, :]
        gx_send[...] = gx_acc[half:, :].astype(bf)
        flow_ref[...] = (flow[...] * 2.0).astype(bf)
        dadgu_ref[...] = nn(back[...].T.astype(bf), x_ref[...])
        dauf_ref[...] = nn(flow[...].T.astype(bf), g_ref[...])


def ffn(x_own, x_other, g_own, g_other, gact, adgu, auf, wgu, adf, augu, tile=TILE):
    rows, width = 2 * x_own.shape[0], x_own.shape[1]
    hidden = wgu.shape[2]
    tiles = -(-hidden // tile)
    half = rows // 2
    cols = lambda r: pl.BlockSpec((r, tile), lambda i: (0, i))
    outs = (
        shape(half, width), shape(half, width, dtype=bf), pltpu.HBM((rows, hidden), bf), shape(rows, RANK, dtype=bf),
        shape(2 * RANK, width), shape(RANK, width), shape(2 * RANK, hidden), shape(RANK, hidden),
    )
    return pl.pallas_call(
        functools.partial(ffn_kernel, tile, tiles, hidden),
        grid=(tiles,),
        out_shape=outs,
        in_specs=[whole(half, width)] * 4 + [cols(rows), whole(2 * RANK, width), whole(RANK, width),
                  pl.BlockSpec((2, width, tile), lambda i: (0, 0, i)), cols(RANK), cols(2 * RANK)],
        out_specs=(whole(half, width), whole(half, width), cols(rows), whole(rows, RANK), whole(2 * RANK, width),
                   whole(RANK, width), cols(2 * RANK), cols(RANK)),
        scratch_shapes=[
            pltpu.VMEM((rows, width), bf), pltpu.VMEM((rows, width), bf), pltpu.VMEM((rows, width), f32),
            pltpu.VMEM((rows, 2 * RANK), bf), pltpu.VMEM((2 * RANK, rows), bf), pltpu.VMEM((rows, RANK), bf),
            pltpu.VMEM((RANK, rows), bf), pltpu.VMEM((rows, RANK), f32), pltpu.VMEM((rows, 2 * RANK), f32),
        ],
        cost_estimate=pl.CostEstimate(flops=8 * rows * width * hidden, bytes_accessed=6 * width * hidden, transcendentals=rows * hidden),
        compiler_params=pltpu.CompilerParams(vmem_limit_bytes=36 << 20),
        name="ffn",
    )(x_own, x_other, in_hbm(g_own), in_hbm(g_other), in_hbm(gact), adgu, auf, in_hbm(wgu), adf, augu)


def down_kernel(bounds, start_refs, act_hbm, wd_hbm, total, act, wd, act_sems, wd_sems):
    low = bounds[0][0]
    copies = []
    for i, (begin, end) in enumerate(bounds):
        rows = slice(begin - low, end - low)
        copies.append((
            pltpu.make_async_copy(act_hbm.at[:, begin:end], act.at[:, rows], act_sems.at[i]),
            pltpu.make_async_copy(wd_hbm.at[begin:end], wd.at[rows], wd_sems.at[i]),
        ))
        for copy in copies[-1]:
            copy.start()
    total[...] = nn(start_refs[0][...], start_refs[1][...]) if len(start_refs) == 2 else start_refs[0][...]
    for i, (begin, end) in enumerate(bounds):
        rows = slice(begin - low, end - low)
        for copy in copies[i]:
            copy.wait()
        total[...] += nn(act[:, rows], wd[rows, :])


def down_first_kernel(bounds, flow_ref, auf_ref, act_hbm, wd_hbm, total, *scratch):
    down_kernel(bounds, (flow_ref, auf_ref), act_hbm, wd_hbm, total, *scratch)


def down_last_kernel(bounds, start_ref, act_hbm, wd_hbm, own_ref, send_ref, total, *scratch):
    down_kernel(bounds, (start_ref,), act_hbm, wd_hbm, total, *scratch)
    half = own_ref.shape[0]
    own_ref[...] = total[:half, :]
    send_ref[...] = total[half:, :].astype(bf)


def down(act, wd, start, bounds, last):
    rows, width = act.shape[0], wd.shape[1]
    half, columns, count = rows // 2, bounds[-1][1] - bounds[0][0], len(bounds)
    outs = (shape(half, width), shape(half, width, dtype=bf)) if last else (shape(rows, width),)
    scratch = [
        pltpu.VMEM((rows, columns), bf), pltpu.VMEM((columns, width), bf), pltpu.SemaphoreType.DMA((count,)),
        pltpu.SemaphoreType.DMA((count,)),
    ]
    return pl.pallas_call(
        functools.partial(down_last_kernel if last else down_first_kernel, bounds),
        out_shape=outs,
        in_specs=[VM] * len(start) + [HB, HB],
        out_specs=(VM,) * len(outs),
        scratch_shapes=([pltpu.VMEM((rows, width), f32)] if last else []) + scratch,
        cost_estimate=pl.CostEstimate(flops=2 * rows * width * columns, bytes_accessed=2 * width * columns, transcendentals=0),
        compiler_params=pltpu.CompilerParams(vmem_limit_bytes=28 << 20),
        name="down",
    )(*start, in_hbm(act), in_hbm(wd))


def per_device(
    tokens, cotangent, positions, adapter_choice, attn_gain, query_weight, query_bias, key_value_weight,
    key_value_bias, output_weight, ffn_gain, gate_upper_weight, down_weight, adapt_in, adapt_out,
):
    dp = lax.axis_index("dp")
    groups = lax.axis_size("seq")
    rings = groups // 2
    width, head_width = query_weight.shape
    heads = head_width // HEAD_DIM
    hidden = down_weight.shape[0]
    token_pos = positions[0]
    tok_count = token_pos.shape[0]
    span = tok_count // 2
    scale = HEAD_DIM ** (-0.5)
    coef = scale * math.log2(math.e)
    wide_in, wide_out = adapt_in.shape[2], adapt_out.shape[2]
    lanes_in = rounded_up(wide_in + 1, 128)
    lanes = lanes_in + rounded_up(wide_out, 128)
    widths = (width, head_width, hidden)
    sizes = (rings, wide_in, wide_out, lanes_in, widths)

    def to_pair(value):
        return lax.ppermute(value, "tensor", [(0, 1), (1, 0)])

    def to_other_sequence(value, pairs=((0, 1), (1, 0))):
        return lax.ppermute(value, "dp", list(pairs))

    def to_side(value):
        return lax.ppermute(value, "seq", [(i, i ^ 1) for i in range(groups)])

    def along_ring(value, steps):
        return lax.ppermute(value, "seq", [(i, (i + 2 * steps) % groups) for i in range(groups)])

    cycle = list(range(0, groups, 2)) + list(range(groups - 1, 0, -2))
    hops = [(cycle[i], cycle[(i + 1) % groups]) for i in range(groups)]

    def to_next(value):
        return lax.ppermute(value, "seq", hops)

    def to_last(value):
        return lax.ppermute(value, "seq", [(end, begin) for begin, end in hops])

    def after(value, *others):
        return lax.optimization_barrier((value, *others))[0]

    inputs, grad_out = tokens[0], cotangent[0]
    half = inputs.shape[0]
    attn_gain, ffn_gain = attn_gain[None], ffn_gain[None]

    def over_ring(piece):
        return [piece] + [along_ring(piece, step) for step in range(1, rings)]

    slice_own, slice_other = call(
        functools.partial(select_kernel, lanes_in, span), "select",
        [shape(RANK, lanes, dtype=bf)] * 2, [adapter_choice, positions, adapt_in, adapt_out],
        [pltpu.VMEM((2, RANK, wide_in), bf), pltpu.VMEM((2, RANK, wide_out), bf), pltpu.SemaphoreType.DMA((4,))],
        smem=2, left=2,
    )
    slice_other = to_other_sequence(slice_other)
    lane = lax.broadcasted_iota(jnp.int32, (RANK, lanes), 1)
    run_lane = (lane >= wide_in) & (lane < lanes_in)
    grad_other = to_pair(grad_out)
    slice_other = after(slice_other, grad_other)
    first_slice = jnp.where((dp == 0) | run_lane, slice_own, slice_other)
    second_slice = jnp.where(dp == 0, slice_other, slice_own)

    (normed,) = call(norm_kernel, "norm", [shape(half, width, dtype=bf)], [inputs, attn_gain])
    normed_other = to_pair(normed)
    arrived = over_ring(jnp.stack([first_slice, second_slice]))
    act_grad = act_back(grad_out, grad_other, down_weight, steps_of(hidden))
    arrived[1] = after(arrived[1], act_grad)
    own_slices = jnp.stack([piece[0] for piece in arrived])
    own_second = jnp.stack([piece[1] for piece in arrived])
    side_slices = to_side(own_slices)
    pair_slices = to_pair(own_slices)
    normed_rows, query_dense, kv_dense = call(
        dense_kernel, "dense", [shape(tok_count, width, dtype=bf), shape(tok_count, head_width), shape(tok_count, 2 * HEAD_DIM)],
        [normed, after(normed_other, own_slices), query_weight, key_value_weight],
        flops=2 * tok_count * width * (head_width + 2 * HEAD_DIM),
    )
    frequency = jnp.power(rope_base, -(jnp.arange(HEAD_DIM // 2, dtype=f32) * 2.0) / HEAD_DIM)
    angles = token_pos.astype(f32)[:, None] * frequency[None, :]
    cosine, sine = jnp.cos(angles), jnp.sin(angles)
    cosine = jnp.concatenate([cosine, cosine], axis=1)
    sine = jnp.concatenate([-sine, sine], axis=1)

    side_slices = after(side_slices, kv_dense)
    first_slices = [own_slices, side_slices, pair_slices, to_pair(side_slices)]
    slices_in = -(-4 * width // wide_in)
    slices_out = -(-(2 * width + 4 * HEAD_DIM) // wide_out)
    flags, adqkv, auq, auk, auv, ado, auo = call(
        functools.partial(unpack_first_kernel, *sizes), "unpack_first",
        [shape(groups, dtype=jnp.int32)]
        + [
            shape(*dims, dtype=bf)
            for dims in (
                (3 * RANK, width), (RANK, head_width), (RANK, HEAD_DIM), (RANK, HEAD_DIM), (RANK, head_width), (RANK, width),
            )
        ],
        list(first_slices),
        [
            pltpu.VMEM((2 * groups, RANK, lanes), bf),
            pltpu.VMEM((RANK, rounded_up(slices_in * wide_in, 128) + 256), f32),
            pltpu.VMEM((RANK, rounded_up(slices_out * wide_out, 128) + 256), f32),
            pltpu.SMEM((groups,), jnp.int32),
        ],
        out_specs=(SM,) + (VM,) * 6,
    )
    kv, low, low_t = call(
        key_value_kernel, "key_value",
        [shape(tok_count, 2 * HEAD_DIM, dtype=bf), shape(tok_count, 3 * RANK, dtype=bf), shape(3 * RANK, tok_count, dtype=bf)],
        [normed_rows, kv_dense, key_value_bias, adqkv, auk, auv, cosine, sine],
        flops=2 * tok_count * width * 2 * RANK,
    )

    (queries,) = call(
        query_kernel, "query", [shape(2, heads, span, HEAD_DIM, dtype=bf)],
        [query_dense, query_bias[None], low, auq, cosine, sine], flops=2 * tok_count * width * RANK,
    )
    state = attn_fwd_own(queries, kv, coef)
    pieces, from_last, from_next = [kv], kv, kv
    for step in range(1, rings + 1):
        from_last, from_next = to_next(from_last), to_last(from_next)
        if step < rings:
            from_last, from_next, _ = lax.optimization_barrier((from_last, from_next, state[0]))
        if step == rings:
            own_second = after(own_second, pieces[-1])
            side_second, pair_second = to_side(own_second), to_pair(own_second)
            state = (after(state[0], side_second, pair_second), *state[1:])
        pieces += [from_last, from_next][: 2 if step < rings else 1]
        indices = tuple(range(2 * step - 1, len(pieces)))
        result = attn_fwd_pieces(flags, indices, queries, pieces[2 * step - 1 :], state, coef, step == rings)
        state = result[-3:]
    mixed, lse = result[0], result[1]

    branch_send, mix_low, mix_low_t = call(
        mix_send_kernel, "mix_send",
        [shape(half, width, dtype=bf), shape(tok_count, RANK, dtype=bf), shape(RANK, tok_count, dtype=bf)],
        [mixed, output_weight, ado, auo], flops=2 * half * width * head_width,
    )
    branch_other = to_pair(branch_send)
    second_slices = [own_second, side_second, pair_second, to_pair(side_second)]
    (branch_own,) = call(
        mix_own_kernel, "mix_own", [shape(half, width)], [mixed, output_weight, mix_low, auo],
        flops=2 * half * width * head_width,
    )
    hidden_rows, normed_ffn = call(
        residual_kernel, "residual", [pltpu.HBM((half, width), f32), shape(half, width, dtype=bf)],
        [inputs, branch_own, after(branch_other, branch_own, second_slices[3]), ffn_gain],
    )
    begin_in, begin_out, first_in, first_out = bases(wide_in, wide_out, widths)
    adgu, augu, adf, auf = call(
        functools.partial(unpack_second_kernel, *sizes), "unpack_second",
        [shape(*dims, dtype=bf) for dims in ((2 * RANK, width), (2 * RANK, hidden), (RANK, hidden), (RANK, width))],
        list(first_slices) + list(second_slices),
        [
            pltpu.VMEM((4 * groups, RANK, lanes), bf),
            pltpu.VMEM((RANK, rounded_up(4 * groups * wide_in, 128) + 256 - first_in), f32),
            pltpu.VMEM((RANK, rounded_up(4 * groups * wide_out, 128) + 256 - first_out), f32),
        ],
    )
    gx_own, gx_send, act, flow, dadgu, dauf, daugu, dadf = ffn(
        normed_ffn, to_pair(normed_ffn), grad_out, grad_other, act_grad, adgu, auf, gate_upper_weight, adf, augu
    )
    ad_lanes = rounded_up(4 * groups * wide_in, 128) + 256
    au_lanes = rounded_up(4 * groups * wide_out, 128) + 256

    def added(*values):
        total = values[0].astype(f32)
        for value in values[1:]:
            total = total + value.astype(f32)
        return total.astype(bf)

    grad_hidden, grad_low = call(
        hidden_back_kernel, "hidden_back", [shape(half, width), shape(half, width, dtype=bf)],
        [hidden_rows, grad_out, gx_own, to_pair(gx_send), ffn_gain],
    )
    grad_low_other = to_pair(grad_low)
    fixed = [output_weight, ado, auo, mixed, mix_low_t]
    outs = [shape(2, heads, span, HEAD_DIM, dtype=bf), shape(2, heads, span), shape(RANK, head_width), shape(RANK, width)]
    partial = call(
        functools.partial(mix_back_kernel, True), "mix_back", outs, [grad_low, *fixed], flops=2 * half * width * head_width,
    )
    grad_mixed, delta, dado, dauo = call(
        functools.partial(mix_back_kernel, False), "mix_back_other", outs,
        [after(grad_low_other, partial[0]), *fixed, *partial], flops=2 * half * width * head_width,
        aliases={6 + i: i for i in range(4)},
    )

    def backward(indices, state_dq):
        return attn_bwd(
            flags, indices, queries, grad_mixed, lse, delta, [pieces[index] for index in indices], state_dq, coef, scale,
            indices == (0,),
        )

    state_dq, from_last, from_next = None, None, None
    for step in range(rings, 0, -1):
        onward, *returned, state_dq = backward((2 * rings - 1,) if step == rings else (2 * step, 2 * step - 1), state_dq)
        if from_last is not None:
            onward = added(onward, from_last)
        if from_next is not None:
            returned = [added(returned[0], from_next)]
        from_last = to_next(onward)
        if returned:
            from_next = to_last(returned[0])
        state_dq = after(state_dq, onward, *returned)
    own_term, state_dq = backward((0,), state_dq)
    gn_query, dadq, dauq = call(
        functools.partial(back_query_kernel, scale), "back_query",
        [shape(tok_count, width), shape(RANK, width), shape(RANK, head_width)],
        [state_dq, query_weight, adqkv, auq, low_t, normed_rows, cosine, sine],
        [pltpu.VMEM((tok_count, head_width), bf)], flops=2 * tok_count * width * head_width,
    )
    from_last = after(from_last, gn_query)
    gn_own, gn_send, dadkv, dauk, dauv = call(
        back_key_value_kernel, "back_key_value",
        [
            shape(half, width), shape(half, width, dtype=bf), shape(2 * RANK, width), shape(RANK, HEAD_DIM),
            shape(RANK, HEAD_DIM),
        ],
        [
            own_term, gn_query, key_value_weight, adqkv, auk, auv, low_t, normed_rows, cosine, sine, from_last, from_next,
        ],
        [pltpu.VMEM((tok_count, width), f32), pltpu.VMEM((tok_count, 2 * RANK), f32)],
        flops=2 * tok_count * width * 2 * HEAD_DIM, limit=20,
    )
    (packed,) = call(
        functools.partial(pack_kernel, *sizes), "pack", [shape(2, 2, rings, 2, RANK, lanes, dtype=bf)],
        [dadq, dadkv, dado, dadgu, dadf, dauq, dauk, dauv, dauo, daugu, dauf],
        [pltpu.VMEM((RANK, ad_lanes), f32), pltpu.VMEM((RANK, au_lanes), f32)],
    )
    from_pair = to_pair(packed[1])
    near, far = added(packed[0, 0], from_pair[0]), added(packed[0, 1], from_pair[1])
    from_side = to_side(far)
    middle = 6 * TILE
    (out_total,) = down(after(act, far), down_weight, (flow, auf), steps_of(middle), False)
    from_side = after(from_side, out_total)
    sums = [added(near[place], from_side[place]) for place in range(rings)]
    from_ring = [along_ring(sums[place], -place) for place in range(1, rings)]
    out_own, out_send = down(after(act, sums[0]), down_weight, (out_total,), steps_of(hidden, middle), True)
    (grad_tokens,) = call(
        token_back_kernel, "token_back", [shape(half, width)],
        [inputs, grad_hidden, gn_own, after(to_pair(gn_send), out_own), attn_gain],
    )
    output = (hidden_rows + (out_own + to_pair(out_send).astype(f32))).astype(bf)
    from_ring[0] = after(from_ring[0], out_own)
    total = added(sums[0], *from_ring)
    other_total = after(to_other_sequence(total[1]), output, grad_tokens)
    factor = adapter_scale * (adapter_choice.shape[0] * tok_count * groups) ** (-0.5)
    adapt_in_grad, adapt_out_grad = call(
        functools.partial(place_kernel, lanes_in, factor), "place",
        [shape(*adapt_in.shape), shape(*adapt_out.shape)],
        [adapter_choice, total[0], other_total], smem=1,
    )
    return (output[None], grad_tokens[None], adapt_in_grad, adapt_out_grad)


def solution(mesh):
    return jax.shard_map(
        per_device,
        mesh=mesh,
        in_specs=(
            P("dp", ("seq", "tensor"), None),
            P("dp", ("seq", "tensor"), None),
            P("dp", "seq"),
            P(),
            P(),
            P(None, "tensor"),
            P("tensor"),
            P(None, None, "tensor"),
            P(None, "tensor"),
            P("tensor", None),
            P(),
            P(None, None, "tensor"),
            P("tensor", None),
            P(None, None, ("dp", "seq", "tensor")),
            P(None, None, ("dp", "seq", "tensor")),
        ),
        out_specs=(
            P("dp", ("seq", "tensor"), None),
            P("dp", ("seq", "tensor"), None),
            P(None, None, ("dp", "seq", "tensor")),
            P(None, None, ("dp", "seq", "tensor")),
        ),
        check_vma=False,
    )
```

```python
import functools
import math

import jax
import jax.numpy as jnp
from jax import lax
from jax.experimental import pallas as pl
from jax.experimental.pallas import tpu as pltpu
from jax.sharding import PartitionSpec as P

HEAD_DIM = 128
RANK = 16
eps = 1e-06
adapter_scale = 2.0
rope_base = 1000000.0
mask_fill = -1e30
bf = jnp.bfloat16
f32 = jnp.float32
VM = pl.BlockSpec(memory_space=pltpu.VMEM)
SM = pl.BlockSpec(memory_space=pltpu.SMEM)


def nn(a, b):
    return jnp.dot(a, b, preferred_element_type=f32)


def nt(a, b):
    return lax.dot_general(a, b, (((1,), (1,)), ((), ())), preferred_element_type=f32)


def shape(*dims, dtype=f32):
    return jax.ShapeDtypeStruct(dims, dtype)


def call(kernel, name, out, ins, scratch=(), flops=0, smem=0, out_specs=None, limit=16, left=0, aliases=None):
    moved = sum(math.prod(v.shape) * v.dtype.itemsize for v in list(ins) + list(out))
    ins = list(ins[: len(ins) - left]) + [in_hbm(value) for value in ins[len(ins) - left :]]
    return pl.pallas_call(
        kernel,
        out_shape=tuple(out),
        in_specs=[SM] * smem + [VM] * (len(ins) - smem - left) + [HB] * left,
        out_specs=out_specs or (VM,) * len(out),
        scratch_shapes=list(scratch),
        input_output_aliases=aliases or {},
        cost_estimate=pl.CostEstimate(flops=flops, bytes_accessed=moved, transcendentals=0),
        compiler_params=pltpu.CompilerParams(vmem_limit_bytes=limit << 20),
        name=name,
    )(*ins)


HB = pl.BlockSpec(memory_space=pltpu.HBM)


def in_hbm(value):
    return pltpu.with_memory_space_constraint(value, pltpu.HBM)


def rounded_up(value, unit):
    return -(-value // unit) * unit


def select_kernel(
    lanes_in, span, choice_hbm, pos_hbm, in_ref, out_ref, own_ref, other_ref, choice_ref, pos_ref, held_in, held_out, sems
):
    wide_in, wide_out = in_ref.shape[2], out_ref.shape[2]
    dp = lax.axis_index("dp")
    choice_copy = pltpu.make_async_copy(choice_hbm, choice_ref, sems.at[4])
    pos_copy = pltpu.make_async_copy(pos_hbm, pos_ref, sems.at[5])
    choice_copy.start()
    pos_copy.start()
    choice_copy.wait()
    copies = []
    for slot, sequence in ((0, dp), (1, 1 - dp)):
        chosen = choice_ref[sequence]
        copies.append(pltpu.make_async_copy(in_ref.at[chosen], held_in.at[slot], sems.at[2 * slot]))
        copies.append(pltpu.make_async_copy(out_ref.at[chosen], held_out.at[slot], sems.at[2 * slot + 1]))
    for copy in copies:
        copy.start()
    pos_copy.wait()
    run = jnp.full((RANK, lanes_in), pos_ref[0, 0] // span, jnp.int32).astype(f32).astype(bf)
    for target in (own_ref, other_ref):
        target[...] = jnp.zeros_like(target)
        target[:, :lanes_in] = run
    for copy in copies:
        copy.wait()
    for slot, target in ((0, own_ref), (1, other_ref)):
        target[:, :wide_in] = held_in[slot]
        target[:, lanes_in : lanes_in + wide_out] = held_out[slot]


def column(begin, size):
    return pl.ds(pl.multiple_of(begin, 128), size)


def source_of(place, side, rings, seq):
    ring = lax.rem(seq // 2 - place + rings, rings)
    own_side = lax.rem(seq, 2)
    return ring * 2 + (own_side if side == 0 else 1 - own_side)


def spread(slots, target, begin, wide, first, low, high):
    held = rounded_up(wide, 128)
    inside = lax.broadcasted_iota(jnp.int32, (RANK, held), 1) < wide
    target[...] = jnp.zeros_like(target)
    for index in range(low // wide, -(-high // wide)):
        part = jnp.where(inside, slots[index, :, begin : begin + held].astype(f32), 0.0)
        part = jnp.concatenate([part, jnp.zeros((RANK, 128), f32)], axis=1)
        offset = index * wide - first
        base = offset // 128 * 128
        if offset != base:
            part = pltpu.roll(part, offset - base, 1)
        target[:, base : base + held + 128] += part


def collect(slots, refs, rings, part):
    seq, shard = lax.axis_index("seq"), lax.axis_index("tensor")
    for number, ref in enumerate(refs):
        side, core = number % 2, shard if number < 2 else 1 - shard
        for place in range(rings):
            slots[part * 4 * rings + source_of(place, side, rings, seq) * 2 + core] = ref[place]


def unpack_first_kernel(
    rings, wide_in, wide_out, lanes_in, widths, own, own_side, pair, pair_side,
    flags_ref, adqkv, auq, auk, auv, ado, auo, slots, ad, au, runs,
):
    shard, seq = lax.axis_index("tensor"), lax.axis_index("seq")
    width, head_width, hidden = widths
    for place in range(rings):
        for side, ref in ((0, own), (1, own_side)):
            run = jnp.max(ref[place, :, wide_in:lanes_in].astype(f32))
            runs[source_of(place, side, rings, seq)] = run.astype(jnp.int32)
    groups = 2 * rings
    place = jnp.where(lax.rem(seq, 2) == 0, seq // 2, groups - 1 - seq // 2)
    for index in range(groups):
        step = (index + 1) // 2
        other = lax.rem(place + (groups - step if index % 2 == 1 else step), groups)
        source = jnp.where(other < rings, 2 * other, 2 * (groups - 1 - other) + 1)
        flags_ref[index] = (runs[source] < runs[seq]).astype(jnp.int32)
    collect(slots, (own, own_side, pair, pair_side), rings, 0)
    spread(slots, ad, 0, wide_in, 0, 0, 4 * width)
    spread(slots, au, lanes_in, wide_out, 0, 0, 2 * width + 4 * HEAD_DIM)
    for index in range(3):
        adqkv[index * RANK : (index + 1) * RANK, :] = ad[:, index * width : (index + 1) * width].astype(bf)
    ado[...] = ad[:, column(3 * width + shard * head_width, head_width)].astype(bf)
    auq[...] = au[:, column(shard * head_width, head_width)].astype(bf)
    auk[...] = au[:, column(width + shard * HEAD_DIM, HEAD_DIM)].astype(bf)
    auv[...] = au[:, column(width + (2 + shard) * HEAD_DIM, HEAD_DIM)].astype(bf)
    base = width + 4 * HEAD_DIM
    auo[...] = au[:, base : base + width].astype(bf)


def bases(wide_in, wide_out, widths):
    width = widths[0]
    begin_in, begin_out = 4 * width, 2 * width + 4 * HEAD_DIM
    return begin_in, begin_out, begin_in // wide_in * wide_in // 128 * 128, begin_out // wide_out * wide_out // 128 * 128


def unpack_second_kernel(
    rings, wide_in, wide_out, lanes_in, widths, *refs
):
    firsts, seconds = refs[:4], refs[4:8]
    adgu, augu, adf, auf, slots, ad, au = refs[8:]
    shard = lax.axis_index("tensor")
    width, head_width, hidden = widths
    collect(slots, firsts, rings, 0)
    collect(slots, seconds, rings, 1)
    begin_in, begin_out, first_in, first_out = bases(wide_in, wide_out, widths)
    total_in, total_out = 8 * rings * wide_in, 8 * rings * wide_out
    spread(slots, ad, 0, wide_in, first_in, begin_in, total_in)
    spread(slots, au, lanes_in, wide_out, first_out, begin_out, total_out)
    base = begin_in - first_in
    for index in range(2):
        adgu[index * RANK : (index + 1) * RANK, :] = ad[:, base + index * width : base + (index + 1) * width].astype(bf)
    adf[...] = ad[:, column(base + 2 * width + shard * hidden, hidden)].astype(bf)
    base = begin_out - first_out
    for index in range(2):
        augu[index * RANK : (index + 1) * RANK, :] = au[
            :, column(base + (2 * index + shard) * hidden, hidden)
        ].astype(bf)
    auf[...] = au[:, base + 4 * hidden : base + 4 * hidden + width].astype(bf)


def put_slices(rings, wide_in, wide_out, lanes_in, ad, au, limits, parts, write):
    dp, seq = lax.axis_index("dp"), lax.axis_index("seq")
    for index in range(4 * rings * parts):
        to_dp, to_seq, to_core = index // (4 * rings), index // 2 % (2 * rings), index % 2
        pieces = []
        for source, wide, (low, high, first) in ((ad, wide_in, limits[0]), (au, wide_out, limits[1])):
            held = rounded_up(wide, 128)
            if index * wide >= high or (index + 1) * wide <= low:
                part = jnp.zeros((RANK, held), f32)
            else:
                offset = index * wide - first
                base = offset // 128 * 128
                part = source[:, base : base + held + 128]
                if offset != base:
                    part = pltpu.roll(part, held + 128 - (offset - base), 1)
                part = part[:, :held]
            pieces.append(part)
            if source is ad and lanes_in > held:
                pieces.append(jnp.zeros((RANK, lanes_in - held), f32))
        packed = jnp.concatenate(pieces, axis=1).astype(bf)
        place = lax.rem(seq // 2 - to_seq // 2 + rings, rings)
        write(to_seq, to_core, place, lax.rem(dp + to_dp, 2), packed)


def pack_kernel(
    rings, wide_in, wide_out, lanes_in, widths,
    dadq, dadkv, dado, dadgu, dadf, dauq, dauk, dauv, dauo, daugu, dauf, out_ref, ad, au,
):
    shard, side = lax.axis_index("tensor"), lax.rem(lax.axis_index("seq"), 2)
    width, head_width, hidden = widths
    ad[...] = jnp.zeros_like(ad)
    au[...] = jnp.zeros_like(au)
    ad[:, :width] = dadq[...]
    for index in range(2):
        ad[:, (1 + index) * width : (2 + index) * width] = dadkv[index * RANK : (index + 1) * RANK, :]
        ad[:, (4 + index) * width : (5 + index) * width] = dadgu[index * RANK : (index + 1) * RANK, :]
    ad[:, column(3 * width + shard * head_width, head_width)] = dado[...]
    ad[:, column(6 * width + shard * hidden, hidden)] = dadf[...]
    au[:, column(shard * head_width, head_width)] = dauq[...]
    au[:, column(width + shard * HEAD_DIM, HEAD_DIM)] = dauk[...]
    au[:, column(width + (2 + shard) * HEAD_DIM, HEAD_DIM)] = dauv[...]
    base = width + 4 * HEAD_DIM
    au[:, base : base + width] = dauo[...]
    base = base + width
    for index in range(2):
        au[:, column(base + (2 * index + shard) * hidden, hidden)] = daugu[index * RANK : (index + 1) * RANK, :]
    au[:, base + 4 * hidden : base + 4 * hidden + width] = dauf[...]

    def write(to_seq, to_core, place, part, packed):
        out_ref[lax.rem(shard + to_core, 2), lax.rem(side + to_seq % 2, 2), place, part] = packed

    limits = ((0, 8 * rings * wide_in, 0), (0, 8 * rings * wide_out, 0))
    put_slices(rings, wide_in, wide_out, lanes_in, ad, au, limits, 2, write)


def place_kernel(lanes_in, factor, choice_ref, own_ref, other_ref, in_ref, out_ref):
    wide_in, wide_out = in_ref.shape[2], out_ref.shape[2]
    dp = lax.axis_index("dp")
    in_ref[...] = jnp.zeros_like(in_ref)
    out_ref[...] = jnp.zeros_like(out_ref)
    for ref, sequence in ((own_ref, dp), (other_ref, 1 - dp)):
        chosen = choice_ref[sequence]
        part = ref[...].astype(f32) * factor
        in_ref[chosen] = in_ref[chosen] + part[:, :wide_in]
        out_ref[chosen] = out_ref[chosen] + part[:, lanes_in : lanes_in + wide_out]


def factor_of(rows):
    return lax.rsqrt(jnp.mean(rows * rows, axis=-1, keepdims=True) + eps)


def norm_back(rows, gain, grad):
    factor = factor_of(rows)
    scaled = rows * factor
    grad_scaled = grad * gain
    return factor * (grad_scaled - scaled * jnp.mean(grad_scaled * scaled, axis=-1, keepdims=True))


def norm_kernel(rows_ref, gain_ref, normed_ref):
    rows = rows_ref[...].astype(f32)
    normed_ref[...] = (rows * factor_of(rows) * gain_ref[...].astype(f32)).astype(bf)


def residual_kernel(rows_ref, own_ref, other_ref, gain_ref, hidden_ref, normed_ref):
    rows = rows_ref[...].astype(f32) + (own_ref[...] + other_ref[...].astype(f32))
    hidden_ref[...] = rows
    normed_ref[...] = (rows * factor_of(rows) * gain_ref[...].astype(f32)).astype(bf)


def hidden_back_kernel(hidden_ref, grad_ref, own_ref, other_ref, gain_ref, out_ref, low_ref):
    grad = own_ref[...] + other_ref[...].astype(f32)
    total = grad_ref[...].astype(f32) + norm_back(hidden_ref[...], gain_ref[...].astype(f32), grad)
    out_ref[...] = total
    low_ref[...] = total.astype(bf)


def token_back_kernel(rows_ref, grad_ref, own_ref, other_ref, gain_ref, out_ref):
    grad = own_ref[...] + other_ref[...].astype(f32)
    out_ref[...] = grad_ref[...] + norm_back(rows_ref[...].astype(f32), gain_ref[...].astype(f32), grad)


def turned(rows, cosine, sine):
    return rows * cosine + pltpu.roll(rows, HEAD_DIM // 2, 1) * sine


def dense_kernel(own_ref, other_ref, wq_ref, wkv_ref, rows_ref, query_ref, kv_ref):
    shard = lax.axis_index("tensor")
    half = own_ref.shape[0]
    rows_ref[pl.ds(pl.multiple_of(shard * half, half), half), :] = own_ref[...]
    rows_ref[pl.ds(pl.multiple_of((1 - shard) * half, half), half), :] = other_ref[...]
    rows = rows_ref[...]
    query_ref[...] = nn(rows, wq_ref[...])
    kv_ref[:, :HEAD_DIM] = nn(rows, wkv_ref[0])
    kv_ref[:, HEAD_DIM:] = nn(rows, wkv_ref[1])


def key_value_kernel(
    rows_ref, dense_ref, bias_ref, adqkv_ref, auk_ref, auv_ref, cos_ref, sin_ref, kv_ref, low_ref, low_t_ref
):
    low = nt(rows_ref[...], adqkv_ref[...])
    low_ref[...] = (2.0 * low).astype(bf)
    low_t_ref[...] = low.T.astype(bf)
    key = dense_ref[:, :HEAD_DIM] + bias_ref[0:1, :].astype(f32) + nn(low_ref[:, RANK : 2 * RANK], auk_ref[...])
    value = dense_ref[:, HEAD_DIM:] + bias_ref[1:2, :].astype(f32) + nn(low_ref[:, 2 * RANK :], auv_ref[...])
    kv_ref[:, :HEAD_DIM] = turned(key, cos_ref[...], sin_ref[...]).astype(bf)
    kv_ref[:, HEAD_DIM:] = value.astype(bf)


def query_kernel(dense_ref, bias_ref, low_ref, auq_ref, cos_ref, sin_ref, q_ref):
    heads, span = q_ref.shape[1], q_ref.shape[2]
    query = dense_ref[...] + bias_ref[...].astype(f32) + nn(low_ref[:, :RANK], auq_ref[...])
    for h in range(heads):
        head = turned(query[:, h * HEAD_DIM : (h + 1) * HEAD_DIM], cos_ref[...], sin_ref[...]).astype(bf)
        q_ref[0, h] = head[:span]
        q_ref[1, h] = head[span:]


def rows_of(own, half):
    shard = lax.axis_index("tensor")
    return pl.ds(pl.multiple_of((shard if own else 1 - shard) * half, half), half)


def mix_send_kernel(mixed_ref, wo_ref, ado_ref, auo_ref, send_ref, low_ref, low_t_ref):
    low = nt(mixed_ref[...], ado_ref[...])
    low_ref[...] = (2.0 * low).astype(bf)
    low_t_ref[...] = low.T.astype(bf)
    rows = rows_of(False, send_ref.shape[0])
    send_ref[...] = (nn(mixed_ref[rows, :], wo_ref[...]) + nn(low_ref[rows, :], auo_ref[...])).astype(bf)


def mix_own_kernel(mixed_ref, wo_ref, low_ref, auo_ref, own_ref):
    rows = rows_of(True, own_ref.shape[0])
    own_ref[...] = nn(mixed_ref[rows, :], wo_ref[...]) + nn(low_ref[rows, :], auo_ref[...])


def mix_back_kernel(own, rows_ref, wo_ref, ado_ref, auo_ref, mixed_ref, low_t_ref, *refs):
    do_ref, delta_ref, dado_ref, dauo_ref = refs[-4:]
    half = rows_ref.shape[0]
    heads = do_ref.shape[1]
    part = lax.axis_index("tensor") if own else 1 - lax.axis_index("tensor")
    places = rows_of(own, half)
    rows, mixed = rows_ref[...], mixed_ref[places, :]
    back = nt(rows, auo_ref[...])
    grad = (nt(rows, wo_ref[...]) + nn((2.0 * back).astype(bf), ado_ref[...])).astype(bf)
    dado = nn(back.T.astype(bf), mixed)
    dauo = nn(low_t_ref[:, places], rows)
    dado_ref[...] = dado if own else refs[2][...] + dado
    dauo_ref[...] = dauo if own else refs[3][...] + dauo
    for h in range(heads):
        cols = slice(h * HEAD_DIM, (h + 1) * HEAD_DIM)
        product = (grad[:, cols].astype(f32) * mixed[:, cols].astype(f32)).T
        do_ref[part, h] = grad[:, cols]
        delta_ref[part, h : h + 1, :] = jnp.sum(product, axis=0, keepdims=True)


def back_query_kernel(
    scale, dq_ref, wq_ref, adq_ref, auq_ref, low_t_ref, rows_ref, cos_ref, sin_ref, total_ref, dadq_ref, dauq_ref, eq
):
    heads, span = dq_ref.shape[1], dq_ref.shape[3]
    for part in range(2):
        rows = slice(part * span, (part + 1) * span)
        for h in range(heads):
            grad = dq_ref[part, h].T * scale
            eq[rows, h * HEAD_DIM : (h + 1) * HEAD_DIM] = turned(grad, cos_ref[rows, :], -sin_ref[rows, :]).astype(bf)
    query = eq[...]
    back = nt(query, auq_ref[...])
    total_ref[...] = nt(query, wq_ref[...]) + nn((2.0 * back).astype(bf), adq_ref[:RANK, :])
    dadq_ref[...] = nn(back.T.astype(bf), rows_ref[...])
    dauq_ref[...] = nn(low_t_ref[:RANK, :], query)


def back_key_value_kernel(
    dkv_ref, query_ref, wkv_ref, adqkv_ref, auk_ref, auv_ref, low_t_ref, rows_ref, cos_ref, sin_ref, *refs
):
    others = refs[: len(refs) - 7]
    own_ref, send_ref, dadkv_ref, dauk_ref, dauv_ref, total, back_ref = refs[len(refs) - 7 :]
    shard = lax.axis_index("tensor")
    half = own_ref.shape[0]
    grad = dkv_ref[...].astype(f32)
    for ref in others:
        grad = grad + ref[...].astype(f32)
    ek = turned(grad[:, :HEAD_DIM], cos_ref[...], -sin_ref[...]).astype(bf)
    ev = grad[:, HEAD_DIM:].astype(bf)
    back_ref[:, :RANK] = nt(ek, auk_ref[...])
    back_ref[:, RANK:] = nt(ev, auv_ref[...])
    back = back_ref[...]
    total[...] = (
        query_ref[...] + nt(ek, wkv_ref[0]) + nt(ev, wkv_ref[1]) + nn((2.0 * back).astype(bf), adqkv_ref[RANK:, :])
    )
    own_ref[...] = total[pl.ds(pl.multiple_of(shard * half, half), half), :]
    send_ref[...] = total[pl.ds(pl.multiple_of((1 - shard) * half, half), half), :].astype(bf)
    dadkv_ref[...] = nn(back.T.astype(bf), rows_ref[...])
    dauk_ref[...] = nn(low_t_ref[RANK : 2 * RANK, :], ek)
    dauv_ref[...] = nn(low_t_ref[2 * RANK :, :], ev)


def future_mask(span):
    return lax.broadcasted_iota(jnp.int32, (span, span), 0) <= lax.broadcasted_iota(jnp.int32, (span, span), 1)

def fold(s, values_t, m, l, o, coef, mask):
    if mask is not None:
        s = jnp.where(mask, s, mask_fill)
    m_next = jnp.maximum(m, jnp.max(s, axis=0, keepdims=True))
    p = jnp.exp2((s - m_next) * coef)
    alpha = jnp.exp2((m - m_next) * coef)
    l_next = l * alpha + jnp.sum(p, axis=0, keepdims=True)
    o_next = o * alpha + nn(values_t, p.astype(bf))
    return m_next, l_next, o_next

def pipelined(items, first, second):
    ahead = first(items[0])
    for i, item in enumerate(items):
        now = ahead
        if i + 1 < len(items):
            ahead = first(items[i + 1])
        second(item, now)

def attn_fwd_own_kernel(coef, q_ref, kv_ref, m_ref, l_ref, o_ref, vt):
    heads, span = q_ref.shape[1], q_ref.shape[2]
    vt[...] = kv_ref[:, HEAD_DIM:].astype(f32).T.astype(bf)
    mask = future_mask(span)
    both_mask = lax.broadcasted_iota(jnp.int32, (2 * span, span), 0) <= lax.broadcasted_iota(jnp.int32, (2 * span, span), 1) + span
    def first(item):
        half, h = item
        return nt(kv_ref[: (half + 1) * span, :HEAD_DIM], q_ref[half, h])
    def second(item, s):
        half, h = item
        m = jnp.full((1, span), mask_fill, f32)
        l = jnp.zeros((1, span), f32)
        o = jnp.zeros((HEAD_DIM, span), f32)
        m, l, o = fold(s, vt[:, : (half + 1) * span], m, l, o, coef, both_mask if half else mask)
        m_ref[half, h : h + 1, :] = m
        l_ref[half, h : h + 1, :] = l
        o_ref[half, h] = o
    pipelined([(half, h) for h in range(heads) for half in range(2)], first, second)

def halves_of(flag, turn):
    return (1 - flag) * turn, flag * turn + (1 - flag)


def attn_fwd_pieces_kernel(coef, indices, last, flag_ref, q_ref, *refs):
    n = len(indices)
    kv_refs = refs[:n]
    m_in, l_in, o_in = refs[n : n + 3]
    if last:
        mixed_ref, lse_ref, m_ref, l_ref, o_ref, vt = refs[n + 3 :]
    else:
        m_ref, l_ref, o_ref, vt = refs[n + 3 :]
    heads, span = q_ref.shape[1], q_ref.shape[2]
    src = [(m_in, l_in, o_in)] + [(m_ref, l_ref, o_ref)] * n
    m_ref[...] = m_in[...]
    l_ref[...] = l_in[...]
    o_ref[...] = o_in[...]
    for i in range(n):
        kv_ref, flag = kv_refs[i], flag_ref[indices[i]]
        vt[...] = kv_ref[:, HEAD_DIM:].astype(f32).T.astype(bf)

        def first(item, kv_ref=kv_ref, flag=flag):
            keys, half = halves_of(flag, item[0])
            return nt(kv_ref[pl.ds(pl.multiple_of(keys * span, span), span), :HEAD_DIM], q_ref[half, item[1]])

        def second(item, s, flag=flag):
            (keys, half), h = halves_of(flag, item[0]), item[1]
            m, l, o = fold(
                s, vt[:, pl.ds(pl.multiple_of(keys * span, span), span)], m_ref[half, h : h + 1, :], l_ref[half, h : h + 1, :],
                o_ref[half, h], coef, None,
            )
            m_ref[half, h : h + 1, :] = m
            l_ref[half, h : h + 1, :] = l
            o_ref[half, h] = o

        pipelined([(turn, h) for turn in range(2) for h in range(heads)], first, second)
    if last:
        for half in range(2):
            for h in range(heads):
                o = o_ref[half, h] / l_ref[half, h : h + 1, :]
                mixed_ref[half * span : (half + 1) * span, h * HEAD_DIM : (h + 1) * HEAD_DIM] = o.T.astype(bf)
        lse_ref[...] = m_ref[...] * coef + jnp.log2(l_ref[...])


def attn_fwd_own(q, kv, coef):
    _, heads, span, _ = q.shape
    st = (jax.ShapeDtypeStruct((2, heads, span), f32),) * 2 + (jax.ShapeDtypeStruct((2, heads, HEAD_DIM, span), f32),)
    return pl.pallas_call(functools.partial(attn_fwd_own_kernel, coef), out_shape=st, in_specs=[VM, VM], out_specs=(VM,) * 3,
        scratch_shapes=[pltpu.VMEM((HEAD_DIM, 2 * span), bf)],
        cost_estimate=pl.CostEstimate(flops=2*2*3*heads*span*span*HEAD_DIM*2, bytes_accessed=4_000_000, transcendentals=0),
        compiler_params=pltpu.CompilerParams(vmem_limit_bytes=20 << 20), name="attn_fwd_own")(q, kv)

def attn_fwd_pieces(flags, indices, q, pieces, state, coef, last):
    _, heads, span, _ = q.shape
    n = len(pieces)
    st = (jax.ShapeDtypeStruct((2, heads, span), f32),) * 2 + (jax.ShapeDtypeStruct((2, heads, HEAD_DIM, span), f32),)
    if last:
        st = (jax.ShapeDtypeStruct((2 * span, heads * HEAD_DIM), bf), jax.ShapeDtypeStruct((2, heads, span), f32)) + st
    r = pl.pallas_call(functools.partial(attn_fwd_pieces_kernel, coef, indices, last), out_shape=st, in_specs=[SM] + [VM] * (n + 4), out_specs=(VM,) * len(st),
        scratch_shapes=[pltpu.VMEM((HEAD_DIM, 2 * span), bf)],
        cost_estimate=pl.CostEstimate(flops=2*2*2*n*heads*span*span*HEAD_DIM*2, bytes_accessed=4_000_000, transcendentals=0),
        compiler_params=pltpu.CompilerParams(vmem_limit_bytes=20 << 20), name="attn_fwd_pieces")(flags, q, *pieces, *state)
    return r

def bwd_block(s, dp, lse_ref, delta_ref, half, h, coef, mask):
    p = jnp.exp2(s * coef - lse_ref[half, h : h + 1, :])
    if mask is not None:
        p = jnp.where(mask, p, 0.0)
    ds = p * (dp - delta_ref[half, h : h + 1, :])
    return p.astype(bf), ds.astype(bf)

def attn_bwd_kernel(coef, scale, indices, own, has_state, flag_ref, q_ref, do_ref, lse_ref, delta_ref, *refs):
    n = len(indices)
    kv_refs = refs[:n]
    k = n
    if has_state:
        dq_in = refs[k]; k += 1
    dkv_refs = refs[k : k + n]
    dq_ref, kt, pbuf, sbuf = refs[k + n :]
    heads, span = q_ref.shape[1], q_ref.shape[2]
    if has_state:
        dq_ref[...] = dq_in[...]
    else:
        dq_ref[...] = jnp.zeros_like(dq_ref)
    def do_item(kv_ref, items, keyrows, mask_of):
        nk = keyrows.stop - keyrows.start
        def first(it):
            i, half, h = it
            return nt(kv_ref[keyrows, :HEAD_DIM], q_ref[half, h]), nt(kv_ref[keyrows, HEAD_DIM:], do_ref[half, h])
        def second(it, sd):
            i, half, h = it
            p, ds = bwd_block(sd[0], sd[1], lse_ref, delta_ref, half, h, coef, mask_of(half))
            cols = slice((i * heads + h) * span, (i * heads + h + 1) * span)
            pbuf[:nk, cols] = p
            sbuf[:nk, cols] = ds
            dq_ref[half, h] += nn(kt[:, keyrows], ds)
        pipelined([(i, half, h) for i, half in enumerate(items) for h in range(heads)], first, second)
        width = len(items) * heads * span
        lo = items[0]
        q_all = q_ref[lo : lo + len(items)].reshape(width, HEAD_DIM)
        do_all = do_ref[lo : lo + len(items)].reshape(width, HEAD_DIM)
        return nn(sbuf[:nk, :width], q_all) * scale, nn(pbuf[:nk, :width], do_all)
    for i in range(n):
        kv_ref, out = kv_refs[i], dkv_refs[i]
        kt[...] = kv_ref[:, :HEAD_DIM].astype(f32).T.astype(bf)
        lo, hi, both = slice(0, span), slice(span, 2 * span), slice(0, 2 * span)
        if own and i == 0:
            mask = future_mask(span)
            dk, dv = do_item(kv_ref, [0, 1], lo, lambda half: mask if half == 0 else None)
            out[lo, :HEAD_DIM] = dk.astype(bf)
            out[lo, HEAD_DIM:] = dv.astype(bf)
            dk, dv = do_item(kv_ref, [1], hi, lambda half: mask)
            out[hi, :HEAD_DIM] = dk.astype(bf)
            out[hi, HEAD_DIM:] = dv.astype(bf)
        else:
            flag = flag_ref[indices[i]]

            def first(item, kv_ref=kv_ref, flag=flag):
                (keys, half), h = halves_of(flag, item[0]), item[1]
                rows = pl.ds(pl.multiple_of(keys * span, span), span)
                return nt(kv_ref[rows, :HEAD_DIM], q_ref[half, h]), nt(kv_ref[rows, HEAD_DIM:], do_ref[half, h])

            def second(item, sd, flag=flag):
                turn, h = item
                keys, half = halves_of(flag, turn)
                p, ds = bwd_block(sd[0], sd[1], lse_ref, delta_ref, half, h, coef, None)
                cols = slice(h * span, (h + 1) * span)
                pbuf[turn * span : (turn + 1) * span, cols] = p
                sbuf[turn * span : (turn + 1) * span, cols] = ds
                dq_ref[half, h] += nn(kt[:, pl.ds(pl.multiple_of(keys * span, span), span)], ds)

            pipelined([(turn, h) for turn in range(2) for h in range(heads)], first, second)
            width = heads * span
            both = []
            for turn in range(2):
                keys, half = halves_of(flag, turn)
                rows = slice(turn * span, (turn + 1) * span)
                both.append((
                    nn(sbuf[rows, :width], q_ref[half].reshape(width, HEAD_DIM)) * scale,
                    nn(pbuf[rows, :width], do_ref[half].reshape(width, HEAD_DIM)),
                ))
            earlier = flag.astype(f32)
            for part in range(2):
                cols = slice(part * HEAD_DIM, (part + 1) * HEAD_DIM)
                out[lo, cols] = (both[0][part] + both[1][part] * earlier).astype(bf)
                out[hi, cols] = (both[1][part] * (1.0 - earlier)).astype(bf)


def attn_bwd(flags, indices, q, do, lse, delta, pieces, dq_state, coef, scale, own):
    _, heads, span, _ = q.shape
    n = len(pieces)
    outs = tuple(jax.ShapeDtypeStruct((2 * span, 2 * HEAD_DIM), bf) for _ in range(n)) + (jax.ShapeDtypeStruct((2, heads, HEAD_DIM, span), f32),)
    ins = [flags, q, do, lse, delta, *pieces] + ([dq_state] if dq_state is not None else [])
    return pl.pallas_call(functools.partial(attn_bwd_kernel, coef, scale, indices, own, dq_state is not None), out_shape=outs,
        in_specs=[SM] + [VM] * (len(ins) - 1), out_specs=(VM,) * len(outs),
        scratch_shapes=[pltpu.VMEM((HEAD_DIM, 2 * span), bf), pltpu.VMEM((2 * span, 2 * heads * span), bf), pltpu.VMEM((2 * span, 2 * heads * span), bf)],
        cost_estimate=pl.CostEstimate(flops=2*5*2*n*heads*span*span*HEAD_DIM*2, bytes_accessed=4_000_000, transcendentals=0),
        compiler_params=pltpu.CompilerParams(vmem_limit_bytes=30 << 20), name="attn_bwd_pieces")(*ins)


TILE = 512


def steps_of(columns, begin=0):
    edges = [begin, begin + TILE // 2, begin + TILE]
    while columns - edges[-1] > 2 * TILE:
        edges.append(edges[-1] + 2 * TILE)
    if columns - edges[-1] > TILE:
        edges.append(edges[-1] + TILE)
    edges.append(columns)
    return list(zip(edges, edges[1:]))


def act_back_kernel(bounds, own_ref, other_ref, wd_hbm, *refs):
    out_hbm, rows_ref, wd, out, in_sems, out_sems = refs[-6:]
    half, first = own_ref.shape[0], bounds[0][0]
    parts = [slice(low - first, high - first) for low, high in bounds]
    copies = [
        pltpu.make_async_copy(wd_hbm.at[low:high], wd.at[part], in_sems.at[i])
        for i, ((low, high), part) in enumerate(zip(bounds, parts))
    ]
    for copy in copies:
        copy.start()
    rows_ref[:half, :] = own_ref[...]
    rows_ref[half:, :] = other_ref[...]
    results = []
    for i, ((low, high), part) in enumerate(zip(bounds, parts)):
        copies[i].wait()
        out[:, part] = nt(rows_ref[...], wd[part, :]).astype(bf)
        result = pltpu.make_async_copy(out.at[:, part], out_hbm.at[:, low:high], out_sems.at[i])
        result.start()
        results.append(result)
    for result in results:
        result.wait()


def act_back(own, other, wd, bounds, held=None):
    half, width = own.shape
    columns, count = bounds[-1][1] - bounds[0][0], len(bounds)
    return pl.pallas_call(
        functools.partial(act_back_kernel, bounds),
        out_shape=pltpu.HBM((2 * half, wd.shape[0]), bf),
        in_specs=[VM, VM, HB] + ([] if held is None else [HB]),
        out_specs=HB,
        scratch_shapes=[
            pltpu.VMEM((2 * half, width), bf), pltpu.VMEM((columns, width), bf), pltpu.VMEM((2 * half, columns), bf),
            pltpu.SemaphoreType.DMA((count,)), pltpu.SemaphoreType.DMA((count,)),
        ],
        input_output_aliases={} if held is None else {3: 0},
        cost_estimate=pl.CostEstimate(flops=4 * half * width * columns, bytes_accessed=2 * width * columns, transcendentals=0),
        compiler_params=pltpu.CompilerParams(vmem_limit_bytes=30 << 20),
        name="act_back",
    )(own, other, in_hbm(wd), *([] if held is None else [in_hbm(held)]))


def whole(*dims):
    return pl.BlockSpec(dims, lambda i: (0,) * len(dims), pipeline_mode=pl.Buffered(1))


def ffn_kernel(
    tile, tiles, hidden, x_own, x_other, g_own, g_other, gact_ref, adgu_ref, auf_ref, wgu_ref, adf_ref, augu_ref,
    gx_own, gx_send, act_ref, flow_ref, dadgu_ref, dauf_ref, daugu_ref, dadf_ref,
    x_ref, g_ref, gx_acc, xlow, xlow_t, fback, fback_t, flow, back,
):
    step = pl.program_id(0)
    half = x_own.shape[0]

    @pl.when(step == 0)
    def prepare():
        for target, own, other in ((x_ref, x_own, x_other), (g_ref, g_own, g_other)):
            target[:half, :] = own[...]
            target[half:, :] = other[...]
        low = nt(x_ref[...], adgu_ref[...])
        xlow[...] = (low * 2.0).astype(bf)
        xlow_t[...] = low.T.astype(bf)
        fb = nt(g_ref[...], auf_ref[...])
        fback[...] = (fb * 2.0).astype(bf)
        fback_t[...] = fb.T.astype(bf)
        gx_acc[...] = jnp.zeros_like(gx_acc)
        flow[...] = jnp.zeros_like(flow)
        back[...] = jnp.zeros_like(back)

    def work(width):
        x = x_ref[...]
        wg, wu = wgu_ref[0, :, :width], wgu_ref[1, :, :width]
        aug, auu, adf = augu_ref[:RANK, :width], augu_ref[RANK:, :width], adf_ref[:, :width]
        gate = nn(x, wg) + nn(xlow[:, :RANK], aug)
        up = nn(x, wu) + nn(xlow[:, RANK:], auu)
        gact = gact_ref[:, :width].astype(f32) + nn(fback[...], adf)
        sig = 1.0 / (1.0 + jnp.exp(-gate))
        silu = gate * sig
        act = (silu * up).astype(bf)
        ggate = (gact * up * (sig + silu * (1.0 - sig))).astype(bf)
        gup = (gact * silu).astype(bf)
        act_ref[:, :width] = act
        flow[...] += nt(act, adf)
        gx_acc[...] += nt(ggate, wg) + nt(gup, wu)
        back[:, :RANK] += nt(ggate, aug)
        back[:, RANK:] += nt(gup, auu)
        daugu_ref[:RANK, :width] = nn(xlow_t[:RANK, :], ggate)
        daugu_ref[RANK:, :width] = nn(xlow_t[RANK:, :], gup)
        dadf_ref[:, :width] = nn(fback_t[...], act)

    tail = hidden - (tiles - 1) * tile
    if tail == tile:
        work(tile)
    else:
        @pl.when(step < tiles - 1)
        def body():
            work(tile)

        @pl.when(step == tiles - 1)
        def part():
            work(tail)

    @pl.when(step == tiles - 1)
    def finish():
        gx_acc[...] += nn((back[...] * 2.0).astype(bf), adgu_ref[...])
        gx_own[...] = gx_acc[:half, :]
        gx_send[...] = gx_acc[half:, :].astype(bf)
        flow_ref[...] = (flow[...] * 2.0).astype(bf)
        dadgu_ref[...] = nn(back[...].T.astype(bf), x_ref[...])
        dauf_ref[...] = nn(flow[...].T.astype(bf), g_ref[...])


def ffn(x_own, x_other, g_own, g_other, gact, adgu, auf, wgu, adf, augu, tile=TILE):
    rows, width = 2 * x_own.shape[0], x_own.shape[1]
    hidden = wgu.shape[2]
    tiles = -(-hidden // tile)
    half = rows // 2
    cols = lambda r: pl.BlockSpec((r, tile), lambda i: (0, i))
    outs = (
        shape(half, width), shape(half, width, dtype=bf), pltpu.HBM((rows, hidden), bf), shape(rows, RANK, dtype=bf),
        shape(2 * RANK, width), shape(RANK, width), shape(2 * RANK, hidden), shape(RANK, hidden),
    )
    return pl.pallas_call(
        functools.partial(ffn_kernel, tile, tiles, hidden),
        grid=(tiles,),
        out_shape=outs,
        in_specs=[whole(half, width)] * 4 + [cols(rows), whole(2 * RANK, width), whole(RANK, width),
                  pl.BlockSpec((2, width, tile), lambda i: (0, 0, i)), cols(RANK), cols(2 * RANK)],
        out_specs=(whole(half, width), whole(half, width), cols(rows), whole(rows, RANK), whole(2 * RANK, width),
                   whole(RANK, width), cols(2 * RANK), cols(RANK)),
        scratch_shapes=[
            pltpu.VMEM((rows, width), bf), pltpu.VMEM((rows, width), bf), pltpu.VMEM((rows, width), f32),
            pltpu.VMEM((rows, 2 * RANK), bf), pltpu.VMEM((2 * RANK, rows), bf), pltpu.VMEM((rows, RANK), bf),
            pltpu.VMEM((RANK, rows), bf), pltpu.VMEM((rows, RANK), f32), pltpu.VMEM((rows, 2 * RANK), f32),
        ],
        cost_estimate=pl.CostEstimate(flops=8 * rows * width * hidden, bytes_accessed=6 * width * hidden, transcendentals=rows * hidden),
        compiler_params=pltpu.CompilerParams(vmem_limit_bytes=36 << 20),
        name="ffn",
    )(x_own, x_other, in_hbm(g_own), in_hbm(g_other), in_hbm(gact), adgu, auf, in_hbm(wgu), adf, augu)


def down_kernel(bounds, start_refs, act_hbm, wd_hbm, total, act, wd, act_sems, wd_sems):
    low = bounds[0][0]
    copies = []
    for i, (begin, end) in enumerate(bounds):
        rows = slice(begin - low, end - low)
        copies.append((
            pltpu.make_async_copy(act_hbm.at[:, begin:end], act.at[:, rows], act_sems.at[i]),
            pltpu.make_async_copy(wd_hbm.at[begin:end], wd.at[rows], wd_sems.at[i]),
        ))
        for copy in copies[-1]:
            copy.start()
    total[...] = nn(start_refs[0][...], start_refs[1][...]) if len(start_refs) == 2 else start_refs[0][...]
    for i, (begin, end) in enumerate(bounds):
        rows = slice(begin - low, end - low)
        for copy in copies[i]:
            copy.wait()
        total[...] += nn(act[:, rows], wd[rows, :])


def down_first_kernel(bounds, flow_ref, auf_ref, act_hbm, wd_hbm, total, *scratch):
    down_kernel(bounds, (flow_ref, auf_ref), act_hbm, wd_hbm, total, *scratch)


def down_last_kernel(bounds, start_ref, act_hbm, wd_hbm, own_ref, send_ref, total, *scratch):
    down_kernel(bounds, (start_ref,), act_hbm, wd_hbm, total, *scratch)
    half = own_ref.shape[0]
    own_ref[...] = total[:half, :]
    send_ref[...] = total[half:, :].astype(bf)


def down(act, wd, start, bounds, last):
    rows, width = act.shape[0], wd.shape[1]
    half, columns, count = rows // 2, bounds[-1][1] - bounds[0][0], len(bounds)
    outs = (shape(half, width), shape(half, width, dtype=bf)) if last else (shape(rows, width),)
    scratch = [
        pltpu.VMEM((rows, columns), bf), pltpu.VMEM((columns, width), bf), pltpu.SemaphoreType.DMA((count,)),
        pltpu.SemaphoreType.DMA((count,)),
    ]
    return pl.pallas_call(
        functools.partial(down_last_kernel if last else down_first_kernel, bounds),
        out_shape=outs,
        in_specs=[VM] * len(start) + [HB, HB],
        out_specs=(VM,) * len(outs),
        scratch_shapes=([pltpu.VMEM((rows, width), f32)] if last else []) + scratch,
        cost_estimate=pl.CostEstimate(flops=2 * rows * width * columns, bytes_accessed=2 * width * columns, transcendentals=0),
        compiler_params=pltpu.CompilerParams(vmem_limit_bytes=28 << 20),
        name="down",
    )(*start, in_hbm(act), in_hbm(wd))


def per_device(
    tokens, cotangent, positions, adapter_choice, attn_gain, query_weight, query_bias, key_value_weight,
    key_value_bias, output_weight, ffn_gain, gate_upper_weight, down_weight, adapt_in, adapt_out,
):
    dp = lax.axis_index("dp")
    groups = lax.axis_size("seq")
    rings = groups // 2
    width, head_width = query_weight.shape
    heads = head_width // HEAD_DIM
    hidden = down_weight.shape[0]
    token_pos = positions[0]
    tok_count = token_pos.shape[0]
    span = tok_count // 2
    scale = HEAD_DIM ** (-0.5)
    coef = scale * math.log2(math.e)
    wide_in, wide_out = adapt_in.shape[2], adapt_out.shape[2]
    lanes_in = rounded_up(wide_in + 1, 128)
    lanes = lanes_in + rounded_up(wide_out, 128)
    widths = (width, head_width, hidden)
    sizes = (rings, wide_in, wide_out, lanes_in, widths)

    def to_pair(value):
        return lax.ppermute(value, "tensor", [(0, 1), (1, 0)])

    def to_other_sequence(value, pairs=((0, 1), (1, 0))):
        return lax.ppermute(value, "dp", list(pairs))

    def to_side(value):
        return lax.ppermute(value, "seq", [(i, i ^ 1) for i in range(groups)])

    def along_ring(value, steps):
        return lax.ppermute(value, "seq", [(i, (i + 2 * steps) % groups) for i in range(groups)])

    cycle = list(range(0, groups, 2)) + list(range(groups - 1, 0, -2))
    hops = [(cycle[i], cycle[(i + 1) % groups]) for i in range(groups)]

    def to_next(value):
        return lax.ppermute(value, "seq", hops)

    def to_last(value):
        return lax.ppermute(value, "seq", [(end, begin) for begin, end in hops])

    def after(value, *others):
        return lax.optimization_barrier((value, *others))[0]

    inputs, grad_out = tokens[0], cotangent[0]
    half = inputs.shape[0]
    attn_gain, ffn_gain = attn_gain[None], ffn_gain[None]

    def over_ring(piece):
        return [piece] + [along_ring(piece, step) for step in range(1, rings)]

    slice_own, slice_other = call(
        functools.partial(select_kernel, lanes_in, span), "select",
        [shape(RANK, lanes, dtype=bf)] * 2, [adapter_choice, positions, adapt_in, adapt_out],
        [
            pltpu.SMEM(adapter_choice.shape, jnp.int32), pltpu.SMEM(positions.shape, jnp.int32),
            pltpu.VMEM((2, RANK, wide_in), bf), pltpu.VMEM((2, RANK, wide_out), bf), pltpu.SemaphoreType.DMA((6,)),
        ],
        left=4,
    )
    slice_other = to_other_sequence(slice_other)
    lane = lax.broadcasted_iota(jnp.int32, (RANK, lanes), 1)
    run_lane = (lane >= wide_in) & (lane < lanes_in)
    grad_other = to_pair(after(grad_out, slice_own))
    slice_other = after(slice_other, grad_other)
    first_slice = jnp.where((dp == 0) | run_lane, slice_own, slice_other)
    second_slice = jnp.where(dp == 0, slice_other, slice_own)

    (normed,) = call(norm_kernel, "norm", [shape(half, width, dtype=bf)], [inputs, attn_gain])
    normed_other = to_pair(normed)
    arrived = over_ring(jnp.stack([first_slice, second_slice]))
    middle = 6 * TILE
    act_grad = act_back(grad_out, grad_other, down_weight, steps_of(middle))
    arrived[1] = after(arrived[1], act_grad)
    own_slices = jnp.stack([piece[0] for piece in arrived])
    own_second = jnp.stack([piece[1] for piece in arrived])
    side_slices = to_side(own_slices)
    pair_slices = to_pair(own_slices)
    normed_rows, query_dense, kv_dense = call(
        dense_kernel, "dense", [shape(tok_count, width, dtype=bf), shape(tok_count, head_width), shape(tok_count, 2 * HEAD_DIM)],
        [normed, after(normed_other, own_slices), query_weight, key_value_weight],
        flops=2 * tok_count * width * (head_width + 2 * HEAD_DIM),
    )
    frequency = jnp.power(rope_base, -(jnp.arange(HEAD_DIM // 2, dtype=f32) * 2.0) / HEAD_DIM)
    angles = token_pos.astype(f32)[:, None] * frequency[None, :]
    cosine, sine = jnp.cos(angles), jnp.sin(angles)
    cosine = jnp.concatenate([cosine, cosine], axis=1)
    sine = jnp.concatenate([-sine, sine], axis=1)

    side_slices = after(side_slices, kv_dense)
    first_slices = [own_slices, side_slices, pair_slices, to_pair(side_slices)]
    slices_in = -(-4 * width // wide_in)
    slices_out = -(-(2 * width + 4 * HEAD_DIM) // wide_out)
    flags, adqkv, auq, auk, auv, ado, auo = call(
        functools.partial(unpack_first_kernel, *sizes), "unpack_first",
        [shape(groups, dtype=jnp.int32)]
        + [
            shape(*dims, dtype=bf)
            for dims in (
                (3 * RANK, width), (RANK, head_width), (RANK, HEAD_DIM), (RANK, HEAD_DIM), (RANK, head_width), (RANK, width),
            )
        ],
        list(first_slices),
        [
            pltpu.VMEM((2 * groups, RANK, lanes), bf),
            pltpu.VMEM((RANK, rounded_up(slices_in * wide_in, 128) + 256), f32),
            pltpu.VMEM((RANK, rounded_up(slices_out * wide_out, 128) + 256), f32),
            pltpu.SMEM((groups,), jnp.int32),
        ],
        out_specs=(SM,) + (VM,) * 6,
    )
    kv, low, low_t = call(
        key_value_kernel, "key_value",
        [shape(tok_count, 2 * HEAD_DIM, dtype=bf), shape(tok_count, 3 * RANK, dtype=bf), shape(3 * RANK, tok_count, dtype=bf)],
        [normed_rows, kv_dense, key_value_bias, adqkv, auk, auv, cosine, sine],
        flops=2 * tok_count * width * 2 * RANK,
    )

    (queries,) = call(
        query_kernel, "query", [shape(2, heads, span, HEAD_DIM, dtype=bf)],
        [query_dense, query_bias[None], low, auq, cosine, sine], flops=2 * tok_count * width * RANK,
    )
    state = attn_fwd_own(queries, kv, coef)
    pieces, from_last, from_next = [kv], kv, kv
    for step in range(1, rings + 1):
        from_last, from_next = to_next(from_last), to_last(from_next)
        if step == 1:
            bounds = [(middle, middle + TILE // 2), (middle + TILE // 2, middle + 2 * TILE), (middle + 2 * TILE, hidden)]
            act_grad = act_back(after(grad_out, state[0]), grad_other, down_weight, bounds, act_grad)
            from_last = after(from_last, act_grad)
        if step < rings:
            from_last, from_next, _ = lax.optimization_barrier((from_last, from_next, state[0]))
        if step == rings:
            own_second = after(own_second, pieces[-1])
            side_second, pair_second = to_side(own_second), to_pair(own_second)
            state = (after(state[0], side_second, pair_second), *state[1:])
        pieces += [from_last, from_next][: 2 if step < rings else 1]
        indices = tuple(range(2 * step - 1, len(pieces)))
        result = attn_fwd_pieces(flags, indices, queries, pieces[2 * step - 1 :], state, coef, step == rings)
        state = result[-3:]
    mixed, lse = result[0], result[1]

    branch_send, mix_low, mix_low_t = call(
        mix_send_kernel, "mix_send",
        [shape(half, width, dtype=bf), shape(tok_count, RANK, dtype=bf), shape(RANK, tok_count, dtype=bf)],
        [mixed, output_weight, ado, auo], flops=2 * half * width * head_width,
    )
    branch_other = to_pair(branch_send)
    second_slices = [own_second, side_second, pair_second, to_pair(side_second)]
    (branch_own,) = call(
        mix_own_kernel, "mix_own", [shape(half, width)], [mixed, output_weight, mix_low, auo],
        flops=2 * half * width * head_width,
    )
    hidden_rows, normed_ffn = call(
        residual_kernel, "residual", [shape(half, width), shape(half, width, dtype=bf)],
        [inputs, branch_own, after(branch_other, branch_own, second_slices[3]), ffn_gain],
    )
    begin_in, begin_out, first_in, first_out = bases(wide_in, wide_out, widths)
    adgu, augu, adf, auf = call(
        functools.partial(unpack_second_kernel, *sizes), "unpack_second",
        [shape(*dims, dtype=bf) for dims in ((2 * RANK, width), (2 * RANK, hidden), (RANK, hidden), (RANK, width))],
        list(first_slices) + list(second_slices),
        [
            pltpu.VMEM((4 * groups, RANK, lanes), bf),
            pltpu.VMEM((RANK, rounded_up(4 * groups * wide_in, 128) + 256 - first_in), f32),
            pltpu.VMEM((RANK, rounded_up(4 * groups * wide_out, 128) + 256 - first_out), f32),
        ],
    )
    gx_own, gx_send, act, flow, dadgu, dauf, daugu, dadf = ffn(
        normed_ffn, to_pair(normed_ffn), grad_out, grad_other, act_grad, adgu, auf, gate_upper_weight, adf, augu
    )
    ad_lanes = rounded_up(4 * groups * wide_in, 128) + 256
    au_lanes = rounded_up(4 * groups * wide_out, 128) + 256

    def added(*values):
        total = values[0].astype(f32)
        for value in values[1:]:
            total = total + value.astype(f32)
        return total.astype(bf)

    grad_hidden, grad_low = call(
        hidden_back_kernel, "hidden_back", [shape(half, width), shape(half, width, dtype=bf)],
        [hidden_rows, grad_out, gx_own, to_pair(gx_send), ffn_gain],
    )
    grad_low_other = to_pair(grad_low)
    fixed = [output_weight, ado, auo, mixed, mix_low_t]
    outs = [shape(2, heads, span, HEAD_DIM, dtype=bf), shape(2, heads, span), shape(RANK, head_width), shape(RANK, width)]
    partial = call(
        functools.partial(mix_back_kernel, True), "mix_back", outs, [grad_low, *fixed], flops=2 * half * width * head_width,
    )
    grad_mixed, delta, dado, dauo = call(
        functools.partial(mix_back_kernel, False), "mix_back_other", outs,
        [after(grad_low_other, partial[0]), *fixed, *partial], flops=2 * half * width * head_width,
        aliases={6 + i: i for i in range(4)},
    )

    def backward(indices, state_dq):
        return attn_bwd(
            flags, indices, queries, grad_mixed, lse, delta, [pieces[index] for index in indices], state_dq, coef, scale,
            indices == (0,),
        )

    state_dq, from_last, from_next = None, None, None
    for step in range(rings, 0, -1):
        onward, *returned, state_dq = backward((2 * rings - 1,) if step == rings else (2 * step, 2 * step - 1), state_dq)
        if from_last is not None:
            onward = added(onward, from_last)
        if from_next is not None:
            returned = [added(returned[0], from_next)]
        from_last = to_next(onward)
        if returned:
            from_next = to_last(returned[0])
        state_dq = after(state_dq, onward, *returned)
    own_term, state_dq = backward((0,), state_dq)
    gn_query, dadq, dauq = call(
        functools.partial(back_query_kernel, scale), "back_query",
        [shape(tok_count, width), shape(RANK, width), shape(RANK, head_width)],
        [state_dq, query_weight, adqkv, auq, low_t, normed_rows, cosine, sine],
        [pltpu.VMEM((tok_count, head_width), bf)], flops=2 * tok_count * width * head_width,
    )
    from_last = after(from_last, gn_query)
    gn_own, gn_send, dadkv, dauk, dauv = call(
        back_key_value_kernel, "back_key_value",
        [
            shape(half, width), shape(half, width, dtype=bf), shape(2 * RANK, width), shape(RANK, HEAD_DIM),
            shape(RANK, HEAD_DIM),
        ],
        [
            own_term, gn_query, key_value_weight, adqkv, auk, auv, low_t, normed_rows, cosine, sine, from_last, from_next,
        ],
        [pltpu.VMEM((tok_count, width), f32), pltpu.VMEM((tok_count, 2 * RANK), f32)],
        flops=2 * tok_count * width * 2 * HEAD_DIM, limit=20,
    )
    (packed,) = call(
        functools.partial(pack_kernel, *sizes), "pack", [shape(2, 2, rings, 2, RANK, lanes, dtype=bf)],
        [dadq, dadkv, dado, dadgu, dadf, dauq, dauk, dauv, dauo, daugu, dauf],
        [pltpu.VMEM((RANK, ad_lanes), f32), pltpu.VMEM((RANK, au_lanes), f32)],
    )
    from_pair = to_pair(packed[1])
    near, far = added(packed[0, 0], from_pair[0]), added(packed[0, 1, 1:], from_pair[1, 1:])
    from_side = to_side(far)
    own_side = to_side(after(added(packed[0, 1, 0], from_pair[1, 0]), far))
    middle = 6 * TILE
    (out_total,) = down(after(act, far), down_weight, (flow, auf), steps_of(middle), False)
    from_side = after(from_side, out_total)
    sums = [added(near[place], from_side[place - 1]) for place in range(1, rings)]
    from_ring = [along_ring(sums[place - 1], -place) for place in range(1, rings)]
    out_own, out_send = down(after(act, *sums), down_weight, (out_total,), steps_of(hidden, middle), True)
    (grad_tokens,) = call(
        token_back_kernel, "token_back", [shape(half, width)],
        [inputs, grad_hidden, gn_own, after(to_pair(gn_send), out_own), attn_gain],
    )
    output = (hidden_rows + (out_own + to_pair(out_send).astype(f32))).astype(bf)
    from_ring[0] = after(from_ring[0], out_own)
    total = added(near[0], own_side, *from_ring)
    other_total = after(to_other_sequence(total[1]), output, grad_tokens)
    factor = adapter_scale * (adapter_choice.shape[0] * tok_count * groups) ** (-0.5)
    adapt_in_grad, adapt_out_grad = call(
        functools.partial(place_kernel, lanes_in, factor), "place",
        [shape(*adapt_in.shape), shape(*adapt_out.shape)],
        [adapter_choice, total[0], other_total], smem=1,
    )
    return (output[None], grad_tokens[None], adapt_in_grad, adapt_out_grad)


def solution(mesh):
    return jax.shard_map(
        per_device,
        mesh=mesh,
        in_specs=(
            P("dp", ("seq", "tensor"), None),
            P("dp", ("seq", "tensor"), None),
            P("dp", "seq"),
            P(),
            P(),
            P(None, "tensor"),
            P("tensor"),
            P(None, None, "tensor"),
            P(None, "tensor"),
            P("tensor", None),
            P(),
            P(None, None, "tensor"),
            P("tensor", None),
            P(None, None, ("dp", "seq", "tensor")),
            P(None, None, ("dp", "seq", "tensor")),
        ),
        out_specs=(
            P("dp", ("seq", "tensor"), None),
            P("dp", ("seq", "tensor"), None),
            P(None, None, ("dp", "seq", "tensor")),
            P(None, None, ("dp", "seq", "tensor")),
        ),
        check_vma=False,
    )
```

```python
import functools
import math

import jax
import jax.numpy as jnp
from jax import lax
from jax.experimental import pallas as pl
from jax.experimental.pallas import tpu as pltpu
from jax.sharding import PartitionSpec as P

HEAD_DIM = 128
RANK = 16
eps = 1e-06
adapter_scale = 2.0
rope_base = 1000000.0
mask_fill = -1e30
bf = jnp.bfloat16
f32 = jnp.float32
VM = pl.BlockSpec(memory_space=pltpu.VMEM)
SM = pl.BlockSpec(memory_space=pltpu.SMEM)


def nn(a, b):
    return jnp.dot(a, b, preferred_element_type=f32)


def nt(a, b):
    return lax.dot_general(a, b, (((1,), (1,)), ((), ())), preferred_element_type=f32)


def shape(*dims, dtype=f32):
    return jax.ShapeDtypeStruct(dims, dtype)


def call(kernel, name, out, ins, scratch=(), flops=0, smem=0, out_specs=None, limit=16, left=0, aliases=None):
    moved = sum(math.prod(v.shape) * v.dtype.itemsize for v in list(ins) + list(out))
    ins = list(ins[: len(ins) - left]) + [in_hbm(value) for value in ins[len(ins) - left :]]
    return pl.pallas_call(
        kernel,
        out_shape=tuple(out),
        in_specs=[SM] * smem + [VM] * (len(ins) - smem - left) + [HB] * left,
        out_specs=out_specs or (VM,) * len(out),
        scratch_shapes=list(scratch),
        input_output_aliases=aliases or {},
        cost_estimate=pl.CostEstimate(flops=flops, bytes_accessed=moved, transcendentals=0),
        compiler_params=pltpu.CompilerParams(vmem_limit_bytes=limit << 20),
        name=name,
    )(*ins)


HB = pl.BlockSpec(memory_space=pltpu.HBM)


def in_hbm(value):
    return pltpu.with_memory_space_constraint(value, pltpu.HBM)


def rounded_up(value, unit):
    return -(-value // unit) * unit


def select_kernel(
    lanes_in, span, choice_hbm, pos_hbm, in_ref, out_ref, own_ref, other_ref, choice_ref, pos_ref, held_in, held_out, sems
):
    wide_in, wide_out = in_ref.shape[2], out_ref.shape[2]
    dp = lax.axis_index("dp")
    choice_copy = pltpu.make_async_copy(choice_hbm, choice_ref, sems.at[4])
    pos_copy = pltpu.make_async_copy(pos_hbm, pos_ref, sems.at[5])
    choice_copy.start()
    pos_copy.start()
    choice_copy.wait()
    copies = []
    for slot, sequence in ((0, dp), (1, 1 - dp)):
        chosen = choice_ref[sequence]
        copies.append(pltpu.make_async_copy(in_ref.at[chosen], held_in.at[slot], sems.at[2 * slot]))
        copies.append(pltpu.make_async_copy(out_ref.at[chosen], held_out.at[slot], sems.at[2 * slot + 1]))
    for copy in copies:
        copy.start()
    pos_copy.wait()
    run = jnp.full((RANK, lanes_in), pos_ref[0, 0] // span, jnp.int32).astype(f32).astype(bf)
    for target in (own_ref, other_ref):
        target[...] = jnp.zeros_like(target)
        target[:, :lanes_in] = run
    for copy in copies:
        copy.wait()
    for slot, target in ((0, own_ref), (1, other_ref)):
        target[:, :wide_in] = held_in[slot]
        target[:, lanes_in : lanes_in + wide_out] = held_out[slot]


def column(begin, size):
    return pl.ds(pl.multiple_of(begin, 128), size)


def source_of(place, side, rings, seq):
    ring = lax.rem(seq // 2 - place + rings, rings)
    own_side = lax.rem(seq, 2)
    return ring * 2 + (own_side if side == 0 else 1 - own_side)


def spread(slots, target, begin, wide, first, low, high):
    held = rounded_up(wide, 128)
    inside = lax.broadcasted_iota(jnp.int32, (RANK, held), 1) < wide
    target[...] = jnp.zeros_like(target)
    for index in range(low // wide, -(-high // wide)):
        part = jnp.where(inside, slots[index, :, begin : begin + held].astype(f32), 0.0)
        part = jnp.concatenate([part, jnp.zeros((RANK, 128), f32)], axis=1)
        offset = index * wide - first
        base = offset // 128 * 128
        if offset != base:
            part = pltpu.roll(part, offset - base, 1)
        target[:, base : base + held + 128] += part


def collect(slots, refs, rings, part):
    seq, shard = lax.axis_index("seq"), lax.axis_index("tensor")
    for number, ref in enumerate(refs):
        side, core = number % 2, shard if number < 2 else 1 - shard
        for place in range(rings):
            slots[part * 4 * rings + source_of(place, side, rings, seq) * 2 + core] = ref[place]


def unpack_first_kernel(
    rings, wide_in, wide_out, lanes_in, widths, own, own_side, pair, pair_side,
    flags_ref, adqkv, auq, auk, auv, ado, auo, slots, ad, au, runs,
):
    shard, seq = lax.axis_index("tensor"), lax.axis_index("seq")
    width, head_width, hidden = widths
    for place in range(rings):
        for side, ref in ((0, own), (1, own_side)):
            run = jnp.max(ref[place, :, wide_in:lanes_in].astype(f32))
            runs[source_of(place, side, rings, seq)] = run.astype(jnp.int32)
    groups = 2 * rings
    place = jnp.where(lax.rem(seq, 2) == 0, seq // 2, groups - 1 - seq // 2)
    for index in range(groups):
        step = (index + 1) // 2
        other = lax.rem(place + (groups - step if index % 2 == 1 else step), groups)
        source = jnp.where(other < rings, 2 * other, 2 * (groups - 1 - other) + 1)
        flags_ref[index] = (runs[source] < runs[seq]).astype(jnp.int32)
    collect(slots, (own, own_side, pair, pair_side), rings, 0)
    spread(slots, ad, 0, wide_in, 0, 0, 4 * width)
    spread(slots, au, lanes_in, wide_out, 0, 0, 2 * width + 4 * HEAD_DIM)
    for index in range(3):
        adqkv[index * RANK : (index + 1) * RANK, :] = ad[:, index * width : (index + 1) * width].astype(bf)
    ado[...] = ad[:, column(3 * width + shard * head_width, head_width)].astype(bf)
    auq[...] = au[:, column(shard * head_width, head_width)].astype(bf)
    auk[...] = au[:, column(width + shard * HEAD_DIM, HEAD_DIM)].astype(bf)
    auv[...] = au[:, column(width + (2 + shard) * HEAD_DIM, HEAD_DIM)].astype(bf)
    base = width + 4 * HEAD_DIM
    auo[...] = au[:, base : base + width].astype(bf)


def bases(wide_in, wide_out, widths):
    width = widths[0]
    begin_in, begin_out = 4 * width, 2 * width + 4 * HEAD_DIM
    return begin_in, begin_out, begin_in // wide_in * wide_in // 128 * 128, begin_out // wide_out * wide_out // 128 * 128


def unpack_second_kernel(
    rings, wide_in, wide_out, lanes_in, widths, *refs
):
    firsts, seconds = refs[:4], refs[4:8]
    adgu, augu, adf, auf, slots, ad, au = refs[8:]
    shard = lax.axis_index("tensor")
    width, head_width, hidden = widths
    collect(slots, firsts, rings, 0)
    collect(slots, seconds, rings, 1)
    begin_in, begin_out, first_in, first_out = bases(wide_in, wide_out, widths)
    total_in, total_out = 8 * rings * wide_in, 8 * rings * wide_out
    spread(slots, ad, 0, wide_in, first_in, begin_in, total_in)
    spread(slots, au, lanes_in, wide_out, first_out, begin_out, total_out)
    base = begin_in - first_in
    for index in range(2):
        adgu[index * RANK : (index + 1) * RANK, :] = ad[:, base + index * width : base + (index + 1) * width].astype(bf)
    adf[...] = ad[:, column(base + 2 * width + shard * hidden, hidden)].astype(bf)
    base = begin_out - first_out
    for index in range(2):
        augu[index * RANK : (index + 1) * RANK, :] = au[
            :, column(base + (2 * index + shard) * hidden, hidden)
        ].astype(bf)
    auf[...] = au[:, base + 4 * hidden : base + 4 * hidden + width].astype(bf)


def put_slices(rings, wide_in, wide_out, lanes_in, ad, au, limits, parts, write):
    dp, seq = lax.axis_index("dp"), lax.axis_index("seq")
    for index in range(4 * rings * parts):
        to_dp, to_seq, to_core = index // (4 * rings), index // 2 % (2 * rings), index % 2
        pieces = []
        for source, wide, (low, high, first) in ((ad, wide_in, limits[0]), (au, wide_out, limits[1])):
            held = rounded_up(wide, 128)
            if index * wide >= high or (index + 1) * wide <= low:
                part = jnp.zeros((RANK, held), f32)
            else:
                offset = index * wide - first
                base = offset // 128 * 128
                part = source[:, base : base + held + 128]
                if offset != base:
                    part = pltpu.roll(part, held + 128 - (offset - base), 1)
                part = part[:, :held]
            pieces.append(part)
            if source is ad and lanes_in > held:
                pieces.append(jnp.zeros((RANK, lanes_in - held), f32))
        packed = jnp.concatenate(pieces, axis=1).astype(bf)
        place = lax.rem(seq // 2 - to_seq // 2 + rings, rings)
        write(to_seq, to_core, place, lax.rem(dp + to_dp, 2), packed)


def pack_kernel(
    rings, wide_in, wide_out, lanes_in, widths,
    dadq, dadkv, dado, dadgu, dadf, dauq, dauk, dauv, dauo, daugu, dauf, out_ref, ad, au,
):
    shard, side = lax.axis_index("tensor"), lax.rem(lax.axis_index("seq"), 2)
    width, head_width, hidden = widths
    ad[...] = jnp.zeros_like(ad)
    au[...] = jnp.zeros_like(au)
    ad[:, :width] = dadq[...]
    for index in range(2):
        ad[:, (1 + index) * width : (2 + index) * width] = dadkv[index * RANK : (index + 1) * RANK, :]
        ad[:, (4 + index) * width : (5 + index) * width] = dadgu[index * RANK : (index + 1) * RANK, :]
    ad[:, column(3 * width + shard * head_width, head_width)] = dado[...]
    ad[:, column(6 * width + shard * hidden, hidden)] = dadf[...]
    au[:, column(shard * head_width, head_width)] = dauq[...]
    au[:, column(width + shard * HEAD_DIM, HEAD_DIM)] = dauk[...]
    au[:, column(width + (2 + shard) * HEAD_DIM, HEAD_DIM)] = dauv[...]
    base = width + 4 * HEAD_DIM
    au[:, base : base + width] = dauo[...]
    base = base + width
    for index in range(2):
        au[:, column(base + (2 * index + shard) * hidden, hidden)] = daugu[index * RANK : (index + 1) * RANK, :]
    au[:, base + 4 * hidden : base + 4 * hidden + width] = dauf[...]

    def write(to_seq, to_core, place, part, packed):
        out_ref[lax.rem(shard + to_core, 2), lax.rem(side + to_seq % 2, 2), place, part] = packed

    limits = ((0, 8 * rings * wide_in, 0), (0, 8 * rings * wide_out, 0))
    put_slices(rings, wide_in, wide_out, lanes_in, ad, au, limits, 2, write)


def place_kernel(lanes_in, factor, choice_ref, own_ref, other_ref, in_ref, out_ref):
    wide_in, wide_out = in_ref.shape[2], out_ref.shape[2]
    dp = lax.axis_index("dp")
    in_ref[...] = jnp.zeros_like(in_ref)
    out_ref[...] = jnp.zeros_like(out_ref)
    for ref, sequence in ((own_ref, dp), (other_ref, 1 - dp)):
        chosen = choice_ref[sequence]
        part = ref[...].astype(f32) * factor
        in_ref[chosen] = in_ref[chosen] + part[:, :wide_in]
        out_ref[chosen] = out_ref[chosen] + part[:, lanes_in : lanes_in + wide_out]


def factor_of(rows):
    return lax.rsqrt(jnp.mean(rows * rows, axis=-1, keepdims=True) + eps)


def norm_back(rows, gain, grad):
    factor = factor_of(rows)
    scaled = rows * factor
    grad_scaled = grad * gain
    return factor * (grad_scaled - scaled * jnp.mean(grad_scaled * scaled, axis=-1, keepdims=True))


def norm_kernel(rows_ref, gain_ref, normed_ref):
    rows = rows_ref[...].astype(f32)
    normed_ref[...] = (rows * factor_of(rows) * gain_ref[...].astype(f32)).astype(bf)


def residual_kernel(rows_ref, own_ref, other_ref, gain_ref, hidden_ref, normed_ref):
    rows = rows_ref[...].astype(f32) + (own_ref[...] + other_ref[...].astype(f32))
    hidden_ref[...] = rows
    normed_ref[...] = (rows * factor_of(rows) * gain_ref[...].astype(f32)).astype(bf)


def hidden_back_kernel(hidden_ref, grad_ref, own_ref, other_ref, gain_ref, out_ref, low_ref):
    grad = own_ref[...] + other_ref[...].astype(f32)
    total = grad_ref[...].astype(f32) + norm_back(hidden_ref[...], gain_ref[...].astype(f32), grad)
    out_ref[...] = total
    low_ref[...] = total.astype(bf)


def token_back_kernel(rows_ref, grad_ref, own_ref, other_ref, gain_ref, out_ref):
    grad = own_ref[...] + other_ref[...].astype(f32)
    out_ref[...] = grad_ref[...] + norm_back(rows_ref[...].astype(f32), gain_ref[...].astype(f32), grad)


def turned(rows, cosine, sine):
    return rows * cosine + pltpu.roll(rows, HEAD_DIM // 2, 1) * sine


def dense_kernel(own_ref, other_ref, wq_ref, wkv_ref, rows_ref, query_ref, kv_ref):
    shard = lax.axis_index("tensor")
    half = own_ref.shape[0]
    rows_ref[pl.ds(pl.multiple_of(shard * half, half), half), :] = own_ref[...]
    rows_ref[pl.ds(pl.multiple_of((1 - shard) * half, half), half), :] = other_ref[...]
    rows = rows_ref[...]
    query_ref[...] = nn(rows, wq_ref[...])
    kv_ref[:, :HEAD_DIM] = nn(rows, wkv_ref[0])
    kv_ref[:, HEAD_DIM:] = nn(rows, wkv_ref[1])


def key_value_kernel(
    rows_ref, dense_ref, bias_ref, adqkv_ref, auk_ref, auv_ref, cos_ref, sin_ref, kv_ref, low_ref, low_t_ref
):
    low = nt(rows_ref[...], adqkv_ref[...])
    low_ref[...] = (2.0 * low).astype(bf)
    low_t_ref[...] = low.T.astype(bf)
    key = dense_ref[:, :HEAD_DIM] + bias_ref[0:1, :].astype(f32) + nn(low_ref[:, RANK : 2 * RANK], auk_ref[...])
    value = dense_ref[:, HEAD_DIM:] + bias_ref[1:2, :].astype(f32) + nn(low_ref[:, 2 * RANK :], auv_ref[...])
    kv_ref[:, :HEAD_DIM] = turned(key, cos_ref[...], sin_ref[...]).astype(bf)
    kv_ref[:, HEAD_DIM:] = value.astype(bf)


def query_kernel(dense_ref, bias_ref, low_ref, auq_ref, cos_ref, sin_ref, q_ref):
    heads, span = q_ref.shape[1], q_ref.shape[2]
    query = dense_ref[...] + bias_ref[...].astype(f32) + nn(low_ref[:, :RANK], auq_ref[...])
    for h in range(heads):
        head = turned(query[:, h * HEAD_DIM : (h + 1) * HEAD_DIM], cos_ref[...], sin_ref[...]).astype(bf)
        q_ref[0, h] = head[:span]
        q_ref[1, h] = head[span:]


def rows_of(own, half):
    shard = lax.axis_index("tensor")
    return pl.ds(pl.multiple_of((shard if own else 1 - shard) * half, half), half)


def mix_send_kernel(mixed_ref, wo_ref, ado_ref, auo_ref, send_ref, low_ref, low_t_ref):
    low = nt(mixed_ref[...], ado_ref[...])
    low_ref[...] = (2.0 * low).astype(bf)
    low_t_ref[...] = low.T.astype(bf)
    rows = rows_of(False, send_ref.shape[0])
    send_ref[...] = (nn(mixed_ref[rows, :], wo_ref[...]) + nn(low_ref[rows, :], auo_ref[...])).astype(bf)


def mix_own_kernel(mixed_ref, wo_ref, low_ref, auo_ref, own_ref):
    rows = rows_of(True, own_ref.shape[0])
    own_ref[...] = nn(mixed_ref[rows, :], wo_ref[...]) + nn(low_ref[rows, :], auo_ref[...])


def mix_back_kernel(own, rows_ref, wo_ref, ado_ref, auo_ref, mixed_ref, low_t_ref, *refs):
    do_ref, delta_ref, dado_ref, dauo_ref = refs[-4:]
    half = rows_ref.shape[0]
    heads = do_ref.shape[1]
    part = lax.axis_index("tensor") if own else 1 - lax.axis_index("tensor")
    places = rows_of(own, half)
    rows, mixed = rows_ref[...], mixed_ref[places, :]
    back = nt(rows, auo_ref[...])
    grad = (nt(rows, wo_ref[...]) + nn((2.0 * back).astype(bf), ado_ref[...])).astype(bf)
    dado = nn(back.T.astype(bf), mixed)
    dauo = nn(low_t_ref[:, places], rows)
    dado_ref[...] = dado if own else refs[2][...] + dado
    dauo_ref[...] = dauo if own else refs[3][...] + dauo
    for h in range(heads):
        cols = slice(h * HEAD_DIM, (h + 1) * HEAD_DIM)
        product = (grad[:, cols].astype(f32) * mixed[:, cols].astype(f32)).T
        do_ref[part, h] = grad[:, cols]
        delta_ref[part, h : h + 1, :] = jnp.sum(product, axis=0, keepdims=True)


def back_query_kernel(
    scale, dq_ref, wq_ref, adq_ref, auq_ref, low_t_ref, rows_ref, cos_ref, sin_ref, total_ref, dadq_ref, dauq_ref, eq
):
    heads, span = dq_ref.shape[1], dq_ref.shape[3]
    for part in range(2):
        rows = slice(part * span, (part + 1) * span)
        for h in range(heads):
            grad = dq_ref[part, h].T * scale
            eq[rows, h * HEAD_DIM : (h + 1) * HEAD_DIM] = turned(grad, cos_ref[rows, :], -sin_ref[rows, :]).astype(bf)
    query = eq[...]
    back = nt(query, auq_ref[...])
    total_ref[...] = nt(query, wq_ref[...]) + nn((2.0 * back).astype(bf), adq_ref[:RANK, :])
    dadq_ref[...] = nn(back.T.astype(bf), rows_ref[...])
    dauq_ref[...] = nn(low_t_ref[:RANK, :], query)


def back_key_value_kernel(
    dkv_ref, query_ref, wkv_ref, adqkv_ref, auk_ref, auv_ref, low_t_ref, rows_ref, cos_ref, sin_ref, *refs
):
    others = refs[: len(refs) - 7]
    own_ref, send_ref, dadkv_ref, dauk_ref, dauv_ref, total, back_ref = refs[len(refs) - 7 :]
    shard = lax.axis_index("tensor")
    half = own_ref.shape[0]
    grad = dkv_ref[...].astype(f32)
    for ref in others:
        grad = grad + ref[...].astype(f32)
    ek = turned(grad[:, :HEAD_DIM], cos_ref[...], -sin_ref[...]).astype(bf)
    ev = grad[:, HEAD_DIM:].astype(bf)
    back_ref[:, :RANK] = nt(ek, auk_ref[...])
    back_ref[:, RANK:] = nt(ev, auv_ref[...])
    back = back_ref[...]
    total[...] = (
        query_ref[...] + nt(ek, wkv_ref[0]) + nt(ev, wkv_ref[1]) + nn((2.0 * back).astype(bf), adqkv_ref[RANK:, :])
    )
    own_ref[...] = total[pl.ds(pl.multiple_of(shard * half, half), half), :]
    send_ref[...] = total[pl.ds(pl.multiple_of((1 - shard) * half, half), half), :].astype(bf)
    dadkv_ref[...] = nn(back.T.astype(bf), rows_ref[...])
    dauk_ref[...] = nn(low_t_ref[RANK : 2 * RANK, :], ek)
    dauv_ref[...] = nn(low_t_ref[2 * RANK :, :], ev)


def future_mask(span):
    return lax.broadcasted_iota(jnp.int32, (span, span), 0) <= lax.broadcasted_iota(jnp.int32, (span, span), 1)

def fold(s, values_t, m, l, o, coef, mask):
    if mask is not None:
        s = jnp.where(mask, s, mask_fill)
    m_next = jnp.maximum(m, jnp.max(s, axis=0, keepdims=True))
    p = jnp.exp2((s - m_next) * coef)
    alpha = jnp.exp2((m - m_next) * coef)
    l_next = l * alpha + jnp.sum(p, axis=0, keepdims=True)
    o_next = o * alpha + nn(values_t, p.astype(bf))
    return m_next, l_next, o_next

def pipelined(items, first, second):
    ahead = first(items[0])
    for i, item in enumerate(items):
        now = ahead
        if i + 1 < len(items):
            ahead = first(items[i + 1])
        second(item, now)

def attn_fwd_own_kernel(coef, q_ref, kv_ref, m_ref, l_ref, o_ref, vt):
    heads, span = q_ref.shape[1], q_ref.shape[2]
    vt[...] = kv_ref[:, HEAD_DIM:].astype(f32).T.astype(bf)
    mask = future_mask(span)
    both_mask = lax.broadcasted_iota(jnp.int32, (2 * span, span), 0) <= lax.broadcasted_iota(jnp.int32, (2 * span, span), 1) + span
    def first(item):
        half, h = item
        return nt(kv_ref[: (half + 1) * span, :HEAD_DIM], q_ref[half, h])
    def second(item, s):
        half, h = item
        m = jnp.full((1, span), mask_fill, f32)
        l = jnp.zeros((1, span), f32)
        o = jnp.zeros((HEAD_DIM, span), f32)
        m, l, o = fold(s, vt[:, : (half + 1) * span], m, l, o, coef, both_mask if half else mask)
        m_ref[half, h : h + 1, :] = m
        l_ref[half, h : h + 1, :] = l
        o_ref[half, h] = o
    pipelined([(half, h) for h in range(heads) for half in range(2)], first, second)

def halves_of(flag, turn):
    return (1 - flag) * turn, flag * turn + (1 - flag)


def attn_fwd_pieces_kernel(coef, indices, last, flag_ref, q_ref, *refs):
    n = len(indices)
    kv_refs = refs[:n]
    m_in, l_in, o_in = refs[n : n + 3]
    if last:
        mixed_ref, lse_ref, m_ref, l_ref, o_ref, vt = refs[n + 3 :]
    else:
        m_ref, l_ref, o_ref, vt = refs[n + 3 :]
    heads, span = q_ref.shape[1], q_ref.shape[2]
    src = [(m_in, l_in, o_in)] + [(m_ref, l_ref, o_ref)] * n
    m_ref[...] = m_in[...]
    l_ref[...] = l_in[...]
    o_ref[...] = o_in[...]
    for i in range(n):
        kv_ref, flag = kv_refs[i], flag_ref[indices[i]]
        vt[...] = kv_ref[:, HEAD_DIM:].astype(f32).T.astype(bf)

        def first(item, kv_ref=kv_ref, flag=flag):
            keys, half = halves_of(flag, item[0])
            return nt(kv_ref[pl.ds(pl.multiple_of(keys * span, span), span), :HEAD_DIM], q_ref[half, item[1]])

        def second(item, s, flag=flag):
            (keys, half), h = halves_of(flag, item[0]), item[1]
            m, l, o = fold(
                s, vt[:, pl.ds(pl.multiple_of(keys * span, span), span)], m_ref[half, h : h + 1, :], l_ref[half, h : h + 1, :],
                o_ref[half, h], coef, None,
            )
            m_ref[half, h : h + 1, :] = m
            l_ref[half, h : h + 1, :] = l
            o_ref[half, h] = o

        pipelined([(turn, h) for turn in range(2) for h in range(heads)], first, second)
    if last:
        for half in range(2):
            for h in range(heads):
                o = o_ref[half, h] / l_ref[half, h : h + 1, :]
                mixed_ref[half * span : (half + 1) * span, h * HEAD_DIM : (h + 1) * HEAD_DIM] = o.T.astype(bf)
        lse_ref[...] = m_ref[...] * coef + jnp.log2(l_ref[...])


def attn_fwd_own(q, kv, coef):
    _, heads, span, _ = q.shape
    st = (jax.ShapeDtypeStruct((2, heads, span), f32),) * 2 + (jax.ShapeDtypeStruct((2, heads, HEAD_DIM, span), f32),)
    return pl.pallas_call(functools.partial(attn_fwd_own_kernel, coef), out_shape=st, in_specs=[VM, VM], out_specs=(VM,) * 3,
        scratch_shapes=[pltpu.VMEM((HEAD_DIM, 2 * span), bf)],
        cost_estimate=pl.CostEstimate(flops=2*2*3*heads*span*span*HEAD_DIM*2, bytes_accessed=4_000_000, transcendentals=0),
        compiler_params=pltpu.CompilerParams(vmem_limit_bytes=20 << 20), name="attn_fwd_own")(q, kv)

def attn_fwd_pieces(flags, indices, q, pieces, state, coef, last):
    _, heads, span, _ = q.shape
    n = len(pieces)
    st = (jax.ShapeDtypeStruct((2, heads, span), f32),) * 2 + (jax.ShapeDtypeStruct((2, heads, HEAD_DIM, span), f32),)
    if last:
        st = (jax.ShapeDtypeStruct((2 * span, heads * HEAD_DIM), bf), jax.ShapeDtypeStruct((2, heads, span), f32)) + st
    r = pl.pallas_call(functools.partial(attn_fwd_pieces_kernel, coef, indices, last), out_shape=st, in_specs=[SM] + [VM] * (n + 4), out_specs=(VM,) * len(st),
        scratch_shapes=[pltpu.VMEM((HEAD_DIM, 2 * span), bf)],
        cost_estimate=pl.CostEstimate(flops=2*2*2*n*heads*span*span*HEAD_DIM*2, bytes_accessed=4_000_000, transcendentals=0),
        compiler_params=pltpu.CompilerParams(vmem_limit_bytes=20 << 20), name="attn_fwd_pieces")(flags, q, *pieces, *state)
    return r

def bwd_block(s, dp, lse_ref, delta_ref, half, h, coef, mask):
    p = jnp.exp2(s * coef - lse_ref[half, h : h + 1, :])
    if mask is not None:
        p = jnp.where(mask, p, 0.0)
    ds = p * (dp - delta_ref[half, h : h + 1, :])
    return p.astype(bf), ds.astype(bf)

def attn_bwd_kernel(coef, scale, indices, own, has_state, flag_ref, q_ref, do_ref, lse_ref, delta_ref, *refs):
    n = len(indices)
    kv_refs = refs[:n]
    k = n
    if has_state:
        dq_in = refs[k]; k += 1
    dkv_refs = refs[k : k + n]
    dq_ref, kt, pbuf, sbuf = refs[k + n :]
    heads, span = q_ref.shape[1], q_ref.shape[2]
    if has_state:
        dq_ref[...] = dq_in[...]
    else:
        dq_ref[...] = jnp.zeros_like(dq_ref)
    def do_item(kv_ref, items, keyrows, mask_of):
        nk = keyrows.stop - keyrows.start
        def first(it):
            i, half, h = it
            return nt(kv_ref[keyrows, :HEAD_DIM], q_ref[half, h]), nt(kv_ref[keyrows, HEAD_DIM:], do_ref[half, h])
        def second(it, sd):
            i, half, h = it
            p, ds = bwd_block(sd[0], sd[1], lse_ref, delta_ref, half, h, coef, mask_of(half))
            cols = slice((i * heads + h) * span, (i * heads + h + 1) * span)
            pbuf[:nk, cols] = p
            sbuf[:nk, cols] = ds
            dq_ref[half, h] += nn(kt[:, keyrows], ds)
        pipelined([(i, half, h) for i, half in enumerate(items) for h in range(heads)], first, second)
        width = len(items) * heads * span
        lo = items[0]
        q_all = q_ref[lo : lo + len(items)].reshape(width, HEAD_DIM)
        do_all = do_ref[lo : lo + len(items)].reshape(width, HEAD_DIM)
        return nn(sbuf[:nk, :width], q_all) * scale, nn(pbuf[:nk, :width], do_all)
    for i in range(n):
        kv_ref, out = kv_refs[i], dkv_refs[i]
        kt[...] = kv_ref[:, :HEAD_DIM].astype(f32).T.astype(bf)
        lo, hi, both = slice(0, span), slice(span, 2 * span), slice(0, 2 * span)
        if own and i == 0:
            mask = future_mask(span)
            dk, dv = do_item(kv_ref, [0, 1], lo, lambda half: mask if half == 0 else None)
            out[lo, :HEAD_DIM] = dk.astype(bf)
            out[lo, HEAD_DIM:] = dv.astype(bf)
            dk, dv = do_item(kv_ref, [1], hi, lambda half: mask)
            out[hi, :HEAD_DIM] = dk.astype(bf)
            out[hi, HEAD_DIM:] = dv.astype(bf)
        else:
            flag = flag_ref[indices[i]]

            def first(item, kv_ref=kv_ref, flag=flag):
                (keys, half), h = halves_of(flag, item[0]), item[1]
                rows = pl.ds(pl.multiple_of(keys * span, span), span)
                return nt(kv_ref[rows, :HEAD_DIM], q_ref[half, h]), nt(kv_ref[rows, HEAD_DIM:], do_ref[half, h])

            def second(item, sd, flag=flag):
                turn, h = item
                keys, half = halves_of(flag, turn)
                p, ds = bwd_block(sd[0], sd[1], lse_ref, delta_ref, half, h, coef, None)
                cols = slice(h * span, (h + 1) * span)
                pbuf[turn * span : (turn + 1) * span, cols] = p
                sbuf[turn * span : (turn + 1) * span, cols] = ds
                dq_ref[half, h] += nn(kt[:, pl.ds(pl.multiple_of(keys * span, span), span)], ds)

            pipelined([(turn, h) for turn in range(2) for h in range(heads)], first, second)
            width = heads * span
            both = []
            for turn in range(2):
                keys, half = halves_of(flag, turn)
                rows = slice(turn * span, (turn + 1) * span)
                both.append((
                    nn(sbuf[rows, :width], q_ref[half].reshape(width, HEAD_DIM)) * scale,
                    nn(pbuf[rows, :width], do_ref[half].reshape(width, HEAD_DIM)),
                ))
            earlier = flag.astype(f32)
            for part in range(2):
                cols = slice(part * HEAD_DIM, (part + 1) * HEAD_DIM)
                out[lo, cols] = (both[0][part] + both[1][part] * earlier).astype(bf)
                out[hi, cols] = (both[1][part] * (1.0 - earlier)).astype(bf)


def attn_bwd(flags, indices, q, do, lse, delta, pieces, dq_state, coef, scale, own):
    _, heads, span, _ = q.shape
    n = len(pieces)
    outs = tuple(jax.ShapeDtypeStruct((2 * span, 2 * HEAD_DIM), bf) for _ in range(n)) + (jax.ShapeDtypeStruct((2, heads, HEAD_DIM, span), f32),)
    ins = [flags, q, do, lse, delta, *pieces] + ([dq_state] if dq_state is not None else [])
    return pl.pallas_call(functools.partial(attn_bwd_kernel, coef, scale, indices, own, dq_state is not None), out_shape=outs,
        in_specs=[SM] + [VM] * (len(ins) - 1), out_specs=(VM,) * len(outs),
        scratch_shapes=[pltpu.VMEM((HEAD_DIM, 2 * span), bf), pltpu.VMEM((2 * span, 2 * heads * span), bf), pltpu.VMEM((2 * span, 2 * heads * span), bf)],
        cost_estimate=pl.CostEstimate(flops=2*5*2*n*heads*span*span*HEAD_DIM*2, bytes_accessed=4_000_000, transcendentals=0),
        compiler_params=pltpu.CompilerParams(vmem_limit_bytes=30 << 20), name="attn_bwd_pieces")(*ins)


TILE = 512


def steps_of(columns, begin=0):
    edges = [begin, begin + TILE // 2, begin + TILE]
    while columns - edges[-1] > 2 * TILE:
        edges.append(edges[-1] + 2 * TILE)
    if columns - edges[-1] > TILE:
        edges.append(edges[-1] + TILE)
    edges.append(columns)
    return list(zip(edges, edges[1:]))


def act_back_kernel(bounds, own_ref, other_ref, wd_hbm, *refs):
    out_hbm, rows_ref, wd, out, in_sems, out_sems = refs[-6:]
    half, first = own_ref.shape[0], bounds[0][0]
    parts = [slice(low - first, high - first) for low, high in bounds]
    copies = [
        pltpu.make_async_copy(wd_hbm.at[low:high], wd.at[part], in_sems.at[i])
        for i, ((low, high), part) in enumerate(zip(bounds, parts))
    ]
    for copy in copies:
        copy.start()
    rows_ref[:half, :] = own_ref[...]
    rows_ref[half:, :] = other_ref[...]
    results = []
    for i, ((low, high), part) in enumerate(zip(bounds, parts)):
        copies[i].wait()
        out[:, part] = nt(rows_ref[...], wd[part, :]).astype(bf)
        result = pltpu.make_async_copy(out.at[:, part], out_hbm.at[:, low:high], out_sems.at[i])
        result.start()
        results.append(result)
    for result in results:
        result.wait()


def act_back(own, other, wd, bounds, held=None):
    half, width = own.shape
    columns, count = bounds[-1][1] - bounds[0][0], len(bounds)
    return pl.pallas_call(
        functools.partial(act_back_kernel, bounds),
        out_shape=pltpu.HBM((2 * half, wd.shape[0]), bf),
        in_specs=[VM, VM, HB] + ([] if held is None else [HB]),
        out_specs=HB,
        scratch_shapes=[
            pltpu.VMEM((2 * half, width), bf), pltpu.VMEM((columns, width), bf), pltpu.VMEM((2 * half, columns), bf),
            pltpu.SemaphoreType.DMA((count,)), pltpu.SemaphoreType.DMA((count,)),
        ],
        input_output_aliases={} if held is None else {3: 0},
        cost_estimate=pl.CostEstimate(flops=4 * half * width * columns, bytes_accessed=2 * width * columns, transcendentals=0),
        compiler_params=pltpu.CompilerParams(vmem_limit_bytes=30 << 20),
        name="act_back",
    )(own, other, in_hbm(wd), *([] if held is None else [in_hbm(held)]))


def whole(*dims):
    return pl.BlockSpec(dims, lambda i: (0,) * len(dims), pipeline_mode=pl.Buffered(1))


def ffn_kernel(
    tile, tiles, hidden, x_own, x_other, g_own, g_other, gact_ref, adgu_ref, auf_ref, wgu_ref, adf_ref, augu_ref,
    gx_own, gx_send, act_ref, flow_ref, dadgu_ref, dauf_ref, daugu_ref, dadf_ref,
    x_ref, g_ref, gx_acc, xlow, xlow_t, fback, fback_t, flow, back,
):
    step = pl.program_id(0)
    half = x_own.shape[0]

    @pl.when(step == 0)
    def prepare():
        for target, own, other in ((x_ref, x_own, x_other), (g_ref, g_own, g_other)):
            target[:half, :] = own[...]
            target[half:, :] = other[...]
        low = nt(x_ref[...], adgu_ref[...])
        xlow[...] = (low * 2.0).astype(bf)
        xlow_t[...] = low.T.astype(bf)
        fb = nt(g_ref[...], auf_ref[...])
        fback[...] = (fb * 2.0).astype(bf)
        fback_t[...] = fb.T.astype(bf)
        gx_acc[...] = jnp.zeros_like(gx_acc)
        flow[...] = jnp.zeros_like(flow)
        back[...] = jnp.zeros_like(back)

    def work(width):
        x = x_ref[...]
        wg, wu = wgu_ref[0, :, :width], wgu_ref[1, :, :width]
        aug, auu, adf = augu_ref[:RANK, :width], augu_ref[RANK:, :width], adf_ref[:, :width]
        gate = nn(x, wg) + nn(xlow[:, :RANK], aug)
        up = nn(x, wu) + nn(xlow[:, RANK:], auu)
        gact = gact_ref[:, :width].astype(f32) + nn(fback[...], adf)
        sig = 1.0 / (1.0 + jnp.exp(-gate))
        silu = gate * sig
        act = (silu * up).astype(bf)
        ggate = (gact * up * (sig + silu * (1.0 - sig))).astype(bf)
        gup = (gact * silu).astype(bf)
        act_ref[:, :width] = act
        flow[...] += nt(act, adf)
        gx_acc[...] += nt(ggate, wg) + nt(gup, wu)
        back[:, :RANK] += nt(ggate, aug)
        back[:, RANK:] += nt(gup, auu)
        daugu_ref[:RANK, :width] = nn(xlow_t[:RANK, :], ggate)
        daugu_ref[RANK:, :width] = nn(xlow_t[RANK:, :], gup)
        dadf_ref[:, :width] = nn(fback_t[...], act)

    tail = hidden - (tiles - 1) * tile
    if tail == tile:
        work(tile)
    else:
        @pl.when(step < tiles - 1)
        def body():
            work(tile)

        @pl.when(step == tiles - 1)
        def part():
            work(tail)

    @pl.when(step == tiles - 1)
    def finish():
        gx_acc[...] += nn((back[...] * 2.0).astype(bf), adgu_ref[...])
        gx_own[...] = gx_acc[:half, :]
        gx_send[...] = gx_acc[half:, :].astype(bf)
        flow_ref[...] = (flow[...] * 2.0).astype(bf)
        dadgu_ref[...] = nn(back[...].T.astype(bf), x_ref[...])
        dauf_ref[...] = nn(flow[...].T.astype(bf), g_ref[...])


def ffn(x_own, x_other, g_own, g_other, gact, adgu, auf, wgu, adf, augu, tile=TILE):
    rows, width = 2 * x_own.shape[0], x_own.shape[1]
    hidden = wgu.shape[2]
    tiles = -(-hidden // tile)
    half = rows // 2
    cols = lambda r: pl.BlockSpec((r, tile), lambda i: (0, i))
    outs = (
        shape(half, width), shape(half, width, dtype=bf), pltpu.HBM((rows, hidden), bf), shape(rows, RANK, dtype=bf),
        shape(2 * RANK, width), shape(RANK, width), shape(2 * RANK, hidden), shape(RANK, hidden),
    )
    return pl.pallas_call(
        functools.partial(ffn_kernel, tile, tiles, hidden),
        grid=(tiles,),
        out_shape=outs,
        in_specs=[whole(half, width)] * 4 + [cols(rows), whole(2 * RANK, width), whole(RANK, width),
                  pl.BlockSpec((2, width, tile), lambda i: (0, 0, i)), cols(RANK), cols(2 * RANK)],
        out_specs=(whole(half, width), whole(half, width), cols(rows), whole(rows, RANK), whole(2 * RANK, width),
                   whole(RANK, width), cols(2 * RANK), cols(RANK)),
        scratch_shapes=[
            pltpu.VMEM((rows, width), bf), pltpu.VMEM((rows, width), bf), pltpu.VMEM((rows, width), f32),
            pltpu.VMEM((rows, 2 * RANK), bf), pltpu.VMEM((2 * RANK, rows), bf), pltpu.VMEM((rows, RANK), bf),
            pltpu.VMEM((RANK, rows), bf), pltpu.VMEM((rows, RANK), f32), pltpu.VMEM((rows, 2 * RANK), f32),
        ],
        cost_estimate=pl.CostEstimate(flops=8 * rows * width * hidden, bytes_accessed=6 * width * hidden, transcendentals=rows * hidden),
        compiler_params=pltpu.CompilerParams(vmem_limit_bytes=36 << 20),
        name="ffn",
    )(x_own, x_other, in_hbm(g_own), in_hbm(g_other), in_hbm(gact), adgu, auf, in_hbm(wgu), adf, augu)


def down_kernel(bounds, start_refs, act_hbm, wd_hbm, total, act, wd, act_sems, wd_sems):
    low = bounds[0][0]
    copies = []
    for i, (begin, end) in enumerate(bounds):
        rows = slice(begin - low, end - low)
        copies.append((
            pltpu.make_async_copy(act_hbm.at[:, begin:end], act.at[:, rows], act_sems.at[i]),
            pltpu.make_async_copy(wd_hbm.at[begin:end], wd.at[rows], wd_sems.at[i]),
        ))
        for copy in copies[-1]:
            copy.start()
    total[...] = nn(start_refs[0][...], start_refs[1][...]) if len(start_refs) == 2 else start_refs[0][...]
    for i, (begin, end) in enumerate(bounds):
        rows = slice(begin - low, end - low)
        for copy in copies[i]:
            copy.wait()
        total[...] += nn(act[:, rows], wd[rows, :])


def down_first_kernel(bounds, flow_ref, auf_ref, act_hbm, wd_hbm, total, *scratch):
    down_kernel(bounds, (flow_ref, auf_ref), act_hbm, wd_hbm, total, *scratch)


def down_last_kernel(bounds, start_ref, act_hbm, wd_hbm, own_ref, send_ref, total, *scratch):
    down_kernel(bounds, (start_ref,), act_hbm, wd_hbm, total, *scratch)
    half = own_ref.shape[0]
    own_ref[...] = total[:half, :]
    send_ref[...] = total[half:, :].astype(bf)


def down(act, wd, start, bounds, last):
    rows, width = act.shape[0], wd.shape[1]
    half, columns, count = rows // 2, bounds[-1][1] - bounds[0][0], len(bounds)
    outs = (shape(half, width), shape(half, width, dtype=bf)) if last else (shape(rows, width),)
    scratch = [
        pltpu.VMEM((rows, columns), bf), pltpu.VMEM((columns, width), bf), pltpu.SemaphoreType.DMA((count,)),
        pltpu.SemaphoreType.DMA((count,)),
    ]
    return pl.pallas_call(
        functools.partial(down_last_kernel if last else down_first_kernel, bounds),
        out_shape=outs,
        in_specs=[VM] * len(start) + [HB, HB],
        out_specs=(VM,) * len(outs),
        scratch_shapes=([pltpu.VMEM((rows, width), f32)] if last else []) + scratch,
        cost_estimate=pl.CostEstimate(flops=2 * rows * width * columns, bytes_accessed=2 * width * columns, transcendentals=0),
        compiler_params=pltpu.CompilerParams(vmem_limit_bytes=28 << 20),
        name="down",
    )(*start, in_hbm(act), in_hbm(wd))


def per_device(
    tokens, cotangent, positions, adapter_choice, attn_gain, query_weight, query_bias, key_value_weight,
    key_value_bias, output_weight, ffn_gain, gate_upper_weight, down_weight, adapt_in, adapt_out,
):
    dp = lax.axis_index("dp")
    groups = lax.axis_size("seq")
    rings = groups // 2
    width, head_width = query_weight.shape
    heads = head_width // HEAD_DIM
    hidden = down_weight.shape[0]
    token_pos = positions[0]
    tok_count = token_pos.shape[0]
    span = tok_count // 2
    scale = HEAD_DIM ** (-0.5)
    coef = scale * math.log2(math.e)
    wide_in, wide_out = adapt_in.shape[2], adapt_out.shape[2]
    lanes_in = rounded_up(wide_in + 1, 128)
    lanes = lanes_in + rounded_up(wide_out, 128)
    widths = (width, head_width, hidden)
    sizes = (rings, wide_in, wide_out, lanes_in, widths)

    def to_pair(value):
        return lax.ppermute(value, "tensor", [(0, 1), (1, 0)])

    def to_other_sequence(value, pairs=((0, 1), (1, 0))):
        return lax.ppermute(value, "dp", list(pairs))

    def to_side(value):
        return lax.ppermute(value, "seq", [(i, i ^ 1) for i in range(groups)])

    def along_ring(value, steps):
        return lax.ppermute(value, "seq", [(i, (i + 2 * steps) % groups) for i in range(groups)])

    cycle = list(range(0, groups, 2)) + list(range(groups - 1, 0, -2))
    hops = [(cycle[i], cycle[(i + 1) % groups]) for i in range(groups)]

    def to_next(value):
        return lax.ppermute(value, "seq", hops)

    def to_last(value):
        return lax.ppermute(value, "seq", [(end, begin) for begin, end in hops])

    def after(value, *others):
        return lax.optimization_barrier((value, *others))[0]

    inputs, grad_out = tokens[0], cotangent[0]
    half = inputs.shape[0]
    attn_gain, ffn_gain = attn_gain[None], ffn_gain[None]

    def over_ring(piece):
        return [piece] + [along_ring(piece, step) for step in range(1, rings)]

    slice_own, slice_other = call(
        functools.partial(select_kernel, lanes_in, span), "select",
        [shape(RANK, lanes, dtype=bf)] * 2, [adapter_choice, positions, adapt_in, adapt_out],
        [
            pltpu.SMEM(adapter_choice.shape, jnp.int32), pltpu.SMEM(positions.shape, jnp.int32),
            pltpu.VMEM((2, RANK, wide_in), bf), pltpu.VMEM((2, RANK, wide_out), bf), pltpu.SemaphoreType.DMA((6,)),
        ],
        left=4,
    )
    slice_other = to_other_sequence(slice_other)
    lane = lax.broadcasted_iota(jnp.int32, (RANK, lanes), 1)
    run_lane = (lane >= wide_in) & (lane < lanes_in)
    grad_other = to_pair(after(grad_out, slice_own))
    slice_other = after(slice_other, grad_other)
    first_slice = jnp.where((dp == 0) | run_lane, slice_own, slice_other)
    second_slice = jnp.where(dp == 0, slice_other, slice_own)

    (normed,) = call(norm_kernel, "norm", [shape(half, width, dtype=bf)], [inputs, attn_gain])
    normed_other = to_pair(normed)
    arrived = over_ring(jnp.stack([first_slice, second_slice]))
    middle = 6 * TILE
    act_grad = act_back(grad_out, grad_other, down_weight, steps_of(middle))
    arrived[1] = after(arrived[1], act_grad)
    own_slices = jnp.stack([piece[0] for piece in arrived])
    own_second = jnp.stack([piece[1] for piece in arrived])
    side_slices = to_side(own_slices)
    pair_slices = to_pair(own_slices)
    normed_rows, query_dense, kv_dense = call(
        dense_kernel, "dense", [shape(tok_count, width, dtype=bf), shape(tok_count, head_width), shape(tok_count, 2 * HEAD_DIM)],
        [normed, after(normed_other, own_slices), query_weight, key_value_weight],
        flops=2 * tok_count * width * (head_width + 2 * HEAD_DIM),
    )
    frequency = jnp.power(rope_base, -(jnp.arange(HEAD_DIM // 2, dtype=f32) * 2.0) / HEAD_DIM)
    angles = token_pos.astype(f32)[:, None] * frequency[None, :]
    cosine, sine = jnp.cos(angles), jnp.sin(angles)
    cosine = jnp.concatenate([cosine, cosine], axis=1)
    sine = jnp.concatenate([-sine, sine], axis=1)

    side_slices = after(side_slices, kv_dense)
    first_slices = [own_slices, side_slices, pair_slices, to_pair(side_slices)]
    side_second = to_side(after(own_second, side_slices))
    slices_in = -(-4 * width // wide_in)
    slices_out = -(-(2 * width + 4 * HEAD_DIM) // wide_out)
    flags, adqkv, auq, auk, auv, ado, auo = call(
        functools.partial(unpack_first_kernel, *sizes), "unpack_first",
        [shape(groups, dtype=jnp.int32)]
        + [
            shape(*dims, dtype=bf)
            for dims in (
                (3 * RANK, width), (RANK, head_width), (RANK, HEAD_DIM), (RANK, HEAD_DIM), (RANK, head_width), (RANK, width),
            )
        ],
        list(first_slices),
        [
            pltpu.VMEM((2 * groups, RANK, lanes), bf),
            pltpu.VMEM((RANK, rounded_up(slices_in * wide_in, 128) + 256), f32),
            pltpu.VMEM((RANK, rounded_up(slices_out * wide_out, 128) + 256), f32),
            pltpu.SMEM((groups,), jnp.int32),
        ],
        out_specs=(SM,) + (VM,) * 6,
    )
    kv, low, low_t = call(
        key_value_kernel, "key_value",
        [shape(tok_count, 2 * HEAD_DIM, dtype=bf), shape(tok_count, 3 * RANK, dtype=bf), shape(3 * RANK, tok_count, dtype=bf)],
        [normed_rows, kv_dense, key_value_bias, adqkv, auk, auv, cosine, sine],
        flops=2 * tok_count * width * 2 * RANK,
    )

    (queries,) = call(
        query_kernel, "query", [shape(2, heads, span, HEAD_DIM, dtype=bf)],
        [query_dense, query_bias[None], low, auq, cosine, sine], flops=2 * tok_count * width * RANK,
    )
    state = attn_fwd_own(queries, kv, coef)
    pieces, from_last, from_next = [kv], kv, kv
    for step in range(1, rings + 1):
        from_last, from_next = to_next(from_last), to_last(from_next)
        if step == 1:
            bounds = [(middle, middle + TILE // 2), (middle + TILE // 2, middle + 2 * TILE), (middle + 2 * TILE, hidden)]
            act_grad = act_back(after(grad_out, state[0], side_second), grad_other, down_weight, bounds, act_grad)
            from_last = after(from_last, act_grad)
        if step < rings:
            from_last, from_next, _ = lax.optimization_barrier((from_last, from_next, state[0]))
        if step == rings:
            pair_second = to_pair(after(own_second, pieces[-1]))
            state = (after(state[0], pair_second), *state[1:])
        pieces += [from_last, from_next][: 2 if step < rings else 1]
        indices = tuple(range(2 * step - 1, len(pieces)))
        result = attn_fwd_pieces(flags, indices, queries, pieces[2 * step - 1 :], state, coef, step == rings)
        state = result[-3:]
    mixed, lse = result[0], result[1]

    branch_send, mix_low, mix_low_t = call(
        mix_send_kernel, "mix_send",
        [shape(half, width, dtype=bf), shape(tok_count, RANK, dtype=bf), shape(RANK, tok_count, dtype=bf)],
        [mixed, output_weight, ado, auo], flops=2 * half * width * head_width,
    )
    branch_other = to_pair(branch_send)
    second_slices = [own_second, side_second, pair_second, to_pair(side_second)]
    (branch_own,) = call(
        mix_own_kernel, "mix_own", [shape(half, width)], [mixed, output_weight, mix_low, auo],
        flops=2 * half * width * head_width,
    )
    hidden_rows, normed_ffn = call(
        residual_kernel, "residual", [shape(half, width), shape(half, width, dtype=bf)],
        [inputs, branch_own, after(branch_other, branch_own, second_slices[3]), ffn_gain],
    )
    begin_in, begin_out, first_in, first_out = bases(wide_in, wide_out, widths)
    adgu, augu, adf, auf = call(
        functools.partial(unpack_second_kernel, *sizes), "unpack_second",
        [shape(*dims, dtype=bf) for dims in ((2 * RANK, width), (2 * RANK, hidden), (RANK, hidden), (RANK, width))],
        list(first_slices) + list(second_slices),
        [
            pltpu.VMEM((4 * groups, RANK, lanes), bf),
            pltpu.VMEM((RANK, rounded_up(4 * groups * wide_in, 128) + 256 - first_in), f32),
            pltpu.VMEM((RANK, rounded_up(4 * groups * wide_out, 128) + 256 - first_out), f32),
        ],
    )
    gx_own, gx_send, act, flow, dadgu, dauf, daugu, dadf = ffn(
        normed_ffn, to_pair(normed_ffn), grad_out, grad_other, act_grad, adgu, auf, gate_upper_weight, adf, augu
    )
    ad_lanes = rounded_up(4 * groups * wide_in, 128) + 256
    au_lanes = rounded_up(4 * groups * wide_out, 128) + 256

    def added(*values):
        total = values[0].astype(f32)
        for value in values[1:]:
            total = total + value.astype(f32)
        return total.astype(bf)

    grad_hidden, grad_low = call(
        hidden_back_kernel, "hidden_back", [shape(half, width), shape(half, width, dtype=bf)],
        [hidden_rows, grad_out, gx_own, to_pair(gx_send), ffn_gain],
    )
    grad_low_other = to_pair(grad_low)
    fixed = [output_weight, ado, auo, mixed, mix_low_t]
    outs = [shape(2, heads, span, HEAD_DIM, dtype=bf), shape(2, heads, span), shape(RANK, head_width), shape(RANK, width)]
    partial = call(
        functools.partial(mix_back_kernel, True), "mix_back", outs, [grad_low, *fixed], flops=2 * half * width * head_width,
    )
    grad_mixed, delta, dado, dauo = call(
        functools.partial(mix_back_kernel, False), "mix_back_other", outs,
        [after(grad_low_other, partial[0]), *fixed, *partial], flops=2 * half * width * head_width,
        aliases={6 + i: i for i in range(4)},
    )

    def backward(indices, state_dq):
        return attn_bwd(
            flags, indices, queries, grad_mixed, lse, delta, [pieces[index] for index in indices], state_dq, coef, scale,
            indices == (0,),
        )

    state_dq, from_last, from_next = None, None, None
    for step in range(rings, 0, -1):
        onward, *returned, state_dq = backward((2 * rings - 1,) if step == rings else (2 * step, 2 * step - 1), state_dq)
        if from_last is not None:
            onward = added(onward, from_last)
        if from_next is not None:
            returned = [added(returned[0], from_next)]
        from_last = to_next(onward)
        if returned:
            from_next = to_last(returned[0])
        state_dq = after(state_dq, onward, *returned)
    own_term, state_dq = backward((0,), state_dq)
    gn_query, dadq, dauq = call(
        functools.partial(back_query_kernel, scale), "back_query",
        [shape(tok_count, width), shape(RANK, width), shape(RANK, head_width)],
        [state_dq, query_weight, adqkv, auq, low_t, normed_rows, cosine, sine],
        [pltpu.VMEM((tok_count, head_width), bf)], flops=2 * tok_count * width * head_width,
    )
    from_last = after(from_last, gn_query)
    gn_own, gn_send, dadkv, dauk, dauv = call(
        back_key_value_kernel, "back_key_value",
        [
            shape(half, width), shape(half, width, dtype=bf), shape(2 * RANK, width), shape(RANK, HEAD_DIM),
            shape(RANK, HEAD_DIM),
        ],
        [
            own_term, gn_query, key_value_weight, adqkv, auk, auv, low_t, normed_rows, cosine, sine, from_last, from_next,
        ],
        [pltpu.VMEM((tok_count, width), f32), pltpu.VMEM((tok_count, 2 * RANK), f32)],
        flops=2 * tok_count * width * 2 * HEAD_DIM, limit=20,
    )
    (packed,) = call(
        functools.partial(pack_kernel, *sizes), "pack", [shape(2, 2, rings, 2, RANK, lanes, dtype=bf)],
        [dadq, dadkv, dado, dadgu, dadf, dauq, dauk, dauv, dauo, daugu, dauf],
        [pltpu.VMEM((RANK, ad_lanes), f32), pltpu.VMEM((RANK, au_lanes), f32)],
    )
    from_pair = to_pair(packed[1])
    near, far = added(packed[0, 0], from_pair[0]), added(packed[0, 1, 1:], from_pair[1, 1:])
    from_side = to_side(far)
    own_side = to_side(after(added(packed[0, 1, 0], from_pair[1, 0]), far))
    middle = 6 * TILE
    (out_total,) = down(after(act, far), down_weight, (flow, auf), steps_of(middle), False)
    from_side = after(from_side, out_total)
    sums = [added(near[place], from_side[place - 1]) for place in range(1, rings)]
    from_ring = [along_ring(sums[place - 1], -place) for place in range(1, rings)]
    out_own, out_send = down(after(act, *sums), down_weight, (out_total,), steps_of(hidden, middle), True)
    from_ring[0] = after(from_ring[0], out_own)
    total = added(near[0], own_side, *from_ring)
    (grad_tokens,) = call(
        token_back_kernel, "token_back", [shape(half, width)],
        [inputs, grad_hidden, gn_own, after(to_pair(gn_send), total), attn_gain],
    )
    output = (hidden_rows + (out_own + to_pair(out_send).astype(f32))).astype(bf)
    other_total = after(to_other_sequence(total[1]), output, grad_tokens)
    factor = adapter_scale * (adapter_choice.shape[0] * tok_count * groups) ** (-0.5)
    adapt_in_grad, adapt_out_grad = call(
        functools.partial(place_kernel, lanes_in, factor), "place",
        [shape(*adapt_in.shape), shape(*adapt_out.shape)],
        [adapter_choice, total[0], other_total], smem=1,
    )
    return (output[None], grad_tokens[None], adapt_in_grad, adapt_out_grad)


def solution(mesh):
    return jax.shard_map(
        per_device,
        mesh=mesh,
        in_specs=(
            P("dp", ("seq", "tensor"), None),
            P("dp", ("seq", "tensor"), None),
            P("dp", "seq"),
            P(),
            P(),
            P(None, "tensor"),
            P("tensor"),
            P(None, None, "tensor"),
            P(None, "tensor"),
            P("tensor", None),
            P(),
            P(None, None, "tensor"),
            P("tensor", None),
            P(None, None, ("dp", "seq", "tensor")),
            P(None, None, ("dp", "seq", "tensor")),
        ),
        out_specs=(
            P("dp", ("seq", "tensor"), None),
            P("dp", ("seq", "tensor"), None),
            P(None, None, ("dp", "seq", "tensor")),
            P(None, None, ("dp", "seq", "tensor")),
        ),
        check_vma=False,
    )
```

```python
import functools
import math

import jax
import jax.numpy as jnp
from jax import lax
from jax.experimental import pallas as pl
from jax.experimental.pallas import tpu as pltpu
from jax.sharding import PartitionSpec as P

HEAD_DIM = 128
RANK = 16
eps = 1e-06
adapter_scale = 2.0
rope_base = 1000000.0
mask_fill = -1e30
bf = jnp.bfloat16
f32 = jnp.float32
VM = pl.BlockSpec(memory_space=pltpu.VMEM)
SM = pl.BlockSpec(memory_space=pltpu.SMEM)


def nn(a, b):
    return jnp.dot(a, b, preferred_element_type=f32)


def nt(a, b):
    return lax.dot_general(a, b, (((1,), (1,)), ((), ())), preferred_element_type=f32)


def shape(*dims, dtype=f32):
    return jax.ShapeDtypeStruct(dims, dtype)


def call(kernel, name, out, ins, scratch=(), flops=0, smem=0, out_specs=None, limit=16, left=0, aliases=None):
    moved = sum(math.prod(v.shape) * v.dtype.itemsize for v in list(ins) + list(out))
    ins = list(ins[: len(ins) - left]) + [in_hbm(value) for value in ins[len(ins) - left :]]
    return pl.pallas_call(
        kernel,
        out_shape=tuple(out),
        in_specs=[SM] * smem + [VM] * (len(ins) - smem - left) + [HB] * left,
        out_specs=out_specs or (VM,) * len(out),
        scratch_shapes=list(scratch),
        input_output_aliases=aliases or {},
        cost_estimate=pl.CostEstimate(flops=flops, bytes_accessed=moved, transcendentals=0),
        compiler_params=pltpu.CompilerParams(vmem_limit_bytes=limit << 20),
        name=name,
    )(*ins)


HB = pl.BlockSpec(memory_space=pltpu.HBM)


def in_hbm(value):
    return pltpu.with_memory_space_constraint(value, pltpu.HBM)


def rounded_up(value, unit):
    return -(-value // unit) * unit


def select_kernel(
    lanes_in, span, choice_hbm, pos_hbm, in_ref, out_ref, own_ref, other_ref, choice_ref, pos_ref, held_in, held_out, sems
):
    wide_in, wide_out = in_ref.shape[2], out_ref.shape[2]
    dp = lax.axis_index("dp")
    choice_copy = pltpu.make_async_copy(choice_hbm, choice_ref, sems.at[4])
    pos_copy = pltpu.make_async_copy(pos_hbm, pos_ref, sems.at[5])
    choice_copy.start()
    pos_copy.start()
    choice_copy.wait()
    copies = []
    for slot, sequence in ((0, dp), (1, 1 - dp)):
        chosen = choice_ref[sequence]
        copies.append(pltpu.make_async_copy(in_ref.at[chosen], held_in.at[slot], sems.at[2 * slot]))
        copies.append(pltpu.make_async_copy(out_ref.at[chosen], held_out.at[slot], sems.at[2 * slot + 1]))
    for copy in copies:
        copy.start()
    pos_copy.wait()
    run = jnp.full((RANK, lanes_in), pos_ref[0, 0] // span, jnp.int32).astype(f32).astype(bf)
    for target in (own_ref, other_ref):
        target[...] = jnp.zeros_like(target)
        target[:, :lanes_in] = run
    for copy in copies:
        copy.wait()
    for slot, target in ((0, own_ref), (1, other_ref)):
        target[:, :wide_in] = held_in[slot]
        target[:, lanes_in : lanes_in + wide_out] = held_out[slot]


def column(begin, size):
    return pl.ds(pl.multiple_of(begin, 128), size)


def source_of(place, side, rings, seq):
    ring = lax.rem(seq // 2 - place + rings, rings)
    own_side = lax.rem(seq, 2)
    return ring * 2 + (own_side if side == 0 else 1 - own_side)


def spread(slots, target, begin, wide, first, low, high):
    held = rounded_up(wide, 128)
    inside = lax.broadcasted_iota(jnp.int32, (RANK, held), 1) < wide
    target[...] = jnp.zeros_like(target)
    for index in range(low // wide, -(-high // wide)):
        part = jnp.where(inside, slots[index, :, begin : begin + held].astype(f32), 0.0)
        part = jnp.concatenate([part, jnp.zeros((RANK, 128), f32)], axis=1)
        offset = index * wide - first
        base = offset // 128 * 128
        if offset != base:
            part = pltpu.roll(part, offset - base, 1)
        target[:, base : base + held + 128] += part


def collect(slots, refs, rings, part):
    seq, shard = lax.axis_index("seq"), lax.axis_index("tensor")
    for number, ref in enumerate(refs):
        side, core = number % 2, shard if number < 2 else 1 - shard
        for place in range(rings):
            slots[part * 4 * rings + source_of(place, side, rings, seq) * 2 + core] = ref[place]


def unpack_first_kernel(
    rings, wide_in, wide_out, lanes_in, widths, own, own_side, pair, pair_side,
    flags_ref, adqkv, auq, auk, auv, ado, auo, slots, ad, au, runs,
):
    shard, seq = lax.axis_index("tensor"), lax.axis_index("seq")
    width, head_width, hidden = widths
    for place in range(rings):
        for side, ref in ((0, own), (1, own_side)):
            run = jnp.max(ref[place, :, wide_in:lanes_in].astype(f32))
            runs[source_of(place, side, rings, seq)] = run.astype(jnp.int32)
    groups = 2 * rings
    place = jnp.where(lax.rem(seq, 2) == 0, seq // 2, groups - 1 - seq // 2)
    for index in range(groups):
        step = (index + 1) // 2
        other = lax.rem(place + (groups - step if index % 2 == 1 else step), groups)
        source = jnp.where(other < rings, 2 * other, 2 * (groups - 1 - other) + 1)
        flags_ref[index] = (runs[source] < runs[seq]).astype(jnp.int32)
    collect(slots, (own, own_side, pair, pair_side), rings, 0)
    spread(slots, ad, 0, wide_in, 0, 0, 4 * width)
    spread(slots, au, lanes_in, wide_out, 0, 0, 2 * width + 4 * HEAD_DIM)
    for index in range(3):
        adqkv[index * RANK : (index + 1) * RANK, :] = ad[:, index * width : (index + 1) * width].astype(bf)
    ado[...] = ad[:, column(3 * width + shard * head_width, head_width)].astype(bf)
    auq[...] = au[:, column(shard * head_width, head_width)].astype(bf)
    auk[...] = au[:, column(width + shard * HEAD_DIM, HEAD_DIM)].astype(bf)
    auv[...] = au[:, column(width + (2 + shard) * HEAD_DIM, HEAD_DIM)].astype(bf)
    base = width + 4 * HEAD_DIM
    auo[...] = au[:, base : base + width].astype(bf)


def bases(wide_in, wide_out, widths):
    width = widths[0]
    begin_in, begin_out = 4 * width, 2 * width + 4 * HEAD_DIM
    return begin_in, begin_out, begin_in // wide_in * wide_in // 128 * 128, begin_out // wide_out * wide_out // 128 * 128


def unpack_second_kernel(
    rings, wide_in, wide_out, lanes_in, widths, *refs
):
    firsts, seconds = refs[:4], refs[4:8]
    adgu, augu, adf, auf, slots, ad, au = refs[8:]
    shard = lax.axis_index("tensor")
    width, head_width, hidden = widths
    collect(slots, firsts, rings, 0)
    collect(slots, seconds, rings, 1)
    begin_in, begin_out, first_in, first_out = bases(wide_in, wide_out, widths)
    total_in, total_out = 8 * rings * wide_in, 8 * rings * wide_out
    spread(slots, ad, 0, wide_in, first_in, begin_in, total_in)
    spread(slots, au, lanes_in, wide_out, first_out, begin_out, total_out)
    base = begin_in - first_in
    for index in range(2):
        adgu[index * RANK : (index + 1) * RANK, :] = ad[:, base + index * width : base + (index + 1) * width].astype(bf)
    adf[...] = ad[:, column(base + 2 * width + shard * hidden, hidden)].astype(bf)
    base = begin_out - first_out
    for index in range(2):
        augu[index * RANK : (index + 1) * RANK, :] = au[
            :, column(base + (2 * index + shard) * hidden, hidden)
        ].astype(bf)
    auf[...] = au[:, base + 4 * hidden : base + 4 * hidden + width].astype(bf)


def put_slices(rings, wide_in, wide_out, lanes_in, ad, au, limits, parts, write):
    dp, seq = lax.axis_index("dp"), lax.axis_index("seq")
    for index in range(4 * rings * parts):
        to_dp, to_seq, to_core = index // (4 * rings), index // 2 % (2 * rings), index % 2
        pieces = []
        for source, wide, (low, high, first) in ((ad, wide_in, limits[0]), (au, wide_out, limits[1])):
            held = rounded_up(wide, 128)
            if index * wide >= high or (index + 1) * wide <= low:
                part = jnp.zeros((RANK, held), f32)
            else:
                offset = index * wide - first
                base = offset // 128 * 128
                part = source[:, base : base + held + 128]
                if offset != base:
                    part = pltpu.roll(part, held + 128 - (offset - base), 1)
                part = part[:, :held]
            pieces.append(part)
            if source is ad and lanes_in > held:
                pieces.append(jnp.zeros((RANK, lanes_in - held), f32))
        packed = jnp.concatenate(pieces, axis=1).astype(bf)
        place = lax.rem(seq // 2 - to_seq // 2 + rings, rings)
        write(to_seq, to_core, place, lax.rem(dp + to_dp, 2), packed)


def pack_kernel(
    rings, wide_in, wide_out, lanes_in, widths,
    dadq, dadkv, dado, dadgu, dadf, dauq, dauk, dauv, dauo, daugu, dauf, out_ref, ad, au,
):
    shard, side = lax.axis_index("tensor"), lax.rem(lax.axis_index("seq"), 2)
    width, head_width, hidden = widths
    ad[...] = jnp.zeros_like(ad)
    au[...] = jnp.zeros_like(au)
    ad[:, :width] = dadq[...]
    for index in range(2):
        ad[:, (1 + index) * width : (2 + index) * width] = dadkv[index * RANK : (index + 1) * RANK, :]
        ad[:, (4 + index) * width : (5 + index) * width] = dadgu[index * RANK : (index + 1) * RANK, :]
    ad[:, column(3 * width + shard * head_width, head_width)] = dado[...]
    ad[:, column(6 * width + shard * hidden, hidden)] = dadf[...]
    au[:, column(shard * head_width, head_width)] = dauq[...]
    au[:, column(width + shard * HEAD_DIM, HEAD_DIM)] = dauk[...]
    au[:, column(width + (2 + shard) * HEAD_DIM, HEAD_DIM)] = dauv[...]
    base = width + 4 * HEAD_DIM
    au[:, base : base + width] = dauo[...]
    base = base + width
    for index in range(2):
        au[:, column(base + (2 * index + shard) * hidden, hidden)] = daugu[index * RANK : (index + 1) * RANK, :]
    au[:, base + 4 * hidden : base + 4 * hidden + width] = dauf[...]

    def write(to_seq, to_core, place, part, packed):
        out_ref[lax.rem(shard + to_core, 2), lax.rem(side + to_seq % 2, 2), place, part] = packed

    limits = ((0, 8 * rings * wide_in, 0), (0, 8 * rings * wide_out, 0))
    put_slices(rings, wide_in, wide_out, lanes_in, ad, au, limits, 2, write)


def place_kernel(lanes_in, factor, choice_ref, own_ref, other_ref, in_ref, out_ref):
    wide_in, wide_out = in_ref.shape[2], out_ref.shape[2]
    dp = lax.axis_index("dp")
    in_ref[...] = jnp.zeros_like(in_ref)
    out_ref[...] = jnp.zeros_like(out_ref)
    for ref, sequence in ((own_ref, dp), (other_ref, 1 - dp)):
        chosen = choice_ref[sequence]
        part = ref[...].astype(f32) * factor
        in_ref[chosen] = in_ref[chosen] + part[:, :wide_in]
        out_ref[chosen] = out_ref[chosen] + part[:, lanes_in : lanes_in + wide_out]


def factor_of(rows):
    return lax.rsqrt(jnp.mean(rows * rows, axis=-1, keepdims=True) + eps)


def norm_back(rows, gain, grad):
    factor = factor_of(rows)
    scaled = rows * factor
    grad_scaled = grad * gain
    return factor * (grad_scaled - scaled * jnp.mean(grad_scaled * scaled, axis=-1, keepdims=True))


def norm_kernel(rows_ref, gain_ref, normed_ref):
    rows = rows_ref[...].astype(f32)
    normed_ref[...] = (rows * factor_of(rows) * gain_ref[...].astype(f32)).astype(bf)


def residual_kernel(rows_ref, own_ref, other_ref, gain_ref, hidden_ref, normed_ref):
    rows = rows_ref[...].astype(f32) + (own_ref[...] + other_ref[...].astype(f32))
    hidden_ref[...] = rows
    normed_ref[...] = (rows * factor_of(rows) * gain_ref[...].astype(f32)).astype(bf)


def hidden_back_kernel(hidden_ref, grad_ref, own_ref, other_ref, gain_ref, out_ref, low_ref):
    grad = own_ref[...] + other_ref[...].astype(f32)
    total = grad_ref[...].astype(f32) + norm_back(hidden_ref[...], gain_ref[...].astype(f32), grad)
    out_ref[...] = total
    low_ref[...] = total.astype(bf)


def token_back_kernel(rows_ref, grad_ref, own_ref, other_ref, gain_ref, out_ref):
    grad = own_ref[...] + other_ref[...].astype(f32)
    out_ref[...] = grad_ref[...] + norm_back(rows_ref[...].astype(f32), gain_ref[...].astype(f32), grad)


def turned(rows, cosine, sine):
    return rows * cosine + pltpu.roll(rows, HEAD_DIM // 2, 1) * sine


def dense_kernel(own_ref, other_ref, wq_ref, wkv_ref, rows_ref, query_ref, kv_ref):
    shard = lax.axis_index("tensor")
    half = own_ref.shape[0]
    rows_ref[pl.ds(pl.multiple_of(shard * half, half), half), :] = own_ref[...]
    rows_ref[pl.ds(pl.multiple_of((1 - shard) * half, half), half), :] = other_ref[...]
    rows = rows_ref[...]
    query_ref[...] = nn(rows, wq_ref[...])
    kv_ref[:, :HEAD_DIM] = nn(rows, wkv_ref[0])
    kv_ref[:, HEAD_DIM:] = nn(rows, wkv_ref[1])


def key_value_kernel(
    rows_ref, dense_ref, bias_ref, adqkv_ref, auk_ref, auv_ref, cos_ref, sin_ref, kv_ref, low_ref, low_t_ref
):
    low = nt(rows_ref[...], adqkv_ref[...])
    low_ref[...] = (2.0 * low).astype(bf)
    low_t_ref[...] = low.T.astype(bf)
    key = dense_ref[:, :HEAD_DIM] + bias_ref[0:1, :].astype(f32) + nn(low_ref[:, RANK : 2 * RANK], auk_ref[...])
    value = dense_ref[:, HEAD_DIM:] + bias_ref[1:2, :].astype(f32) + nn(low_ref[:, 2 * RANK :], auv_ref[...])
    kv_ref[:, :HEAD_DIM] = turned(key, cos_ref[...], sin_ref[...]).astype(bf)
    kv_ref[:, HEAD_DIM:] = value.astype(bf)


def query_kernel(dense_ref, bias_ref, low_ref, auq_ref, cos_ref, sin_ref, q_ref):
    heads, span = q_ref.shape[1], q_ref.shape[2]
    query = dense_ref[...] + bias_ref[...].astype(f32) + nn(low_ref[:, :RANK], auq_ref[...])
    for h in range(heads):
        head = turned(query[:, h * HEAD_DIM : (h + 1) * HEAD_DIM], cos_ref[...], sin_ref[...]).astype(bf)
        q_ref[0, h] = head[:span]
        q_ref[1, h] = head[span:]


def rows_of(own, half):
    shard = lax.axis_index("tensor")
    return pl.ds(pl.multiple_of((shard if own else 1 - shard) * half, half), half)


def mix_send_kernel(mixed_ref, wo_ref, ado_ref, auo_ref, send_ref, low_ref, low_t_ref):
    low = nt(mixed_ref[...], ado_ref[...])
    low_ref[...] = (2.0 * low).astype(bf)
    low_t_ref[...] = low.T.astype(bf)
    rows = rows_of(False, send_ref.shape[0])
    send_ref[...] = (nn(mixed_ref[rows, :], wo_ref[...]) + nn(low_ref[rows, :], auo_ref[...])).astype(bf)


def mix_own_kernel(mixed_ref, wo_ref, low_ref, auo_ref, own_ref):
    rows = rows_of(True, own_ref.shape[0])
    own_ref[...] = nn(mixed_ref[rows, :], wo_ref[...]) + nn(low_ref[rows, :], auo_ref[...])


def mix_back_kernel(own, rows_ref, wo_ref, ado_ref, auo_ref, mixed_ref, low_t_ref, *refs):
    do_ref, delta_ref, dado_ref, dauo_ref = refs[-4:]
    half = rows_ref.shape[0]
    heads = do_ref.shape[1]
    part = lax.axis_index("tensor") if own else 1 - lax.axis_index("tensor")
    places = rows_of(own, half)
    rows, mixed = rows_ref[...], mixed_ref[places, :]
    back = nt(rows, auo_ref[...])
    grad = (nt(rows, wo_ref[...]) + nn((2.0 * back).astype(bf), ado_ref[...])).astype(bf)
    dado = nn(back.T.astype(bf), mixed)
    dauo = nn(low_t_ref[:, places], rows)
    dado_ref[...] = dado if own else refs[2][...] + dado
    dauo_ref[...] = dauo if own else refs[3][...] + dauo
    for h in range(heads):
        cols = slice(h * HEAD_DIM, (h + 1) * HEAD_DIM)
        product = (grad[:, cols].astype(f32) * mixed[:, cols].astype(f32)).T
        do_ref[part, h] = grad[:, cols]
        delta_ref[part, h : h + 1, :] = jnp.sum(product, axis=0, keepdims=True)


def back_query_kernel(
    scale, dq_ref, wq_ref, adq_ref, auq_ref, low_t_ref, rows_ref, cos_ref, sin_ref, total_ref, dadq_ref, dauq_ref, eq
):
    heads, span = dq_ref.shape[1], dq_ref.shape[3]
    for part in range(2):
        rows = slice(part * span, (part + 1) * span)
        for h in range(heads):
            grad = dq_ref[part, h].T * scale
            eq[rows, h * HEAD_DIM : (h + 1) * HEAD_DIM] = turned(grad, cos_ref[rows, :], -sin_ref[rows, :]).astype(bf)
    query = eq[...]
    back = nt(query, auq_ref[...])
    total_ref[...] = nt(query, wq_ref[...]) + nn((2.0 * back).astype(bf), adq_ref[:RANK, :])
    dadq_ref[...] = nn(back.T.astype(bf), rows_ref[...])
    dauq_ref[...] = nn(low_t_ref[:RANK, :], query)


def back_key_value_kernel(
    dkv_ref, query_ref, wkv_ref, adqkv_ref, auk_ref, auv_ref, low_t_ref, rows_ref, cos_ref, sin_ref, *refs
):
    others = refs[: len(refs) - 7]
    own_ref, send_ref, dadkv_ref, dauk_ref, dauv_ref, total, back_ref = refs[len(refs) - 7 :]
    shard = lax.axis_index("tensor")
    half = own_ref.shape[0]
    grad = dkv_ref[...].astype(f32)
    for ref in others:
        grad = grad + ref[...].astype(f32)
    ek = turned(grad[:, :HEAD_DIM], cos_ref[...], -sin_ref[...]).astype(bf)
    ev = grad[:, HEAD_DIM:].astype(bf)
    back_ref[:, :RANK] = nt(ek, auk_ref[...])
    back_ref[:, RANK:] = nt(ev, auv_ref[...])
    back = back_ref[...]
    total[...] = (
        query_ref[...] + nt(ek, wkv_ref[0]) + nt(ev, wkv_ref[1]) + nn((2.0 * back).astype(bf), adqkv_ref[RANK:, :])
    )
    own_ref[...] = total[pl.ds(pl.multiple_of(shard * half, half), half), :]
    send_ref[...] = total[pl.ds(pl.multiple_of((1 - shard) * half, half), half), :].astype(bf)
    dadkv_ref[...] = nn(back.T.astype(bf), rows_ref[...])
    dauk_ref[...] = nn(low_t_ref[RANK : 2 * RANK, :], ek)
    dauv_ref[...] = nn(low_t_ref[2 * RANK :, :], ev)


def future_mask(span):
    return lax.broadcasted_iota(jnp.int32, (span, span), 0) <= lax.broadcasted_iota(jnp.int32, (span, span), 1)

EXTRA = 16


def weights_of(s, m, coef, mask):
    if mask is not None:
        s = jnp.where(mask, s, mask_fill)
    m_next = jnp.maximum(m, jnp.max(s, axis=0, keepdims=True))
    p = jnp.exp2((s - m_next) * coef)
    alpha = jnp.exp2((m - m_next) * coef)
    return m_next, alpha, p.astype(bf)


def put_values(vt, kv_ref):
    vt[:HEAD_DIM, :] = kv_ref[:, HEAD_DIM:].astype(f32).T.astype(bf)


def put_ones(vt):
    vt[HEAD_DIM:, :] = jnp.ones((EXTRA, vt.shape[1]), bf)


def pipelined(items, first, second):
    ahead = first(items[0])
    for i, item in enumerate(items):
        now = ahead
        if i + 1 < len(items):
            ahead = first(items[i + 1])
        second(item, now)

def pipelined_three(items, first, second, third):
    ahead, behind = first(items[0]), None
    for i, item in enumerate(items):
        now = ahead
        if i + 1 < len(items):
            ahead = first(items[i + 1])
        done = second(item, now)
        if behind is not None:
            third(*behind)
        behind = (item, done)
    third(*behind)


def attn_fwd_own_kernel(coef, q_ref, kv_ref, m_ref, o_ref, vt):
    heads, span = q_ref.shape[1], q_ref.shape[2]
    put_ones(vt)
    put_values(vt, kv_ref)
    mask = future_mask(span)
    row, place = (lax.broadcasted_iota(jnp.int32, (2 * span, span), axis) for axis in range(2))
    both_mask = row <= place + span

    def first(item):
        half, h = item
        return nt(kv_ref[: (half + 1) * span, :HEAD_DIM], q_ref[half, h])

    def second(item, s):
        half, h = item
        m, _, p = weights_of(s, jnp.full((1, span), mask_fill, f32), coef, both_mask if half else mask)
        m_ref[half, h : h + 1, :] = m
        return p

    def third(item, p):
        half, h = item
        o_ref[half, h] = nn(vt[:, : (half + 1) * span], p)

    pipelined_three([(half, h) for h in range(heads) for half in range(2)], first, second, third)


def halves_of(flag, turn):
    return (1 - flag) * turn, flag * turn + (1 - flag)


def attn_fwd_pieces_kernel(coef, indices, last, flag_ref, q_ref, *refs):
    n = len(indices)
    kv_refs, (m_in, o_in), refs = refs[:n], refs[n : n + 2], refs[n + 2 :]
    if last:
        mixed_ref, lse_ref, m_ref, o_ref, vt = refs
    else:
        m_ref, o_ref, vt = refs
    heads, span = q_ref.shape[1], q_ref.shape[2]
    put_ones(vt)
    m_ref[...] = m_in[...]
    o_ref[...] = o_in[...]
    for i in range(n):
        kv_ref, flag = kv_refs[i], flag_ref[indices[i]]
        put_values(vt, kv_ref)

        def first(item, kv_ref=kv_ref, flag=flag):
            keys, half = halves_of(flag, item[0])
            return nt(kv_ref[pl.ds(pl.multiple_of(keys * span, span), span), :HEAD_DIM], q_ref[half, item[1]])

        def second(item, s, flag=flag):
            half, h = halves_of(flag, item[0])[1], item[1]
            m, alpha, p = weights_of(s, m_ref[half, h : h + 1, :], coef, None)
            m_ref[half, h : h + 1, :] = m
            return alpha, p

        def third(item, weights, flag=flag):
            (keys, half), h = halves_of(flag, item[0]), item[1]
            alpha, p = weights
            values_t = vt[:, pl.ds(pl.multiple_of(keys * span, span), span)]
            o_ref[half, h] = o_ref[half, h] * alpha + nn(values_t, p)

        pipelined_three([(turn, h) for turn in range(2) for h in range(heads)], first, second, third)
    if last:
        for half in range(2):
            for h in range(heads):
                sums = o_ref[half, h, HEAD_DIM : HEAD_DIM + 1, :]
                o = o_ref[half, h, :HEAD_DIM, :] / sums
                mixed_ref[half * span : (half + 1) * span, h * HEAD_DIM : (h + 1) * HEAD_DIM] = o.T.astype(bf)
                lse_ref[half, h : h + 1, :] = m_ref[half, h : h + 1, :] * coef + jnp.log2(sums)


def attn_state(heads, span):
    return (shape(2, heads, span), shape(2, heads, HEAD_DIM + EXTRA, span))


def attn_fwd_own(q, kv, coef):
    _, heads, span, _ = q.shape
    return call(
        functools.partial(attn_fwd_own_kernel, coef), "attn_fwd_own", attn_state(heads, span), [q, kv],
        [pltpu.VMEM((HEAD_DIM + EXTRA, 2 * span), bf)], flops=24 * heads * span * span * HEAD_DIM, limit=20,
    )


def attn_fwd_pieces(flags, indices, q, pieces, state, coef, last):
    _, heads, span, _ = q.shape
    outs = attn_state(heads, span)
    if last:
        outs = (shape(2 * span, heads * HEAD_DIM, dtype=bf), shape(2, heads, span)) + outs
    return call(
        functools.partial(attn_fwd_pieces_kernel, coef, indices, last), "attn_fwd_pieces", outs, [flags, q, *pieces, *state],
        [pltpu.VMEM((HEAD_DIM + EXTRA, 2 * span), bf)], flops=16 * len(pieces) * heads * span * span * HEAD_DIM, smem=1, limit=20,
    )


def bwd_block(s, dp, lse_ref, delta_ref, half, h, coef, mask):
    p = jnp.exp2(s * coef - lse_ref[half, h : h + 1, :])
    if mask is not None:
        p = jnp.where(mask, p, 0.0)
    ds = p * (dp - delta_ref[half, h : h + 1, :])
    return p.astype(bf), ds.astype(bf)

def attn_bwd_kernel(coef, scale, indices, own, has_state, flag_ref, q_ref, do_ref, lse_ref, delta_ref, *refs):
    n = len(indices)
    kv_refs = refs[:n]
    k = n
    if has_state:
        dq_in = refs[k]; k += 1
    dkv_refs = refs[k : k + n]
    dq_ref, kt, pbuf, sbuf = refs[k + n :]
    heads, span = q_ref.shape[1], q_ref.shape[2]
    if has_state:
        dq_ref[...] = dq_in[...]
    else:
        dq_ref[...] = jnp.zeros_like(dq_ref)
    def do_item(kv_ref, items, keyrows, mask_of):
        nk = keyrows.stop - keyrows.start
        def first(it):
            i, half, h = it
            return nt(kv_ref[keyrows, :HEAD_DIM], q_ref[half, h]), nt(kv_ref[keyrows, HEAD_DIM:], do_ref[half, h])
        def second(it, sd):
            i, half, h = it
            p, ds = bwd_block(sd[0], sd[1], lse_ref, delta_ref, half, h, coef, mask_of(half))
            cols = slice((i * heads + h) * span, (i * heads + h + 1) * span)
            pbuf[:nk, cols] = p
            sbuf[:nk, cols] = ds
            return ds
        def third(it, ds):
            i, half, h = it
            dq_ref[half, h] += nn(kt[:, keyrows], ds)
        pipelined_three([(i, half, h) for i, half in enumerate(items) for h in range(heads)], first, second, third)
        width = len(items) * heads * span
        lo = items[0]
        q_all = q_ref[lo : lo + len(items)].reshape(width, HEAD_DIM)
        do_all = do_ref[lo : lo + len(items)].reshape(width, HEAD_DIM)
        return nn(sbuf[:nk, :width], q_all) * scale, nn(pbuf[:nk, :width], do_all)
    for i in range(n):
        kv_ref, out = kv_refs[i], dkv_refs[i]
        kt[...] = kv_ref[:, :HEAD_DIM].astype(f32).T.astype(bf)
        lo, hi, both = slice(0, span), slice(span, 2 * span), slice(0, 2 * span)
        if own and i == 0:
            mask = future_mask(span)
            dk, dv = do_item(kv_ref, [0, 1], lo, lambda half: mask if half == 0 else None)
            out[lo, :HEAD_DIM] = dk.astype(bf)
            out[lo, HEAD_DIM:] = dv.astype(bf)
            dk, dv = do_item(kv_ref, [1], hi, lambda half: mask)
            out[hi, :HEAD_DIM] = dk.astype(bf)
            out[hi, HEAD_DIM:] = dv.astype(bf)
        else:
            flag = flag_ref[indices[i]]

            def first(item, kv_ref=kv_ref, flag=flag):
                (keys, half), h = halves_of(flag, item[0]), item[1]
                rows = pl.ds(pl.multiple_of(keys * span, span), span)
                return nt(kv_ref[rows, :HEAD_DIM], q_ref[half, h]), nt(kv_ref[rows, HEAD_DIM:], do_ref[half, h])

            def second(item, sd, flag=flag):
                turn, h = item
                half = halves_of(flag, turn)[1]
                p, ds = bwd_block(sd[0], sd[1], lse_ref, delta_ref, half, h, coef, None)
                cols = slice(h * span, (h + 1) * span)
                pbuf[turn * span : (turn + 1) * span, cols] = p
                sbuf[turn * span : (turn + 1) * span, cols] = ds
                return ds

            def third(item, ds, flag=flag):
                (keys, half), h = halves_of(flag, item[0]), item[1]
                dq_ref[half, h] += nn(kt[:, pl.ds(pl.multiple_of(keys * span, span), span)], ds)

            pipelined_three([(turn, h) for turn in range(2) for h in range(heads)], first, second, third)
            width = heads * span
            both = []
            for turn in range(2):
                keys, half = halves_of(flag, turn)
                rows = slice(turn * span, (turn + 1) * span)
                both.append((
                    nn(sbuf[rows, :width], q_ref[half].reshape(width, HEAD_DIM)) * scale,
                    nn(pbuf[rows, :width], do_ref[half].reshape(width, HEAD_DIM)),
                ))
            earlier = flag.astype(f32)
            for part in range(2):
                cols = slice(part * HEAD_DIM, (part + 1) * HEAD_DIM)
                out[lo, cols] = (both[0][part] + both[1][part] * earlier).astype(bf)
                out[hi, cols] = (both[1][part] * (1.0 - earlier)).astype(bf)


def attn_bwd(flags, indices, q, do, lse, delta, pieces, dq_state, coef, scale, own):
    _, heads, span, _ = q.shape
    n = len(pieces)
    outs = tuple(jax.ShapeDtypeStruct((2 * span, 2 * HEAD_DIM), bf) for _ in range(n)) + (jax.ShapeDtypeStruct((2, heads, HEAD_DIM, span), f32),)
    ins = [flags, q, do, lse, delta, *pieces] + ([dq_state] if dq_state is not None else [])
    return pl.pallas_call(functools.partial(attn_bwd_kernel, coef, scale, indices, own, dq_state is not None), out_shape=outs,
        in_specs=[SM] + [VM] * (len(ins) - 1), out_specs=(VM,) * len(outs),
        scratch_shapes=[pltpu.VMEM((HEAD_DIM, 2 * span), bf), pltpu.VMEM((2 * span, 2 * heads * span), bf), pltpu.VMEM((2 * span, 2 * heads * span), bf)],
        cost_estimate=pl.CostEstimate(flops=2*5*2*n*heads*span*span*HEAD_DIM*2, bytes_accessed=4_000_000, transcendentals=0),
        compiler_params=pltpu.CompilerParams(vmem_limit_bytes=30 << 20), name="attn_bwd_pieces")(*ins)


TILE = 512


def steps_of(columns, begin=0):
    edges = [begin, begin + TILE // 2, begin + TILE]
    while columns - edges[-1] > 2 * TILE:
        edges.append(edges[-1] + 2 * TILE)
    if columns - edges[-1] > TILE:
        edges.append(edges[-1] + TILE)
    edges.append(columns)
    return list(zip(edges, edges[1:]))


def act_back_kernel(bounds, own_ref, other_ref, wd_hbm, *refs):
    out_hbm, rows_ref, wd, out, in_sems, out_sems = refs[-6:]
    half, first = own_ref.shape[0], bounds[0][0]
    parts = [slice(low - first, high - first) for low, high in bounds]
    copies = [
        pltpu.make_async_copy(wd_hbm.at[low:high], wd.at[part], in_sems.at[i])
        for i, ((low, high), part) in enumerate(zip(bounds, parts))
    ]
    for copy in copies:
        copy.start()
    rows_ref[:half, :] = own_ref[...]
    rows_ref[half:, :] = other_ref[...]
    results = []
    for i, ((low, high), part) in enumerate(zip(bounds, parts)):
        copies[i].wait()
        out[:, part] = nt(rows_ref[...], wd[part, :]).astype(bf)
        result = pltpu.make_async_copy(out.at[:, part], out_hbm.at[:, low:high], out_sems.at[i])
        result.start()
        results.append(result)
    for result in results:
        result.wait()


def act_back(own, other, wd, bounds, held=None):
    half, width = own.shape
    columns, count = bounds[-1][1] - bounds[0][0], len(bounds)
    return pl.pallas_call(
        functools.partial(act_back_kernel, bounds),
        out_shape=pltpu.HBM((2 * half, wd.shape[0]), bf),
        in_specs=[VM, VM, HB] + ([] if held is None else [HB]),
        out_specs=HB,
        scratch_shapes=[
            pltpu.VMEM((2 * half, width), bf), pltpu.VMEM((columns, width), bf), pltpu.VMEM((2 * half, columns), bf),
            pltpu.SemaphoreType.DMA((count,)), pltpu.SemaphoreType.DMA((count,)),
        ],
        input_output_aliases={} if held is None else {3: 0},
        cost_estimate=pl.CostEstimate(flops=4 * half * width * columns, bytes_accessed=2 * width * columns, transcendentals=0),
        compiler_params=pltpu.CompilerParams(vmem_limit_bytes=30 << 20),
        name="act_back",
    )(own, other, in_hbm(wd), *([] if held is None else [in_hbm(held)]))


def whole(*dims):
    return pl.BlockSpec(dims, lambda i: (0,) * len(dims), pipeline_mode=pl.Buffered(1))


def ffn_kernel(
    tile, tiles, hidden, x_own, x_other, g_own, g_other, gact_ref, adgu_ref, auf_ref, wgu_ref, adf_ref, augu_ref,
    gx_own, gx_send, act_ref, flow_ref, dadgu_ref, dauf_ref, daugu_ref, dadf_ref,
    x_ref, g_ref, gx_acc, xlow, xlow_t, fback, fback_t, flow, back,
):
    step = pl.program_id(0)
    half = x_own.shape[0]

    @pl.when(step == 0)
    def prepare():
        for target, own, other in ((x_ref, x_own, x_other), (g_ref, g_own, g_other)):
            target[:half, :] = own[...]
            target[half:, :] = other[...]
        low = nt(x_ref[...], adgu_ref[...])
        xlow[...] = (low * 2.0).astype(bf)
        xlow_t[...] = low.T.astype(bf)
        fb = nt(g_ref[...], auf_ref[...])
        fback[...] = (fb * 2.0).astype(bf)
        fback_t[...] = fb.T.astype(bf)
        gx_acc[...] = jnp.zeros_like(gx_acc)
        flow[...] = jnp.zeros_like(flow)
        back[...] = jnp.zeros_like(back)

    def work(width):
        x = x_ref[...]
        wg, wu = wgu_ref[0, :, :width], wgu_ref[1, :, :width]
        aug, auu, adf = augu_ref[:RANK, :width], augu_ref[RANK:, :width], adf_ref[:, :width]
        gate = nn(x, wg) + nn(xlow[:, :RANK], aug)
        up = nn(x, wu) + nn(xlow[:, RANK:], auu)
        gact = gact_ref[:, :width].astype(f32) + nn(fback[...], adf)
        sig = 1.0 / (1.0 + jnp.exp(-gate))
        silu = gate * sig
        act = (silu * up).astype(bf)
        ggate = (gact * up * (sig + silu * (1.0 - sig))).astype(bf)
        gup = (gact * silu).astype(bf)
        act_ref[:, :width] = act
        flow[...] += nt(act, adf)
        gx_acc[...] += nt(ggate, wg) + nt(gup, wu)
        back[:, :RANK] += nt(ggate, aug)
        back[:, RANK:] += nt(gup, auu)
        daugu_ref[:RANK, :width] = nn(xlow_t[:RANK, :], ggate)
        daugu_ref[RANK:, :width] = nn(xlow_t[RANK:, :], gup)
        dadf_ref[:, :width] = nn(fback_t[...], act)

    tail = hidden - (tiles - 1) * tile
    if tail == tile:
        work(tile)
    else:
        @pl.when(step < tiles - 1)
        def body():
            work(tile)

        @pl.when(step == tiles - 1)
        def part():
            work(tail)

    @pl.when(step == tiles - 1)
    def finish():
        gx_acc[...] += nn((back[...] * 2.0).astype(bf), adgu_ref[...])
        gx_own[...] = gx_acc[:half, :]
        gx_send[...] = gx_acc[half:, :].astype(bf)
        flow_ref[...] = (flow[...] * 2.0).astype(bf)
        dadgu_ref[...] = nn(back[...].T.astype(bf), x_ref[...])
        dauf_ref[...] = nn(flow[...].T.astype(bf), g_ref[...])


def ffn(x_own, x_other, g_own, g_other, gact, adgu, auf, wgu, adf, augu, tile=TILE):
    rows, width = 2 * x_own.shape[0], x_own.shape[1]
    hidden = wgu.shape[2]
    tiles = -(-hidden // tile)
    half = rows // 2
    cols = lambda r: pl.BlockSpec((r, tile), lambda i: (0, i))
    outs = (
        shape(half, width), shape(half, width, dtype=bf), pltpu.HBM((rows, hidden), bf), shape(rows, RANK, dtype=bf),
        shape(2 * RANK, width), shape(RANK, width), shape(2 * RANK, hidden), shape(RANK, hidden),
    )
    return pl.pallas_call(
        functools.partial(ffn_kernel, tile, tiles, hidden),
        grid=(tiles,),
        out_shape=outs,
        in_specs=[whole(half, width)] * 4 + [cols(rows), whole(2 * RANK, width), whole(RANK, width),
                  pl.BlockSpec((2, width, tile), lambda i: (0, 0, i)), cols(RANK), cols(2 * RANK)],
        out_specs=(whole(half, width), whole(half, width), cols(rows), whole(rows, RANK), whole(2 * RANK, width),
                   whole(RANK, width), cols(2 * RANK), cols(RANK)),
        scratch_shapes=[
            pltpu.VMEM((rows, width), bf), pltpu.VMEM((rows, width), bf), pltpu.VMEM((rows, width), f32),
            pltpu.VMEM((rows, 2 * RANK), bf), pltpu.VMEM((2 * RANK, rows), bf), pltpu.VMEM((rows, RANK), bf),
            pltpu.VMEM((RANK, rows), bf), pltpu.VMEM((rows, RANK), f32), pltpu.VMEM((rows, 2 * RANK), f32),
        ],
        cost_estimate=pl.CostEstimate(flops=8 * rows * width * hidden, bytes_accessed=6 * width * hidden, transcendentals=rows * hidden),
        compiler_params=pltpu.CompilerParams(vmem_limit_bytes=36 << 20),
        name="ffn",
    )(x_own, x_other, in_hbm(g_own), in_hbm(g_other), in_hbm(gact), adgu, auf, in_hbm(wgu), adf, augu)


def down_kernel(bounds, start_refs, act_hbm, wd_hbm, total, act, wd, act_sems, wd_sems):
    low = bounds[0][0]
    copies = []
    for i, (begin, end) in enumerate(bounds):
        rows = slice(begin - low, end - low)
        copies.append((
            pltpu.make_async_copy(act_hbm.at[:, begin:end], act.at[:, rows], act_sems.at[i]),
            pltpu.make_async_copy(wd_hbm.at[begin:end], wd.at[rows], wd_sems.at[i]),
        ))
        for copy in copies[-1]:
            copy.start()
    total[...] = nn(start_refs[0][...], start_refs[1][...]) if len(start_refs) == 2 else start_refs[0][...]
    for i, (begin, end) in enumerate(bounds):
        rows = slice(begin - low, end - low)
        for copy in copies[i]:
            copy.wait()
        total[...] += nn(act[:, rows], wd[rows, :])


def down_first_kernel(bounds, flow_ref, auf_ref, act_hbm, wd_hbm, total, *scratch):
    down_kernel(bounds, (flow_ref, auf_ref), act_hbm, wd_hbm, total, *scratch)


def down_last_kernel(bounds, start_ref, act_hbm, wd_hbm, own_ref, send_ref, total, *scratch):
    down_kernel(bounds, (start_ref,), act_hbm, wd_hbm, total, *scratch)
    half = own_ref.shape[0]
    own_ref[...] = total[:half, :]
    send_ref[...] = total[half:, :].astype(bf)


def down(act, wd, start, bounds, last):
    rows, width = act.shape[0], wd.shape[1]
    half, columns, count = rows // 2, bounds[-1][1] - bounds[0][0], len(bounds)
    outs = (shape(half, width), shape(half, width, dtype=bf)) if last else (shape(rows, width),)
    scratch = [
        pltpu.VMEM((rows, columns), bf), pltpu.VMEM((columns, width), bf), pltpu.SemaphoreType.DMA((count,)),
        pltpu.SemaphoreType.DMA((count,)),
    ]
    return pl.pallas_call(
        functools.partial(down_last_kernel if last else down_first_kernel, bounds),
        out_shape=outs,
        in_specs=[VM] * len(start) + [HB, HB],
        out_specs=(VM,) * len(outs),
        scratch_shapes=([pltpu.VMEM((rows, width), f32)] if last else []) + scratch,
        cost_estimate=pl.CostEstimate(flops=2 * rows * width * columns, bytes_accessed=2 * width * columns, transcendentals=0),
        compiler_params=pltpu.CompilerParams(vmem_limit_bytes=28 << 20),
        name="down",
    )(*start, in_hbm(act), in_hbm(wd))


def per_device(
    tokens, cotangent, positions, adapter_choice, attn_gain, query_weight, query_bias, key_value_weight,
    key_value_bias, output_weight, ffn_gain, gate_upper_weight, down_weight, adapt_in, adapt_out,
):
    dp = lax.axis_index("dp")
    groups = lax.axis_size("seq")
    rings = groups // 2
    width, head_width = query_weight.shape
    heads = head_width // HEAD_DIM
    hidden = down_weight.shape[0]
    token_pos = positions[0]
    tok_count = token_pos.shape[0]
    span = tok_count // 2
    scale = HEAD_DIM ** (-0.5)
    coef = scale * math.log2(math.e)
    wide_in, wide_out = adapt_in.shape[2], adapt_out.shape[2]
    lanes_in = rounded_up(wide_in + 1, 128)
    lanes = lanes_in + rounded_up(wide_out, 128)
    widths = (width, head_width, hidden)
    sizes = (rings, wide_in, wide_out, lanes_in, widths)

    def to_pair(value):
        return lax.ppermute(value, "tensor", [(0, 1), (1, 0)])

    def to_other_sequence(value, pairs=((0, 1), (1, 0))):
        return lax.ppermute(value, "dp", list(pairs))

    def to_side(value):
        return lax.ppermute(value, "seq", [(i, i ^ 1) for i in range(groups)])

    def along_ring(value, steps):
        return lax.ppermute(value, "seq", [(i, (i + 2 * steps) % groups) for i in range(groups)])

    cycle = list(range(0, groups, 2)) + list(range(groups - 1, 0, -2))
    hops = [(cycle[i], cycle[(i + 1) % groups]) for i in range(groups)]

    def to_next(value):
        return lax.ppermute(value, "seq", hops)

    def to_last(value):
        return lax.ppermute(value, "seq", [(end, begin) for begin, end in hops])

    def after(value, *others):
        return lax.optimization_barrier((value, *others))[0]

    inputs, grad_out = tokens[0], cotangent[0]
    half = inputs.shape[0]
    attn_gain, ffn_gain = attn_gain[None], ffn_gain[None]

    def over_ring(piece):
        return [piece] + [along_ring(piece, step) for step in range(1, rings)]

    slice_own, slice_other = call(
        functools.partial(select_kernel, lanes_in, span), "select",
        [shape(RANK, lanes, dtype=bf)] * 2, [adapter_choice, positions, adapt_in, adapt_out],
        [
            pltpu.SMEM(adapter_choice.shape, jnp.int32), pltpu.SMEM(positions.shape, jnp.int32),
            pltpu.VMEM((2, RANK, wide_in), bf), pltpu.VMEM((2, RANK, wide_out), bf), pltpu.SemaphoreType.DMA((6,)),
        ],
        left=4,
    )
    slice_other = to_other_sequence(slice_other)
    lane = lax.broadcasted_iota(jnp.int32, (RANK, lanes), 1)
    run_lane = (lane >= wide_in) & (lane < lanes_in)
    grad_other = to_pair(after(grad_out, slice_own))
    slice_other = after(slice_other, grad_other)
    first_slice = jnp.where((dp == 0) | run_lane, slice_own, slice_other)
    second_slice = jnp.where(dp == 0, slice_other, slice_own)

    (normed,) = call(norm_kernel, "norm", [shape(half, width, dtype=bf)], [inputs, attn_gain])
    normed_other = to_pair(normed)
    arrived = over_ring(jnp.stack([first_slice, second_slice]))
    middle = 6 * TILE
    act_grad = act_back(grad_out, grad_other, down_weight, steps_of(middle))
    arrived[1] = after(arrived[1], act_grad)
    own_slices = jnp.stack([piece[0] for piece in arrived])
    own_second = jnp.stack([piece[1] for piece in arrived])
    side_slices = to_side(own_slices)
    pair_slices = to_pair(own_slices)
    normed_rows, query_dense, kv_dense = call(
        dense_kernel, "dense", [shape(tok_count, width, dtype=bf), shape(tok_count, head_width), shape(tok_count, 2 * HEAD_DIM)],
        [normed, after(normed_other, own_slices), query_weight, key_value_weight],
        flops=2 * tok_count * width * (head_width + 2 * HEAD_DIM),
    )
    frequency = jnp.power(rope_base, -(jnp.arange(HEAD_DIM // 2, dtype=f32) * 2.0) / HEAD_DIM)
    angles = token_pos.astype(f32)[:, None] * frequency[None, :]
    cosine, sine = jnp.cos(angles), jnp.sin(angles)
    cosine = jnp.concatenate([cosine, cosine], axis=1)
    sine = jnp.concatenate([-sine, sine], axis=1)

    side_slices = after(side_slices, kv_dense)
    first_slices = [own_slices, side_slices, pair_slices, to_pair(side_slices)]
    side_second = to_side(after(own_second, side_slices))
    slices_in = -(-4 * width // wide_in)
    slices_out = -(-(2 * width + 4 * HEAD_DIM) // wide_out)
    flags, adqkv, auq, auk, auv, ado, auo = call(
        functools.partial(unpack_first_kernel, *sizes), "unpack_first",
        [shape(groups, dtype=jnp.int32)]
        + [
            shape(*dims, dtype=bf)
            for dims in (
                (3 * RANK, width), (RANK, head_width), (RANK, HEAD_DIM), (RANK, HEAD_DIM), (RANK, head_width), (RANK, width),
            )
        ],
        list(first_slices),
        [
            pltpu.VMEM((2 * groups, RANK, lanes), bf),
            pltpu.VMEM((RANK, rounded_up(slices_in * wide_in, 128) + 256), f32),
            pltpu.VMEM((RANK, rounded_up(slices_out * wide_out, 128) + 256), f32),
            pltpu.SMEM((groups,), jnp.int32),
        ],
        out_specs=(SM,) + (VM,) * 6,
    )
    kv, low, low_t = call(
        key_value_kernel, "key_value",
        [shape(tok_count, 2 * HEAD_DIM, dtype=bf), shape(tok_count, 3 * RANK, dtype=bf), shape(3 * RANK, tok_count, dtype=bf)],
        [normed_rows, kv_dense, key_value_bias, adqkv, auk, auv, cosine, sine],
        flops=2 * tok_count * width * 2 * RANK,
    )

    (queries,) = call(
        query_kernel, "query", [shape(2, heads, span, HEAD_DIM, dtype=bf)],
        [query_dense, query_bias[None], low, auq, cosine, sine], flops=2 * tok_count * width * RANK,
    )
    state = attn_fwd_own(queries, kv, coef)
    pieces, from_last, from_next = [kv], kv, kv
    for step in range(1, rings + 1):
        from_last, from_next = to_next(from_last), to_last(from_next)
        if step == 1:
            bounds = [(middle, middle + TILE // 2), (middle + TILE // 2, middle + 2 * TILE), (middle + 2 * TILE, hidden)]
            act_grad = act_back(after(grad_out, state[0], side_second), grad_other, down_weight, bounds, act_grad)
            from_last = after(from_last, act_grad)
        if step < rings:
            from_last, from_next, _ = lax.optimization_barrier((from_last, from_next, state[0]))
        if step == rings:
            pair_second = to_pair(after(own_second, pieces[-1]))
            state = (after(state[0], pair_second), *state[1:])
        pieces += [from_last, from_next][: 2 if step < rings else 1]
        indices = tuple(range(2 * step - 1, len(pieces)))
        result = attn_fwd_pieces(flags, indices, queries, pieces[2 * step - 1 :], state, coef, step == rings)
        state = result[-2:]
    mixed, lse = result[0], result[1]

    branch_send, mix_low, mix_low_t = call(
        mix_send_kernel, "mix_send",
        [shape(half, width, dtype=bf), shape(tok_count, RANK, dtype=bf), shape(RANK, tok_count, dtype=bf)],
        [mixed, output_weight, ado, auo], flops=2 * half * width * head_width,
    )
    branch_other = to_pair(branch_send)
    second_slices = [own_second, side_second, pair_second, to_pair(side_second)]
    (branch_own,) = call(
        mix_own_kernel, "mix_own", [shape(half, width)], [mixed, output_weight, mix_low, auo],
        flops=2 * half * width * head_width,
    )
    hidden_rows, normed_ffn = call(
        residual_kernel, "residual", [shape(half, width), shape(half, width, dtype=bf)],
        [inputs, branch_own, after(branch_other, branch_own, second_slices[3]), ffn_gain],
    )
    begin_in, begin_out, first_in, first_out = bases(wide_in, wide_out, widths)
    adgu, augu, adf, auf = call(
        functools.partial(unpack_second_kernel, *sizes), "unpack_second",
        [shape(*dims, dtype=bf) for dims in ((2 * RANK, width), (2 * RANK, hidden), (RANK, hidden), (RANK, width))],
        list(first_slices) + list(second_slices),
        [
            pltpu.VMEM((4 * groups, RANK, lanes), bf),
            pltpu.VMEM((RANK, rounded_up(4 * groups * wide_in, 128) + 256 - first_in), f32),
            pltpu.VMEM((RANK, rounded_up(4 * groups * wide_out, 128) + 256 - first_out), f32),
        ],
    )
    gx_own, gx_send, act, flow, dadgu, dauf, daugu, dadf = ffn(
        normed_ffn, to_pair(normed_ffn), grad_out, grad_other, act_grad, adgu, auf, gate_upper_weight, adf, augu
    )
    ad_lanes = rounded_up(4 * groups * wide_in, 128) + 256
    au_lanes = rounded_up(4 * groups * wide_out, 128) + 256

    def added(*values):
        total = values[0].astype(f32)
        for value in values[1:]:
            total = total + value.astype(f32)
        return total.astype(bf)

    grad_hidden, grad_low = call(
        hidden_back_kernel, "hidden_back", [shape(half, width), shape(half, width, dtype=bf)],
        [hidden_rows, grad_out, gx_own, to_pair(gx_send), ffn_gain],
    )
    grad_low_other = to_pair(grad_low)
    fixed = [output_weight, ado, auo, mixed, mix_low_t]
    outs = [shape(2, heads, span, HEAD_DIM, dtype=bf), shape(2, heads, span), shape(RANK, head_width), shape(RANK, width)]
    partial = call(
        functools.partial(mix_back_kernel, True), "mix_back", outs, [grad_low, *fixed], flops=2 * half * width * head_width,
    )
    grad_mixed, delta, dado, dauo = call(
        functools.partial(mix_back_kernel, False), "mix_back_other", outs,
        [after(grad_low_other, partial[0]), *fixed, *partial], flops=2 * half * width * head_width,
        aliases={6 + i: i for i in range(4)},
    )

    def backward(indices, state_dq):
        return attn_bwd(
            flags, indices, queries, grad_mixed, lse, delta, [pieces[index] for index in indices], state_dq, coef, scale,
            indices == (0,),
        )

    state_dq, from_last, from_next = None, None, None
    for step in range(rings, 0, -1):
        onward, *returned, state_dq = backward((2 * rings - 1,) if step == rings else (2 * step, 2 * step - 1), state_dq)
        if from_last is not None:
            onward = added(onward, from_last)
        if from_next is not None:
            returned = [added(returned[0], from_next)]
        from_last = to_next(onward)
        if returned:
            from_next = to_last(returned[0])
        state_dq = after(state_dq, onward, *returned)
    own_term, state_dq = backward((0,), state_dq)
    gn_query, dadq, dauq = call(
        functools.partial(back_query_kernel, scale), "back_query",
        [shape(tok_count, width), shape(RANK, width), shape(RANK, head_width)],
        [state_dq, query_weight, adqkv, auq, low_t, normed_rows, cosine, sine],
        [pltpu.VMEM((tok_count, head_width), bf)], flops=2 * tok_count * width * head_width,
    )
    from_last = after(from_last, gn_query)
    gn_own, gn_send, dadkv, dauk, dauv = call(
        back_key_value_kernel, "back_key_value",
        [
            shape(half, width), shape(half, width, dtype=bf), shape(2 * RANK, width), shape(RANK, HEAD_DIM),
            shape(RANK, HEAD_DIM),
        ],
        [
            own_term, gn_query, key_value_weight, adqkv, auk, auv, low_t, normed_rows, cosine, sine, from_last, from_next,
        ],
        [pltpu.VMEM((tok_count, width), f32), pltpu.VMEM((tok_count, 2 * RANK), f32)],
        flops=2 * tok_count * width * 2 * HEAD_DIM, limit=20,
    )
    (packed,) = call(
        functools.partial(pack_kernel, *sizes), "pack", [shape(2, 2, rings, 2, RANK, lanes, dtype=bf)],
        [dadq, dadkv, dado, dadgu, dadf, dauq, dauk, dauv, dauo, daugu, dauf],
        [pltpu.VMEM((RANK, ad_lanes), f32), pltpu.VMEM((RANK, au_lanes), f32)],
    )
    from_pair = to_pair(packed[1])
    near, far = added(packed[0, 0], from_pair[0]), added(packed[0, 1, 1:], from_pair[1, 1:])
    from_side = to_side(far)
    own_side = to_side(after(added(packed[0, 1, 0], from_pair[1, 0]), far))
    middle = 6 * TILE
    (out_total,) = down(after(act, far), down_weight, (flow, auf), steps_of(middle), False)
    from_side = after(from_side, out_total)
    sums = [added(near[place], from_side[place - 1]) for place in range(1, rings)]
    from_ring = [along_ring(sums[place - 1], -place) for place in range(1, rings)]
    out_own, out_send = down(after(act, *sums), down_weight, (out_total,), steps_of(hidden, middle), True)
    from_ring[0] = after(from_ring[0], out_own)
    total = added(near[0], own_side, *from_ring)
    (grad_tokens,) = call(
        token_back_kernel, "token_back", [shape(half, width)],
        [inputs, grad_hidden, gn_own, after(to_pair(gn_send), total), attn_gain],
    )
    output = (hidden_rows + (out_own + to_pair(out_send).astype(f32))).astype(bf)
    other_total = after(to_other_sequence(total[1]), output, grad_tokens)
    factor = adapter_scale * (adapter_choice.shape[0] * tok_count * groups) ** (-0.5)
    adapt_in_grad, adapt_out_grad = call(
        functools.partial(place_kernel, lanes_in, factor), "place",
        [shape(*adapt_in.shape), shape(*adapt_out.shape)],
        [adapter_choice, total[0], other_total], smem=1,
    )
    return (output[None], grad_tokens[None], adapt_in_grad, adapt_out_grad)


def solution(mesh):
    return jax.shard_map(
        per_device,
        mesh=mesh,
        in_specs=(
            P("dp", ("seq", "tensor"), None),
            P("dp", ("seq", "tensor"), None),
            P("dp", "seq"),
            P(),
            P(),
            P(None, "tensor"),
            P("tensor"),
            P(None, None, "tensor"),
            P(None, "tensor"),
            P("tensor", None),
            P(),
            P(None, None, "tensor"),
            P("tensor", None),
            P(None, None, ("dp", "seq", "tensor")),
            P(None, None, ("dp", "seq", "tensor")),
        ),
        out_specs=(
            P("dp", ("seq", "tensor"), None),
            P("dp", ("seq", "tensor"), None),
            P(None, None, ("dp", "seq", "tensor")),
            P(None, None, ("dp", "seq", "tensor")),
        ),
        check_vma=False,
    )
```

```python
import functools
import math

import jax
import jax.numpy as jnp
from jax import lax
from jax.experimental import pallas as pl
from jax.experimental.pallas import tpu as pltpu
from jax.sharding import PartitionSpec as P

HEAD_DIM = 128
RANK = 16
eps = 1e-06
adapter_scale = 2.0
rope_base = 1000000.0
mask_fill = -1e30
bf = jnp.bfloat16
f32 = jnp.float32
VM = pl.BlockSpec(memory_space=pltpu.VMEM)
SM = pl.BlockSpec(memory_space=pltpu.SMEM)


def nn(a, b):
    return jnp.dot(a, b, preferred_element_type=f32)


def nt(a, b):
    return lax.dot_general(a, b, (((1,), (1,)), ((), ())), preferred_element_type=f32)


def shape(*dims, dtype=f32):
    return jax.ShapeDtypeStruct(dims, dtype)


def call(kernel, name, out, ins, scratch=(), flops=0, smem=0, out_specs=None, limit=16, left=0, aliases=None):
    moved = sum(math.prod(v.shape) * v.dtype.itemsize for v in list(ins) + list(out))
    ins = list(ins[: len(ins) - left]) + [in_hbm(value) for value in ins[len(ins) - left :]]
    return pl.pallas_call(
        kernel,
        out_shape=tuple(out),
        in_specs=[SM] * smem + [VM] * (len(ins) - smem - left) + [HB] * left,
        out_specs=out_specs or (VM,) * len(out),
        scratch_shapes=list(scratch),
        input_output_aliases=aliases or {},
        cost_estimate=pl.CostEstimate(flops=flops, bytes_accessed=moved, transcendentals=0),
        compiler_params=pltpu.CompilerParams(vmem_limit_bytes=limit << 20),
        name=name,
    )(*ins)


HB = pl.BlockSpec(memory_space=pltpu.HBM)


def in_hbm(value):
    return pltpu.with_memory_space_constraint(value, pltpu.HBM)


def rounded_up(value, unit):
    return -(-value // unit) * unit


def select_kernel(
    lanes_in, span, choice_hbm, pos_hbm, in_ref, out_ref, own_ref, other_ref, choice_ref, pos_ref, held_in, held_out, sems
):
    wide_in, wide_out = in_ref.shape[2], out_ref.shape[2]
    dp = lax.axis_index("dp")
    choice_copy = pltpu.make_async_copy(choice_hbm, choice_ref, sems.at[4])
    pos_copy = pltpu.make_async_copy(pos_hbm, pos_ref, sems.at[5])
    choice_copy.start()
    pos_copy.start()
    choice_copy.wait()
    copies = []
    for slot, sequence in ((0, dp), (1, 1 - dp)):
        chosen = choice_ref[sequence]
        copies.append(pltpu.make_async_copy(in_ref.at[chosen], held_in.at[slot], sems.at[2 * slot]))
        copies.append(pltpu.make_async_copy(out_ref.at[chosen], held_out.at[slot], sems.at[2 * slot + 1]))
    for copy in copies:
        copy.start()
    pos_copy.wait()
    run = jnp.full((RANK, lanes_in), pos_ref[0, 0] // span, jnp.int32).astype(f32).astype(bf)
    for target in (own_ref, other_ref):
        target[...] = jnp.zeros_like(target)
        target[:, :lanes_in] = run
    for copy in copies:
        copy.wait()
    for slot, target in ((0, own_ref), (1, other_ref)):
        target[:, :wide_in] = held_in[slot]
        target[:, lanes_in : lanes_in + wide_out] = held_out[slot]


def column(begin, size):
    return pl.ds(pl.multiple_of(begin, 128), size)


def source_of(place, side, rings, seq):
    ring = lax.rem(seq // 2 - place + rings, rings)
    own_side = lax.rem(seq, 2)
    return ring * 2 + (own_side if side == 0 else 1 - own_side)


def spread(slots, target, begin, wide, first, low, high):
    held = rounded_up(wide, 128)
    inside = lax.broadcasted_iota(jnp.int32, (RANK, held), 1) < wide
    target[...] = jnp.zeros_like(target)
    for index in range(low // wide, -(-high // wide)):
        part = jnp.where(inside, slots[index, :, begin : begin + held].astype(f32), 0.0)
        part = jnp.concatenate([part, jnp.zeros((RANK, 128), f32)], axis=1)
        offset = index * wide - first
        base = offset // 128 * 128
        if offset != base:
            part = pltpu.roll(part, offset - base, 1)
        target[:, base : base + held + 128] += part


def collect(slots, refs, rings, part):
    seq, shard = lax.axis_index("seq"), lax.axis_index("tensor")
    for number, ref in enumerate(refs):
        side, core = number % 2, shard if number < 2 else 1 - shard
        for place in range(rings):
            slots[part * 4 * rings + source_of(place, side, rings, seq) * 2 + core] = ref[place]


def unpack_first_kernel(
    rings, wide_in, wide_out, lanes_in, widths, own, own_side, pair, pair_side,
    flags_ref, adqkv, auq, auk, auv, ado, auo, slots, ad, au, runs,
):
    shard, seq = lax.axis_index("tensor"), lax.axis_index("seq")
    width, head_width, hidden = widths
    for place in range(rings):
        for side, ref in ((0, own), (1, own_side)):
            run = jnp.max(ref[place, :, wide_in:lanes_in].astype(f32))
            run = run.astype(jnp.int32)
            runs[source_of(place, side, rings, seq)] = jnp.minimum(run, 4 * rings - 1 - run)
    groups = 2 * rings
    own_run = jnp.max(own[0, :, wide_in:lanes_in].astype(f32)).astype(jnp.int32)
    swap = (own_run >= groups).astype(jnp.int32)
    place = jnp.where(lax.rem(seq, 2) == 0, seq // 2, groups - 1 - seq // 2)
    for index in range(groups):
        step = (index + 1) // 2
        other = lax.rem(place + (groups - step if index % 2 == 1 else step), groups)
        source = jnp.where(other < rings, 2 * other, 2 * (groups - 1 - other) + 1)
        flag = swap if index == 0 else (runs[source] < runs[seq]).astype(jnp.int32)
        flags_ref[index : index + 1, :] = jnp.full((1, 128), flag, jnp.int32).astype(f32)
    collect(slots, (own, own_side, pair, pair_side), rings, 0)
    spread(slots, ad, 0, wide_in, 0, 0, 4 * width)
    spread(slots, au, lanes_in, wide_out, 0, 0, 2 * width + 4 * HEAD_DIM)
    for index in range(3):
        adqkv[index * RANK : (index + 1) * RANK, :] = ad[:, index * width : (index + 1) * width].astype(bf)
    ado[...] = ad[:, column(3 * width + shard * head_width, head_width)].astype(bf)
    auq[...] = au[:, column(shard * head_width, head_width)].astype(bf)
    auk[...] = au[:, column(width + shard * HEAD_DIM, HEAD_DIM)].astype(bf)
    auv[...] = au[:, column(width + (2 + shard) * HEAD_DIM, HEAD_DIM)].astype(bf)
    base = width + 4 * HEAD_DIM
    auo[...] = au[:, base : base + width].astype(bf)


def bases(wide_in, wide_out, widths):
    width = widths[0]
    begin_in, begin_out = 4 * width, 2 * width + 4 * HEAD_DIM
    return begin_in, begin_out, begin_in // wide_in * wide_in // 128 * 128, begin_out // wide_out * wide_out // 128 * 128


def unpack_second_kernel(
    rings, wide_in, wide_out, lanes_in, widths, *refs
):
    firsts, seconds = refs[:4], refs[4:8]
    adgu, augu, adf, auf, slots, ad, au = refs[8:]
    shard = lax.axis_index("tensor")
    width, head_width, hidden = widths
    collect(slots, firsts, rings, 0)
    collect(slots, seconds, rings, 1)
    begin_in, begin_out, first_in, first_out = bases(wide_in, wide_out, widths)
    total_in, total_out = 8 * rings * wide_in, 8 * rings * wide_out
    spread(slots, ad, 0, wide_in, first_in, begin_in, total_in)
    spread(slots, au, lanes_in, wide_out, first_out, begin_out, total_out)
    base = begin_in - first_in
    for index in range(2):
        adgu[index * RANK : (index + 1) * RANK, :] = ad[:, base + index * width : base + (index + 1) * width].astype(bf)
    adf[...] = ad[:, column(base + 2 * width + shard * hidden, hidden)].astype(bf)
    base = begin_out - first_out
    for index in range(2):
        augu[index * RANK : (index + 1) * RANK, :] = au[
            :, column(base + (2 * index + shard) * hidden, hidden)
        ].astype(bf)
    auf[...] = au[:, base + 4 * hidden : base + 4 * hidden + width].astype(bf)


def put_slices(rings, wide_in, wide_out, lanes_in, ad, au, limits, parts, write):
    dp, seq = lax.axis_index("dp"), lax.axis_index("seq")
    for index in range(4 * rings * parts):
        to_dp, to_seq, to_core = index // (4 * rings), index // 2 % (2 * rings), index % 2
        pieces = []
        for source, wide, (low, high, first) in ((ad, wide_in, limits[0]), (au, wide_out, limits[1])):
            held = rounded_up(wide, 128)
            if index * wide >= high or (index + 1) * wide <= low:
                part = jnp.zeros((RANK, held), f32)
            else:
                offset = index * wide - first
                base = offset // 128 * 128
                part = source[:, base : base + held + 128]
                if offset != base:
                    part = pltpu.roll(part, held + 128 - (offset - base), 1)
                part = part[:, :held]
            pieces.append(part)
            if source is ad and lanes_in > held:
                pieces.append(jnp.zeros((RANK, lanes_in - held), f32))
        packed = jnp.concatenate(pieces, axis=1).astype(bf)
        place = lax.rem(seq // 2 - to_seq // 2 + rings, rings)
        write(to_seq, to_core, place, lax.rem(dp + to_dp, 2), packed)


def pack_kernel(
    rings, wide_in, wide_out, lanes_in, widths,
    dadq, dadkv, dado, dadgu, dadf, dauq, dauk, dauv, dauo, daugu, dauf, out_ref, ad, au,
):
    shard, side = lax.axis_index("tensor"), lax.rem(lax.axis_index("seq"), 2)
    width, head_width, hidden = widths
    ad[...] = jnp.zeros_like(ad)
    au[...] = jnp.zeros_like(au)
    ad[:, :width] = dadq[...]
    for index in range(2):
        ad[:, (1 + index) * width : (2 + index) * width] = dadkv[index * RANK : (index + 1) * RANK, :]
        ad[:, (4 + index) * width : (5 + index) * width] = dadgu[index * RANK : (index + 1) * RANK, :]
    ad[:, column(3 * width + shard * head_width, head_width)] = dado[...]
    ad[:, column(6 * width + shard * hidden, hidden)] = dadf[...]
    au[:, column(shard * head_width, head_width)] = dauq[...]
    au[:, column(width + shard * HEAD_DIM, HEAD_DIM)] = dauk[...]
    au[:, column(width + (2 + shard) * HEAD_DIM, HEAD_DIM)] = dauv[...]
    base = width + 4 * HEAD_DIM
    au[:, base : base + width] = dauo[...]
    base = base + width
    for index in range(2):
        au[:, column(base + (2 * index + shard) * hidden, hidden)] = daugu[index * RANK : (index + 1) * RANK, :]
    au[:, base + 4 * hidden : base + 4 * hidden + width] = dauf[...]

    def write(to_seq, to_core, place, part, packed):
        out_ref[lax.rem(shard + to_core, 2), lax.rem(side + to_seq % 2, 2), place, part] = packed

    limits = ((0, 8 * rings * wide_in, 0), (0, 8 * rings * wide_out, 0))
    put_slices(rings, wide_in, wide_out, lanes_in, ad, au, limits, 2, write)


def place_kernel(lanes_in, factor, choice_ref, own_ref, other_ref, in_ref, out_ref):
    wide_in, wide_out = in_ref.shape[2], out_ref.shape[2]
    dp = lax.axis_index("dp")
    in_ref[...] = jnp.zeros_like(in_ref)
    out_ref[...] = jnp.zeros_like(out_ref)
    for ref, sequence in ((own_ref, dp), (other_ref, 1 - dp)):
        chosen = choice_ref[sequence]
        part = ref[...].astype(f32) * factor
        in_ref[chosen] = in_ref[chosen] + part[:, :wide_in]
        out_ref[chosen] = out_ref[chosen] + part[:, lanes_in : lanes_in + wide_out]


def factor_of(rows):
    return lax.rsqrt(jnp.mean(rows * rows, axis=-1, keepdims=True) + eps)


def norm_back(rows, gain, grad):
    factor = factor_of(rows)
    scaled = rows * factor
    grad_scaled = grad * gain
    return factor * (grad_scaled - scaled * jnp.mean(grad_scaled * scaled, axis=-1, keepdims=True))


def norm_kernel(rows_ref, gain_ref, normed_ref):
    rows = rows_ref[...].astype(f32)
    normed_ref[...] = (rows * factor_of(rows) * gain_ref[...].astype(f32)).astype(bf)


def residual_kernel(rows_ref, own_ref, other_ref, gain_ref, hidden_ref, normed_ref):
    rows = rows_ref[...].astype(f32) + (own_ref[...] + other_ref[...].astype(f32))
    hidden_ref[...] = rows
    normed_ref[...] = (rows * factor_of(rows) * gain_ref[...].astype(f32)).astype(bf)


def hidden_back_kernel(hidden_ref, grad_ref, own_ref, other_ref, gain_ref, out_ref, low_ref):
    grad = own_ref[...] + other_ref[...].astype(f32)
    total = grad_ref[...].astype(f32) + norm_back(hidden_ref[...], gain_ref[...].astype(f32), grad)
    out_ref[...] = total
    low_ref[...] = total.astype(bf)


def token_back_kernel(rows_ref, grad_ref, own_ref, other_ref, gain_ref, out_ref):
    grad = own_ref[...] + other_ref[...].astype(f32)
    out_ref[...] = grad_ref[...] + norm_back(rows_ref[...].astype(f32), gain_ref[...].astype(f32), grad)


def flag_of(flag_ref, index):
    return jnp.max(flag_ref[index : index + 1, :]).astype(jnp.int32)


def place_of(flag_ref, half):
    swap = flag_of(flag_ref, 0)
    return half + swap - 2 * half * swap


def place_rows(flag_ref, half, span):
    return pl.ds(pl.multiple_of(place_of(flag_ref, half) * span, span), span)


def turned(rows, cosine, sine):
    return rows * cosine + pltpu.roll(rows, HEAD_DIM // 2, 1) * sine


def dense_kernel(own_ref, other_ref, wq_ref, wkv_ref, rows_ref, query_ref, kv_ref):
    shard = lax.axis_index("tensor")
    half = own_ref.shape[0]
    rows_ref[pl.ds(pl.multiple_of(shard * half, half), half), :] = own_ref[...]
    rows_ref[pl.ds(pl.multiple_of((1 - shard) * half, half), half), :] = other_ref[...]
    rows = rows_ref[...]
    query_ref[...] = nn(rows, wq_ref[...])
    kv_ref[:, :HEAD_DIM] = nn(rows, wkv_ref[0])
    kv_ref[:, HEAD_DIM:] = nn(rows, wkv_ref[1])


def key_value_kernel(
    flag_ref, rows_ref, dense_ref, bias_ref, adqkv_ref, auk_ref, auv_ref, cos_ref, sin_ref, kv_ref, low_ref, low_t_ref
):
    low = nt(rows_ref[...], adqkv_ref[...])
    low_ref[...] = (2.0 * low).astype(bf)
    low_t_ref[...] = low.T.astype(bf)
    key = dense_ref[:, :HEAD_DIM] + bias_ref[0:1, :].astype(f32) + nn(low_ref[:, RANK : 2 * RANK], auk_ref[...])
    value = dense_ref[:, HEAD_DIM:] + bias_ref[1:2, :].astype(f32) + nn(low_ref[:, 2 * RANK :], auv_ref[...])
    key, value = turned(key, cos_ref[...], sin_ref[...]).astype(bf), value.astype(bf)
    span = key.shape[0] // 2
    for half in range(2):
        rows = place_rows(flag_ref, half, span)
        kv_ref[rows, :HEAD_DIM] = key[half * span : (half + 1) * span]
        kv_ref[rows, HEAD_DIM:] = value[half * span : (half + 1) * span]


def query_kernel(flag_ref, dense_ref, bias_ref, low_ref, auq_ref, cos_ref, sin_ref, q_ref):
    heads, span = q_ref.shape[1], q_ref.shape[2]
    query = dense_ref[...] + bias_ref[...].astype(f32) + nn(low_ref[:, :RANK], auq_ref[...])
    for h in range(heads):
        head = turned(query[:, h * HEAD_DIM : (h + 1) * HEAD_DIM], cos_ref[...], sin_ref[...]).astype(bf)
        q_ref[place_of(flag_ref, 0), h] = head[:span]
        q_ref[place_of(flag_ref, 1), h] = head[span:]


def rows_of(own, half):
    shard = lax.axis_index("tensor")
    return pl.ds(pl.multiple_of((shard if own else 1 - shard) * half, half), half)


def mix_send_kernel(mixed_ref, wo_ref, ado_ref, auo_ref, send_ref, low_ref, low_t_ref):
    low = nt(mixed_ref[...], ado_ref[...])
    low_ref[...] = (2.0 * low).astype(bf)
    low_t_ref[...] = low.T.astype(bf)
    rows = rows_of(False, send_ref.shape[0])
    send_ref[...] = (nn(mixed_ref[rows, :], wo_ref[...]) + nn(low_ref[rows, :], auo_ref[...])).astype(bf)


def mix_own_kernel(mixed_ref, wo_ref, low_ref, auo_ref, own_ref):
    rows = rows_of(True, own_ref.shape[0])
    own_ref[...] = nn(mixed_ref[rows, :], wo_ref[...]) + nn(low_ref[rows, :], auo_ref[...])


def mix_back_kernel(own, flag_ref, rows_ref, wo_ref, ado_ref, auo_ref, mixed_ref, low_t_ref, *refs):
    do_ref, delta_ref, dado_ref, dauo_ref = refs[-4:]
    half = rows_ref.shape[0]
    heads = do_ref.shape[1]
    part = place_of(flag_ref, lax.axis_index("tensor") if own else 1 - lax.axis_index("tensor"))
    places = rows_of(own, half)
    rows, mixed = rows_ref[...], mixed_ref[places, :]
    back = nt(rows, auo_ref[...])
    grad = (nt(rows, wo_ref[...]) + nn((2.0 * back).astype(bf), ado_ref[...])).astype(bf)
    dado = nn(back.T.astype(bf), mixed)
    dauo = nn(low_t_ref[:, places], rows)
    dado_ref[...] = dado if own else refs[2][...] + dado
    dauo_ref[...] = dauo if own else refs[3][...] + dauo
    for h in range(heads):
        cols = slice(h * HEAD_DIM, (h + 1) * HEAD_DIM)
        product = (grad[:, cols].astype(f32) * mixed[:, cols].astype(f32)).T
        do_ref[part, h] = grad[:, cols]
        delta_ref[part, h : h + 1, :] = jnp.sum(product, axis=0, keepdims=True)


def back_query_kernel(
    scale, flag_ref, dq_ref, wq_ref, adq_ref, auq_ref, low_t_ref, rows_ref, cos_ref, sin_ref, total_ref, dadq_ref, dauq_ref, eq
):
    heads, span = dq_ref.shape[1], dq_ref.shape[3]
    for part in range(2):
        rows = slice(part * span, (part + 1) * span)
        for h in range(heads):
            grad = dq_ref[place_of(flag_ref, part), h].T * scale
            eq[rows, h * HEAD_DIM : (h + 1) * HEAD_DIM] = turned(grad, cos_ref[rows, :], -sin_ref[rows, :]).astype(bf)
    query = eq[...]
    back = nt(query, auq_ref[...])
    total_ref[...] = nt(query, wq_ref[...]) + nn((2.0 * back).astype(bf), adq_ref[:RANK, :])
    dadq_ref[...] = nn(back.T.astype(bf), rows_ref[...])
    dauq_ref[...] = nn(low_t_ref[:RANK, :], query)


def back_key_value_kernel(
    flag_ref, dkv_ref, query_ref, wkv_ref, adqkv_ref, auk_ref, auv_ref, low_t_ref, rows_ref, cos_ref, sin_ref, *refs
):
    others = refs[: len(refs) - 7]
    own_ref, send_ref, dadkv_ref, dauk_ref, dauv_ref, total, back_ref = refs[len(refs) - 7 :]
    shard = lax.axis_index("tensor")
    half = own_ref.shape[0]
    grad = dkv_ref[...].astype(f32)
    for ref in others:
        grad = grad + ref[...].astype(f32)
    grad = jnp.where(place_of(flag_ref, 0) == 1, jnp.concatenate([grad[half:], grad[:half]], axis=0), grad)
    ek = turned(grad[:, :HEAD_DIM], cos_ref[...], -sin_ref[...]).astype(bf)
    ev = grad[:, HEAD_DIM:].astype(bf)
    back_ref[:, :RANK] = nt(ek, auk_ref[...])
    back_ref[:, RANK:] = nt(ev, auv_ref[...])
    back = back_ref[...]
    total[...] = (
        query_ref[...] + nt(ek, wkv_ref[0]) + nt(ev, wkv_ref[1]) + nn((2.0 * back).astype(bf), adqkv_ref[RANK:, :])
    )
    own_ref[...] = total[pl.ds(pl.multiple_of(shard * half, half), half), :]
    send_ref[...] = total[pl.ds(pl.multiple_of((1 - shard) * half, half), half), :].astype(bf)
    dadkv_ref[...] = nn(back.T.astype(bf), rows_ref[...])
    dauk_ref[...] = nn(low_t_ref[RANK : 2 * RANK, :], ek)
    dauv_ref[...] = nn(low_t_ref[2 * RANK :, :], ev)


def future_mask(span):
    return lax.broadcasted_iota(jnp.int32, (span, span), 0) <= lax.broadcasted_iota(jnp.int32, (span, span), 1)

EXTRA = 16


def weights_of(s, m, coef, mask):
    if mask is not None:
        s = jnp.where(mask, s, mask_fill)
    m_next = jnp.maximum(m, jnp.max(s, axis=0, keepdims=True))
    p = jnp.exp2((s - m_next) * coef)
    alpha = jnp.exp2((m - m_next) * coef)
    return m_next, alpha, p.astype(bf)


def put_values(vt, kv_ref):
    vt[:HEAD_DIM, :] = kv_ref[:, HEAD_DIM:].astype(f32).T.astype(bf)


def put_ones(vt):
    vt[HEAD_DIM:, :] = jnp.ones((EXTRA, vt.shape[1]), bf)


def pipelined(items, first, second):
    ahead = first(items[0])
    for i, item in enumerate(items):
        now = ahead
        if i + 1 < len(items):
            ahead = first(items[i + 1])
        second(item, now)

def pipelined_three(items, first, second, third):
    ahead, behind = first(items[0]), None
    for i, item in enumerate(items):
        now = ahead
        if i + 1 < len(items):
            ahead = first(items[i + 1])
        done = second(item, now)
        if behind is not None:
            third(*behind)
        behind = (item, done)
    third(*behind)


def attn_fwd_own_kernel(coef, q_ref, kv_ref, m_ref, o_ref, vt):
    heads, span = q_ref.shape[1], q_ref.shape[2]
    put_ones(vt)
    put_values(vt, kv_ref)
    mask = future_mask(span)
    row, place = (lax.broadcasted_iota(jnp.int32, (2 * span, span), axis) for axis in range(2))
    both_mask = row <= place + span

    def first(item):
        half, h = item
        return nt(kv_ref[: (half + 1) * span, :HEAD_DIM], q_ref[half, h])

    def second(item, s):
        half, h = item
        m, _, p = weights_of(s, jnp.full((1, span), mask_fill, f32), coef, both_mask if half else mask)
        m_ref[half, h : h + 1, :] = m
        return p

    def third(item, p):
        half, h = item
        o_ref[half, h] = nn(vt[:, : (half + 1) * span], p)

    pipelined_three([(half, h) for h in range(heads) for half in range(2)], first, second, third)


def halves_of(flag, turn):
    return (1 - flag) * turn, flag * turn + (1 - flag)


def attn_fwd_pieces_kernel(coef, indices, last, flag_ref, q_ref, *refs):
    n = len(indices)
    kv_refs, (m_in, o_in), refs = refs[:n], refs[n : n + 2], refs[n + 2 :]
    if last:
        mixed_ref, lse_ref, m_ref, o_ref, vt = refs
    else:
        m_ref, o_ref, vt = refs
    heads, span = q_ref.shape[1], q_ref.shape[2]
    put_ones(vt)
    m_ref[...] = m_in[...]
    o_ref[...] = o_in[...]
    for i in range(n):
        kv_ref, flag = kv_refs[i], flag_of(flag_ref, indices[i])
        put_values(vt, kv_ref)

        def first(item, kv_ref=kv_ref, flag=flag):
            keys, half = halves_of(flag, item[0])
            return nt(kv_ref[pl.ds(pl.multiple_of(keys * span, span), span), :HEAD_DIM], q_ref[half, item[1]])

        def second(item, s, flag=flag):
            half, h = halves_of(flag, item[0])[1], item[1]
            m, alpha, p = weights_of(s, m_ref[half, h : h + 1, :], coef, None)
            m_ref[half, h : h + 1, :] = m
            return alpha, p

        def third(item, weights, flag=flag):
            (keys, half), h = halves_of(flag, item[0]), item[1]
            alpha, p = weights
            values_t = vt[:, pl.ds(pl.multiple_of(keys * span, span), span)]
            o_ref[half, h] = o_ref[half, h] * alpha + nn(values_t, p)

        pipelined_three([(turn, h) for turn in range(2) for h in range(heads)], first, second, third)
    if last:
        for half in range(2):
            for h in range(heads):
                sums = o_ref[half, h, HEAD_DIM : HEAD_DIM + 1, :]
                o = o_ref[half, h, :HEAD_DIM, :] / sums
                mixed_ref[place_rows(flag_ref, half, span), h * HEAD_DIM : (h + 1) * HEAD_DIM] = o.T.astype(bf)
                lse_ref[half, h : h + 1, :] = m_ref[half, h : h + 1, :] * coef + jnp.log2(sums)


def attn_state(heads, span):
    return (shape(2, heads, span), shape(2, heads, HEAD_DIM + EXTRA, span))


def attn_fwd_own(q, kv, coef):
    _, heads, span, _ = q.shape
    return call(
        functools.partial(attn_fwd_own_kernel, coef), "attn_fwd_own", attn_state(heads, span), [q, kv],
        [pltpu.VMEM((HEAD_DIM + EXTRA, 2 * span), bf)], flops=24 * heads * span * span * HEAD_DIM, limit=20,
    )


def attn_fwd_pieces(flags, indices, q, pieces, state, coef, last):
    _, heads, span, _ = q.shape
    outs = attn_state(heads, span)
    if last:
        outs = (shape(2 * span, heads * HEAD_DIM, dtype=bf), shape(2, heads, span)) + outs
    return call(
        functools.partial(attn_fwd_pieces_kernel, coef, indices, last), "attn_fwd_pieces", outs, [flags, q, *pieces, *state],
        [pltpu.VMEM((HEAD_DIM + EXTRA, 2 * span), bf)], flops=16 * len(pieces) * heads * span * span * HEAD_DIM, limit=20,
    )


def bwd_block(s, dp, lse_ref, delta_ref, half, h, coef, mask):
    p = jnp.exp2(s * coef - lse_ref[half, h : h + 1, :])
    if mask is not None:
        p = jnp.where(mask, p, 0.0)
    ds = p * (dp - delta_ref[half, h : h + 1, :])
    return p.astype(bf), ds.astype(bf)

def attn_bwd_kernel(coef, scale, indices, own, has_state, flag_ref, q_ref, do_ref, lse_ref, delta_ref, *refs):
    n = len(indices)
    kv_refs = refs[:n]
    k = n
    if has_state:
        dq_in = refs[k]; k += 1
    dkv_refs = refs[k : k + n]
    dq_ref, kt, pbuf, sbuf = refs[k + n :]
    heads, span = q_ref.shape[1], q_ref.shape[2]
    if has_state:
        dq_ref[...] = dq_in[...]
    else:
        dq_ref[...] = jnp.zeros_like(dq_ref)
    def do_item(kv_ref, items, keyrows, mask_of):
        nk = keyrows.stop - keyrows.start
        def first(it):
            i, half, h = it
            return nt(kv_ref[keyrows, :HEAD_DIM], q_ref[half, h]), nt(kv_ref[keyrows, HEAD_DIM:], do_ref[half, h])
        def second(it, sd):
            i, half, h = it
            p, ds = bwd_block(sd[0], sd[1], lse_ref, delta_ref, half, h, coef, mask_of(half))
            cols = slice((i * heads + h) * span, (i * heads + h + 1) * span)
            pbuf[:nk, cols] = p
            sbuf[:nk, cols] = ds
            return ds
        def third(it, ds):
            i, half, h = it
            dq_ref[half, h] += nn(kt[:, keyrows], ds)
        pipelined_three([(i, half, h) for i, half in enumerate(items) for h in range(heads)], first, second, third)
        width = len(items) * heads * span
        lo = items[0]
        q_all = q_ref[lo : lo + len(items)].reshape(width, HEAD_DIM)
        do_all = do_ref[lo : lo + len(items)].reshape(width, HEAD_DIM)
        return nn(sbuf[:nk, :width], q_all) * scale, nn(pbuf[:nk, :width], do_all)
    for i in range(n):
        kv_ref, out = kv_refs[i], dkv_refs[i]
        kt[...] = kv_ref[:, :HEAD_DIM].astype(f32).T.astype(bf)
        lo, hi, both = slice(0, span), slice(span, 2 * span), slice(0, 2 * span)
        if own and i == 0:
            mask = future_mask(span)
            dk, dv = do_item(kv_ref, [0, 1], lo, lambda half: mask if half == 0 else None)
            out[lo, :HEAD_DIM] = dk.astype(bf)
            out[lo, HEAD_DIM:] = dv.astype(bf)
            dk, dv = do_item(kv_ref, [1], hi, lambda half: mask)
            out[hi, :HEAD_DIM] = dk.astype(bf)
            out[hi, HEAD_DIM:] = dv.astype(bf)
        else:
            flag = flag_of(flag_ref, indices[i])

            def first(item, kv_ref=kv_ref, flag=flag):
                (keys, half), h = halves_of(flag, item[0]), item[1]
                rows = pl.ds(pl.multiple_of(keys * span, span), span)
                return nt(kv_ref[rows, :HEAD_DIM], q_ref[half, h]), nt(kv_ref[rows, HEAD_DIM:], do_ref[half, h])

            def second(item, sd, flag=flag):
                turn, h = item
                half = halves_of(flag, turn)[1]
                p, ds = bwd_block(sd[0], sd[1], lse_ref, delta_ref, half, h, coef, None)
                cols = slice(h * span, (h + 1) * span)
                pbuf[turn * span : (turn + 1) * span, cols] = p
                sbuf[turn * span : (turn + 1) * span, cols] = ds
                return ds

            def third(item, ds, flag=flag):
                (keys, half), h = halves_of(flag, item[0]), item[1]
                dq_ref[half, h] += nn(kt[:, pl.ds(pl.multiple_of(keys * span, span), span)], ds)

            pipelined_three([(turn, h) for turn in range(2) for h in range(heads)], first, second, third)
            width = heads * span
            both = []
            for turn in range(2):
                keys, half = halves_of(flag, turn)
                rows = slice(turn * span, (turn + 1) * span)
                both.append((
                    nn(sbuf[rows, :width], q_ref[half].reshape(width, HEAD_DIM)) * scale,
                    nn(pbuf[rows, :width], do_ref[half].reshape(width, HEAD_DIM)),
                ))
            earlier = flag.astype(f32)
            for part in range(2):
                cols = slice(part * HEAD_DIM, (part + 1) * HEAD_DIM)
                out[lo, cols] = (both[0][part] + both[1][part] * earlier).astype(bf)
                out[hi, cols] = (both[1][part] * (1.0 - earlier)).astype(bf)


def attn_bwd(flags, indices, q, do, lse, delta, pieces, dq_state, coef, scale, own):
    _, heads, span, _ = q.shape
    n = len(pieces)
    outs = tuple(jax.ShapeDtypeStruct((2 * span, 2 * HEAD_DIM), bf) for _ in range(n)) + (jax.ShapeDtypeStruct((2, heads, HEAD_DIM, span), f32),)
    ins = [flags, q, do, lse, delta, *pieces] + ([dq_state] if dq_state is not None else [])
    return pl.pallas_call(functools.partial(attn_bwd_kernel, coef, scale, indices, own, dq_state is not None), out_shape=outs,
        in_specs=[VM] * len(ins), out_specs=(VM,) * len(outs),
        scratch_shapes=[pltpu.VMEM((HEAD_DIM, 2 * span), bf), pltpu.VMEM((2 * span, 2 * heads * span), bf), pltpu.VMEM((2 * span, 2 * heads * span), bf)],
        cost_estimate=pl.CostEstimate(flops=2*5*2*n*heads*span*span*HEAD_DIM*2, bytes_accessed=4_000_000, transcendentals=0),
        compiler_params=pltpu.CompilerParams(vmem_limit_bytes=30 << 20), name="attn_bwd_pieces")(*ins)


TILE = 512


def steps_of(columns, begin=0):
    edges = [begin, begin + TILE // 2, begin + TILE]
    while columns - edges[-1] > 2 * TILE:
        edges.append(edges[-1] + 2 * TILE)
    if columns - edges[-1] > TILE:
        edges.append(edges[-1] + TILE)
    edges.append(columns)
    return list(zip(edges, edges[1:]))


def act_back_kernel(bounds, own_ref, other_ref, wd_hbm, *refs):
    out_hbm, rows_ref, wd, out, in_sems, out_sems = refs[-6:]
    half, first = own_ref.shape[0], bounds[0][0]
    parts = [slice(low - first, high - first) for low, high in bounds]
    copies = [
        pltpu.make_async_copy(wd_hbm.at[low:high], wd.at[part], in_sems.at[i])
        for i, ((low, high), part) in enumerate(zip(bounds, parts))
    ]
    for copy in copies:
        copy.start()
    rows_ref[:half, :] = own_ref[...]
    rows_ref[half:, :] = other_ref[...]
    results = []
    for i, ((low, high), part) in enumerate(zip(bounds, parts)):
        copies[i].wait()
        out[:, part] = nt(rows_ref[...], wd[part, :]).astype(bf)
        result = pltpu.make_async_copy(out.at[:, part], out_hbm.at[:, low:high], out_sems.at[i])
        result.start()
        results.append(result)
    for result in results:
        result.wait()


def act_back(own, other, wd, bounds, held=None):
    half, width = own.shape
    columns, count = bounds[-1][1] - bounds[0][0], len(bounds)
    return pl.pallas_call(
        functools.partial(act_back_kernel, bounds),
        out_shape=pltpu.HBM((2 * half, wd.shape[0]), bf),
        in_specs=[VM, VM, HB] + ([] if held is None else [HB]),
        out_specs=HB,
        scratch_shapes=[
            pltpu.VMEM((2 * half, width), bf), pltpu.VMEM((columns, width), bf), pltpu.VMEM((2 * half, columns), bf),
            pltpu.SemaphoreType.DMA((count,)), pltpu.SemaphoreType.DMA((count,)),
        ],
        input_output_aliases={} if held is None else {3: 0},
        cost_estimate=pl.CostEstimate(flops=4 * half * width * columns, bytes_accessed=2 * width * columns, transcendentals=0),
        compiler_params=pltpu.CompilerParams(vmem_limit_bytes=30 << 20),
        name="act_back",
    )(own, other, in_hbm(wd), *([] if held is None else [in_hbm(held)]))


def whole(*dims):
    return pl.BlockSpec(dims, lambda i: (0,) * len(dims), pipeline_mode=pl.Buffered(1))


def ffn_kernel(
    tile, tiles, hidden, x_own, x_other, g_own, g_other, gact_ref, adgu_ref, auf_ref, wgu_ref, adf_ref, augu_ref,
    gx_own, gx_send, act_ref, flow_ref, dadgu_ref, dauf_ref, daugu_ref, dadf_ref,
    x_ref, g_ref, gx_acc, xlow, xlow_t, fback, fback_t, flow, back,
):
    step = pl.program_id(0)
    half = x_own.shape[0]

    @pl.when(step == 0)
    def prepare():
        for target, own, other in ((x_ref, x_own, x_other), (g_ref, g_own, g_other)):
            target[:half, :] = own[...]
            target[half:, :] = other[...]
        low = nt(x_ref[...], adgu_ref[...])
        xlow[...] = (low * 2.0).astype(bf)
        xlow_t[...] = low.T.astype(bf)
        fb = nt(g_ref[...], auf_ref[...])
        fback[...] = (fb * 2.0).astype(bf)
        fback_t[...] = fb.T.astype(bf)
        gx_acc[...] = jnp.zeros_like(gx_acc)
        flow[...] = jnp.zeros_like(flow)
        back[...] = jnp.zeros_like(back)

    def work(width):
        x = x_ref[...]
        wg, wu = wgu_ref[0, :, :width], wgu_ref[1, :, :width]
        aug, auu, adf = augu_ref[:RANK, :width], augu_ref[RANK:, :width], adf_ref[:, :width]
        gate = nn(x, wg) + nn(xlow[:, :RANK], aug)
        up = nn(x, wu) + nn(xlow[:, RANK:], auu)
        gact = gact_ref[:, :width].astype(f32) + nn(fback[...], adf)
        sig = 1.0 / (1.0 + jnp.exp(-gate))
        silu = gate * sig
        act = (silu * up).astype(bf)
        ggate = (gact * up * (sig + silu * (1.0 - sig))).astype(bf)
        gup = (gact * silu).astype(bf)
        act_ref[:, :width] = act
        flow[...] += nt(act, adf)
        gx_acc[...] += nt(ggate, wg) + nt(gup, wu)
        back[:, :RANK] += nt(ggate, aug)
        back[:, RANK:] += nt(gup, auu)
        daugu_ref[:RANK, :width] = nn(xlow_t[:RANK, :], ggate)
        daugu_ref[RANK:, :width] = nn(xlow_t[RANK:, :], gup)
        dadf_ref[:, :width] = nn(fback_t[...], act)

    tail = hidden - (tiles - 1) * tile
    if tail == tile:
        work(tile)
    else:
        @pl.when(step < tiles - 1)
        def body():
            work(tile)

        @pl.when(step == tiles - 1)
        def part():
            work(tail)

    @pl.when(step == tiles - 1)
    def finish():
        gx_acc[...] += nn((back[...] * 2.0).astype(bf), adgu_ref[...])
        gx_own[...] = gx_acc[:half, :]
        gx_send[...] = gx_acc[half:, :].astype(bf)
        flow_ref[...] = (flow[...] * 2.0).astype(bf)
        dadgu_ref[...] = nn(back[...].T.astype(bf), x_ref[...])
        dauf_ref[...] = nn(flow[...].T.astype(bf), g_ref[...])


def ffn(x_own, x_other, g_own, g_other, gact, adgu, auf, wgu, adf, augu, tile=TILE):
    rows, width = 2 * x_own.shape[0], x_own.shape[1]
    hidden = wgu.shape[2]
    tiles = -(-hidden // tile)
    half = rows // 2
    cols = lambda r: pl.BlockSpec((r, tile), lambda i: (0, i))
    outs = (
        shape(half, width), shape(half, width, dtype=bf), pltpu.HBM((rows, hidden), bf), shape(rows, RANK, dtype=bf),
        shape(2 * RANK, width), shape(RANK, width), shape(2 * RANK, hidden), shape(RANK, hidden),
    )
    return pl.pallas_call(
        functools.partial(ffn_kernel, tile, tiles, hidden),
        grid=(tiles,),
        out_shape=outs,
        in_specs=[whole(half, width)] * 4 + [cols(rows), whole(2 * RANK, width), whole(RANK, width),
                  pl.BlockSpec((2, width, tile), lambda i: (0, 0, i)), cols(RANK), cols(2 * RANK)],
        out_specs=(whole(half, width), whole(half, width), cols(rows), whole(rows, RANK), whole(2 * RANK, width),
                   whole(RANK, width), cols(2 * RANK), cols(RANK)),
        scratch_shapes=[
            pltpu.VMEM((rows, width), bf), pltpu.VMEM((rows, width), bf), pltpu.VMEM((rows, width), f32),
            pltpu.VMEM((rows, 2 * RANK), bf), pltpu.VMEM((2 * RANK, rows), bf), pltpu.VMEM((rows, RANK), bf),
            pltpu.VMEM((RANK, rows), bf), pltpu.VMEM((rows, RANK), f32), pltpu.VMEM((rows, 2 * RANK), f32),
        ],
        cost_estimate=pl.CostEstimate(flops=8 * rows * width * hidden, bytes_accessed=6 * width * hidden, transcendentals=rows * hidden),
        compiler_params=pltpu.CompilerParams(vmem_limit_bytes=36 << 20),
        name="ffn",
    )(x_own, x_other, in_hbm(g_own), in_hbm(g_other), in_hbm(gact), adgu, auf, in_hbm(wgu), adf, augu)


def down_kernel(bounds, start_refs, act_hbm, wd_hbm, total, act, wd, act_sems, wd_sems):
    low = bounds[0][0]
    copies = []
    for i, (begin, end) in enumerate(bounds):
        rows = slice(begin - low, end - low)
        copies.append((
            pltpu.make_async_copy(act_hbm.at[:, begin:end], act.at[:, rows], act_sems.at[i]),
            pltpu.make_async_copy(wd_hbm.at[begin:end], wd.at[rows], wd_sems.at[i]),
        ))
        for copy in copies[-1]:
            copy.start()
    total[...] = nn(start_refs[0][...], start_refs[1][...]) if len(start_refs) == 2 else start_refs[0][...]
    for i, (begin, end) in enumerate(bounds):
        rows = slice(begin - low, end - low)
        for copy in copies[i]:
            copy.wait()
        total[...] += nn(act[:, rows], wd[rows, :])


def down_first_kernel(bounds, flow_ref, auf_ref, act_hbm, wd_hbm, total, *scratch):
    down_kernel(bounds, (flow_ref, auf_ref), act_hbm, wd_hbm, total, *scratch)


def down_last_kernel(bounds, start_ref, act_hbm, wd_hbm, own_ref, send_ref, total, *scratch):
    down_kernel(bounds, (start_ref,), act_hbm, wd_hbm, total, *scratch)
    half = own_ref.shape[0]
    own_ref[...] = total[:half, :]
    send_ref[...] = total[half:, :].astype(bf)


def down(act, wd, start, bounds, last):
    rows, width = act.shape[0], wd.shape[1]
    half, columns, count = rows // 2, bounds[-1][1] - bounds[0][0], len(bounds)
    outs = (shape(half, width), shape(half, width, dtype=bf)) if last else (shape(rows, width),)
    scratch = [
        pltpu.VMEM((rows, columns), bf), pltpu.VMEM((columns, width), bf), pltpu.SemaphoreType.DMA((count,)),
        pltpu.SemaphoreType.DMA((count,)),
    ]
    return pl.pallas_call(
        functools.partial(down_last_kernel if last else down_first_kernel, bounds),
        out_shape=outs,
        in_specs=[VM] * len(start) + [HB, HB],
        out_specs=(VM,) * len(outs),
        scratch_shapes=([pltpu.VMEM((rows, width), f32)] if last else []) + scratch,
        cost_estimate=pl.CostEstimate(flops=2 * rows * width * columns, bytes_accessed=2 * width * columns, transcendentals=0),
        compiler_params=pltpu.CompilerParams(vmem_limit_bytes=28 << 20),
        name="down",
    )(*start, in_hbm(act), in_hbm(wd))


def per_device(
    tokens, cotangent, positions, adapter_choice, attn_gain, query_weight, query_bias, key_value_weight,
    key_value_bias, output_weight, ffn_gain, gate_upper_weight, down_weight, adapt_in, adapt_out,
):
    dp = lax.axis_index("dp")
    groups = lax.axis_size("seq")
    rings = groups // 2
    width, head_width = query_weight.shape
    heads = head_width // HEAD_DIM
    hidden = down_weight.shape[0]
    token_pos = positions[0]
    tok_count = token_pos.shape[0]
    span = tok_count // 2
    scale = HEAD_DIM ** (-0.5)
    coef = scale * math.log2(math.e)
    wide_in, wide_out = adapt_in.shape[2], adapt_out.shape[2]
    lanes_in = rounded_up(wide_in + 1, 128)
    lanes = lanes_in + rounded_up(wide_out, 128)
    widths = (width, head_width, hidden)
    sizes = (rings, wide_in, wide_out, lanes_in, widths)

    def to_pair(value):
        return lax.ppermute(value, "tensor", [(0, 1), (1, 0)])

    def to_other_sequence(value, pairs=((0, 1), (1, 0))):
        return lax.ppermute(value, "dp", list(pairs))

    def to_side(value):
        return lax.ppermute(value, "seq", [(i, i ^ 1) for i in range(groups)])

    def along_ring(value, steps):
        return lax.ppermute(value, "seq", [(i, (i + 2 * steps) % groups) for i in range(groups)])

    cycle = list(range(0, groups, 2)) + list(range(groups - 1, 0, -2))
    hops = [(cycle[i], cycle[(i + 1) % groups]) for i in range(groups)]

    def to_next(value):
        return lax.ppermute(value, "seq", hops)

    def to_last(value):
        return lax.ppermute(value, "seq", [(end, begin) for begin, end in hops])

    def after(value, *others):
        return lax.optimization_barrier((value, *others))[0]

    inputs, grad_out = tokens[0], cotangent[0]
    half = inputs.shape[0]
    attn_gain, ffn_gain = attn_gain[None], ffn_gain[None]

    def over_ring(piece):
        return [piece] + [along_ring(piece, step) for step in range(1, rings)]

    slice_own, slice_other = call(
        functools.partial(select_kernel, lanes_in, span), "select",
        [shape(RANK, lanes, dtype=bf)] * 2, [adapter_choice, positions, adapt_in, adapt_out],
        [
            pltpu.SMEM(adapter_choice.shape, jnp.int32), pltpu.SMEM(positions.shape, jnp.int32),
            pltpu.VMEM((2, RANK, wide_in), bf), pltpu.VMEM((2, RANK, wide_out), bf), pltpu.SemaphoreType.DMA((6,)),
        ],
        left=4,
    )
    slice_other = to_other_sequence(slice_other)
    lane = lax.broadcasted_iota(jnp.int32, (RANK, lanes), 1)
    run_lane = (lane >= wide_in) & (lane < lanes_in)
    grad_other = to_pair(after(grad_out, slice_own))
    slice_other = after(slice_other, grad_other)
    first_slice = jnp.where((dp == 0) | run_lane, slice_own, slice_other)
    second_slice = jnp.where(dp == 0, slice_other, slice_own)

    (normed,) = call(norm_kernel, "norm", [shape(half, width, dtype=bf)], [inputs, attn_gain])
    normed_other = to_pair(normed)
    arrived = over_ring(jnp.stack([first_slice, second_slice]))
    middle = 6 * TILE
    act_grad = act_back(grad_out, grad_other, down_weight, steps_of(middle))
    arrived[1] = after(arrived[1], act_grad)
    own_slices = jnp.stack([piece[0] for piece in arrived])
    own_second = jnp.stack([piece[1] for piece in arrived])
    side_slices = to_side(own_slices)
    pair_slices = to_pair(own_slices)
    normed_rows, query_dense, kv_dense = call(
        dense_kernel, "dense", [shape(tok_count, width, dtype=bf), shape(tok_count, head_width), shape(tok_count, 2 * HEAD_DIM)],
        [normed, after(normed_other, own_slices), query_weight, key_value_weight],
        flops=2 * tok_count * width * (head_width + 2 * HEAD_DIM),
    )
    frequency = jnp.power(rope_base, -(jnp.arange(HEAD_DIM // 2, dtype=f32) * 2.0) / HEAD_DIM)
    angles = token_pos.astype(f32)[:, None] * frequency[None, :]
    cosine, sine = jnp.cos(angles), jnp.sin(angles)
    cosine = jnp.concatenate([cosine, cosine], axis=1)
    sine = jnp.concatenate([-sine, sine], axis=1)

    side_slices = after(side_slices, kv_dense)
    first_slices = [own_slices, side_slices, pair_slices, to_pair(side_slices)]
    side_second = to_side(after(own_second, side_slices))
    slices_in = -(-4 * width // wide_in)
    slices_out = -(-(2 * width + 4 * HEAD_DIM) // wide_out)
    flags, adqkv, auq, auk, auv, ado, auo = call(
        functools.partial(unpack_first_kernel, *sizes), "unpack_first",
        [shape(rounded_up(groups, 8), 128)]
        + [
            shape(*dims, dtype=bf)
            for dims in (
                (3 * RANK, width), (RANK, head_width), (RANK, HEAD_DIM), (RANK, HEAD_DIM), (RANK, head_width), (RANK, width),
            )
        ],
        list(first_slices),
        [
            pltpu.VMEM((2 * groups, RANK, lanes), bf),
            pltpu.VMEM((RANK, rounded_up(slices_in * wide_in, 128) + 256), f32),
            pltpu.VMEM((RANK, rounded_up(slices_out * wide_out, 128) + 256), f32),
            pltpu.SMEM((groups,), jnp.int32),
        ],
    )
    kv, low, low_t = call(
        key_value_kernel, "key_value",
        [shape(tok_count, 2 * HEAD_DIM, dtype=bf), shape(tok_count, 3 * RANK, dtype=bf), shape(3 * RANK, tok_count, dtype=bf)],
        [flags, normed_rows, kv_dense, key_value_bias, adqkv, auk, auv, cosine, sine],
        flops=2 * tok_count * width * 2 * RANK,
    )

    (queries,) = call(
        query_kernel, "query", [shape(2, heads, span, HEAD_DIM, dtype=bf)],
        [flags, query_dense, query_bias[None], low, auq, cosine, sine], flops=2 * tok_count * width * RANK,
    )
    state = attn_fwd_own(queries, kv, coef)
    pieces, from_last, from_next = [kv], kv, kv
    for step in range(1, rings + 1):
        from_last, from_next = to_next(from_last), to_last(from_next)
        if step == 1:
            bounds = [(middle, middle + TILE // 2), (middle + TILE // 2, middle + 2 * TILE), (middle + 2 * TILE, hidden)]
            act_grad = act_back(after(grad_out, state[0], side_second), grad_other, down_weight, bounds, act_grad)
            from_last = after(from_last, act_grad)
        if step < rings:
            from_last, from_next, _ = lax.optimization_barrier((from_last, from_next, state[0]))
        if step == rings:
            pair_second = to_pair(after(own_second, pieces[-1]))
            state = (after(state[0], pair_second), *state[1:])
        pieces += [from_last, from_next][: 2 if step < rings else 1]
        indices = tuple(range(2 * step - 1, len(pieces)))
        result = attn_fwd_pieces(flags, indices, queries, pieces[2 * step - 1 :], state, coef, step == rings)
        state = result[-2:]
    mixed, lse = result[0], result[1]

    branch_send, mix_low, mix_low_t = call(
        mix_send_kernel, "mix_send",
        [shape(half, width, dtype=bf), shape(tok_count, RANK, dtype=bf), shape(RANK, tok_count, dtype=bf)],
        [mixed, output_weight, ado, auo], flops=2 * half * width * head_width,
    )
    branch_other = to_pair(branch_send)
    second_slices = [own_second, side_second, pair_second, to_pair(side_second)]
    (branch_own,) = call(
        mix_own_kernel, "mix_own", [shape(half, width)], [mixed, output_weight, mix_low, auo],
        flops=2 * half * width * head_width,
    )
    hidden_rows, normed_ffn = call(
        residual_kernel, "residual", [shape(half, width), shape(half, width, dtype=bf)],
        [inputs, branch_own, after(branch_other, branch_own, second_slices[3]), ffn_gain],
    )
    begin_in, begin_out, first_in, first_out = bases(wide_in, wide_out, widths)
    adgu, augu, adf, auf = call(
        functools.partial(unpack_second_kernel, *sizes), "unpack_second",
        [shape(*dims, dtype=bf) for dims in ((2 * RANK, width), (2 * RANK, hidden), (RANK, hidden), (RANK, width))],
        list(first_slices) + list(second_slices),
        [
            pltpu.VMEM((4 * groups, RANK, lanes), bf),
            pltpu.VMEM((RANK, rounded_up(4 * groups * wide_in, 128) + 256 - first_in), f32),
            pltpu.VMEM((RANK, rounded_up(4 * groups * wide_out, 128) + 256 - first_out), f32),
        ],
    )
    gx_own, gx_send, act, flow, dadgu, dauf, daugu, dadf = ffn(
        normed_ffn, to_pair(normed_ffn), grad_out, grad_other, act_grad, adgu, auf, gate_upper_weight, adf, augu
    )
    ad_lanes = rounded_up(4 * groups * wide_in, 128) + 256
    au_lanes = rounded_up(4 * groups * wide_out, 128) + 256

    def added(*values):
        total = values[0].astype(f32)
        for value in values[1:]:
            total = total + value.astype(f32)
        return total.astype(bf)

    grad_hidden, grad_low = call(
        hidden_back_kernel, "hidden_back", [shape(half, width), shape(half, width, dtype=bf)],
        [hidden_rows, grad_out, gx_own, to_pair(gx_send), ffn_gain],
    )
    grad_low_other = to_pair(grad_low)
    fixed = [output_weight, ado, auo, mixed, mix_low_t]
    outs = [shape(2, heads, span, HEAD_DIM, dtype=bf), shape(2, heads, span), shape(RANK, head_width), shape(RANK, width)]
    partial = call(
        functools.partial(mix_back_kernel, True), "mix_back", outs, [flags, grad_low, *fixed], flops=2 * half * width * head_width,
    )
    grad_mixed, delta, dado, dauo = call(
        functools.partial(mix_back_kernel, False), "mix_back_other", outs,
        [flags, after(grad_low_other, partial[0]), *fixed, *partial], flops=2 * half * width * head_width,
        aliases={7 + i: i for i in range(4)},
    )

    def backward(indices, state_dq):
        return attn_bwd(
            flags, indices, queries, grad_mixed, lse, delta, [pieces[index] for index in indices], state_dq, coef, scale,
            indices == (0,),
        )

    state_dq, from_last, from_next = None, None, None
    for step in range(rings, 0, -1):
        onward, *returned, state_dq = backward((2 * rings - 1,) if step == rings else (2 * step, 2 * step - 1), state_dq)
        if from_last is not None:
            onward = added(onward, from_last)
        if from_next is not None:
            returned = [added(returned[0], from_next)]
        from_last = to_next(onward)
        if returned:
            from_next = to_last(returned[0])
        state_dq = after(state_dq, onward, *returned)
    own_term, state_dq = backward((0,), state_dq)
    gn_query, dadq, dauq = call(
        functools.partial(back_query_kernel, scale), "back_query",
        [shape(tok_count, width), shape(RANK, width), shape(RANK, head_width)],
        [flags, state_dq, query_weight, adqkv, auq, low_t, normed_rows, cosine, sine],
        [pltpu.VMEM((tok_count, head_width), bf)], flops=2 * tok_count * width * head_width,
    )
    from_last = after(from_last, gn_query)
    gn_own, gn_send, dadkv, dauk, dauv = call(
        back_key_value_kernel, "back_key_value",
        [
            shape(half, width), shape(half, width, dtype=bf), shape(2 * RANK, width), shape(RANK, HEAD_DIM),
            shape(RANK, HEAD_DIM),
        ],
        [
            flags, own_term, gn_query, key_value_weight, adqkv, auk, auv, low_t, normed_rows, cosine, sine, from_last, from_next,
        ],
        [pltpu.VMEM((tok_count, width), f32), pltpu.VMEM((tok_count, 2 * RANK), f32)],
        flops=2 * tok_count * width * 2 * HEAD_DIM, limit=20,
    )
    (packed,) = call(
        functools.partial(pack_kernel, *sizes), "pack", [shape(2, 2, rings, 2, RANK, lanes, dtype=bf)],
        [dadq, dadkv, dado, dadgu, dadf, dauq, dauk, dauv, dauo, daugu, dauf],
        [pltpu.VMEM((RANK, ad_lanes), f32), pltpu.VMEM((RANK, au_lanes), f32)],
    )
    from_pair = to_pair(packed[1])
    near, far = added(packed[0, 0], from_pair[0]), added(packed[0, 1, 1:], from_pair[1, 1:])
    from_side = to_side(far)
    own_side = to_side(after(added(packed[0, 1, 0], from_pair[1, 0]), far))
    middle = 5 * TILE
    (out_total,) = down(after(act, far), down_weight, (flow, auf), steps_of(middle), False)
    from_side = after(from_side, out_total)
    sums = [added(near[place], from_side[place - 1]) for place in range(1, rings)]
    from_ring = [along_ring(sums[place - 1], -place) for place in range(1, rings)]
    out_own, out_send = down(after(act, *sums), down_weight, (out_total,), steps_of(hidden, middle), True)
    from_ring[0] = after(from_ring[0], out_own)
    total = added(near[0], own_side, *from_ring)
    (grad_tokens,) = call(
        token_back_kernel, "token_back", [shape(half, width)],
        [inputs, grad_hidden, gn_own, after(to_pair(gn_send), total), attn_gain],
    )
    output = (hidden_rows + (out_own + to_pair(out_send).astype(f32))).astype(bf)
    other_total = after(to_other_sequence(total[1]), output, grad_tokens)
    factor = adapter_scale * (adapter_choice.shape[0] * tok_count * groups) ** (-0.5)
    adapt_in_grad, adapt_out_grad = call(
        functools.partial(place_kernel, lanes_in, factor), "place",
        [shape(*adapt_in.shape), shape(*adapt_out.shape)],
        [adapter_choice, total[0], other_total], smem=1,
    )
    return (output[None], grad_tokens[None], adapt_in_grad, adapt_out_grad)


def solution(mesh):
    return jax.shard_map(
        per_device,
        mesh=mesh,
        in_specs=(
            P("dp", ("seq", "tensor"), None),
            P("dp", ("seq", "tensor"), None),
            P("dp", "seq"),
            P(),
            P(),
            P(None, "tensor"),
            P("tensor"),
            P(None, None, "tensor"),
            P(None, "tensor"),
            P("tensor", None),
            P(),
            P(None, None, "tensor"),
            P("tensor", None),
            P(None, None, ("dp", "seq", "tensor")),
            P(None, None, ("dp", "seq", "tensor")),
        ),
        out_specs=(
            P("dp", ("seq", "tensor"), None),
            P("dp", ("seq", "tensor"), None),
            P(None, None, ("dp", "seq", "tensor")),
            P(None, None, ("dp", "seq", "tensor")),
        ),
        check_vma=False,
    )
```

```python
import functools
import math

import jax
import jax.numpy as jnp
from jax import lax
from jax.experimental import pallas as pl
from jax.experimental.pallas import tpu as pltpu
from jax.sharding import PartitionSpec as P

HEAD_DIM = 128
RANK = 16
eps = 1e-06
adapter_scale = 2.0
rope_base = 1000000.0
mask_fill = -1e30
bf = jnp.bfloat16
f32 = jnp.float32
VM = pl.BlockSpec(memory_space=pltpu.VMEM)
SM = pl.BlockSpec(memory_space=pltpu.SMEM)


def nn(a, b):
    return jnp.dot(a, b, preferred_element_type=f32)


def nt(a, b):
    return lax.dot_general(a, b, (((1,), (1,)), ((), ())), preferred_element_type=f32)


def shape(*dims, dtype=f32):
    return jax.ShapeDtypeStruct(dims, dtype)


def call(kernel, name, out, ins, scratch=(), flops=0, smem=0, out_specs=None, limit=16, left=0, aliases=None):
    moved = sum(math.prod(v.shape) * v.dtype.itemsize for v in list(ins) + list(out))
    ins = list(ins[: len(ins) - left]) + [in_hbm(value) for value in ins[len(ins) - left :]]
    return pl.pallas_call(
        kernel,
        out_shape=tuple(out),
        in_specs=[SM] * smem + [VM] * (len(ins) - smem - left) + [HB] * left,
        out_specs=out_specs or (VM,) * len(out),
        scratch_shapes=list(scratch),
        input_output_aliases=aliases or {},
        cost_estimate=pl.CostEstimate(flops=flops, bytes_accessed=moved, transcendentals=0),
        compiler_params=pltpu.CompilerParams(vmem_limit_bytes=limit << 20),
        name=name,
    )(*ins)


HB = pl.BlockSpec(memory_space=pltpu.HBM)


def in_hbm(value):
    return pltpu.with_memory_space_constraint(value, pltpu.HBM)


def rounded_up(value, unit):
    return -(-value // unit) * unit


def select_kernel(
    lanes_in, span, choice_hbm, pos_hbm, in_ref, out_ref, own_ref, other_ref, chosen_ref, choice_ref, pos_ref, held_in, held_out, sems
):
    wide_in, wide_out = in_ref.shape[2], out_ref.shape[2]
    dp = lax.axis_index("dp")
    choice_copy = pltpu.make_async_copy(choice_hbm, choice_ref, sems.at[4])
    pos_copy = pltpu.make_async_copy(pos_hbm, pos_ref, sems.at[5])
    choice_copy.start()
    pos_copy.start()
    choice_copy.wait()
    copies = []
    for slot, sequence in ((0, dp), (1, 1 - dp)):
        chosen = choice_ref[sequence]
        chosen_ref[slot : slot + 1, :] = jnp.full((1, 128), chosen, jnp.int32).astype(f32)
        copies.append(pltpu.make_async_copy(in_ref.at[chosen], held_in.at[slot], sems.at[2 * slot]))
        copies.append(pltpu.make_async_copy(out_ref.at[chosen], held_out.at[slot], sems.at[2 * slot + 1]))
    for copy in copies:
        copy.start()
    pos_copy.wait()
    run = jnp.full((RANK, lanes_in), pos_ref[0, 0] // span, jnp.int32).astype(f32).astype(bf)
    for target in (own_ref, other_ref):
        target[...] = jnp.zeros_like(target)
        target[:, :lanes_in] = run
    for copy in copies:
        copy.wait()
    for slot, target in ((0, own_ref), (1, other_ref)):
        target[:, :wide_in] = held_in[slot]
        target[:, lanes_in : lanes_in + wide_out] = held_out[slot]


def column(begin, size):
    return pl.ds(pl.multiple_of(begin, 128), size)


def source_of(place, side, rings, seq):
    ring = lax.rem(seq // 2 - place + rings, rings)
    own_side = lax.rem(seq, 2)
    return ring * 2 + (own_side if side == 0 else 1 - own_side)


def spread(slots, target, begin, wide, first, low, high):
    held = rounded_up(wide, 128)
    inside = lax.broadcasted_iota(jnp.int32, (RANK, held), 1) < wide
    target[...] = jnp.zeros_like(target)
    for index in range(low // wide, -(-high // wide)):
        part = jnp.where(inside, slots[index, :, begin : begin + held].astype(f32), 0.0)
        part = jnp.concatenate([part, jnp.zeros((RANK, 128), f32)], axis=1)
        offset = index * wide - first
        base = offset // 128 * 128
        if offset != base:
            part = pltpu.roll(part, offset - base, 1)
        target[:, base : base + held + 128] += part


def collect(slots, refs, rings, part):
    seq, shard = lax.axis_index("seq"), lax.axis_index("tensor")
    for number, ref in enumerate(refs):
        side, core = number % 2, shard if number < 2 else 1 - shard
        for place in range(rings):
            slots[part * 4 * rings + source_of(place, side, rings, seq) * 2 + core] = ref[place]


def unpack_first_kernel(
    rings, wide_in, wide_out, lanes_in, widths, own, own_side, pair, pair_side,
    flags_ref, adqkv, auq, auk, auv, ado, auo, slots, ad, au, runs,
):
    shard, seq = lax.axis_index("tensor"), lax.axis_index("seq")
    width, head_width, hidden = widths
    for place in range(rings):
        for side, ref in ((0, own), (1, own_side)):
            run = jnp.max(ref[place, :, wide_in:lanes_in].astype(f32))
            run = run.astype(jnp.int32)
            runs[source_of(place, side, rings, seq)] = jnp.minimum(run, 4 * rings - 1 - run)
    groups = 2 * rings
    own_run = jnp.max(own[0, :, wide_in:lanes_in].astype(f32)).astype(jnp.int32)
    swap = (own_run >= groups).astype(jnp.int32)
    place = jnp.where(lax.rem(seq, 2) == 0, seq // 2, groups - 1 - seq // 2)
    for index in range(groups):
        step = (index + 1) // 2
        other = lax.rem(place + (groups - step if index % 2 == 1 else step), groups)
        source = jnp.where(other < rings, 2 * other, 2 * (groups - 1 - other) + 1)
        flag = swap if index == 0 else (runs[source] < runs[seq]).astype(jnp.int32)
        flags_ref[index : index + 1, :] = jnp.full((1, 128), flag, jnp.int32).astype(f32)
    collect(slots, (own, own_side, pair, pair_side), rings, 0)
    spread(slots, ad, 0, wide_in, 0, 0, 4 * width)
    spread(slots, au, lanes_in, wide_out, 0, 0, 2 * width + 4 * HEAD_DIM)
    for index in range(3):
        adqkv[index * RANK : (index + 1) * RANK, :] = ad[:, index * width : (index + 1) * width].astype(bf)
    ado[...] = ad[:, column(3 * width + shard * head_width, head_width)].astype(bf)
    auq[...] = au[:, column(shard * head_width, head_width)].astype(bf)
    auk[...] = au[:, column(width + shard * HEAD_DIM, HEAD_DIM)].astype(bf)
    auv[...] = au[:, column(width + (2 + shard) * HEAD_DIM, HEAD_DIM)].astype(bf)
    base = width + 4 * HEAD_DIM
    auo[...] = au[:, base : base + width].astype(bf)


def bases(wide_in, wide_out, widths):
    width = widths[0]
    begin_in, begin_out = 4 * width, 2 * width + 4 * HEAD_DIM
    return begin_in, begin_out, begin_in // wide_in * wide_in // 128 * 128, begin_out // wide_out * wide_out // 128 * 128


def unpack_second_kernel(
    rings, wide_in, wide_out, lanes_in, widths, *refs
):
    firsts, seconds = refs[:4], refs[4:8]
    adgu, augu, adf, auf, slots, ad, au = refs[8:]
    shard = lax.axis_index("tensor")
    width, head_width, hidden = widths
    collect(slots, firsts, rings, 0)
    collect(slots, seconds, rings, 1)
    begin_in, begin_out, first_in, first_out = bases(wide_in, wide_out, widths)
    total_in, total_out = 8 * rings * wide_in, 8 * rings * wide_out
    spread(slots, ad, 0, wide_in, first_in, begin_in, total_in)
    spread(slots, au, lanes_in, wide_out, first_out, begin_out, total_out)
    base = begin_in - first_in
    for index in range(2):
        adgu[index * RANK : (index + 1) * RANK, :] = ad[:, base + index * width : base + (index + 1) * width].astype(bf)
    adf[...] = ad[:, column(base + 2 * width + shard * hidden, hidden)].astype(bf)
    base = begin_out - first_out
    for index in range(2):
        augu[index * RANK : (index + 1) * RANK, :] = au[
            :, column(base + (2 * index + shard) * hidden, hidden)
        ].astype(bf)
    auf[...] = au[:, base + 4 * hidden : base + 4 * hidden + width].astype(bf)


def put_slices(rings, wide_in, wide_out, lanes_in, ad, au, limits, parts, write):
    dp, seq = lax.axis_index("dp"), lax.axis_index("seq")
    for index in range(4 * rings * parts):
        to_dp, to_seq, to_core = index // (4 * rings), index // 2 % (2 * rings), index % 2
        pieces = []
        for source, wide, (low, high, first) in ((ad, wide_in, limits[0]), (au, wide_out, limits[1])):
            held = rounded_up(wide, 128)
            if index * wide >= high or (index + 1) * wide <= low:
                part = jnp.zeros((RANK, held), f32)
            else:
                offset = index * wide - first
                base = offset // 128 * 128
                part = source[:, base : base + held + 128]
                if offset != base:
                    part = pltpu.roll(part, held + 128 - (offset - base), 1)
                part = part[:, :held]
            pieces.append(part)
            if source is ad and lanes_in > held:
                pieces.append(jnp.zeros((RANK, lanes_in - held), f32))
        packed = jnp.concatenate(pieces, axis=1).astype(bf)
        place = lax.rem(seq // 2 - to_seq // 2 + rings, rings)
        write(to_seq, to_core, place, lax.rem(dp + to_dp, 2), packed)


def pack_kernel(
    rings, wide_in, wide_out, lanes_in, widths,
    dadq, dadkv, dado, dadgu, dadf, dauq, dauk, dauv, dauo, daugu, dauf, out_ref, ad, au,
):
    shard, side = lax.axis_index("tensor"), lax.rem(lax.axis_index("seq"), 2)
    width, head_width, hidden = widths
    ad[...] = jnp.zeros_like(ad)
    au[...] = jnp.zeros_like(au)
    ad[:, :width] = dadq[...]
    for index in range(2):
        ad[:, (1 + index) * width : (2 + index) * width] = dadkv[index * RANK : (index + 1) * RANK, :]
        ad[:, (4 + index) * width : (5 + index) * width] = dadgu[index * RANK : (index + 1) * RANK, :]
    ad[:, column(3 * width + shard * head_width, head_width)] = dado[...]
    ad[:, column(6 * width + shard * hidden, hidden)] = dadf[...]
    au[:, column(shard * head_width, head_width)] = dauq[...]
    au[:, column(width + shard * HEAD_DIM, HEAD_DIM)] = dauk[...]
    au[:, column(width + (2 + shard) * HEAD_DIM, HEAD_DIM)] = dauv[...]
    base = width + 4 * HEAD_DIM
    au[:, base : base + width] = dauo[...]
    base = base + width
    for index in range(2):
        au[:, column(base + (2 * index + shard) * hidden, hidden)] = daugu[index * RANK : (index + 1) * RANK, :]
    au[:, base + 4 * hidden : base + 4 * hidden + width] = dauf[...]

    def write(to_seq, to_core, place, part, packed):
        out_ref[lax.rem(shard + to_core, 2), lax.rem(side + to_seq % 2, 2), place, part] = packed

    limits = ((0, 8 * rings * wide_in, 0), (0, 8 * rings * wide_out, 0))
    put_slices(rings, wide_in, wide_out, lanes_in, ad, au, limits, 2, write)


def place_kernel(lanes_in, factor, chosen_ref, own_ref, other_ref, in_ref, out_ref):
    wide_in, wide_out = in_ref.shape[2], out_ref.shape[2]
    in_ref[...] = jnp.zeros_like(in_ref)
    out_ref[...] = jnp.zeros_like(out_ref)
    for slot, ref in enumerate((own_ref, other_ref)):
        chosen = flag_of(chosen_ref, slot)
        part = ref[...].astype(f32) * factor
        in_ref[chosen] = in_ref[chosen] + part[:, :wide_in]
        out_ref[chosen] = out_ref[chosen] + part[:, lanes_in : lanes_in + wide_out]


def factor_of(rows):
    return lax.rsqrt(jnp.mean(rows * rows, axis=-1, keepdims=True) + eps)


def norm_back(rows, gain, grad):
    factor = factor_of(rows)
    scaled = rows * factor
    grad_scaled = grad * gain
    return factor * (grad_scaled - scaled * jnp.mean(grad_scaled * scaled, axis=-1, keepdims=True))


def norm_kernel(rows_ref, gain_ref, normed_ref):
    rows = rows_ref[...].astype(f32)
    normed_ref[...] = (rows * factor_of(rows) * gain_ref[...].astype(f32)).astype(bf)


def residual_kernel(rows_ref, own_ref, other_ref, gain_ref, hidden_ref, normed_ref):
    rows = rows_ref[...].astype(f32) + (own_ref[...] + other_ref[...].astype(f32))
    hidden_ref[...] = rows
    normed_ref[...] = (rows * factor_of(rows) * gain_ref[...].astype(f32)).astype(bf)


def hidden_back_kernel(hidden_ref, grad_ref, own_ref, other_ref, gain_ref, out_ref, low_ref):
    grad = own_ref[...] + other_ref[...].astype(f32)
    total = grad_ref[...].astype(f32) + norm_back(hidden_ref[...], gain_ref[...].astype(f32), grad)
    out_ref[...] = total
    low_ref[...] = total.astype(bf)


def token_back_kernel(rows_ref, grad_ref, own_ref, other_ref, gain_ref, out_ref):
    grad = own_ref[...] + other_ref[...].astype(f32)
    out_ref[...] = grad_ref[...] + norm_back(rows_ref[...].astype(f32), gain_ref[...].astype(f32), grad)


def flag_of(flag_ref, index):
    return jnp.max(flag_ref[index : index + 1, :]).astype(jnp.int32)


def place_of(flag_ref, half):
    swap = flag_of(flag_ref, 0)
    return half + swap - 2 * half * swap


def place_rows(flag_ref, half, span):
    return pl.ds(pl.multiple_of(place_of(flag_ref, half) * span, span), span)


def turned(rows, cosine, sine):
    return rows * cosine + pltpu.roll(rows, HEAD_DIM // 2, 1) * sine


def dense_kernel(own_ref, other_ref, wq_ref, wkv_ref, rows_ref, query_ref, kv_ref):
    shard = lax.axis_index("tensor")
    half = own_ref.shape[0]
    rows_ref[pl.ds(pl.multiple_of(shard * half, half), half), :] = own_ref[...]
    rows_ref[pl.ds(pl.multiple_of((1 - shard) * half, half), half), :] = other_ref[...]
    rows = rows_ref[...]
    query_ref[...] = nn(rows, wq_ref[...])
    kv_ref[:, :HEAD_DIM] = nn(rows, wkv_ref[0])
    kv_ref[:, HEAD_DIM:] = nn(rows, wkv_ref[1])


def key_value_kernel(
    flag_ref, rows_ref, dense_ref, bias_ref, adqkv_ref, auk_ref, auv_ref, cos_ref, sin_ref, kv_ref, low_ref, low_t_ref
):
    low = nt(rows_ref[...], adqkv_ref[...])
    low_ref[...] = (2.0 * low).astype(bf)
    low_t_ref[...] = low.T.astype(bf)
    key = dense_ref[:, :HEAD_DIM] + bias_ref[0:1, :].astype(f32) + nn(low_ref[:, RANK : 2 * RANK], auk_ref[...])
    value = dense_ref[:, HEAD_DIM:] + bias_ref[1:2, :].astype(f32) + nn(low_ref[:, 2 * RANK :], auv_ref[...])
    key, value = turned(key, cos_ref[...], sin_ref[...]).astype(bf), value.astype(bf)
    span = key.shape[0] // 2
    for half in range(2):
        rows = place_rows(flag_ref, half, span)
        kv_ref[rows, :HEAD_DIM] = key[half * span : (half + 1) * span]
        kv_ref[rows, HEAD_DIM:] = value[half * span : (half + 1) * span]


def query_kernel(flag_ref, dense_ref, bias_ref, low_ref, auq_ref, cos_ref, sin_ref, q_ref):
    heads, span = q_ref.shape[1], q_ref.shape[2]
    query = dense_ref[...] + bias_ref[...].astype(f32) + nn(low_ref[:, :RANK], auq_ref[...])
    for h in range(heads):
        head = turned(query[:, h * HEAD_DIM : (h + 1) * HEAD_DIM], cos_ref[...], sin_ref[...]).astype(bf)
        q_ref[place_of(flag_ref, 0), h] = head[:span]
        q_ref[place_of(flag_ref, 1), h] = head[span:]


def rows_of(own, half):
    shard = lax.axis_index("tensor")
    return pl.ds(pl.multiple_of((shard if own else 1 - shard) * half, half), half)


def mix_send_kernel(mixed_ref, wo_ref, ado_ref, auo_ref, send_ref, low_ref, low_t_ref):
    low = nt(mixed_ref[...], ado_ref[...])
    low_ref[...] = (2.0 * low).astype(bf)
    low_t_ref[...] = low.T.astype(bf)
    rows = rows_of(False, send_ref.shape[0])
    send_ref[...] = (nn(mixed_ref[rows, :], wo_ref[...]) + nn(low_ref[rows, :], auo_ref[...])).astype(bf)


def mix_own_kernel(mixed_ref, wo_ref, low_ref, auo_ref, own_ref):
    rows = rows_of(True, own_ref.shape[0])
    own_ref[...] = nn(mixed_ref[rows, :], wo_ref[...]) + nn(low_ref[rows, :], auo_ref[...])


def mix_back_kernel(own, flag_ref, rows_ref, wo_ref, ado_ref, auo_ref, mixed_ref, low_t_ref, *refs):
    do_ref, delta_ref, dado_ref, dauo_ref = refs[-4:]
    half = rows_ref.shape[0]
    heads = do_ref.shape[1]
    part = place_of(flag_ref, lax.axis_index("tensor") if own else 1 - lax.axis_index("tensor"))
    places = rows_of(own, half)
    rows, mixed = rows_ref[...], mixed_ref[places, :]
    back = nt(rows, auo_ref[...])
    grad = (nt(rows, wo_ref[...]) + nn((2.0 * back).astype(bf), ado_ref[...])).astype(bf)
    dado = nn(back.T.astype(bf), mixed)
    dauo = nn(low_t_ref[:, places], rows)
    dado_ref[...] = dado if own else refs[2][...] + dado
    dauo_ref[...] = dauo if own else refs[3][...] + dauo
    for h in range(heads):
        cols = slice(h * HEAD_DIM, (h + 1) * HEAD_DIM)
        product = (grad[:, cols].astype(f32) * mixed[:, cols].astype(f32)).T
        do_ref[part, h] = grad[:, cols]
        delta_ref[part, h : h + 1, :] = jnp.sum(product, axis=0, keepdims=True)


def back_query_kernel(
    scale, flag_ref, dq_ref, wq_ref, adq_ref, auq_ref, low_t_ref, rows_ref, cos_ref, sin_ref, total_ref, dadq_ref, dauq_ref, eq
):
    heads, span = dq_ref.shape[1], dq_ref.shape[3]
    for part in range(2):
        rows = slice(part * span, (part + 1) * span)
        for h in range(heads):
            grad = dq_ref[place_of(flag_ref, part), h].T * scale
            eq[rows, h * HEAD_DIM : (h + 1) * HEAD_DIM] = turned(grad, cos_ref[rows, :], -sin_ref[rows, :]).astype(bf)
    query = eq[...]
    back = nt(query, auq_ref[...])
    total_ref[...] = nt(query, wq_ref[...]) + nn((2.0 * back).astype(bf), adq_ref[:RANK, :])
    dadq_ref[...] = nn(back.T.astype(bf), rows_ref[...])
    dauq_ref[...] = nn(low_t_ref[:RANK, :], query)


def back_key_value_kernel(
    flag_ref, dkv_ref, query_ref, wkv_ref, adqkv_ref, auk_ref, auv_ref, low_t_ref, rows_ref, cos_ref, sin_ref, *refs
):
    others = refs[: len(refs) - 7]
    own_ref, send_ref, dadkv_ref, dauk_ref, dauv_ref, total, back_ref = refs[len(refs) - 7 :]
    shard = lax.axis_index("tensor")
    half = own_ref.shape[0]
    grad = dkv_ref[...].astype(f32)
    for ref in others:
        grad = grad + ref[...].astype(f32)
    grad = jnp.where(place_of(flag_ref, 0) == 1, jnp.concatenate([grad[half:], grad[:half]], axis=0), grad)
    ek = turned(grad[:, :HEAD_DIM], cos_ref[...], -sin_ref[...]).astype(bf)
    ev = grad[:, HEAD_DIM:].astype(bf)
    back_ref[:, :RANK] = nt(ek, auk_ref[...])
    back_ref[:, RANK:] = nt(ev, auv_ref[...])
    back = back_ref[...]
    total[...] = (
        query_ref[...] + nt(ek, wkv_ref[0]) + nt(ev, wkv_ref[1]) + nn((2.0 * back).astype(bf), adqkv_ref[RANK:, :])
    )
    own_ref[...] = total[pl.ds(pl.multiple_of(shard * half, half), half), :]
    send_ref[...] = total[pl.ds(pl.multiple_of((1 - shard) * half, half), half), :].astype(bf)
    dadkv_ref[...] = nn(back.T.astype(bf), rows_ref[...])
    dauk_ref[...] = nn(low_t_ref[RANK : 2 * RANK, :], ek)
    dauv_ref[...] = nn(low_t_ref[2 * RANK :, :], ev)


def future_mask(span):
    return lax.broadcasted_iota(jnp.int32, (span, span), 0) <= lax.broadcasted_iota(jnp.int32, (span, span), 1)

EXTRA = 16


def weights_of(s, m, coef, mask):
    if mask is not None:
        s = jnp.where(mask, s, mask_fill)
    m_next = jnp.maximum(m, jnp.max(s, axis=0, keepdims=True))
    p = jnp.exp2((s - m_next) * coef)
    alpha = jnp.exp2((m - m_next) * coef)
    return m_next, alpha, p.astype(bf)


def put_values(vt, kv_ref):
    vt[:HEAD_DIM, :] = kv_ref[:, HEAD_DIM:].astype(f32).T.astype(bf)


def put_ones(vt):
    vt[HEAD_DIM:, :] = jnp.ones((EXTRA, vt.shape[1]), bf)


def pipelined(items, first, second):
    ahead = first(items[0])
    for i, item in enumerate(items):
        now = ahead
        if i + 1 < len(items):
            ahead = first(items[i + 1])
        second(item, now)

def pipelined_three(items, first, second, third):
    ahead, behind = first(items[0]), None
    for i, item in enumerate(items):
        now = ahead
        if i + 1 < len(items):
            ahead = first(items[i + 1])
        done = second(item, now)
        if behind is not None:
            third(*behind)
        behind = (item, done)
    third(*behind)


def attn_fwd_own_kernel(coef, q_ref, kv_ref, m_ref, o_ref, vt):
    heads, span = q_ref.shape[1], q_ref.shape[2]
    put_ones(vt)
    put_values(vt, kv_ref)
    mask = future_mask(span)
    row, place = (lax.broadcasted_iota(jnp.int32, (2 * span, span), axis) for axis in range(2))
    both_mask = row <= place + span

    def first(item):
        half, h = item
        return nt(kv_ref[: (half + 1) * span, :HEAD_DIM], q_ref[half, h])

    def second(item, s):
        half, h = item
        m, _, p = weights_of(s, jnp.full((1, span), mask_fill, f32), coef, both_mask if half else mask)
        m_ref[half, h : h + 1, :] = m
        return p

    def third(item, p):
        half, h = item
        o_ref[half, h] = nn(vt[:, : (half + 1) * span], p)

    pipelined_three([(half, h) for h in range(heads) for half in range(2)], first, second, third)


def halves_of(flag, turn):
    return (1 - flag) * turn, flag * turn + (1 - flag)


def attn_fwd_pieces_kernel(coef, indices, last, flag_ref, q_ref, *refs):
    n = len(indices)
    kv_refs, (m_in, o_in), refs = refs[:n], refs[n : n + 2], refs[n + 2 :]
    if last:
        mixed_ref, lse_ref, m_ref, o_ref, vt = refs
    else:
        m_ref, o_ref, vt = refs
    heads, span = q_ref.shape[1], q_ref.shape[2]
    put_ones(vt)
    m_ref[...] = m_in[...]
    o_ref[...] = o_in[...]
    for i in range(n):
        kv_ref, flag = kv_refs[i], flag_of(flag_ref, indices[i])
        put_values(vt, kv_ref)

        def first(item, kv_ref=kv_ref, flag=flag):
            keys, half = halves_of(flag, item[0])
            return nt(kv_ref[pl.ds(pl.multiple_of(keys * span, span), span), :HEAD_DIM], q_ref[half, item[1]])

        def second(item, s, flag=flag):
            half, h = halves_of(flag, item[0])[1], item[1]
            m, alpha, p = weights_of(s, m_ref[half, h : h + 1, :], coef, None)
            m_ref[half, h : h + 1, :] = m
            return alpha, p

        def third(item, weights, flag=flag):
            (keys, half), h = halves_of(flag, item[0]), item[1]
            alpha, p = weights
            values_t = vt[:, pl.ds(pl.multiple_of(keys * span, span), span)]
            o_ref[half, h] = o_ref[half, h] * alpha + nn(values_t, p)

        pipelined_three([(turn, h) for turn in range(2) for h in range(heads)], first, second, third)
    if last:
        for half in range(2):
            for h in range(heads):
                sums = o_ref[half, h, HEAD_DIM : HEAD_DIM + 1, :]
                o = o_ref[half, h, :HEAD_DIM, :] / sums
                mixed_ref[place_rows(flag_ref, half, span), h * HEAD_DIM : (h + 1) * HEAD_DIM] = o.T.astype(bf)
                lse_ref[half, h : h + 1, :] = m_ref[half, h : h + 1, :] * coef + jnp.log2(sums)


def attn_state(heads, span):
    return (shape(2, heads, span), shape(2, heads, HEAD_DIM + EXTRA, span))


def attn_fwd_own(q, kv, coef):
    _, heads, span, _ = q.shape
    return call(
        functools.partial(attn_fwd_own_kernel, coef), "attn_fwd_own", attn_state(heads, span), [q, kv],
        [pltpu.VMEM((HEAD_DIM + EXTRA, 2 * span), bf)], flops=24 * heads * span * span * HEAD_DIM, limit=20,
    )


def attn_fwd_pieces(flags, indices, q, pieces, state, coef, last):
    _, heads, span, _ = q.shape
    outs = attn_state(heads, span)
    if last:
        outs = (shape(2 * span, heads * HEAD_DIM, dtype=bf), shape(2, heads, span)) + outs
    return call(
        functools.partial(attn_fwd_pieces_kernel, coef, indices, last), "attn_fwd_pieces", outs, [flags, q, *pieces, *state],
        [pltpu.VMEM((HEAD_DIM + EXTRA, 2 * span), bf)], flops=16 * len(pieces) * heads * span * span * HEAD_DIM, limit=20,
    )


def bwd_block(s, dp, lse_ref, delta_ref, half, h, coef, mask):
    p = jnp.exp2(s * coef - lse_ref[half, h : h + 1, :])
    if mask is not None:
        p = jnp.where(mask, p, 0.0)
    ds = p * (dp - delta_ref[half, h : h + 1, :])
    return p.astype(bf), ds.astype(bf)

def attn_bwd_kernel(coef, scale, indices, own, has_state, flag_ref, q_ref, do_ref, lse_ref, delta_ref, *refs):
    n = len(indices)
    kv_refs = refs[:n]
    k = n
    if has_state:
        dq_in = refs[k]; k += 1
    dkv_refs = refs[k : k + n]
    dq_ref, kt, pbuf, sbuf = refs[k + n :]
    heads, span = q_ref.shape[1], q_ref.shape[2]
    if has_state:
        dq_ref[...] = dq_in[...]
    else:
        dq_ref[...] = jnp.zeros_like(dq_ref)
    def do_item(kv_ref, items, keyrows, mask_of):
        nk = keyrows.stop - keyrows.start
        def first(it):
            i, half, h = it
            return nt(kv_ref[keyrows, :HEAD_DIM], q_ref[half, h]), nt(kv_ref[keyrows, HEAD_DIM:], do_ref[half, h])
        def second(it, sd):
            i, half, h = it
            p, ds = bwd_block(sd[0], sd[1], lse_ref, delta_ref, half, h, coef, mask_of(half))
            cols = slice((i * heads + h) * span, (i * heads + h + 1) * span)
            pbuf[:nk, cols] = p
            sbuf[:nk, cols] = ds
            return ds
        def third(it, ds):
            i, half, h = it
            dq_ref[half, h] += nn(kt[:, keyrows], ds)
        pipelined_three([(i, half, h) for i, half in enumerate(items) for h in range(heads)], first, second, third)
        width = len(items) * heads * span
        lo = items[0]
        q_all = q_ref[lo : lo + len(items)].reshape(width, HEAD_DIM)
        do_all = do_ref[lo : lo + len(items)].reshape(width, HEAD_DIM)
        return nn(sbuf[:nk, :width], q_all) * scale, nn(pbuf[:nk, :width], do_all)
    for i in range(n):
        kv_ref, out = kv_refs[i], dkv_refs[i]
        kt[...] = kv_ref[:, :HEAD_DIM].astype(f32).T.astype(bf)
        lo, hi, both = slice(0, span), slice(span, 2 * span), slice(0, 2 * span)
        if own and i == 0:
            mask = future_mask(span)
            dk, dv = do_item(kv_ref, [0, 1], lo, lambda half: mask if half == 0 else None)
            out[lo, :HEAD_DIM] = dk.astype(bf)
            out[lo, HEAD_DIM:] = dv.astype(bf)
            dk, dv = do_item(kv_ref, [1], hi, lambda half: mask)
            out[hi, :HEAD_DIM] = dk.astype(bf)
            out[hi, HEAD_DIM:] = dv.astype(bf)
        else:
            flag = flag_of(flag_ref, indices[i])

            def first(item, kv_ref=kv_ref, flag=flag):
                (keys, half), h = halves_of(flag, item[0]), item[1]
                rows = pl.ds(pl.multiple_of(keys * span, span), span)
                return nt(kv_ref[rows, :HEAD_DIM], q_ref[half, h]), nt(kv_ref[rows, HEAD_DIM:], do_ref[half, h])

            def second(item, sd, flag=flag):
                turn, h = item
                half = halves_of(flag, turn)[1]
                p, ds = bwd_block(sd[0], sd[1], lse_ref, delta_ref, half, h, coef, None)
                cols = slice(h * span, (h + 1) * span)
                pbuf[turn * span : (turn + 1) * span, cols] = p
                sbuf[turn * span : (turn + 1) * span, cols] = ds
                return ds

            def third(item, ds, flag=flag):
                (keys, half), h = halves_of(flag, item[0]), item[1]
                dq_ref[half, h] += nn(kt[:, pl.ds(pl.multiple_of(keys * span, span), span)], ds)

            pipelined_three([(turn, h) for turn in range(2) for h in range(heads)], first, second, third)
            width = heads * span
            both = []
            for turn in range(2):
                keys, half = halves_of(flag, turn)
                rows = slice(turn * span, (turn + 1) * span)
                both.append((
                    nn(sbuf[rows, :width], q_ref[half].reshape(width, HEAD_DIM)) * scale,
                    nn(pbuf[rows, :width], do_ref[half].reshape(width, HEAD_DIM)),
                ))
            earlier = flag.astype(f32)
            for part in range(2):
                cols = slice(part * HEAD_DIM, (part + 1) * HEAD_DIM)
                out[lo, cols] = (both[0][part] + both[1][part] * earlier).astype(bf)
                out[hi, cols] = (both[1][part] * (1.0 - earlier)).astype(bf)


def attn_bwd(flags, indices, q, do, lse, delta, pieces, dq_state, coef, scale, own):
    _, heads, span, _ = q.shape
    n = len(pieces)
    outs = tuple(jax.ShapeDtypeStruct((2 * span, 2 * HEAD_DIM), bf) for _ in range(n)) + (jax.ShapeDtypeStruct((2, heads, HEAD_DIM, span), f32),)
    ins = [flags, q, do, lse, delta, *pieces] + ([dq_state] if dq_state is not None else [])
    return pl.pallas_call(functools.partial(attn_bwd_kernel, coef, scale, indices, own, dq_state is not None), out_shape=outs,
        in_specs=[VM] * len(ins), out_specs=(VM,) * len(outs),
        scratch_shapes=[pltpu.VMEM((HEAD_DIM, 2 * span), bf), pltpu.VMEM((2 * span, 2 * heads * span), bf), pltpu.VMEM((2 * span, 2 * heads * span), bf)],
        cost_estimate=pl.CostEstimate(flops=2*5*2*n*heads*span*span*HEAD_DIM*2, bytes_accessed=4_000_000, transcendentals=0),
        compiler_params=pltpu.CompilerParams(vmem_limit_bytes=30 << 20), name="attn_bwd_pieces")(*ins)


TILE = 512


def steps_of(columns, begin=0):
    edges = [begin, begin + TILE // 2, begin + TILE]
    while columns - edges[-1] > 2 * TILE:
        edges.append(edges[-1] + 2 * TILE)
    if columns - edges[-1] > TILE:
        edges.append(edges[-1] + TILE)
    edges.append(columns)
    return list(zip(edges, edges[1:]))


def act_back_kernel(bounds, own_ref, other_ref, wd_hbm, *refs):
    out_hbm, rows_ref, wd, out, in_sems, out_sems = refs[-6:]
    half, first = own_ref.shape[0], bounds[0][0]
    parts = [slice(low - first, high - first) for low, high in bounds]
    copies = [
        pltpu.make_async_copy(wd_hbm.at[low:high], wd.at[part], in_sems.at[i])
        for i, ((low, high), part) in enumerate(zip(bounds, parts))
    ]
    for copy in copies:
        copy.start()
    rows_ref[:half, :] = own_ref[...]
    rows_ref[half:, :] = other_ref[...]
    results = []
    for i, ((low, high), part) in enumerate(zip(bounds, parts)):
        copies[i].wait()
        out[:, part] = nt(rows_ref[...], wd[part, :]).astype(bf)
        result = pltpu.make_async_copy(out.at[:, part], out_hbm.at[:, low:high], out_sems.at[i])
        result.start()
        results.append(result)
    for result in results:
        result.wait()


def act_back(own, other, wd, bounds, held=None):
    half, width = own.shape
    columns, count = bounds[-1][1] - bounds[0][0], len(bounds)
    return pl.pallas_call(
        functools.partial(act_back_kernel, bounds),
        out_shape=pltpu.HBM((2 * half, wd.shape[0]), bf),
        in_specs=[VM, VM, HB] + ([] if held is None else [HB]),
        out_specs=HB,
        scratch_shapes=[
            pltpu.VMEM((2 * half, width), bf), pltpu.VMEM((columns, width), bf), pltpu.VMEM((2 * half, columns), bf),
            pltpu.SemaphoreType.DMA((count,)), pltpu.SemaphoreType.DMA((count,)),
        ],
        input_output_aliases={} if held is None else {3: 0},
        cost_estimate=pl.CostEstimate(flops=4 * half * width * columns, bytes_accessed=2 * width * columns, transcendentals=0),
        compiler_params=pltpu.CompilerParams(vmem_limit_bytes=30 << 20),
        name="act_back",
    )(own, other, in_hbm(wd), *([] if held is None else [in_hbm(held)]))


def whole(*dims):
    return pl.BlockSpec(dims, lambda i: (0,) * len(dims), pipeline_mode=pl.Buffered(1))


def ffn_kernel(
    tile, tiles, hidden, x_own, x_other, g_own, g_other, gact_ref, adgu_ref, auf_ref, wgu_ref, adf_ref, augu_ref,
    gx_own, gx_send, act_ref, flow_ref, dadgu_ref, dauf_ref, daugu_ref, dadf_ref,
    x_ref, g_ref, gx_acc, xlow, xlow_t, fback, fback_t, flow, back,
):
    step = pl.program_id(0)
    half = x_own.shape[0]

    @pl.when(step == 0)
    def prepare():
        for target, own, other in ((x_ref, x_own, x_other), (g_ref, g_own, g_other)):
            target[:half, :] = own[...]
            target[half:, :] = other[...]
        low = nt(x_ref[...], adgu_ref[...])
        xlow[...] = (low * 2.0).astype(bf)
        xlow_t[...] = low.T.astype(bf)
        fb = nt(g_ref[...], auf_ref[...])
        fback[...] = (fb * 2.0).astype(bf)
        fback_t[...] = fb.T.astype(bf)
        gx_acc[...] = jnp.zeros_like(gx_acc)
        flow[...] = jnp.zeros_like(flow)
        back[...] = jnp.zeros_like(back)

    def work(width):
        x = x_ref[...]
        wg, wu = wgu_ref[0, :, :width], wgu_ref[1, :, :width]
        aug, auu, adf = augu_ref[:RANK, :width], augu_ref[RANK:, :width], adf_ref[:, :width]
        gate = nn(x, wg) + nn(xlow[:, :RANK], aug)
        up = nn(x, wu) + nn(xlow[:, RANK:], auu)
        gact = gact_ref[:, :width].astype(f32) + nn(fback[...], adf)
        sig = 1.0 / (1.0 + jnp.exp(-gate))
        silu = gate * sig
        act = (silu * up).astype(bf)
        ggate = (gact * up * (sig + silu * (1.0 - sig))).astype(bf)
        gup = (gact * silu).astype(bf)
        act_ref[:, :width] = act
        flow[...] += nt(act, adf)
        gx_acc[...] += nt(ggate, wg) + nt(gup, wu)
        back[:, :RANK] += nt(ggate, aug)
        back[:, RANK:] += nt(gup, auu)
        daugu_ref[:RANK, :width] = nn(xlow_t[:RANK, :], ggate)
        daugu_ref[RANK:, :width] = nn(xlow_t[RANK:, :], gup)
        dadf_ref[:, :width] = nn(fback_t[...], act)

    tail = hidden - (tiles - 1) * tile
    if tail == tile:
        work(tile)
    else:
        @pl.when(step < tiles - 1)
        def body():
            work(tile)

        @pl.when(step == tiles - 1)
        def part():
            work(tail)

    @pl.when(step == tiles - 1)
    def finish():
        gx_acc[...] += nn((back[...] * 2.0).astype(bf), adgu_ref[...])
        gx_own[...] = gx_acc[:half, :]
        gx_send[...] = gx_acc[half:, :].astype(bf)
        flow_ref[...] = (flow[...] * 2.0).astype(bf)
        dadgu_ref[...] = nn(back[...].T.astype(bf), x_ref[...])
        dauf_ref[...] = nn(flow[...].T.astype(bf), g_ref[...])


def ffn(x_own, x_other, g_own, g_other, gact, adgu, auf, wgu, adf, augu, tile=TILE):
    rows, width = 2 * x_own.shape[0], x_own.shape[1]
    hidden = wgu.shape[2]
    tiles = -(-hidden // tile)
    half = rows // 2
    cols = lambda r: pl.BlockSpec((r, tile), lambda i: (0, i))
    outs = (
        shape(half, width), shape(half, width, dtype=bf), pltpu.HBM((rows, hidden), bf), shape(rows, RANK, dtype=bf),
        shape(2 * RANK, width), shape(RANK, width), shape(2 * RANK, hidden), shape(RANK, hidden),
    )
    return pl.pallas_call(
        functools.partial(ffn_kernel, tile, tiles, hidden),
        grid=(tiles,),
        out_shape=outs,
        in_specs=[whole(half, width)] * 4 + [cols(rows), whole(2 * RANK, width), whole(RANK, width),
                  pl.BlockSpec((2, width, tile), lambda i: (0, 0, i)), cols(RANK), cols(2 * RANK)],
        out_specs=(whole(half, width), whole(half, width), cols(rows), whole(rows, RANK), whole(2 * RANK, width),
                   whole(RANK, width), cols(2 * RANK), cols(RANK)),
        scratch_shapes=[
            pltpu.VMEM((rows, width), bf), pltpu.VMEM((rows, width), bf), pltpu.VMEM((rows, width), f32),
            pltpu.VMEM((rows, 2 * RANK), bf), pltpu.VMEM((2 * RANK, rows), bf), pltpu.VMEM((rows, RANK), bf),
            pltpu.VMEM((RANK, rows), bf), pltpu.VMEM((rows, RANK), f32), pltpu.VMEM((rows, 2 * RANK), f32),
        ],
        cost_estimate=pl.CostEstimate(flops=8 * rows * width * hidden, bytes_accessed=6 * width * hidden, transcendentals=rows * hidden),
        compiler_params=pltpu.CompilerParams(vmem_limit_bytes=36 << 20),
        name="ffn",
    )(x_own, x_other, in_hbm(g_own), in_hbm(g_other), in_hbm(gact), adgu, auf, in_hbm(wgu), adf, augu)


def down_kernel(bounds, start_refs, act_hbm, wd_hbm, total, act, wd, act_sems, wd_sems):
    low = bounds[0][0]
    copies = []
    for i, (begin, end) in enumerate(bounds):
        rows = slice(begin - low, end - low)
        copies.append((
            pltpu.make_async_copy(act_hbm.at[:, begin:end], act.at[:, rows], act_sems.at[i]),
            pltpu.make_async_copy(wd_hbm.at[begin:end], wd.at[rows], wd_sems.at[i]),
        ))
        for copy in copies[-1]:
            copy.start()
    total[...] = nn(start_refs[0][...], start_refs[1][...]) if len(start_refs) == 2 else start_refs[0][...]
    for i, (begin, end) in enumerate(bounds):
        rows = slice(begin - low, end - low)
        for copy in copies[i]:
            copy.wait()
        total[...] += nn(act[:, rows], wd[rows, :])


def down_first_kernel(bounds, flow_ref, auf_ref, act_hbm, wd_hbm, total, *scratch):
    down_kernel(bounds, (flow_ref, auf_ref), act_hbm, wd_hbm, total, *scratch)


def down_last_kernel(bounds, start_ref, act_hbm, wd_hbm, own_ref, send_ref, total, *scratch):
    down_kernel(bounds, (start_ref,), act_hbm, wd_hbm, total, *scratch)
    half = own_ref.shape[0]
    own_ref[...] = total[:half, :]
    send_ref[...] = total[half:, :].astype(bf)


def down(act, wd, start, bounds, last):
    rows, width = act.shape[0], wd.shape[1]
    half, columns, count = rows // 2, bounds[-1][1] - bounds[0][0], len(bounds)
    outs = (shape(half, width), shape(half, width, dtype=bf)) if last else (shape(rows, width),)
    scratch = [
        pltpu.VMEM((rows, columns), bf), pltpu.VMEM((columns, width), bf), pltpu.SemaphoreType.DMA((count,)),
        pltpu.SemaphoreType.DMA((count,)),
    ]
    return pl.pallas_call(
        functools.partial(down_last_kernel if last else down_first_kernel, bounds),
        out_shape=outs,
        in_specs=[VM] * len(start) + [HB, HB],
        out_specs=(VM,) * len(outs),
        scratch_shapes=([pltpu.VMEM((rows, width), f32)] if last else []) + scratch,
        cost_estimate=pl.CostEstimate(flops=2 * rows * width * columns, bytes_accessed=2 * width * columns, transcendentals=0),
        compiler_params=pltpu.CompilerParams(vmem_limit_bytes=28 << 20),
        name="down",
    )(*start, in_hbm(act), in_hbm(wd))


def per_device(
    tokens, cotangent, positions, adapter_choice, attn_gain, query_weight, query_bias, key_value_weight,
    key_value_bias, output_weight, ffn_gain, gate_upper_weight, down_weight, adapt_in, adapt_out,
):
    dp = lax.axis_index("dp")
    groups = lax.axis_size("seq")
    rings = groups // 2
    width, head_width = query_weight.shape
    heads = head_width // HEAD_DIM
    hidden = down_weight.shape[0]
    token_pos = positions[0]
    tok_count = token_pos.shape[0]
    span = tok_count // 2
    scale = HEAD_DIM ** (-0.5)
    coef = scale * math.log2(math.e)
    wide_in, wide_out = adapt_in.shape[2], adapt_out.shape[2]
    lanes_in = rounded_up(wide_in + 1, 128)
    lanes = lanes_in + rounded_up(wide_out, 128)
    widths = (width, head_width, hidden)
    sizes = (rings, wide_in, wide_out, lanes_in, widths)

    def to_pair(value):
        return lax.ppermute(value, "tensor", [(0, 1), (1, 0)])

    def to_other_sequence(value, pairs=((0, 1), (1, 0))):
        return lax.ppermute(value, "dp", list(pairs))

    def to_side(value):
        return lax.ppermute(value, "seq", [(i, i ^ 1) for i in range(groups)])

    def along_ring(value, steps):
        return lax.ppermute(value, "seq", [(i, (i + 2 * steps) % groups) for i in range(groups)])

    cycle = list(range(0, groups, 2)) + list(range(groups - 1, 0, -2))
    hops = [(cycle[i], cycle[(i + 1) % groups]) for i in range(groups)]

    def to_next(value):
        return lax.ppermute(value, "seq", hops)

    def to_last(value):
        return lax.ppermute(value, "seq", [(end, begin) for begin, end in hops])

    def after(value, *others):
        return lax.optimization_barrier((value, *others))[0]

    inputs, grad_out = tokens[0], cotangent[0]
    half = inputs.shape[0]
    attn_gain, ffn_gain = attn_gain[None], ffn_gain[None]

    def over_ring(piece):
        return [piece] + [along_ring(piece, step) for step in range(1, rings)]

    slice_own, slice_other, chosen = call(
        functools.partial(select_kernel, lanes_in, span), "select",
        [shape(RANK, lanes, dtype=bf)] * 2 + [shape(8, 128)], [adapter_choice, positions, adapt_in, adapt_out],
        [
            pltpu.SMEM(adapter_choice.shape, jnp.int32), pltpu.SMEM(positions.shape, jnp.int32),
            pltpu.VMEM((2, RANK, wide_in), bf), pltpu.VMEM((2, RANK, wide_out), bf), pltpu.SemaphoreType.DMA((6,)),
        ],
        left=4,
    )
    slice_other = to_other_sequence(slice_other)
    lane = lax.broadcasted_iota(jnp.int32, (RANK, lanes), 1)
    run_lane = (lane >= wide_in) & (lane < lanes_in)
    grad_other = to_pair(after(grad_out, slice_own))
    slice_other = after(slice_other, grad_other)
    first_slice = jnp.where((dp == 0) | run_lane, slice_own, slice_other)
    second_slice = jnp.where(dp == 0, slice_other, slice_own)

    (normed,) = call(norm_kernel, "norm", [shape(half, width, dtype=bf)], [inputs, attn_gain])
    normed_other = to_pair(normed)
    arrived = over_ring(jnp.stack([first_slice, second_slice]))
    middle = 6 * TILE
    act_grad = act_back(grad_out, grad_other, down_weight, steps_of(middle))
    arrived[1] = after(arrived[1], act_grad)
    own_slices = jnp.stack([piece[0] for piece in arrived])
    own_second = jnp.stack([piece[1] for piece in arrived])
    side_slices = to_side(own_slices)
    pair_slices = to_pair(own_slices)
    normed_rows, query_dense, kv_dense = call(
        dense_kernel, "dense", [shape(tok_count, width, dtype=bf), shape(tok_count, head_width), shape(tok_count, 2 * HEAD_DIM)],
        [normed, after(normed_other, own_slices), query_weight, key_value_weight],
        flops=2 * tok_count * width * (head_width + 2 * HEAD_DIM),
    )
    frequency = jnp.power(rope_base, -(jnp.arange(HEAD_DIM // 2, dtype=f32) * 2.0) / HEAD_DIM)
    angles = token_pos.astype(f32)[:, None] * frequency[None, :]
    cosine, sine = jnp.cos(angles), jnp.sin(angles)
    cosine = jnp.concatenate([cosine, cosine], axis=1)
    sine = jnp.concatenate([-sine, sine], axis=1)

    side_slices = after(side_slices, kv_dense)
    first_slices = [own_slices, side_slices, pair_slices, to_pair(side_slices)]
    side_second = to_side(after(own_second, side_slices))
    slices_in = -(-4 * width // wide_in)
    slices_out = -(-(2 * width + 4 * HEAD_DIM) // wide_out)
    flags, adqkv, auq, auk, auv, ado, auo = call(
        functools.partial(unpack_first_kernel, *sizes), "unpack_first",
        [shape(rounded_up(groups, 8), 128)]
        + [
            shape(*dims, dtype=bf)
            for dims in (
                (3 * RANK, width), (RANK, head_width), (RANK, HEAD_DIM), (RANK, HEAD_DIM), (RANK, head_width), (RANK, width),
            )
        ],
        list(first_slices),
        [
            pltpu.VMEM((2 * groups, RANK, lanes), bf),
            pltpu.VMEM((RANK, rounded_up(slices_in * wide_in, 128) + 256), f32),
            pltpu.VMEM((RANK, rounded_up(slices_out * wide_out, 128) + 256), f32),
            pltpu.SMEM((groups,), jnp.int32),
        ],
    )
    kv, low, low_t = call(
        key_value_kernel, "key_value",
        [shape(tok_count, 2 * HEAD_DIM, dtype=bf), shape(tok_count, 3 * RANK, dtype=bf), shape(3 * RANK, tok_count, dtype=bf)],
        [flags, normed_rows, kv_dense, key_value_bias, adqkv, auk, auv, cosine, sine],
        flops=2 * tok_count * width * 2 * RANK,
    )

    (queries,) = call(
        query_kernel, "query", [shape(2, heads, span, HEAD_DIM, dtype=bf)],
        [flags, query_dense, query_bias[None], low, auq, cosine, sine], flops=2 * tok_count * width * RANK,
    )
    state = attn_fwd_own(queries, kv, coef)
    pieces, from_last, from_next = [kv], kv, kv
    for step in range(1, rings + 1):
        from_last, from_next = to_next(from_last), to_last(from_next)
        if step == 1:
            bounds = [(middle, middle + TILE // 2), (middle + TILE // 2, middle + 2 * TILE), (middle + 2 * TILE, hidden)]
            act_grad = act_back(after(grad_out, state[0], side_second), grad_other, down_weight, bounds, act_grad)
            from_last = after(from_last, act_grad)
        if step < rings:
            from_last, from_next, _ = lax.optimization_barrier((from_last, from_next, state[0]))
        if step == rings:
            pair_second = to_pair(after(own_second, pieces[-1]))
            state = (after(state[0], pair_second), *state[1:])
        pieces += [from_last, from_next][: 2 if step < rings else 1]
        indices = tuple(range(2 * step - 1, len(pieces)))
        result = attn_fwd_pieces(flags, indices, queries, pieces[2 * step - 1 :], state, coef, step == rings)
        state = result[-2:]
    mixed, lse = result[0], result[1]

    branch_send, mix_low, mix_low_t = call(
        mix_send_kernel, "mix_send",
        [shape(half, width, dtype=bf), shape(tok_count, RANK, dtype=bf), shape(RANK, tok_count, dtype=bf)],
        [mixed, output_weight, ado, auo], flops=2 * half * width * head_width,
    )
    branch_other = to_pair(branch_send)
    second_slices = [own_second, side_second, pair_second, to_pair(side_second)]
    (branch_own,) = call(
        mix_own_kernel, "mix_own", [shape(half, width)], [mixed, output_weight, mix_low, auo],
        flops=2 * half * width * head_width,
    )
    hidden_rows, normed_ffn = call(
        residual_kernel, "residual", [shape(half, width), shape(half, width, dtype=bf)],
        [inputs, branch_own, after(branch_other, branch_own, second_slices[3]), ffn_gain],
    )
    begin_in, begin_out, first_in, first_out = bases(wide_in, wide_out, widths)
    adgu, augu, adf, auf = call(
        functools.partial(unpack_second_kernel, *sizes), "unpack_second",
        [shape(*dims, dtype=bf) for dims in ((2 * RANK, width), (2 * RANK, hidden), (RANK, hidden), (RANK, width))],
        list(first_slices) + list(second_slices),
        [
            pltpu.VMEM((4 * groups, RANK, lanes), bf),
            pltpu.VMEM((RANK, rounded_up(4 * groups * wide_in, 128) + 256 - first_in), f32),
            pltpu.VMEM((RANK, rounded_up(4 * groups * wide_out, 128) + 256 - first_out), f32),
        ],
    )
    gx_own, gx_send, act, flow, dadgu, dauf, daugu, dadf = ffn(
        normed_ffn, to_pair(normed_ffn), grad_out, grad_other, act_grad, adgu, auf, gate_upper_weight, adf, augu
    )
    ad_lanes = rounded_up(4 * groups * wide_in, 128) + 256
    au_lanes = rounded_up(4 * groups * wide_out, 128) + 256

    def added(*values):
        total = values[0].astype(f32)
        for value in values[1:]:
            total = total + value.astype(f32)
        return total.astype(bf)

    grad_hidden, grad_low = call(
        hidden_back_kernel, "hidden_back", [shape(half, width), shape(half, width, dtype=bf)],
        [hidden_rows, grad_out, gx_own, to_pair(gx_send), ffn_gain],
    )
    grad_low_other = to_pair(grad_low)
    fixed = [output_weight, ado, auo, mixed, mix_low_t]
    outs = [shape(2, heads, span, HEAD_DIM, dtype=bf), shape(2, heads, span), shape(RANK, head_width), shape(RANK, width)]
    partial = call(
        functools.partial(mix_back_kernel, True), "mix_back", outs, [flags, grad_low, *fixed], flops=2 * half * width * head_width,
    )
    grad_mixed, delta, dado, dauo = call(
        functools.partial(mix_back_kernel, False), "mix_back_other", outs,
        [flags, after(grad_low_other, partial[0]), *fixed, *partial], flops=2 * half * width * head_width,
        aliases={7 + i: i for i in range(4)},
    )

    def backward(indices, state_dq):
        return attn_bwd(
            flags, indices, queries, grad_mixed, lse, delta, [pieces[index] for index in indices], state_dq, coef, scale,
            indices == (0,),
        )

    state_dq, from_last, from_next = None, None, None
    for step in range(rings, 0, -1):
        onward, *returned, state_dq = backward((2 * rings - 1,) if step == rings else (2 * step, 2 * step - 1), state_dq)
        if from_last is not None:
            onward = added(onward, from_last)
        if from_next is not None:
            returned = [added(returned[0], from_next)]
        from_last = to_next(onward)
        if returned:
            from_next = to_last(returned[0])
        state_dq = after(state_dq, onward, *returned)
    own_term, state_dq = backward((0,), state_dq)
    gn_query, dadq, dauq = call(
        functools.partial(back_query_kernel, scale), "back_query",
        [shape(tok_count, width), shape(RANK, width), shape(RANK, head_width)],
        [flags, state_dq, query_weight, adqkv, auq, low_t, normed_rows, cosine, sine],
        [pltpu.VMEM((tok_count, head_width), bf)], flops=2 * tok_count * width * head_width,
    )
    from_last = after(from_last, gn_query)
    gn_own, gn_send, dadkv, dauk, dauv = call(
        back_key_value_kernel, "back_key_value",
        [
            shape(half, width), shape(half, width, dtype=bf), shape(2 * RANK, width), shape(RANK, HEAD_DIM),
            shape(RANK, HEAD_DIM),
        ],
        [
            flags, own_term, gn_query, key_value_weight, adqkv, auk, auv, low_t, normed_rows, cosine, sine, from_last, from_next,
        ],
        [pltpu.VMEM((tok_count, width), f32), pltpu.VMEM((tok_count, 2 * RANK), f32)],
        flops=2 * tok_count * width * 2 * HEAD_DIM, limit=20,
    )
    (packed,) = call(
        functools.partial(pack_kernel, *sizes), "pack", [shape(2, 2, rings, 2, RANK, lanes, dtype=bf)],
        [dadq, dadkv, dado, dadgu, dadf, dauq, dauk, dauv, dauo, daugu, dauf],
        [pltpu.VMEM((RANK, ad_lanes), f32), pltpu.VMEM((RANK, au_lanes), f32)],
    )
    from_pair = to_pair(packed[1])
    near, far = added(packed[0, 0], from_pair[0]), added(packed[0, 1, 1:], from_pair[1, 1:])
    from_side = to_side(far)
    own_side = to_side(after(added(packed[0, 1, 0], from_pair[1, 0]), far))
    middle = 5 * TILE
    (out_total,) = down(after(act, far), down_weight, (flow, auf), steps_of(middle), False)
    from_side = after(from_side, out_total)
    sums = [added(near[place], from_side[place - 1]) for place in range(1, rings)]
    from_ring = [along_ring(sums[place - 1], -place) for place in range(1, rings)]
    out_own, out_send = down(after(act, *sums), down_weight, (out_total,), steps_of(hidden, middle), True)
    from_ring[0] = after(from_ring[0], out_own)
    total = added(near[0], own_side, *from_ring)
    (grad_tokens,) = call(
        token_back_kernel, "token_back", [shape(half, width)],
        [inputs, grad_hidden, gn_own, after(to_pair(gn_send), total), attn_gain],
    )
    output = (hidden_rows + (out_own + to_pair(out_send).astype(f32))).astype(bf)
    other_total = after(to_other_sequence(total[1]), output, grad_tokens)
    factor = adapter_scale * (adapter_choice.shape[0] * tok_count * groups) ** (-0.5)
    adapt_in_grad, adapt_out_grad = call(
        functools.partial(place_kernel, lanes_in, factor), "place",
        [shape(*adapt_in.shape), shape(*adapt_out.shape)],
        [chosen, total[0], other_total],
    )
    return (output[None], grad_tokens[None], adapt_in_grad, adapt_out_grad)


def solution(mesh):
    return jax.shard_map(
        per_device,
        mesh=mesh,
        in_specs=(
            P("dp", ("seq", "tensor"), None),
            P("dp", ("seq", "tensor"), None),
            P("dp", "seq"),
            P(),
            P(),
            P(None, "tensor"),
            P("tensor"),
            P(None, None, "tensor"),
            P(None, "tensor"),
            P("tensor", None),
            P(),
            P(None, None, "tensor"),
            P("tensor", None),
            P(None, None, ("dp", "seq", "tensor")),
            P(None, None, ("dp", "seq", "tensor")),
        ),
        out_specs=(
            P("dp", ("seq", "tensor"), None),
            P("dp", ("seq", "tensor"), None),
            P(None, None, ("dp", "seq", "tensor")),
            P(None, None, ("dp", "seq", "tensor")),
        ),
        check_vma=False,
    )
```
